32 devices in a mesh: fsdp: 8 (over y, x, core), rep: 4 (over z).
Axes of the slice: x: 2, y: 2, z: 4, core: 2. Of those that a mesh axis runs over, the one named last changes fastest.
Arguments:
- tokens: bfloat16 [13312, 768], P(('fsdp', 'rep')), may hold values from -6 to 6
- starts: int32 [32, 4], P(('fsdp', 'rep')), may hold values from 0 to 415, as said below
- routes: int32 [13312, 1], P(('fsdp', 'rep')), may hold values from 0 to 2; in each aligned block of 416 rows (0 to 415, 416 to 831, ...) at most 208 rows name the same one
- norm1_gain: bfloat16 [768], P('fsdp'), may hold values from 0.5 to 1.5
- norm1_bias: bfloat16 [768], P('fsdp'), may hold values from -1 to 1
- query_weight: bfloat16 [768, 768], P('fsdp'), may hold values from -0.21875 to 0.21875
- query_bias: bfloat16 [768], P('fsdp'), may hold values from -1.5 to 1.5
- key_weight: bfloat16 [768, 768], P('fsdp'), may hold values from -0.21875 to 0.21875
- value_weight: bfloat16 [768, 768], P('fsdp'), may hold values from -0.21875 to 0.21875
- value_bias: bfloat16 [768], P('fsdp'), may hold values from -1 to 1
- out_weight: bfloat16 [768, 768], P('fsdp'), may hold values from -2 to 2
- out_bias: bfloat16 [768], P('fsdp'), may hold values from -1 to 1
- norm2_gain: bfloat16 [768], P('fsdp'), may hold values from 0.5 to 1.5
- norm2_bias: bfloat16 [768], P('fsdp'), may hold values from -1 to 1
- expert_in: bfloat16 [3, 768, 3072], P(None, 'fsdp'), may hold values from -0.21875 to 0.21875
- expert_in_bias: bfloat16 [3, 3072], P(None, 'fsdp'), may hold values from -1 to 1
- expert_out: bfloat16 [3, 3072, 768], P(None, 'fsdp'), may hold values from -0.109375 to 0.109375
- expert_out_bias: bfloat16 [3, 768], P(None, 'fsdp'), may hold values from -1 to 1
- cotangent: bfloat16 [13312, 768], P(('fsdp', 'rep')), may hold values from -6 to 6
Outputs:
- output: bfloat16 [13312, 768], P(('fsdp', 'rep'))
- input_grad: float32 [13312, 768], P(('fsdp', 'rep'))
- grad_norm1_gain: float32 [768], P('fsdp')
- grad_norm1_bias: float32 [768], P('fsdp')
- grad_query_weight: float32 [768, 768], P('fsdp')
- grad_query_bias: float32 [768], P('fsdp')
- grad_key_weight: float32 [768, 768], P('fsdp')
- grad_value_weight: float32 [768, 768], P('fsdp')
- grad_value_bias: float32 [768], P('fsdp')
- grad_out_weight: float32 [768, 768], P('fsdp')
- grad_out_bias: float32 [768], P('fsdp')
- grad_norm2_gain: float32 [768], P('fsdp')
- grad_norm2_bias: float32 [768], P('fsdp')
- grad_expert_in: float32 [3, 768, 3072], P(None, 'fsdp')
- grad_expert_in_bias: float32 [3, 3072], P(None, 'fsdp')
- grad_expert_out: float32 [3, 3072, 768], P(None, 'fsdp')
- grad_expert_out_bias: float32 [3, 768], P(None, 'fsdp')
The draws below stay inside these ranges and needn't reach their ends.
Inputs may be any that keep to these rules, and one draw needn't show every extreme that they name: Each row's first start is 0 and its starts rise strictly. `routes`: in each aligned block of 416 tokens (the tokens of one device) no expert is named by more than 208 tokens, and in some blocks one expert is named by exactly 208.
All inputs are finite; a program needn't handle non-finite values.
Results may differ from the reference program's by a relative error of at most 0.017.
Values may be sent and summed in bfloat16 or wider, within the bound.
No kernel may reach another device: no remote copies, remote signals or barrier semaphores. Data moves between devices by JAX's collectives and lax.ppermute only.
A program may use at most 256 MiB of HBM per device.

```python
import math
import jax
import jax.numpy as jnp
import numpy as np
from jax import lax

D = 768
HEADS = 12
HEAD = 64
FF = 3072
EXPERTS = 3
SEQ = 416
SEGS = 4
ROWS_DEV = 1
TOK_DEV = 416
CAP = 208
ROWS = 32
TOKENS = 13312


def draw_starts(key, part):
    key = jax.random.fold_in(key, 7)
    draw_scores = jax.random.randint(key, (ROWS, SEQ - 1), 0, 1 << 20) * SEQ + jnp.arange(SEQ - 1, dtype=jnp.int32)[None, :]
    chosen = jnp.argsort(draw_scores, axis=1)[:, :SEGS - 1] + 1
    chosen = jnp.sort(chosen, axis=1).astype(jnp.int32)
    return jnp.concatenate([jnp.zeros((ROWS, 1), jnp.int32), chosen], 1)


def block_scale(rng, shape, shards, low, largest):
    level = 1.0
    for dim, parts in shards:
        heights = jax.random.uniform(jax.random.fold_in(jax.random.fold_in(rng, 6), dim), (parts,), jnp.float32, low / len(shards), largest / len(shards))
        level = level * jnp.repeat(jnp.exp(heights), shape[dim] // parts).reshape((-1,) + (1,) * (len(shape) - 1 - dim))
    return level


def routed_block(rng, own, number, rows, number_of, top, most, slope):
    sequence = jax.random.permutation(rng, number_of)
    crowded, ordinary = shares(number_of, rows * top, most, slope, True), shares(number_of, rows * top, most, slope, False)
    places = jnp.arange(number_of)

    def named(sizes, offset_by):
        used = int((sizes > 0).sum())
        fixed = max(1, used // 4)
        moved = fixed + (places - fixed + offset_by * (used - fixed)) % max(1, number_of - fixed)
        return jnp.zeros((number_of,), jnp.int32).at[sequence[jnp.where(places < fixed, places, moved)]].set(jnp.asarray(sizes, jnp.int32))

    sizes = jnp.where(number % 4 == 0, named(crowded, number // 4), named(ordinary, number - number // 4 - 1))
    mixed = jax.random.permutation(jax.random.fold_in(own, 3), number_of)
    donor, taker = mixed[0:number_of // 2 * 2:2], mixed[1:number_of // 2 * 2:2]
    room = jnp.minimum(sizes[donor] - 1, most - sizes[taker]) // 2
    room = jnp.where((donor == sequence[0]) | (taker == sequence[0]) | (sizes[taker] == 0), 0, jnp.maximum(room, 0))
    moved = jax.random.randint(jax.random.fold_in(own, 4), (number_of // 2,), 0, 1 << 20) % (room + 1)
    sizes = sizes.at[donor].add(-moved).at[taker].add(moved)
    labels = jnp.searchsorted(jnp.cumsum(sizes), jnp.arange(rows * top), side="right").astype(jnp.int32)
    listing = labels.reshape(top, rows).T
    listing = listing[jax.random.permutation(jax.random.fold_in(own, 1), rows)]
    offset_by = jax.random.randint(jax.random.fold_in(own, 2), (rows, 1), 0, top)
    return jnp.take_along_axis(listing, (jnp.arange(top)[None, :] + offset_by) % top, axis=1)


def shares(count, total, most, slope, full):
    weights = [(1 << 20) // math.isqrt(standing ** slope) + 1 for standing in range(1, count + 1)]
    largest = most if full else min(most, max(-(-total // count), total * weights[0] // sum(weights)))
    least = 1 if total - largest >= count - 1 else 0
    counts, rest = [largest] + [least] * (count - 1), total - largest - least * (count - 1)
    while rest > 0:
        movable = [i for i in range(1, count) if counts[i] < largest] or [i for i in range(1, count) if counts[i] < most]
        whole, budget = sum([weights[i] for i in movable]), rest
        for i in movable:
            addition = min(most - counts[i], max(1, budget * weights[i] // whole), rest)
            counts[i] = counts[i] + addition
            rest = rest - addition
    return np.array(counts)


def normal_values(rng, dims, deviation, most, cuts=(), held_as=jnp.bfloat16):
    level = block_scale(rng, dims, cuts, -0.22, 0.18) if cuts else 1.0
    drawn = jax.random.normal(rng, dims, jnp.float32) * deviation * level
    return jnp.minimum(jnp.maximum(drawn, -most), most).astype(held_as)


def setup_inputs(seed: int = 0) -> dict:
    keys = jax.random.split(jax.random.key(seed), 20)
    tokens = normal_values(keys[0], (TOKENS, D), 1.0, 6.0, ((0, 32),))
    starts = draw_starts(jax.random.fold_in(keys[19], 71), 0)
    routes_keys = jax.random.split(jax.random.fold_in(keys[2], 1), TOKENS // TOK_DEV)
    routes_turns = jax.random.permutation(jax.random.fold_in(keys[2], 3), TOKENS // TOK_DEV)
    routes = jax.vmap(lambda own, number: routed_block(jax.random.fold_in(keys[2], 2), own, number, TOK_DEV, EXPERTS, 1, CAP, 1))(routes_keys, routes_turns).reshape((TOKENS, 1))
    norm1_gain = jnp.clip(1.0 + 0.1 * jax.random.normal(keys[3], (D,), jnp.float32), 0.5, 1.5).astype(jnp.bfloat16)
    norm1_bias = normal_values(keys[4], (D,), 0.2, 1.0, ((0, 8),))
    query_weight = normal_values(keys[5], (D, D), D ** -0.5, 0.21875, ((0, 8),))
    query_bias = normal_values(keys[6], (D,), 0.3, 1.5, ((0, 8),))
    key_weight = normal_values(keys[7], (D, D), D ** -0.5, 0.21875, ((0, 8),))
    value_weight = normal_values(keys[8], (D, D), D ** -0.5, 0.21875, ((0, 8),))
    value_bias = normal_values(keys[9], (D,), 0.2, 1.0, ((0, 8),))
    out_weight = normal_values(keys[10], (D, D), (D * 4 // SEQ) ** -0.5, 2.0, ((0, 8),))
    out_bias = normal_values(keys[11], (D,), 0.2, 1.0, ((0, 8),))
    norm2_gain = jnp.clip(1.0 + 0.1 * jax.random.normal(keys[12], (D,), jnp.float32), 0.5, 1.5).astype(jnp.bfloat16)
    norm2_bias = normal_values(keys[13], (D,), 0.2, 1.0, ((0, 8),))
    expert_in = normal_values(keys[14], (EXPERTS, D, FF), D ** -0.5, 0.21875, ((1, 8),))
    expert_in_bias = normal_values(keys[15], (EXPERTS, FF), 0.2, 1.0, ((1, 8),))
    expert_out = normal_values(keys[16], (EXPERTS, FF, D), FF ** -0.5, 0.109375, ((1, 8),))
    expert_out_bias = normal_values(keys[17], (EXPERTS, D), 0.2, 1.0, ((1, 8),))
    cotangent = normal_values(keys[18], (TOKENS, D), 1.0, 6.0, ((0, 32),))
    return {"tokens": tokens, "starts": starts, "routes": routes, "norm1_gain": norm1_gain, "norm1_bias": norm1_bias, "query_weight": query_weight, "query_bias": query_bias, "key_weight": key_weight, "value_weight": value_weight, "value_bias": value_bias, "out_weight": out_weight, "out_bias": out_bias, "norm2_gain": norm2_gain, "norm2_bias": norm2_bias, "expert_in": expert_in, "expert_in_bias": expert_in_bias, "expert_out": expert_out, "expert_out_bias": expert_out_bias, "cotangent": cotangent}


@jax.custom_vjp
def low(v):
    return lax.optimization_barrier(v.astype(jnp.bfloat16)).astype(jnp.float32)

@jax.custom_vjp
def low_back(v):
    return v

def low_keep(v):
    return (low(v), None)

def low_pass(kept, grad):
    return (grad,)

def back_keep(v):
    return (v, None)

def back_low(kept, grad):
    return (low(grad),)
low.defvjp(low_keep, low_pass)
low_back.defvjp(back_keep, back_low)
EPSILON = 1e-05
MASKED = -1000000000.0

def matmul_high(left, right):
    return jnp.dot(left, right, precision=lax.Precision.HIGHEST, preferred_element_type=jnp.float32)

def normalize(inputs, gain, shift):
    mean = lax.optimization_barrier(jnp.mean(inputs, -1, keepdims=True))
    centred = inputs - mean
    inverse = lax.rsqrt(lax.optimization_barrier(jnp.mean(centred * centred, -1, keepdims=True)) + EPSILON)
    return centred * inverse * gain + shift

def gelu_exact(inputs):
    return 0.5 * inputs * (1.0 + lax.erf(inputs * 0.7071067811865476))

def block_forward(params, inputs, start_rows, route_ids):
    gain_one, shift_one, w_query, b_query, w_key, w_value, b_value, w_out, b_out, gain_two, shift_two, w_in, b_in, w_down, b_down = params
    tok_count = inputs.shape[0]
    seq_rows = start_rows.shape[0]
    seq_len = tok_count // seq_rows
    head_shape = (seq_rows, seq_len, HEADS, HEAD)
    normed_one = low(normalize(inputs, gain_one, shift_one))
    queries = low_back(low(matmul_high(normed_one, w_query) + b_query)).reshape(head_shape)
    keys_mat = low_back(low(matmul_high(normed_one, w_key))).reshape(head_shape)
    values = low_back(low(matmul_high(normed_one, w_value) + b_value)).reshape(head_shape)
    position = jnp.arange(seq_len, dtype=jnp.int32)
    segment = lax.optimization_barrier(jnp.sum((position[None, :, None] >= start_rows[:, None, :]).astype(jnp.int32), -1))
    same_seg = (segment[:, :, None] == segment[:, None, :])[:, None]
    scores = jnp.einsum('rqhd,rkhd->rhqk', queries, keys_mat, precision=lax.Precision.HIGHEST) * HEAD ** (-0.5)
    scores = jnp.where(same_seg, low_back(scores), MASKED)
    row_max = lax.optimization_barrier(jnp.max(scores, -1, keepdims=True))
    exp_scores = jnp.exp(scores - row_max)
    probs = low(exp_scores / lax.optimization_barrier(jnp.sum(exp_scores, -1, keepdims=True)))
    mixed = jnp.einsum('rhqk,rkhd->rqhd', probs, values, precision=lax.Precision.HIGHEST)
    mixed = low_back(low(mixed.reshape(tok_count, D)))
    hidden = inputs + low_back(matmul_high(mixed, w_out) + b_out)
    normed_two = low(normalize(hidden, gain_two, shift_two))
    member = (route_ids[:, None] == jnp.arange(EXPERTS, dtype=jnp.int32)[None, :]).astype(jnp.int32)
    rank = lax.optimization_barrier(jnp.sum(jnp.cumsum(member, 0) * member, 1)) - 1
    slot_ids = (route_ids * CAP + rank).astype(jnp.int32)
    packed = jnp.zeros((EXPERTS * CAP, D), jnp.float32).at[slot_ids].set(normed_two).reshape(EXPERTS, CAP, D)
    pre_act = jnp.einsum('ecd,edf->ecf', packed, w_in, precision=lax.Precision.HIGHEST) + b_in[:, None, :]
    act_low = low(gelu_exact(low_back(pre_act)))
    result = jnp.einsum('ecf,efd->ecd', act_low, w_down, precision=lax.Precision.HIGHEST) + b_down[:, None, :]
    routed = low_back(result.reshape(EXPERTS * CAP, D)[slot_ids])
    return hidden + routed

def reference(tokens, starts, routes, norm1_gain, norm1_bias, query_weight, query_bias, key_weight, value_weight, value_bias, out_weight, out_bias, norm2_gain, norm2_bias, expert_in, expert_in_bias, expert_out, expert_out_bias, cotangent):
    params = tuple((weight.astype(jnp.float32) for weight in (norm1_gain, norm1_bias, query_weight, query_bias, key_weight, value_weight, value_bias, out_weight, out_bias, norm2_gain, norm2_bias, expert_in, expert_in_bias, expert_out, expert_out_bias)))
    inputs = tokens.astype(jnp.float32).reshape(-1, TOK_DEV, D)
    start_blocks = starts.reshape(-1, ROWS_DEV, SEGS)
    route_blocks = routes.reshape(-1, TOK_DEV)
    step_fn = jax.checkpoint(block_forward)

    def forward(weights, inputs_all):

        def visit(carry, pieces):
            block_in, block_starts, block_routes = pieces
            return (carry, step_fn(weights, block_in, block_starts, block_routes))
        _, outputs = lax.scan(visit, jnp.zeros((), jnp.float32), (inputs_all, start_blocks, route_blocks))
        return outputs
    outputs, pullback = jax.vjp(forward, params, inputs)
    grad_params, grad_inputs = pullback(cotangent.astype(jnp.float32).reshape(inputs.shape))
    return (outputs.reshape(-1, D).astype(jnp.bfloat16), grad_inputs.reshape(-1, D), grad_params[0], grad_params[1], grad_params[2], grad_params[3], grad_params[4], grad_params[5], grad_params[6], grad_params[7], grad_params[8], grad_params[9], grad_params[10], grad_params[11], grad_params[12], grad_params[13], grad_params[14])
```

```python
import jax
import jax.numpy as jnp
from jax import lax
from jax.experimental import pallas as pl
from jax.experimental.pallas import tpu as pltpu
from jax.sharding import PartitionSpec as P

HEAD = 64
EXPERTS = 3
CAP = 208


EPSILON = 1e-05
MASKED = -1000000000.0


def normalize(inputs, gain, shift):
    mean = jnp.mean(inputs, -1, keepdims=True)
    centred = inputs - mean
    inverse = lax.rsqrt(jnp.mean(centred * centred, -1, keepdims=True) + EPSILON)
    return centred * inverse * gain + shift


def norm_back(inputs, gain, gradient):
    mean = jnp.mean(inputs, -1, keepdims=True)
    centred = inputs - mean
    inverse = lax.rsqrt(jnp.mean(centred * centred, -1, keepdims=True) + EPSILON)
    normed = centred * inverse
    grad_normed = gradient * gain
    grad_inputs = inverse * (
        grad_normed
        - jnp.mean(grad_normed, -1, keepdims=True)
        - normed * jnp.mean(grad_normed * normed, -1, keepdims=True)
    )
    return (grad_inputs, jnp.sum(gradient * normed, 0), jnp.sum(gradient, 0))


def gelu_exact(inputs):
    return 0.5 * inputs * (1.0 + lax.erf(inputs * 0.7071067811865476))


def gelu_slope(inputs):
    return (
        0.5 * (1.0 + lax.erf(inputs * 0.7071067811865476))
        + inputs * jnp.exp(-0.5 * inputs * inputs) * 0.3989422804014327
    )


def per_device_weights(
    tokens,
    starts,
    routes,
    norm1_gain,
    norm1_bias,
    query_weight,
    query_bias,
    key_weight,
    value_weight,
    value_bias,
    out_weight,
    out_bias,
    norm2_gain,
    norm2_bias,
    expert_in,
    expert_in_bias,
    expert_out,
    expert_out_bias,
    cotangent,
):
    seq_rows = starts.shape[0]
    tok_count = tokens.shape[0]
    seq_len = tok_count // seq_rows
    model_width = tokens.shape[1]
    head_count = model_width // HEAD
    head_shape = (seq_rows, seq_len, head_count, HEAD)
    scale_factor = HEAD ** (-0.5)
    gain_one, shift_one, w_query, b_query, w_key, w_value, b_value, w_out, b_out = (
        lax.all_gather(norm1_gain, "fsdp", axis=0, tiled=True),
        lax.all_gather(norm1_bias, "fsdp", axis=0, tiled=True),
        lax.all_gather(query_weight, "fsdp", axis=0, tiled=True),
        lax.all_gather(query_bias, "fsdp", axis=0, tiled=True),
        lax.all_gather(key_weight, "fsdp", axis=0, tiled=True),
        lax.all_gather(value_weight, "fsdp", axis=0, tiled=True),
        lax.all_gather(value_bias, "fsdp", axis=0, tiled=True),
        lax.all_gather(out_weight, "fsdp", axis=0, tiled=True),
        lax.all_gather(out_bias, "fsdp", axis=0, tiled=True),
    )
    resid_in = tokens.astype(jnp.float32)
    normed_one = normalize(
        resid_in, gain_one.astype(jnp.float32), shift_one.astype(jnp.float32)
    ).astype(jnp.bfloat16)
    queries = (
        (
            jnp.dot(normed_one, w_query, preferred_element_type=jnp.float32)
            + b_query.astype(jnp.float32)
        )
        .astype(jnp.bfloat16)
        .reshape(head_shape)
    )
    keys_mat = (
        jnp.dot(normed_one, w_key, preferred_element_type=jnp.float32)
        .astype(jnp.bfloat16)
        .reshape(head_shape)
    )
    values = (
        (
            jnp.dot(normed_one, w_value, preferred_element_type=jnp.float32)
            + b_value.astype(jnp.float32)
        )
        .astype(jnp.bfloat16)
        .reshape(head_shape)
    )
    position = jnp.arange(seq_len, dtype=jnp.int32)
    segment = jnp.sum((position[None, :, None] >= starts[:, None, :]).astype(jnp.int32), -1)
    same_seg = (segment[:, :, None] == segment[:, None, :])[:, None]

    def scores_of(query_part, key_part):
        raw_scores = (
            jnp.einsum("rqhd,rkhd->rhqk", query_part, key_part, preferred_element_type=jnp.float32)
            * scale_factor
        )
        return jnp.where(same_seg, raw_scores, MASKED)

    scores = scores_of(queries, keys_mat)
    row_max = jnp.max(scores, -1, keepdims=True)
    exp_scores = jnp.exp(scores - row_max)
    row_total = jnp.sum(exp_scores, -1, keepdims=True)
    log_total = row_max + jnp.log(row_total)
    probs_low = (exp_scores / row_total).astype(jnp.bfloat16)
    mixed = jnp.einsum("rhqk,rkhd->rqhd", probs_low, values, preferred_element_type=jnp.float32)
    mixed = mixed.reshape(tok_count, model_width).astype(jnp.bfloat16)
    hidden = (
        resid_in
        + jnp.dot(mixed, w_out, preferred_element_type=jnp.float32)
        + b_out.astype(jnp.float32)
    )
    gain_two, shift_two, w_in, b_in, w_down, b_down = (
        lax.all_gather(norm2_gain, "fsdp", axis=0, tiled=True),
        lax.all_gather(norm2_bias, "fsdp", axis=0, tiled=True),
        lax.all_gather(expert_in, "fsdp", axis=1, tiled=True),
        lax.all_gather(expert_in_bias, "fsdp", axis=1, tiled=True),
        lax.all_gather(expert_out, "fsdp", axis=1, tiled=True),
        lax.all_gather(expert_out_bias, "fsdp", axis=1, tiled=True),
    )
    normed_two = normalize(
        hidden, gain_two.astype(jnp.float32), shift_two.astype(jnp.float32)
    ).astype(jnp.bfloat16)
    route_ids = routes[:, 0]
    member = (route_ids[:, None] == jnp.arange(EXPERTS, dtype=jnp.int32)[None, :]).astype(jnp.int32)
    rank = jnp.sum(jnp.cumsum(member, 0) * member, 1) - 1
    slot_ids = route_ids * CAP + rank
    packed = (
        jnp.zeros((EXPERTS * CAP, model_width), jnp.bfloat16)
        .at[slot_ids]
        .set(normed_two)
        .reshape(EXPERTS, CAP, model_width)
    )
    pre_act = (
        jnp.einsum("ecd,edf->ecf", packed, w_in, preferred_element_type=jnp.float32)
        + b_in.astype(jnp.float32)[:, None, :]
    )
    act_low = gelu_exact(pre_act).astype(jnp.bfloat16)
    result = (
        jnp.einsum("ecf,efd->ecd", act_low, w_down, preferred_element_type=jnp.float32)
        + b_down.astype(jnp.float32)[:, None, :]
    )
    routed = result.reshape(EXPERTS * CAP, model_width)[slot_ids]
    output = (hidden + routed).astype(jnp.bfloat16)
    gain_two_back, w_in_back, w_down_back = (
        lax.all_gather(norm2_gain, "fsdp", axis=0, tiled=True),
        lax.all_gather(expert_in, "fsdp", axis=1, tiled=True),
        lax.all_gather(expert_out, "fsdp", axis=1, tiled=True),
    )
    grad_output = cotangent.astype(jnp.float32)
    grad_packed = (
        jnp.zeros((EXPERTS * CAP, model_width), jnp.bfloat16)
        .at[slot_ids]
        .set(cotangent)
        .reshape(EXPERTS, CAP, model_width)
    )
    grad_down_bias = jnp.sum(grad_packed.astype(jnp.float32), 1)
    grad_down = jnp.einsum("ecf,ecd->efd", act_low, grad_packed, preferred_element_type=jnp.float32)
    grad_act = jnp.einsum(
        "ecd,efd->ecf", grad_packed, w_down_back, preferred_element_type=jnp.float32
    )
    grad_pre = (grad_act * gelu_slope(pre_act)).astype(jnp.bfloat16)
    grad_in_bias = jnp.sum(grad_pre.astype(jnp.float32), 1)
    grad_in = jnp.einsum("ecd,ecf->edf", packed, grad_pre, preferred_element_type=jnp.float32)
    grad_slots = jnp.einsum(
        "ecf,edf->ecd", grad_pre, w_in_back, preferred_element_type=jnp.float32
    ).reshape(EXPERTS * CAP, model_width)
    grad_normed_two = grad_slots[slot_ids]
    grad_from_norm, grad_gain_two, grad_shift_two = norm_back(
        hidden, gain_two_back.astype(jnp.float32), grad_normed_two
    )
    grad_hidden = grad_output + grad_from_norm
    column_in, column_down = (
        lax.psum_scatter(
            grad_in.astype(jnp.bfloat16), "rep", scatter_dimension=2, tiled=True
        ).astype(jnp.float32),
        lax.psum_scatter(
            grad_down.astype(jnp.bfloat16), "rep", scatter_dimension=2, tiled=True
        ).astype(jnp.float32),
    )
    share_in, share_down, part_gain_two, part_shift_two, part_in_bias, part_down_bias = (
        lax.psum_scatter(column_in, "fsdp", scatter_dimension=1, tiled=True),
        lax.psum_scatter(column_down, "fsdp", scatter_dimension=1, tiled=True),
        lax.psum_scatter(grad_gain_two, "fsdp", scatter_dimension=0, tiled=True),
        lax.psum_scatter(grad_shift_two, "fsdp", scatter_dimension=0, tiled=True),
        lax.psum_scatter(grad_in_bias, "fsdp", scatter_dimension=1, tiled=True),
        lax.psum_scatter(grad_down_bias, "fsdp", scatter_dimension=1, tiled=True),
    )
    sum_in, sum_down, stack_gain_two, stack_shift_two, stack_in_bias, stack_down_bias = (
        lax.all_gather(share_in.astype(jnp.bfloat16), "rep", axis=2, tiled=True).astype(
            share_in.dtype
        ),
        lax.all_gather(share_down.astype(jnp.bfloat16), "rep", axis=2, tiled=True).astype(
            share_down.dtype
        ),
        lax.all_gather(part_gain_two[None].astype(jnp.bfloat16), "rep", axis=0, tiled=True).astype(
            jnp.float32
        ),
        lax.all_gather(part_shift_two[None].astype(jnp.bfloat16), "rep", axis=0, tiled=True).astype(
            jnp.float32
        ),
        lax.all_gather(part_in_bias[None].astype(jnp.bfloat16), "rep", axis=0, tiled=True).astype(
            jnp.float32
        ),
        lax.all_gather(part_down_bias[None].astype(jnp.bfloat16), "rep", axis=0, tiled=True).astype(
            jnp.float32
        ),
    )
    sum_gain_two = jnp.sum(stack_gain_two, 0)
    sum_shift_two = jnp.sum(stack_shift_two, 0)
    sum_in_bias = jnp.sum(stack_in_bias, 0)
    sum_down_bias = jnp.sum(stack_down_bias, 0)
    gain_one_back, w_query_back, w_key_back, w_value_back, w_out_back = (
        lax.all_gather(norm1_gain, "fsdp", axis=0, tiled=True),
        lax.all_gather(query_weight, "fsdp", axis=0, tiled=True),
        lax.all_gather(key_weight, "fsdp", axis=0, tiled=True),
        lax.all_gather(value_weight, "fsdp", axis=0, tiled=True),
        lax.all_gather(out_weight, "fsdp", axis=0, tiled=True),
    )
    grad_branch = grad_hidden.astype(jnp.bfloat16)
    grad_out_bias = jnp.sum(grad_branch.astype(jnp.float32), 0)
    grad_out_weight = jnp.einsum(
        "td,te->de", mixed, grad_branch, preferred_element_type=jnp.float32
    )
    grad_mixed = (
        jnp.einsum("te,de->td", grad_branch, w_out_back, preferred_element_type=jnp.float32)
        .astype(jnp.bfloat16)
        .reshape(head_shape)
    )
    scores_again = scores_of(queries, keys_mat)
    probs = jnp.exp(scores_again - log_total)
    probs_again = probs.astype(jnp.bfloat16)
    grad_values = jnp.einsum(
        "rhqk,rqhd->rkhd", probs_again, grad_mixed, preferred_element_type=jnp.float32
    )
    grad_values = grad_values.astype(jnp.bfloat16).reshape(tok_count, model_width)
    grad_probs = jnp.einsum(
        "rqhd,rkhd->rhqk", grad_mixed, values, preferred_element_type=jnp.float32
    )
    grad_scores = (probs * (grad_probs - jnp.sum(grad_probs * probs, -1, keepdims=True))).astype(
        jnp.bfloat16
    )
    grad_queries = (
        (
            jnp.einsum("rhqk,rkhd->rqhd", grad_scores, keys_mat, preferred_element_type=jnp.float32)
            * scale_factor
        )
        .astype(jnp.bfloat16)
        .reshape(tok_count, model_width)
    )
    grad_keys = (
        (
            jnp.einsum("rhqk,rqhd->rkhd", grad_scores, queries, preferred_element_type=jnp.float32)
            * scale_factor
        )
        .astype(jnp.bfloat16)
        .reshape(tok_count, model_width)
    )
    grad_query_bias = jnp.sum(grad_queries.astype(jnp.float32), 0)
    grad_value_bias = jnp.sum(grad_values.astype(jnp.float32), 0)
    grad_query_weight = jnp.einsum(
        "td,te->de", normed_one, grad_queries, preferred_element_type=jnp.float32
    )
    grad_key_weight = jnp.einsum(
        "td,te->de", normed_one, grad_keys, preferred_element_type=jnp.float32
    )
    grad_value_weight = jnp.einsum(
        "td,te->de", normed_one, grad_values, preferred_element_type=jnp.float32
    )
    grad_normed_one = (
        jnp.einsum("te,de->td", grad_queries, w_query_back, preferred_element_type=jnp.float32)
        + jnp.einsum("te,de->td", grad_keys, w_key_back, preferred_element_type=jnp.float32)
        + jnp.einsum("te,de->td", grad_values, w_value_back, preferred_element_type=jnp.float32)
    )
    grad_from_first, grad_gain_one, grad_shift_one = norm_back(
        resid_in, gain_one_back.astype(jnp.float32), grad_normed_one
    )
    input_grad = grad_hidden + grad_from_first
    column_query, column_key, column_value, column_out = (
        lax.psum_scatter(
            grad_query_weight.astype(jnp.bfloat16), "rep", scatter_dimension=1, tiled=True
        ).astype(jnp.float32),
        lax.psum_scatter(
            grad_key_weight.astype(jnp.bfloat16), "rep", scatter_dimension=1, tiled=True
        ).astype(jnp.float32),
        lax.psum_scatter(
            grad_value_weight.astype(jnp.bfloat16), "rep", scatter_dimension=1, tiled=True
        ).astype(jnp.float32),
        lax.psum_scatter(
            grad_out_weight.astype(jnp.bfloat16), "rep", scatter_dimension=1, tiled=True
        ).astype(jnp.float32),
    )
    (
        share_query,
        share_key,
        share_value,
        share_out,
        part_gain_one,
        part_shift_one,
        part_query_bias,
        part_value_bias,
        part_out_bias,
    ) = (
        lax.psum_scatter(column_query, "fsdp", scatter_dimension=0, tiled=True),
        lax.psum_scatter(column_key, "fsdp", scatter_dimension=0, tiled=True),
        lax.psum_scatter(column_value, "fsdp", scatter_dimension=0, tiled=True),
        lax.psum_scatter(column_out, "fsdp", scatter_dimension=0, tiled=True),
        lax.psum_scatter(grad_gain_one, "fsdp", scatter_dimension=0, tiled=True),
        lax.psum_scatter(grad_shift_one, "fsdp", scatter_dimension=0, tiled=True),
        lax.psum_scatter(grad_query_bias, "fsdp", scatter_dimension=0, tiled=True),
        lax.psum_scatter(grad_value_bias, "fsdp", scatter_dimension=0, tiled=True),
        lax.psum_scatter(grad_out_bias, "fsdp", scatter_dimension=0, tiled=True),
    )
    (
        sum_query,
        sum_key,
        sum_value,
        sum_out,
        stack_gain_one,
        stack_shift_one,
        stack_query_bias,
        stack_value_bias,
        stack_out_bias,
    ) = (
        lax.all_gather(share_query.astype(jnp.bfloat16), "rep", axis=1, tiled=True).astype(
            share_query.dtype
        ),
        lax.all_gather(share_key.astype(jnp.bfloat16), "rep", axis=1, tiled=True).astype(
            share_key.dtype
        ),
        lax.all_gather(share_value.astype(jnp.bfloat16), "rep", axis=1, tiled=True).astype(
            share_value.dtype
        ),
        lax.all_gather(share_out.astype(jnp.bfloat16), "rep", axis=1, tiled=True).astype(
            share_out.dtype
        ),
        lax.all_gather(part_gain_one[None].astype(jnp.bfloat16), "rep", axis=0, tiled=True).astype(
            jnp.float32
        ),
        lax.all_gather(part_shift_one[None].astype(jnp.bfloat16), "rep", axis=0, tiled=True).astype(
            jnp.float32
        ),
        lax.all_gather(
            part_query_bias[None].astype(jnp.bfloat16), "rep", axis=0, tiled=True
        ).astype(jnp.float32),
        lax.all_gather(
            part_value_bias[None].astype(jnp.bfloat16), "rep", axis=0, tiled=True
        ).astype(jnp.float32),
        lax.all_gather(part_out_bias[None].astype(jnp.bfloat16), "rep", axis=0, tiled=True).astype(
            jnp.float32
        ),
    )
    sum_gain_one = jnp.sum(stack_gain_one, 0)
    sum_shift_one = jnp.sum(stack_shift_one, 0)
    sum_query_bias = jnp.sum(stack_query_bias, 0)
    sum_value_bias = jnp.sum(stack_value_bias, 0)
    sum_out_bias = jnp.sum(stack_out_bias, 0)
    return (
        output,
        input_grad,
        sum_gain_one,
        sum_shift_one,
        sum_query,
        sum_query_bias,
        sum_key,
        sum_value,
        sum_value_bias,
        sum_out,
        sum_out_bias,
        sum_gain_two,
        sum_shift_two,
        sum_in,
        sum_in_bias,
        sum_down,
        sum_down_bias,
    )


def dot_nn(a,b): return lax.dot_general(a,b,(((1,),(0,)),((),())),preferred_element_type=jnp.float32)
def dot_nt(a,b): return lax.dot_general(a,b,(((1,),(1,)),((),())),preferred_element_type=jnp.float32)
def dot_tn(a,b): return lax.dot_general(a,b,(((0,),(0,)),((),())),preferred_element_type=jnp.float32)

def moe_kernel(n, cap, meta, *refs):
    E=3
    xin=refs[:n]; gin=refs[n:2*n]
    w_in,w_out,b_in=refs[2*n:2*n+3]
    res_e,res_o,dsl_e,dsl_o,gwo,gwi,gb=refs[2*n+3:2*n+10]
    X,G,R,S,XS,GS,ACT,DP,sem,osem=refs[2*n+10:]
    copies=[]
    for j in range(n):
        for src,dst,k in ((xin[j],X,0),(gin[j],G,1)):
            c=pltpu.make_async_copy(src,dst.at[j],sem.at[k,j]); c.start(); copies.append(c)
    def zero(j,c):
        R[j]=jnp.zeros_like(R[j]); S[j]=jnp.zeros_like(S[j]); return c
    lax.fori_loop(0,n,zero,0)
    for c in copies: c.wait()
    T=2*cap
    for e in range(E):
        def tile(t,carry):
            base=pl.multiple_of(t*T,T)
            masks=[];starts=[]
            for q in range(2):
                j=2*t+q
                st=pl.multiple_of(meta[j,3*e],16); lo=meta[j,3*e+1]; hi=meta[j,3*e+2]
                row=lax.broadcasted_iota(jnp.int32,(cap,1),0)
                m=(row>=lo)&(row<hi)
                masks.append(m);starts.append(st)
                XS[pl.ds(base+q*cap,cap),:]=X[j,pl.ds(st,cap),:]
                g=G[j,pl.ds(st,cap),:]
                GS[pl.ds(base+q*cap,cap),:]=jnp.where(m,g,jnp.zeros_like(g))
            xs=XS[pl.ds(base,T),:]
            gs=GS[pl.ds(base,T),:]
            pre=dot_nn(xs,w_in[e])+b_in[e]
            cdf=0.5*(1.0+lax.erf(pre*0.7071067811865476))
            act=(pre*cdf).astype(jnp.bfloat16)
            slope=cdf+pre*jnp.exp(-0.5*pre*pre)*0.3989422804014327
            da=dot_nt(gs,w_out[e])
            dp=(da*slope).astype(jnp.bfloat16)
            ACT[pl.ds(base,T),:]=act
            DP[pl.ds(base,T),:]=dp
            ds=dot_nt(dp,w_in[e]).astype(jnp.bfloat16)
            rs=dot_nn(act,w_out[e]).astype(jnp.bfloat16)
            for q in range(2):
                j=2*t+q
                for dst,v in ((R,rs),(S,ds)):
                    old=dst[j,pl.ds(starts[q],cap),:]
                    dst[j,pl.ds(starts[q],cap),:]=jnp.where(masks[q],v[q*cap:(q+1)*cap],old)
            return carry
        lax.fori_loop(0,n//2,tile,0)
        gwo[e]=dot_tn(ACT[...],GS[...]).astype(jnp.bfloat16)
        gwi[e]=dot_tn(XS[...],DP[...]).astype(jnp.bfloat16)
        gb[e]=jnp.sum(DP[...].astype(jnp.float32),0,keepdims=True)
    outs=[]
    for j in range(n):
        for k,(src,de,do) in enumerate(((S,dsl_e,dsl_o),(R,res_e,res_o))):
            dst=(de if j%2==0 else do).at[j//2]
            c=pltpu.make_async_copy(src.at[j],dst,osem.at[k,j]); c.start(); outs.append(c)
    for c in outs: c.wait()

def moe(meta,xs,gs,w_in,w_out,b_in,cap):
    n=len(xs); rows,d=xs[0].shape; E,_,f=w_in.shape
    bf=jnp.bfloat16
    any_=pl.BlockSpec(memory_space=pl.ANY); vm=pl.BlockSpec(memory_space=pltpu.VMEM)
    sd=jax.ShapeDtypeStruct
    return pl.pallas_call(
        lambda *r: moe_kernel(n,cap,*r),
        out_shape=(sd((n//2,rows,d),bf),)*4+(sd((E,f,d),bf),sd((E,d,f),bf),sd((E,1,f),jnp.float32)),
        in_specs=[pl.BlockSpec(memory_space=pltpu.SMEM)]+[any_]*(2*n)+[vm]*3,
        out_specs=(any_,)*4+(vm,)*3,
        scratch_shapes=[pltpu.VMEM((n,rows,d),bf)]*4+[pltpu.VMEM((n*cap,d),bf)]*2+[pltpu.VMEM((n*cap,f),bf)]*2+[pltpu.SemaphoreType.DMA((2,n)),pltpu.SemaphoreType.DMA((2,n))],
        compiler_params=pltpu.CompilerParams(vmem_limit_bytes=60*1024*1024),
        name="moe",
    )(meta,*xs,*gs,w_in,w_out,b_in)


ROWS16 = 16
LANES = 128
BF = jnp.bfloat16
F32 = jnp.float32


def swap(v, n, mask, axis="fsdp"):
    return lax.ppermute(v, axis, [(i, i ^ mask) for i in range(n)])


def gather_pieces(v, n):
    pieces = {0: v, 1: swap(v, n, 1)}
    for m in range(2, n, 2):
        pieces[m] = swap(v, n, m)
        pieces[m ^ 1] = swap(pieces[m], n, 1)
    return [pieces[m] for m in range(n)]


def scatter_sum(even, odd, n):
    other = swap(odd, n, 1)
    terms = [(even[i].astype(F32) + other[i].astype(F32)).astype(BF) for i in range(n // 2)]
    total = terms[0].astype(F32)
    for i in range(1, n // 2):
        total = total + swap(terms[i], n, 2 * i).astype(F32)
    return total


def line_sum(v):
    idx = lax.axis_index("rep")
    inward = lax.ppermute(v, "rep", [(0, 1), (3, 2)])
    part = (v.astype(F32) + inward.astype(F32)).astype(BF)
    across = lax.ppermute(part, "rep", [(1, 2), (2, 1)])
    total = (part.astype(F32) + across.astype(F32)).astype(BF)
    outward = lax.ppermute(total, "rep", [(1, 0), (2, 3)])
    return jnp.where((idx == 0) | (idx == 3), outward, total).astype(F32)


def per_device_tokens(
    n,
    tokens,
    starts,
    routes,
    norm1_gain,
    norm1_bias,
    query_weight,
    query_bias,
    key_weight,
    value_weight,
    value_bias,
    out_weight,
    out_bias,
    norm2_gain,
    norm2_bias,
    expert_in,
    expert_in_bias,
    expert_out,
    expert_out_bias,
    cotangent,
):
    me = lax.axis_index("fsdp")
    seq_rows = starts.shape[0]
    tok_count, width = tokens.shape
    seq_len = tok_count // seq_rows
    shard = width // n
    ff_shard = expert_out.shape[1]
    head_count = width // HEAD
    head_shape = (seq_rows, seq_len, head_count, HEAD)
    scale_factor = HEAD ** (-0.5)

    vectors = jnp.stack(
        [norm1_gain, norm1_bias, query_bias, value_bias, out_bias, norm2_gain, norm2_bias], 1
    )
    vectors = jnp.concatenate([vectors, expert_out_bias.T], 1)
    n_vec = vectors.shape[1]
    pad = jnp.zeros((shard, LANES - n_vec), BF)
    first = jnp.concatenate([query_weight, key_weight, value_weight, vectors, pad], 1)

    def assemble(v):
        whole = jnp.zeros((width, v.shape[1]), v.dtype)
        for m, piece in enumerate(gather_pieces(v, n)):
            whole = lax.dynamic_update_slice(whole, piece, ((me ^ m) * shard, 0))
        return whole

    first_all = assemble(first)
    w_qkv = first_all[:, : 3 * width]
    vec = first_all[:, 3 * width : 3 * width + n_vec].T.astype(F32)
    gain_one, shift_one, b_query, b_value, b_out, gain_two, shift_two = (vec[i] for i in range(7))
    b_down = vec[7:]
    w_out = assemble(out_weight)

    route_ids = routes[:, 0]
    member = (route_ids[:, None] == jnp.arange(EXPERTS, dtype=jnp.int32)[None, :]).astype(jnp.int32)
    rank = jnp.sum(jnp.cumsum(member, 0) * member, 1) - 1
    counts = jnp.sum(member, 0)
    padded = (counts + ROWS16 - 1) // ROWS16 * ROWS16
    base = jnp.cumsum(padded) - padded
    slots = tok_count + ROWS16 * (EXPERTS - 1)
    position = jnp.sum(member * base[None, :], 1) + rank
    place = (jnp.arange(slots, dtype=jnp.int32)[:, None] == position[None, :]).astype(BF)
    begin = jnp.minimum(base, slots - CAP)
    meta = jnp.stack([begin, base - begin, base - begin + padded], 1).reshape(1, 3 * EXPERTS)
    meta_all = lax.all_gather(meta, "fsdp", axis=0, tiled=True)
    meta_rel = jnp.take(meta_all, me ^ jnp.arange(n), axis=0)

    def sort(v):
        return jnp.dot(place, v, preferred_element_type=F32).astype(BF)

    def unsort(v):
        return lax.dot_general(
            place, v.astype(BF), (((0,), (0,)), ((), ())), preferred_element_type=F32
        )

    grad_pieces = gather_pieces(sort(cotangent), n)

    w_in = jnp.zeros((EXPERTS, width, ff_shard), BF)
    for m in range(n):
        piece = lax.dynamic_slice(
            expert_in, (0, 0, (me ^ m) * ff_shard), (EXPERTS, shard, ff_shard)
        )
        if m:
            piece = swap(piece, n, m)
        w_in = lax.dynamic_update_slice(w_in, piece, (0, (me ^ m) * shard, 0))

    resid_in = tokens.astype(F32)
    normed_one = normalize(resid_in, gain_one, shift_one).astype(BF)
    qkv = jnp.dot(normed_one, w_qkv, preferred_element_type=F32)
    queries = (qkv[:, :width] + b_query).astype(BF).reshape(head_shape)
    keys_mat = qkv[:, width : 2 * width].astype(BF).reshape(head_shape)
    values = (qkv[:, 2 * width :] + b_value).astype(BF).reshape(head_shape)
    pos = jnp.arange(seq_len, dtype=jnp.int32)
    segment = jnp.sum((pos[None, :, None] >= starts[:, None, :]).astype(jnp.int32), -1)
    same_seg = (segment[:, :, None] == segment[:, None, :])[:, None]

    def scores_of(query_part, key_part):
        raw_scores = (
            jnp.einsum("rqhd,rkhd->rhqk", query_part, key_part, preferred_element_type=F32)
            * scale_factor
        )
        return jnp.where(same_seg, raw_scores, MASKED)

    scores = scores_of(queries, keys_mat)
    row_max = jnp.max(scores, -1, keepdims=True)
    exp_scores = jnp.exp(scores - row_max)
    row_total = jnp.sum(exp_scores, -1, keepdims=True)
    log_total = row_max + jnp.log(row_total)
    probs_low = (exp_scores / row_total).astype(BF)
    mixed = jnp.einsum("rhqk,rkhd->rqhd", probs_low, values, preferred_element_type=F32)
    mixed = mixed.reshape(tok_count, width).astype(BF)
    hidden = resid_in + jnp.dot(mixed, w_out, preferred_element_type=F32) + b_out
    normed_two = normalize(hidden, gain_two, shift_two).astype(BF)

    token_pieces = gather_pieces(sort(normed_two), n)
    res_e, res_o, dsl_e, dsl_o, g_down, g_in, g_in_bias = moe(
        meta_rel,
        token_pieces,
        grad_pieces,
        w_in,
        expert_out,
        expert_in_bias.astype(F32)[:, None, :],
        CAP,
    )
    grad_normed_two = unsort(scatter_sum(dsl_e, dsl_o, n))
    routed = unsort(scatter_sum(res_e, res_o, n)) + jnp.dot(
        member.astype(F32), b_down, precision=lax.Precision.HIGHEST
    )
    output = (hidden + routed).astype(BF)

    grad_output = cotangent.astype(F32)
    g_down_bias = lax.dot_general(
        member.astype(BF), cotangent, (((0,), (0,)), ((), ())), preferred_element_type=F32
    )
    grad_from_norm, g_gain_two, g_shift_two = norm_back(hidden, gain_two, grad_normed_two)
    grad_hidden = grad_output + grad_from_norm

    sum_down = jnp.stack([line_sum(g_down[e]) for e in range(EXPERTS)])
    sum_in_bias = line_sum(g_in_bias[:, 0].astype(BF))
    mine = jnp.zeros((EXPERTS, shard, n * ff_shard), BF)
    for m in range(n):
        piece = lax.dynamic_slice(g_in, (0, (me ^ m) * shard, 0), (EXPERTS, shard, ff_shard))
        if m:
            piece = swap(piece, n, m)
        mine = lax.dynamic_update_slice(mine, piece, (0, 0, (me ^ m) * ff_shard))
    sum_in = jnp.stack([line_sum(mine[e]) for e in range(EXPERTS)])

    grad_branch = grad_hidden.astype(BF)
    g_out_bias = jnp.sum(grad_branch.astype(F32), 0)
    g_out_weight = jnp.einsum("td,te->de", mixed, grad_branch, preferred_element_type=F32)

    def shares(v):
        even = [
            lax.dynamic_slice(v, ((me ^ m) * shard, 0), (shard, v.shape[1]))
            for m in range(0, n, 2)
        ]
        odd = [
            lax.dynamic_slice(v, ((me ^ m) * shard, 0), (shard, v.shape[1]))
            for m in range(1, n, 2)
        ]
        return even, jnp.stack(odd)

    sum_out = line_sum(scatter_sum(*shares(g_out_weight.astype(BF)), n).astype(BF))

    grad_mixed = (
        jnp.einsum("te,de->td", grad_branch, w_out, preferred_element_type=F32)
        .astype(BF)
        .reshape(head_shape)
    )
    scores_again = scores_of(queries, keys_mat)
    probs = jnp.exp(scores_again - log_total)
    probs_again = probs.astype(BF)
    grad_values = jnp.einsum("rhqk,rqhd->rkhd", probs_again, grad_mixed, preferred_element_type=F32)
    grad_values = grad_values.astype(BF).reshape(tok_count, width)
    grad_probs = jnp.einsum("rqhd,rkhd->rhqk", grad_mixed, values, preferred_element_type=F32)
    grad_scores = (probs * (grad_probs - jnp.sum(grad_probs * probs, -1, keepdims=True))).astype(BF)
    grad_queries = (
        (
            jnp.einsum("rhqk,rkhd->rqhd", grad_scores, keys_mat, preferred_element_type=F32)
            * scale_factor
        )
        .astype(BF)
        .reshape(tok_count, width)
    )
    grad_keys = (
        (
            jnp.einsum("rhqk,rqhd->rkhd", grad_scores, queries, preferred_element_type=F32)
            * scale_factor
        )
        .astype(BF)
        .reshape(tok_count, width)
    )
    g_query_bias = jnp.sum(grad_queries.astype(F32), 0)
    g_value_bias = jnp.sum(grad_values.astype(F32), 0)
    grad_qkv = jnp.concatenate([grad_queries, grad_keys, grad_values], 1)
    g_qkv_weight = jnp.einsum("td,te->de", normed_one, grad_qkv, preferred_element_type=F32)
    grad_normed_one = jnp.einsum("te,de->td", grad_qkv, w_qkv, preferred_element_type=F32)
    grad_from_first, g_gain_one, g_shift_one = norm_back(resid_in, gain_one, grad_normed_one)
    input_grad = grad_hidden + grad_from_first

    g_vec = jnp.stack(
        [g_gain_one, g_shift_one, g_query_bias, g_value_bias, g_out_bias, g_gain_two, g_shift_two], 1
    )
    g_vec = jnp.concatenate([g_vec, g_down_bias.T], 1).astype(BF)
    last = jnp.concatenate(
        [g_qkv_weight.astype(BF), g_vec, jnp.zeros((width, LANES - n_vec), BF)], 1
    )
    sum_last = line_sum(scatter_sum(*shares(last), n).astype(BF))
    sum_vec = sum_last[:, 3 * width : 3 * width + n_vec].T
    return (
        output,
        input_grad,
        sum_vec[0],
        sum_vec[1],
        sum_last[:, :width],
        sum_vec[2],
        sum_last[:, width : 2 * width],
        sum_last[:, 2 * width : 3 * width],
        sum_vec[3],
        sum_out,
        sum_vec[4],
        sum_vec[5],
        sum_vec[6],
        sum_in,
        sum_in_bias,
        sum_down,
        sum_vec[7:],
    )


def plan_of(n, replicas):
    if n == 8 and replicas == 4:
        return lambda *args: per_device_tokens(n, *args)
    return per_device_weights


def solution(mesh):
    in_specs = (
        P(("fsdp", "rep"), None),
        P(("fsdp", "rep"), None),
        P(("fsdp", "rep"), None),
        P("fsdp"),
        P("fsdp"),
        P("fsdp", None),
        P("fsdp"),
        P("fsdp", None),
        P("fsdp", None),
        P("fsdp"),
        P("fsdp", None),
        P("fsdp"),
        P("fsdp"),
        P("fsdp"),
        P(None, "fsdp", None),
        P(None, "fsdp"),
        P(None, "fsdp", None),
        P(None, "fsdp"),
        P(("fsdp", "rep"), None),
    )
    out_specs = (
        P(("fsdp", "rep"), None),
        P(("fsdp", "rep"), None),
        P("fsdp"),
        P("fsdp"),
        P("fsdp", None),
        P("fsdp"),
        P("fsdp", None),
        P("fsdp", None),
        P("fsdp"),
        P("fsdp", None),
        P("fsdp"),
        P("fsdp"),
        P("fsdp"),
        P(None, "fsdp", None),
        P(None, "fsdp"),
        P(None, "fsdp", None),
        P(None, "fsdp"),
    )
    per_device = plan_of(mesh.shape["fsdp"], mesh.shape["rep"])
    return jax.shard_map(
        per_device, mesh=mesh, in_specs=in_specs, out_specs=out_specs, check_vma=False
    )
```

```python
import jax
import jax.numpy as jnp
from jax import lax
from jax.experimental import pallas as pl
from jax.experimental.pallas import tpu as pltpu
from jax.sharding import PartitionSpec as P

HEAD = 64
EXPERTS = 3
CAP = 208


EPSILON = 1e-05
MASKED = -1000000000.0


def normalize(inputs, gain, shift):
    mean = jnp.mean(inputs, -1, keepdims=True)
    centred = inputs - mean
    inverse = lax.rsqrt(jnp.mean(centred * centred, -1, keepdims=True) + EPSILON)
    return centred * inverse * gain + shift


def norm_back(inputs, gain, gradient):
    mean = jnp.mean(inputs, -1, keepdims=True)
    centred = inputs - mean
    inverse = lax.rsqrt(jnp.mean(centred * centred, -1, keepdims=True) + EPSILON)
    normed = centred * inverse
    grad_normed = gradient * gain
    grad_inputs = inverse * (
        grad_normed
        - jnp.mean(grad_normed, -1, keepdims=True)
        - normed * jnp.mean(grad_normed * normed, -1, keepdims=True)
    )
    return (grad_inputs, jnp.sum(gradient * normed, 0), jnp.sum(gradient, 0))


def gelu_exact(inputs):
    return 0.5 * inputs * (1.0 + lax.erf(inputs * 0.7071067811865476))


def gelu_slope(inputs):
    return (
        0.5 * (1.0 + lax.erf(inputs * 0.7071067811865476))
        + inputs * jnp.exp(-0.5 * inputs * inputs) * 0.3989422804014327
    )


def per_device_weights(
    tokens,
    starts,
    routes,
    norm1_gain,
    norm1_bias,
    query_weight,
    query_bias,
    key_weight,
    value_weight,
    value_bias,
    out_weight,
    out_bias,
    norm2_gain,
    norm2_bias,
    expert_in,
    expert_in_bias,
    expert_out,
    expert_out_bias,
    cotangent,
):
    seq_rows = starts.shape[0]
    tok_count = tokens.shape[0]
    seq_len = tok_count // seq_rows
    model_width = tokens.shape[1]
    head_count = model_width // HEAD
    head_shape = (seq_rows, seq_len, head_count, HEAD)
    scale_factor = HEAD ** (-0.5)
    gain_one, shift_one, w_query, b_query, w_key, w_value, b_value, w_out, b_out = (
        lax.all_gather(norm1_gain, "fsdp", axis=0, tiled=True),
        lax.all_gather(norm1_bias, "fsdp", axis=0, tiled=True),
        lax.all_gather(query_weight, "fsdp", axis=0, tiled=True),
        lax.all_gather(query_bias, "fsdp", axis=0, tiled=True),
        lax.all_gather(key_weight, "fsdp", axis=0, tiled=True),
        lax.all_gather(value_weight, "fsdp", axis=0, tiled=True),
        lax.all_gather(value_bias, "fsdp", axis=0, tiled=True),
        lax.all_gather(out_weight, "fsdp", axis=0, tiled=True),
        lax.all_gather(out_bias, "fsdp", axis=0, tiled=True),
    )
    resid_in = tokens.astype(jnp.float32)
    normed_one = normalize(
        resid_in, gain_one.astype(jnp.float32), shift_one.astype(jnp.float32)
    ).astype(jnp.bfloat16)
    queries = (
        (
            jnp.dot(normed_one, w_query, preferred_element_type=jnp.float32)
            + b_query.astype(jnp.float32)
        )
        .astype(jnp.bfloat16)
        .reshape(head_shape)
    )
    keys_mat = (
        jnp.dot(normed_one, w_key, preferred_element_type=jnp.float32)
        .astype(jnp.bfloat16)
        .reshape(head_shape)
    )
    values = (
        (
            jnp.dot(normed_one, w_value, preferred_element_type=jnp.float32)
            + b_value.astype(jnp.float32)
        )
        .astype(jnp.bfloat16)
        .reshape(head_shape)
    )
    position = jnp.arange(seq_len, dtype=jnp.int32)
    segment = jnp.sum((position[None, :, None] >= starts[:, None, :]).astype(jnp.int32), -1)
    same_seg = (segment[:, :, None] == segment[:, None, :])[:, None]

    def scores_of(query_part, key_part):
        raw_scores = (
            jnp.einsum("rqhd,rkhd->rhqk", query_part, key_part, preferred_element_type=jnp.float32)
            * scale_factor
        )
        return jnp.where(same_seg, raw_scores, MASKED)

    scores = scores_of(queries, keys_mat)
    row_max = jnp.max(scores, -1, keepdims=True)
    exp_scores = jnp.exp(scores - row_max)
    row_total = jnp.sum(exp_scores, -1, keepdims=True)
    log_total = row_max + jnp.log(row_total)
    probs_low = (exp_scores / row_total).astype(jnp.bfloat16)
    mixed = jnp.einsum("rhqk,rkhd->rqhd", probs_low, values, preferred_element_type=jnp.float32)
    mixed = mixed.reshape(tok_count, model_width).astype(jnp.bfloat16)
    hidden = (
        resid_in
        + jnp.dot(mixed, w_out, preferred_element_type=jnp.float32)
        + b_out.astype(jnp.float32)
    )
    gain_two, shift_two, w_in, b_in, w_down, b_down = (
        lax.all_gather(norm2_gain, "fsdp", axis=0, tiled=True),
        lax.all_gather(norm2_bias, "fsdp", axis=0, tiled=True),
        lax.all_gather(expert_in, "fsdp", axis=1, tiled=True),
        lax.all_gather(expert_in_bias, "fsdp", axis=1, tiled=True),
        lax.all_gather(expert_out, "fsdp", axis=1, tiled=True),
        lax.all_gather(expert_out_bias, "fsdp", axis=1, tiled=True),
    )
    normed_two = normalize(
        hidden, gain_two.astype(jnp.float32), shift_two.astype(jnp.float32)
    ).astype(jnp.bfloat16)
    route_ids = routes[:, 0]
    member = (route_ids[:, None] == jnp.arange(EXPERTS, dtype=jnp.int32)[None, :]).astype(jnp.int32)
    rank = jnp.sum(jnp.cumsum(member, 0) * member, 1) - 1
    slot_ids = route_ids * CAP + rank
    packed = (
        jnp.zeros((EXPERTS * CAP, model_width), jnp.bfloat16)
        .at[slot_ids]
        .set(normed_two)
        .reshape(EXPERTS, CAP, model_width)
    )
    pre_act = (
        jnp.einsum("ecd,edf->ecf", packed, w_in, preferred_element_type=jnp.float32)
        + b_in.astype(jnp.float32)[:, None, :]
    )
    act_low = gelu_exact(pre_act).astype(jnp.bfloat16)
    result = (
        jnp.einsum("ecf,efd->ecd", act_low, w_down, preferred_element_type=jnp.float32)
        + b_down.astype(jnp.float32)[:, None, :]
    )
    routed = result.reshape(EXPERTS * CAP, model_width)[slot_ids]
    output = (hidden + routed).astype(jnp.bfloat16)
    gain_two_back, w_in_back, w_down_back = (
        lax.all_gather(norm2_gain, "fsdp", axis=0, tiled=True),
        lax.all_gather(expert_in, "fsdp", axis=1, tiled=True),
        lax.all_gather(expert_out, "fsdp", axis=1, tiled=True),
    )
    grad_output = cotangent.astype(jnp.float32)
    grad_packed = (
        jnp.zeros((EXPERTS * CAP, model_width), jnp.bfloat16)
        .at[slot_ids]
        .set(cotangent)
        .reshape(EXPERTS, CAP, model_width)
    )
    grad_down_bias = jnp.sum(grad_packed.astype(jnp.float32), 1)
    grad_down = jnp.einsum("ecf,ecd->efd", act_low, grad_packed, preferred_element_type=jnp.float32)
    grad_act = jnp.einsum(
        "ecd,efd->ecf", grad_packed, w_down_back, preferred_element_type=jnp.float32
    )
    grad_pre = (grad_act * gelu_slope(pre_act)).astype(jnp.bfloat16)
    grad_in_bias = jnp.sum(grad_pre.astype(jnp.float32), 1)
    grad_in = jnp.einsum("ecd,ecf->edf", packed, grad_pre, preferred_element_type=jnp.float32)
    grad_slots = jnp.einsum(
        "ecf,edf->ecd", grad_pre, w_in_back, preferred_element_type=jnp.float32
    ).reshape(EXPERTS * CAP, model_width)
    grad_normed_two = grad_slots[slot_ids]
    grad_from_norm, grad_gain_two, grad_shift_two = norm_back(
        hidden, gain_two_back.astype(jnp.float32), grad_normed_two
    )
    grad_hidden = grad_output + grad_from_norm
    column_in, column_down = (
        lax.psum_scatter(
            grad_in.astype(jnp.bfloat16), "rep", scatter_dimension=2, tiled=True
        ).astype(jnp.float32),
        lax.psum_scatter(
            grad_down.astype(jnp.bfloat16), "rep", scatter_dimension=2, tiled=True
        ).astype(jnp.float32),
    )
    share_in, share_down, part_gain_two, part_shift_two, part_in_bias, part_down_bias = (
        lax.psum_scatter(column_in, "fsdp", scatter_dimension=1, tiled=True),
        lax.psum_scatter(column_down, "fsdp", scatter_dimension=1, tiled=True),
        lax.psum_scatter(grad_gain_two, "fsdp", scatter_dimension=0, tiled=True),
        lax.psum_scatter(grad_shift_two, "fsdp", scatter_dimension=0, tiled=True),
        lax.psum_scatter(grad_in_bias, "fsdp", scatter_dimension=1, tiled=True),
        lax.psum_scatter(grad_down_bias, "fsdp", scatter_dimension=1, tiled=True),
    )
    sum_in, sum_down, stack_gain_two, stack_shift_two, stack_in_bias, stack_down_bias = (
        lax.all_gather(share_in.astype(jnp.bfloat16), "rep", axis=2, tiled=True).astype(
            share_in.dtype
        ),
        lax.all_gather(share_down.astype(jnp.bfloat16), "rep", axis=2, tiled=True).astype(
            share_down.dtype
        ),
        lax.all_gather(part_gain_two[None].astype(jnp.bfloat16), "rep", axis=0, tiled=True).astype(
            jnp.float32
        ),
        lax.all_gather(part_shift_two[None].astype(jnp.bfloat16), "rep", axis=0, tiled=True).astype(
            jnp.float32
        ),
        lax.all_gather(part_in_bias[None].astype(jnp.bfloat16), "rep", axis=0, tiled=True).astype(
            jnp.float32
        ),
        lax.all_gather(part_down_bias[None].astype(jnp.bfloat16), "rep", axis=0, tiled=True).astype(
            jnp.float32
        ),
    )
    sum_gain_two = jnp.sum(stack_gain_two, 0)
    sum_shift_two = jnp.sum(stack_shift_two, 0)
    sum_in_bias = jnp.sum(stack_in_bias, 0)
    sum_down_bias = jnp.sum(stack_down_bias, 0)
    gain_one_back, w_query_back, w_key_back, w_value_back, w_out_back = (
        lax.all_gather(norm1_gain, "fsdp", axis=0, tiled=True),
        lax.all_gather(query_weight, "fsdp", axis=0, tiled=True),
        lax.all_gather(key_weight, "fsdp", axis=0, tiled=True),
        lax.all_gather(value_weight, "fsdp", axis=0, tiled=True),
        lax.all_gather(out_weight, "fsdp", axis=0, tiled=True),
    )
    grad_branch = grad_hidden.astype(jnp.bfloat16)
    grad_out_bias = jnp.sum(grad_branch.astype(jnp.float32), 0)
    grad_out_weight = jnp.einsum(
        "td,te->de", mixed, grad_branch, preferred_element_type=jnp.float32
    )
    grad_mixed = (
        jnp.einsum("te,de->td", grad_branch, w_out_back, preferred_element_type=jnp.float32)
        .astype(jnp.bfloat16)
        .reshape(head_shape)
    )
    scores_again = scores_of(queries, keys_mat)
    probs = jnp.exp(scores_again - log_total)
    probs_again = probs.astype(jnp.bfloat16)
    grad_values = jnp.einsum(
        "rhqk,rqhd->rkhd", probs_again, grad_mixed, preferred_element_type=jnp.float32
    )
    grad_values = grad_values.astype(jnp.bfloat16).reshape(tok_count, model_width)
    grad_probs = jnp.einsum(
        "rqhd,rkhd->rhqk", grad_mixed, values, preferred_element_type=jnp.float32
    )
    grad_scores = (probs * (grad_probs - jnp.sum(grad_probs * probs, -1, keepdims=True))).astype(
        jnp.bfloat16
    )
    grad_queries = (
        (
            jnp.einsum("rhqk,rkhd->rqhd", grad_scores, keys_mat, preferred_element_type=jnp.float32)
            * scale_factor
        )
        .astype(jnp.bfloat16)
        .reshape(tok_count, model_width)
    )
    grad_keys = (
        (
            jnp.einsum("rhqk,rqhd->rkhd", grad_scores, queries, preferred_element_type=jnp.float32)
            * scale_factor
        )
        .astype(jnp.bfloat16)
        .reshape(tok_count, model_width)
    )
    grad_query_bias = jnp.sum(grad_queries.astype(jnp.float32), 0)
    grad_value_bias = jnp.sum(grad_values.astype(jnp.float32), 0)
    grad_query_weight = jnp.einsum(
        "td,te->de", normed_one, grad_queries, preferred_element_type=jnp.float32
    )
    grad_key_weight = jnp.einsum(
        "td,te->de", normed_one, grad_keys, preferred_element_type=jnp.float32
    )
    grad_value_weight = jnp.einsum(
        "td,te->de", normed_one, grad_values, preferred_element_type=jnp.float32
    )
    grad_normed_one = (
        jnp.einsum("te,de->td", grad_queries, w_query_back, preferred_element_type=jnp.float32)
        + jnp.einsum("te,de->td", grad_keys, w_key_back, preferred_element_type=jnp.float32)
        + jnp.einsum("te,de->td", grad_values, w_value_back, preferred_element_type=jnp.float32)
    )
    grad_from_first, grad_gain_one, grad_shift_one = norm_back(
        resid_in, gain_one_back.astype(jnp.float32), grad_normed_one
    )
    input_grad = grad_hidden + grad_from_first
    column_query, column_key, column_value, column_out = (
        lax.psum_scatter(
            grad_query_weight.astype(jnp.bfloat16), "rep", scatter_dimension=1, tiled=True
        ).astype(jnp.float32),
        lax.psum_scatter(
            grad_key_weight.astype(jnp.bfloat16), "rep", scatter_dimension=1, tiled=True
        ).astype(jnp.float32),
        lax.psum_scatter(
            grad_value_weight.astype(jnp.bfloat16), "rep", scatter_dimension=1, tiled=True
        ).astype(jnp.float32),
        lax.psum_scatter(
            grad_out_weight.astype(jnp.bfloat16), "rep", scatter_dimension=1, tiled=True
        ).astype(jnp.float32),
    )
    (
        share_query,
        share_key,
        share_value,
        share_out,
        part_gain_one,
        part_shift_one,
        part_query_bias,
        part_value_bias,
        part_out_bias,
    ) = (
        lax.psum_scatter(column_query, "fsdp", scatter_dimension=0, tiled=True),
        lax.psum_scatter(column_key, "fsdp", scatter_dimension=0, tiled=True),
        lax.psum_scatter(column_value, "fsdp", scatter_dimension=0, tiled=True),
        lax.psum_scatter(column_out, "fsdp", scatter_dimension=0, tiled=True),
        lax.psum_scatter(grad_gain_one, "fsdp", scatter_dimension=0, tiled=True),
        lax.psum_scatter(grad_shift_one, "fsdp", scatter_dimension=0, tiled=True),
        lax.psum_scatter(grad_query_bias, "fsdp", scatter_dimension=0, tiled=True),
        lax.psum_scatter(grad_value_bias, "fsdp", scatter_dimension=0, tiled=True),
        lax.psum_scatter(grad_out_bias, "fsdp", scatter_dimension=0, tiled=True),
    )
    (
        sum_query,
        sum_key,
        sum_value,
        sum_out,
        stack_gain_one,
        stack_shift_one,
        stack_query_bias,
        stack_value_bias,
        stack_out_bias,
    ) = (
        lax.all_gather(share_query.astype(jnp.bfloat16), "rep", axis=1, tiled=True).astype(
            share_query.dtype
        ),
        lax.all_gather(share_key.astype(jnp.bfloat16), "rep", axis=1, tiled=True).astype(
            share_key.dtype
        ),
        lax.all_gather(share_value.astype(jnp.bfloat16), "rep", axis=1, tiled=True).astype(
            share_value.dtype
        ),
        lax.all_gather(share_out.astype(jnp.bfloat16), "rep", axis=1, tiled=True).astype(
            share_out.dtype
        ),
        lax.all_gather(part_gain_one[None].astype(jnp.bfloat16), "rep", axis=0, tiled=True).astype(
            jnp.float32
        ),
        lax.all_gather(part_shift_one[None].astype(jnp.bfloat16), "rep", axis=0, tiled=True).astype(
            jnp.float32
        ),
        lax.all_gather(
            part_query_bias[None].astype(jnp.bfloat16), "rep", axis=0, tiled=True
        ).astype(jnp.float32),
        lax.all_gather(
            part_value_bias[None].astype(jnp.bfloat16), "rep", axis=0, tiled=True
        ).astype(jnp.float32),
        lax.all_gather(part_out_bias[None].astype(jnp.bfloat16), "rep", axis=0, tiled=True).astype(
            jnp.float32
        ),
    )
    sum_gain_one = jnp.sum(stack_gain_one, 0)
    sum_shift_one = jnp.sum(stack_shift_one, 0)
    sum_query_bias = jnp.sum(stack_query_bias, 0)
    sum_value_bias = jnp.sum(stack_value_bias, 0)
    sum_out_bias = jnp.sum(stack_out_bias, 0)
    return (
        output,
        input_grad,
        sum_gain_one,
        sum_shift_one,
        sum_query,
        sum_query_bias,
        sum_key,
        sum_value,
        sum_value_bias,
        sum_out,
        sum_out_bias,
        sum_gain_two,
        sum_shift_two,
        sum_in,
        sum_in_bias,
        sum_down,
        sum_down_bias,
    )


LANES = 128
BF = jnp.bfloat16
F32 = jnp.float32
VMEM_BYTES = 60 * 1024 * 1024
SMEM = pl.BlockSpec(memory_space=pltpu.SMEM)
VMEM = pl.BlockSpec(memory_space=pltpu.VMEM)
ANYWHERE = pl.BlockSpec(memory_space=pl.ANY)


def dot_nn(a, b):
    return lax.dot_general(a, b, (((1,), (0,)), ((), ())), preferred_element_type=F32)


def dot_nt(a, b):
    return lax.dot_general(a, b, (((1,), (1,)), ((), ())), preferred_element_type=F32)


def dot_tn(a, b):
    return lax.dot_general(a, b, (((0,), (0,)), ((), ())), preferred_element_type=F32)


def kernel_call(body, name, out_shape, in_specs, out_specs, scratch, flops, args):
    return pl.pallas_call(
        body,
        out_shape=out_shape,
        in_specs=in_specs,
        out_specs=out_specs,
        scratch_shapes=scratch,
        compiler_params=pltpu.CompilerParams(vmem_limit_bytes=VMEM_BYTES),
        cost_estimate=pl.CostEstimate(
            flops=int(flops), bytes_accessed=8 << 20, transcendentals=0
        ),
        name=name,
    )(*args)


def sds(shape, dtype=BF):
    return jax.ShapeDtypeStruct(shape, dtype)


def center(v):
    mean = jnp.mean(v, -1, keepdims=True)
    centred = v - mean
    inverse = lax.rsqrt(jnp.mean(centred * centred, -1, keepdims=True) + EPSILON)
    return centred * inverse, inverse


def norm_grad(normed, inverse, gain, gradient):
    dn = gradient * gain
    return inverse * (
        dn - jnp.mean(dn, -1, keepdims=True) - normed * jnp.mean(dn * normed, -1, keepdims=True)
    )


def exact_rows(place, v):
    high = v.astype(BF)
    rest = (v - high.astype(F32)).astype(BF)
    return dot_nn(place, high) + dot_nn(place, rest)


def segment_bias(starts, length, segs):
    col = lax.broadcasted_iota(jnp.int32, (length, 1), 0)
    row = lax.broadcasted_iota(jnp.int32, (1, length), 1)
    col_seg = jnp.zeros((length, 1), jnp.int32)
    row_seg = jnp.zeros((1, length), jnp.int32)
    for k in range(segs):
        col_seg = col_seg + jnp.where(col >= starts[0, k], 1, 0)
        row_seg = row_seg + jnp.where(row >= starts[0, k], 1, 0)
    return jnp.where(col_seg == row_seg, 0.0, MASKED)


def load_pieces(me, refs, layout, dst, sems, part=None):
    copies = []
    for i, (ref, (mask, offset, rows, shard)) in enumerate(zip(refs, layout, strict=True)):
        at = pl.multiple_of((me ^ mask) * shard + offset, 16)
        src = ref if part is None else ref.at[part]
        copy = pltpu.make_async_copy(src, dst.at[pl.ds(at, rows)], sems.at[i])
        copy.start()
        copies.append(copy)
    return copies


def attention_forward(layout, segs, *refs):
    count = len(layout)
    me_ref, starts, tokens, vec = refs[:4]
    pieces = refs[4 : 4 + count]
    qkv, mixed, lse, n1_out, weights, v_t, mixed_t, bias, sems = refs[4 + count :]
    tok, width = tokens.shape
    copies = load_pieces(me_ref[0], pieces, layout, weights, sems)
    bias[...] = segment_bias(starts, tok, segs)
    normed, _ = center(tokens[...].astype(F32))
    n1_out[...] = (normed * vec[0:1, :] + vec[1:2, :]).astype(BF)
    for copy in copies:
        copy.wait()
    for i in range(3):
        part = dot_nn(n1_out[...], weights[:, i * width : (i + 1) * width])
        if i != 1:
            part = part + (vec[2:3, :] if i == 0 else vec[3:4, :])
        part = part.astype(BF)
        if i == 0:
            part = part * jnp.asarray(HEAD**-0.5, BF)
        qkv[:, i * width : (i + 1) * width] = part
    v_t[...] = qkv[:, 2 * width :].T
    half = lax.broadcasted_iota(jnp.int32, (1, LANES), 1) < HEAD

    def pair(p, carry):
        at = pl.multiple_of(p * LANES, LANES)
        q_pair = qkv[:, pl.ds(at, LANES)]
        k_pair = qkv[:, pl.ds(pl.multiple_of(width + p * LANES, LANES), LANES)]
        for s in range(2):
            q_one = jnp.where(half if s == 0 else ~half, q_pair, jnp.zeros_like(q_pair))
            scores = dot_nt(k_pair, q_one) + bias[...]
            top = jnp.max(scores, 0, keepdims=True)
            e = jnp.exp(scores - top)
            total = jnp.sum(e, 0, keepdims=True)
            probs = (e * (1.0 / total)).astype(BF)
            rows = pl.ds(pl.multiple_of(p * LANES + s * HEAD, HEAD), HEAD)
            mixed_t[rows, :] = dot_nn(v_t[rows, :], probs)
            lse[pl.ds(2 * p + s, 1), :] = top + jnp.log(total)
        return carry

    lax.fori_loop(0, width // LANES, pair, 0)
    mixed[...] = mixed_t[...].T.astype(BF)


def call_attention_forward(me, starts, tokens, vec, pieces, layout):
    tok, width = tokens.shape
    heads16 = (width // HEAD + 7) // 8 * 8
    return kernel_call(
        lambda *refs: attention_forward(layout, starts.shape[1], *refs),
        "attention_forward",
        (sds((tok, 3 * width)), sds((tok, width)), sds((heads16, tok), F32), sds((tok, width))),
        [SMEM, SMEM, VMEM, VMEM] + [ANYWHERE] * len(pieces),
        (VMEM,) * 4,
        [
            pltpu.VMEM((width, 3 * width), BF),
            pltpu.VMEM((width, tok), BF),
            pltpu.VMEM((width, tok), F32),
            pltpu.VMEM((tok, tok), F32),
            pltpu.SemaphoreType.DMA((len(pieces),)),
        ],
        2 * tok * width * 3 * width * 3,
        (me, starts, tokens, vec, *pieces),
    )


def attention_backward(n, layout, segs, n_vec, *refs):
    count = len(layout)
    me_ref, starts, tokens, vec, vec_grads, qkv, lse, n1, g_mixed, g_hidden = refs[:10]
    pieces = refs[10 : 10 + count]
    input_grad, keep, send = refs[10 + count : 13 + count]
    weights, k_t, gq_t, bias, g_qkv, g_w, v_rows, sems, out_sems = refs[13 + count :]
    tok, width = tokens.shape
    shard = width // n
    me = me_ref[0]
    copies = load_pieces(me, pieces, layout, weights, sems)
    bias[...] = segment_bias(starts, tok, segs)
    k_t[...] = qkv[:, width : 2 * width].T
    half = lax.broadcasted_iota(jnp.int32, (1, LANES), 1) < HEAD

    def pair(p, carry):
        at = pl.ds(pl.multiple_of(p * LANES, LANES), LANES)
        at_k = pl.ds(pl.multiple_of(width + p * LANES, LANES), LANES)
        at_v = pl.ds(pl.multiple_of(2 * width + p * LANES, LANES), LANES)
        q_pair, k_pair, v_pair, gm_pair = qkv[:, at], qkv[:, at_k], qkv[:, at_v], g_mixed[:, at]
        gv, gk = [], []
        for s in range(2):
            own = half if s == 0 else ~half
            q_one = jnp.where(own, q_pair, jnp.zeros_like(q_pair))
            gm_one = jnp.where(own, gm_pair, jnp.zeros_like(gm_pair))
            scores = dot_nt(k_pair, q_one) + bias[...]
            probs = jnp.exp(scores - lse[pl.ds(2 * p + s, 1), :])
            g_probs = dot_nt(v_pair, gm_one)
            delta = jnp.sum(probs * g_probs, 0, keepdims=True)
            g_scores = (probs * (g_probs - delta)).astype(BF)
            gv.append(dot_nn(probs.astype(BF), gm_pair))
            gk.append(dot_nn(g_scores, q_pair))
            rows = pl.ds(pl.multiple_of(p * LANES + s * HEAD, HEAD), HEAD)
            gq_t[rows, :] = dot_nn(k_t[rows, :], g_scores)
        g_qkv[:, at_v] = jnp.where(half, gv[0], gv[1]).astype(BF)
        g_qkv[:, at_k] = jnp.where(half, gk[0], gk[1]).astype(BF)
        return carry

    lax.fori_loop(0, width // LANES, pair, 0)
    g_qkv[:, :width] = (gq_t[...].T * (HEAD**-0.5)).astype(BF)
    for i in range(3):
        cols = slice(i * width, (i + 1) * width)
        g_w[:, cols] = dot_tn(n1[...], g_qkv[:, cols]).astype(BF)
    for copy in copies:
        copy.wait()
    g_n1 = jnp.zeros((tok, width), F32)
    for i in range(3):
        cols = slice(i * width, (i + 1) * width)
        g_n1 = g_n1 + dot_nt(g_qkv[:, cols], weights[:, cols])
    normed, inverse = center(tokens[...].astype(F32))
    input_grad[...] = g_hidden[...] + norm_grad(normed, inverse, vec[0:1, :], g_n1)
    v_rows[...] = jnp.zeros_like(v_rows)
    v_rows[0:1, :] = jnp.sum(g_n1 * normed, 0, keepdims=True)
    v_rows[1:2, :] = jnp.sum(g_n1, 0, keepdims=True)
    v_rows[2:3, :] = jnp.sum(g_qkv[:, :width].astype(F32), 0, keepdims=True)
    v_rows[3:4, :] = jnp.sum(g_qkv[:, 2 * width :].astype(F32), 0, keepdims=True)
    v_rows[4 : n_vec, :] = vec_grads[4 : n_vec, :]
    g_w[:, 3 * width :] = v_rows[...].T.astype(BF)
    outs = []
    for m in range(n):
        src = g_w.at[pl.ds(pl.multiple_of((me ^ m) * shard, 16), shard)]
        copy = pltpu.make_async_copy(src, (send if m % 2 else keep).at[m // 2], out_sems.at[m])
        copy.start()
        outs.append(copy)
    for copy in outs:
        copy.wait()


def call_attention_backward(
    n, me, starts, tokens, vec, vec_grads, qkv, lse, n1, g_mixed, g_hidden, pieces, layout, n_vec
):
    tok, width = tokens.shape
    shard = width // n
    return kernel_call(
        lambda *refs: attention_backward(n, layout, starts.shape[1], n_vec, *refs),
        "attention_backward",
        (sds((tok, width), F32),) + (sds((n // 2, shard, 3 * width + LANES)),) * 2,
        [SMEM, SMEM] + [VMEM] * 8 + [ANYWHERE] * len(pieces),
        (VMEM, ANYWHERE, ANYWHERE),
        [
            pltpu.VMEM((width, 3 * width), BF),
            pltpu.VMEM((width, tok), BF),
            pltpu.VMEM((width, tok), F32),
            pltpu.VMEM((tok, tok), F32),
            pltpu.VMEM((tok, 3 * width), BF),
            pltpu.VMEM((width, 3 * width + LANES), BF),
            pltpu.VMEM((LANES, width), F32),
            pltpu.SemaphoreType.DMA((len(pieces),)),
            pltpu.SemaphoreType.DMA((n,)),
        ],
        2 * tok * width * 3 * width * 5,
        (me, starts, tokens, vec, vec_grads, qkv, lse, n1, g_mixed, g_hidden, *pieces),
    )


def mix_out(layout, *refs):
    count = len(layout)
    me_ref, mixed, tokens, vec, place = refs[:5]
    pieces = refs[5 : 5 + count]
    hidden, sorted_two, weights, sems = refs[5 + count :]
    copies = load_pieces(me_ref[0], pieces, layout, weights, sems, EXPERTS)
    for copy in copies:
        copy.wait()
    value = tokens[...].astype(F32) + dot_nn(mixed[...], weights[...]) + vec[4:5, :]
    hidden[...] = value
    normed, _ = center(value)
    sorted_two[...] = dot_nn(place[...], (normed * vec[5:6, :] + vec[6:7, :]).astype(BF)).astype(BF)


def call_mix_out(me, mixed, tokens, vec, place, pieces, layout):
    tok, width = tokens.shape
    return kernel_call(
        lambda *refs: mix_out(layout, *refs),
        "mix_out",
        (sds((tok, width), F32), sds((place.shape[0], width))),
        [SMEM] + [VMEM] * 4 + [ANYWHERE] * len(pieces),
        (VMEM, VMEM),
        [pltpu.VMEM((width, width), BF), pltpu.SemaphoreType.DMA((len(pieces),))],
        2 * tok * width * width * 3,
        (me, mixed, tokens, vec, place, *pieces),
    )


def load_blocks(refs, layout, dst, sems):
    copies = []
    for i, (ref, (block, offset, rows)) in enumerate(zip(refs, layout, strict=True)):
        copy = pltpu.make_async_copy(ref, dst.at[block, pl.ds(offset, rows)], sems.at[i])
        copy.start()
        copies.append(copy)
    return copies


def load_expert_weights(me, refs, layout, dst, sems):
    copies = []
    for i, (ref, (mask, offset, rows, shard)) in enumerate(zip(refs, layout, strict=True)):
        at = pl.multiple_of((me ^ mask) * shard + offset, 16)
        copy = pltpu.make_async_copy(ref.at[pl.ds(0, EXPERTS)], dst.at[:, pl.ds(at, rows)], sems.at[i])
        copy.start()
        copies.append(copy)
    return copies


def window(meta, block, e):
    begin = pl.multiple_of(meta[block, 3 * e], 16)
    row = lax.broadcasted_iota(jnp.int32, (CAP, 1), 0)
    return pl.ds(begin, CAP), (row >= meta[block, 3 * e + 1]) & (row < meta[block, 3 * e + 2])


def experts(nb, lay_x, lay_g, lay_w, *refs):
    cx, cg, cw = len(lay_x), len(lay_g), len(lay_w)
    me_ref, meta, b_in = refs[:3]
    at = 3
    x_refs, at = refs[at : at + cx], at + cx
    g_refs, at = refs[at : at + cg], at + cg
    w_refs, at = refs[at : at + cw], at + cw
    down_mine, down_other = refs[at : at + 2]
    res, dsl, act_out, dp_out = refs[at + 2 : at + 6]
    x_all, g_all, w_in, w_down, res_s, dsl_s, xs, gs, sx, sg, sw, sd, so = refs[at + 6 :]
    me = me_ref[0]
    shard_ff = down_mine.shape[1]
    core = me % 2
    copies = load_expert_weights(me, w_refs, lay_w, w_in, sw)
    for i, ref in enumerate((down_mine, down_other)):
        rows = pl.ds(pl.multiple_of((core if i == 0 else 1 - core) * shard_ff, 16), shard_ff)
        copy = pltpu.make_async_copy(ref, w_down.at[:, rows], sd.at[i])
        copy.start()
        copies.append(copy)
    copies += load_blocks(x_refs, lay_x, x_all, sx) + load_blocks(g_refs, lay_g, g_all, sg)
    res_s[...] = jnp.zeros_like(res_s)
    dsl_s[...] = jnp.zeros_like(dsl_s)
    for copy in copies:
        copy.wait()

    def expert(e, carry):
        spans = []
        for b in range(nb):
            span, inside = window(meta, b, e)
            spans.append((span, inside))
            g = g_all[b, span, :]
            xs[b * CAP : (b + 1) * CAP, :] = x_all[b, span, :]
            gs[b * CAP : (b + 1) * CAP, :] = jnp.where(inside, g, jnp.zeros_like(g))
        pre = dot_nn(xs[...], w_in[e]) + b_in[e]
        cdf = 0.5 * (1.0 + lax.erf(pre * 0.7071067811865476))
        act = (pre * cdf).astype(BF)
        slope = cdf + pre * jnp.exp(-0.5 * pre * pre) * 0.3989422804014327
        dp = (dot_nt(gs[...], w_down[e]) * slope).astype(BF)
        act_out[e] = act
        dp_out[e] = dp
        for dst, value in ((dsl_s, dot_nt(dp, w_in[e])), (res_s, dot_nn(act, w_down[e]))):
            value = value.astype(BF)
            for b, (span, inside) in enumerate(spans):
                dst[b, span, :] = jnp.where(inside, value[b * CAP : (b + 1) * CAP], dst[b, span, :])
        return carry

    lax.fori_loop(0, EXPERTS, expert, 0)
    outs = []
    for i, (src, dst) in enumerate(((dsl_s, dsl), (res_s, res))):
        copy = pltpu.make_async_copy(src, dst, so.at[i])
        copy.start()
        outs.append(copy)
    for copy in outs:
        copy.wait()


def call_experts(nb, me, meta, b_in, xp, lay_x, gp, lay_g, wp, lay_w, down_mine, down_other):
    rows, width = max(o + r for _, o, r in lay_x), xp[0].shape[1]
    ff = 2 * down_mine.shape[1]
    dma = pltpu.SemaphoreType.DMA
    return kernel_call(
        lambda *refs: experts(nb, lay_x, lay_g, lay_w, *refs),
        "experts",
        (sds((nb, rows, width)),) * 2 + (sds((EXPERTS, nb * CAP, ff)),) * 2,
        [SMEM, SMEM, VMEM] + [ANYWHERE] * (len(xp) + len(gp) + len(wp) + 2),
        (ANYWHERE, ANYWHERE, VMEM, VMEM),
        [pltpu.VMEM((nb, rows, width), BF)] * 2
        + [pltpu.VMEM((EXPERTS, width, ff), BF), pltpu.VMEM((EXPERTS, ff, width), BF)]
        + [pltpu.VMEM((nb, rows, width), BF)] * 2
        + [pltpu.VMEM((nb * CAP, width), BF)] * 2
        + [dma((len(xp),)), dma((len(gp),)), dma((len(wp),)), dma((2,)), dma((2,))],
        2 * nb * CAP * EXPERTS * width * ff * 4,
        (me, meta, b_in, *xp, *gp, *wp, down_mine, down_other),
    )


def expert_grads(n, calls, lay_x, lay_g, *refs):
    cx, cg, cc = len(lay_x), len(lay_g), len(calls)
    me_ref, meta = refs[:2]
    at = 2
    x_refs, at = refs[at : at + cx], at + cx
    g_refs, at = refs[at : at + cg], at + cg
    acts, at = refs[at : at + cc], at + cc
    dps, at = refs[at : at + cc], at + cc
    down_keep, down_send, in_keep, in_send = refs[at : at + 4]
    x_all, g_all, act_s, dp_s, xs, gs, g_down, g_in, sx, sg, sa, sp, so = refs[at + 4 :]
    me = me_ref[0]
    core = me % 2
    blocks = sum(calls)
    _, width, ff = g_in.shape
    shard = width // n
    copies = load_blocks(x_refs, lay_x, x_all, sx) + load_blocks(g_refs, lay_g, g_all, sg)
    first = 0
    for i, nb in enumerate(calls):
        for src, dst, sem in ((acts[i], act_s, sa), (dps[i], dp_s, sp)):
            copy = pltpu.make_async_copy(src, dst.at[:, pl.ds(first * CAP, nb * CAP)], sem.at[i])
            copy.start()
            copies.append(copy)
        first += nb
    for copy in copies:
        copy.wait()
    down_rows = EXPERTS * (ff // 2)

    def expert(e, carry):
        for b in range(blocks):
            span, inside = window(meta, b, e)
            g = g_all[b, span, :]
            xs[b * CAP : (b + 1) * CAP, :] = x_all[b, span, :]
            gs[b * CAP : (b + 1) * CAP, :] = jnp.where(inside, g, jnp.zeros_like(g))
        g_down[e] = dot_tn(act_s[e], gs[...]).astype(BF)
        g_in[e] = dot_tn(xs[...], dp_s[e]).astype(BF)
        return carry

    lax.fori_loop(0, EXPERTS, expert, 0)
    lane = jnp.zeros((16, width - ff // 2), F32)
    row = lax.broadcasted_iota(jnp.int32, (16, 1), 0)
    low = jnp.zeros((16, ff // 2), F32)
    high = jnp.zeros((16, ff // 2), F32)
    for e in range(EXPERTS):
        total = jnp.sum(dp_s[e].astype(F32), 0, keepdims=True)
        low = low + jnp.where(row == e, total[:, : ff // 2], 0.0)
        high = high + jnp.where(row == e, total[:, ff // 2 :], 0.0)
    first_core = core == 0
    tail = pl.ds(down_rows, 16)
    down_keep[tail, :] = jnp.concatenate([jnp.where(first_core, low, high), lane], 1).astype(BF)
    down_send[tail, :] = jnp.concatenate([jnp.where(first_core, high, low), lane], 1).astype(BF)
    half = ff // 2
    outs = []
    for e in range(EXPERTS):
        for i, dst in enumerate((down_keep, down_send)):
            src = g_down.at[e, pl.ds(pl.multiple_of((core if i == 0 else 1 - core) * half, 16), half)]
            outs.append(
                pltpu.make_async_copy(src, dst.at[pl.ds(e * half, half)], so.at[2 * e + i])
            )
    for m in range(n):
        src = g_in.at[:, pl.ds(pl.multiple_of((me ^ m) * shard, 16), shard)]
        dst = (in_send if m % 2 else in_keep).at[m // 2]
        outs.append(pltpu.make_async_copy(src, dst, so.at[2 * EXPERTS + m]))
    for copy in outs:
        copy.start()
    for copy in outs:
        copy.wait()


def call_expert_grads(n, me, meta, xp, lay_x, gp, lay_g, acts, dps, calls):
    rows, width = max(o + r for _, o, r in lay_x), xp[0].shape[1]
    ff = acts[0].shape[2]
    blocks = sum(calls)
    dma = pltpu.SemaphoreType.DMA
    shard = width // n
    down = EXPERTS * (ff // 2) + 16
    return kernel_call(
        lambda *refs: expert_grads(n, calls, lay_x, lay_g, *refs),
        "expert_grads",
        (sds((down, width)),) * 2 + (sds((n // 2, EXPERTS, shard, ff)),) * 2,
        [SMEM, SMEM] + [ANYWHERE] * (len(xp) + len(gp) + 2 * len(calls)),
        (VMEM, VMEM, ANYWHERE, ANYWHERE),
        [pltpu.VMEM((blocks, rows, width), BF)] * 2
        + [pltpu.VMEM((EXPERTS, blocks * CAP, ff), BF)] * 2
        + [pltpu.VMEM((blocks * CAP, width), BF)] * 2
        + [pltpu.VMEM((EXPERTS, ff, width), BF), pltpu.VMEM((EXPERTS, width, ff), BF)]
        + [dma((len(xp),)), dma((len(gp),)), dma((len(calls),)), dma((len(calls),))]
        + [dma((2 * EXPERTS + n,))],
        2 * blocks * CAP * EXPERTS * width * ff * 2,
        (me, meta, *xp, *gp, *acts, *dps),
    )


def mix_out_backward(n, layout, terms, *refs):
    count = len(layout)
    me_ref, place_t, hidden, cot, vec, mixed, down_bias = refs[:7]
    got = refs[7 : 7 + terms]
    pieces = refs[7 + terms : 7 + terms + count]
    g_hidden, g_mixed, vec_grads, keep, send = refs[7 + terms + count : 12 + terms + count]
    weights, g_w, sems, out_sems = refs[12 + terms + count :]
    me = me_ref[0]
    tok, width = hidden.shape
    shard = width // n
    copies = load_pieces(me, pieces, layout, weights, sems, EXPERTS)
    total = got[0][...].astype(F32)
    for ref in got[1:]:
        total = total + ref[...].astype(F32)
    gradient = exact_rows(place_t[...], total)
    normed, inverse = center(hidden[...])
    value = cot[...].astype(F32) + norm_grad(normed, inverse, vec[5:6, :], gradient)
    g_hidden[...] = value
    branch = value.astype(BF)
    vec_grads[...] = jnp.zeros_like(vec_grads)
    vec_grads[4:5, :] = jnp.sum(branch.astype(F32), 0, keepdims=True)
    vec_grads[5:6, :] = jnp.sum(gradient * normed, 0, keepdims=True)
    vec_grads[6:7, :] = jnp.sum(gradient, 0, keepdims=True)
    vec_grads[7 : 7 + EXPERTS, :] = down_bias[...]
    for copy in copies:
        copy.wait()
    g_mixed[...] = dot_nt(branch, weights[...]).astype(BF)
    g_w[...] = dot_tn(mixed[...], branch).astype(BF)
    outs = []
    for m in range(n):
        src = g_w.at[pl.ds(pl.multiple_of((me ^ m) * shard, 16), shard)]
        copy = pltpu.make_async_copy(src, (send if m % 2 else keep).at[m // 2], out_sems.at[m])
        copy.start()
        outs.append(copy)
    for copy in outs:
        copy.wait()


def call_mix_out_backward(n, me, place_t, hidden, cot, vec, mixed, down_bias, got, pieces, layout):
    tok, width = hidden.shape
    shard = width // n
    return kernel_call(
        lambda *refs: mix_out_backward(n, layout, len(got), *refs),
        "mix_out_backward",
        (sds((tok, width), F32), sds((tok, width)), sds((16, width), F32))
        + (sds((n // 2, shard, width)),) * 2,
        [SMEM] + [VMEM] * (6 + len(got)) + [ANYWHERE] * len(pieces),
        (VMEM, VMEM, VMEM, ANYWHERE, ANYWHERE),
        [pltpu.VMEM((width, width), BF)] * 2
        + [pltpu.SemaphoreType.DMA((len(pieces),)), pltpu.SemaphoreType.DMA((n,))],
        2 * tok * width * width * 3,
        (me, place_t, hidden, cot, vec, mixed, down_bias, *got, *pieces),
    )


def finish_output(terms, *refs):
    place_t, hidden, route, vec = refs[:4]
    got = refs[4 : 4 + terms]
    out = refs[4 + terms]
    total = got[0][...].astype(F32)
    for ref in got[1:]:
        total = total + ref[...].astype(F32)
    value = hidden[...] + exact_rows(place_t[...], total)
    for e in range(EXPERTS):
        value = value + jnp.where(route[...] == e, vec[7 + e : 8 + e, :], 0.0)
    out[...] = value.astype(BF)


def call_finish_output(place_t, hidden, route, vec, got):
    return kernel_call(
        lambda *refs: finish_output(len(got), *refs),
        "finish_output",
        sds(hidden.shape),
        [VMEM] * (4 + len(got)),
        VMEM,
        [],
        4 * place_t.size * hidden.shape[1],
        (place_t, hidden, route, vec, *got),
    )


def swap(v, n, mask):
    return lax.ppermute(v, "fsdp", [(i, i ^ mask) for i in range(n)])


def gather_chips(v, n):
    rows = v.shape[0]
    half = rows // 32 * 16
    along, across = swap(v, n, 2), swap(v, n, 4)
    return [
        (v, 0, 0),
        (along, 2, 0),
        (across, 4, 0),
        (swap(along[:half], n, 4), 6, 0),
        (swap(across[half:], n, 2), 6, half),
    ]


def gather_all(v, n):
    pieces = gather_chips(v, n)
    return pieces + [(swap(p, n, 1), mask ^ 1, offset) for p, mask, offset in pieces]


def layout_of(pieces, shard):
    return [(mask, offset, p.shape[0], shard) for p, mask, offset in pieces]


def blocks_of(pieces, masks):
    return [(masks.index(mask), offset, p.shape[0]) for p, mask, offset in pieces]


def scatter_chips(terms, n):
    return [terms[0]] + [swap(terms[i], n, 2 * i) for i in range(1, n // 2)]


def add_low(*terms):
    total = terms[0].astype(F32)
    for term in terms[1:]:
        total = total + term.astype(F32)
    return total.astype(BF)


def scatter_all(keep, send, n):
    other = swap(send, n, 1)
    return add_low(*scatter_chips([add_low(keep[i], other[i]) for i in range(n // 2)], n))


def line_in(v):
    return add_low(v, lax.ppermute(v, "rep", [(0, 1), (3, 2)]))


def line_across(v):
    return add_low(v, lax.ppermute(v, "rep", [(1, 2), (2, 1)]))


def line_out(v):
    at = lax.axis_index("rep")
    return jnp.where((at == 0) | (at == 3), lax.ppermute(v, "rep", [(1, 0), (2, 3)]), v)


def line_sum(v):
    return line_out(line_across(line_in(v)))


def per_device_tokens(
    n,
    tokens,
    starts,
    routes,
    norm1_gain,
    norm1_bias,
    query_weight,
    query_bias,
    key_weight,
    value_weight,
    value_bias,
    out_weight,
    out_bias,
    norm2_gain,
    norm2_bias,
    expert_in,
    expert_in_bias,
    expert_out,
    expert_out_bias,
    cotangent,
):
    index = lax.axis_index("fsdp")
    me = index.astype(jnp.int32).reshape(1)
    tok_count, width = tokens.shape
    shard = width // n
    ff_shard = expert_out.shape[1]
    ff_pair = 2 * ff_shard
    masks = list(range(0, n, 2))
    order = index ^ jnp.arange(n, dtype=jnp.int32)

    w_qkv = gather_all(jnp.concatenate([query_weight, key_weight, value_weight], 1), n)

    route_ids = routes[:, 0]
    member = (route_ids[:, None] == jnp.arange(EXPERTS, dtype=jnp.int32)[None, :]).astype(jnp.int32)
    rank = jnp.sum(jnp.cumsum(member, 0) * member, 1) - 1
    counts = jnp.sum(member, 0)
    padded = (counts + 15) // 16
    base = jnp.cumsum(padded) - padded
    slots = tok_count + 16 * (EXPERTS - 1)
    position = jnp.sum(member * base[None, :], 1) * 16 + rank
    slot = jnp.arange(slots, dtype=jnp.int32)
    place = (slot[:, None] == position[None, :]).astype(BF)
    place_t = (position[:, None] == slot[None, :]).astype(BF)
    begin = jnp.minimum(base, (slots - CAP) // 16)
    meta = jnp.stack([begin, base - begin, base - begin + padded], 1).reshape(3 * EXPERTS)

    vectors = [norm1_gain, norm1_bias, query_bias, value_bias, out_bias, norm2_gain, norm2_bias]
    n_vec = len(vectors) + EXPERTS
    small = jnp.concatenate([jnp.stack(vectors), expert_out_bias], 0)
    small = jnp.pad(small, ((0, 0), (0, LANES - shard)))
    meta_row = jnp.pad(meta.astype(BF), (0, LANES - meta.shape[0]))[None]
    bias_rows = expert_in_bias.reshape(-1, LANES)
    small = jnp.concatenate([small, meta_row, bias_rows], 0)
    small = jnp.pad(small, ((0, 32 - small.shape[0]), (0, 0)))
    small_all = lax.all_gather(small, "fsdp", axis=0, tiled=False)
    vec = small_all[:, :n_vec, :shard].transpose(1, 0, 2).reshape(n_vec, width).astype(F32)
    vec = jnp.pad(vec, ((0, 16 - n_vec), (0, 0)))
    by_mask = jnp.take(small_all, order, axis=0)
    meta_rel = by_mask[:, n_vec, : 3 * EXPERTS].astype(jnp.int32)[0::2] * 16
    pair_bias = lax.dynamic_slice(small_all, (index // 2 * 2, n_vec + 1, 0), (2,) + bias_rows.shape)
    b_in = pair_bias.reshape(2, EXPERTS, ff_shard).transpose(1, 0, 2).reshape(EXPERTS, 1, ff_pair).astype(F32)

    def in_piece(mask):
        cols = (index ^ mask) // 2 * ff_pair
        part = lax.dynamic_slice(expert_in, (0, 0, cols), (EXPERTS, shard, ff_pair))
        return jnp.concatenate([part, out_weight[None]], 0)

    w_two = [(swap(in_piece(m), n, m) if m else in_piece(m), m, 0) for m in masks]
    w_two = w_two + [(swap(p, n, 1), m ^ 1, 0) for p, m, _ in w_two]
    lay_two = [(m, 0, shard, shard) for _, m, _ in w_two]
    w_two = [p for p, _, _ in w_two]
    down_other = swap(expert_out, n, 1)

    def sort(v):
        return dot_nn(place, v).astype(BF)

    grad_pieces = gather_chips(sort(cotangent), n)
    down_bias = dot_tn(member.astype(BF), cotangent)

    lay_qkv = layout_of(w_qkv, shard)
    w_qkv = [p for p, _, _ in w_qkv]
    qkv, mixed, lse, n1 = call_attention_forward(me, starts, tokens, vec, w_qkv, lay_qkv)
    hidden, sorted_two = call_mix_out(me, mixed, tokens, vec, place, w_two, lay_two)
    token_pieces = gather_chips(sorted_two, n)

    calls = ((0,), (1, 2), (3,))
    res, dsl, acts, dps = [], [], [], []
    for call in calls:
        here = [masks[i] for i in call]
        xp = [p for p in token_pieces if p[1] in here]
        gp = [p for p in grad_pieces if p[1] in here]
        r, d, a, p = call_experts(
            len(call),
            me,
            meta_rel[call[0] : call[-1] + 1],
            b_in,
            [v for v, _, _ in xp],
            blocks_of(xp, here),
            [v for v, _, _ in gp],
            blocks_of(gp, here),
            w_two,
            lay_two,
            expert_out,
            down_other,
        )
        res += [r[i] for i in range(len(call))]
        dsl += [d[i] for i in range(len(call))]
        acts.append(a)
        dps.append(p)
    got_dsl = scatter_chips(dsl, n)
    down_keep, down_send, in_keep, in_send = call_expert_grads(
        n,
        me,
        meta_rel,
        [v for v, _, _ in token_pieces],
        blocks_of(token_pieces, masks),
        [v for v, _, _ in grad_pieces],
        blocks_of(grad_pieces, masks),
        acts,
        dps,
        tuple(len(call) for call in calls),
    )
    got_res = scatter_chips(res, n)
    route = routes
    output = call_finish_output(place_t, hidden, route, vec, got_res)

    g_hidden, g_mixed, vec_grads, out_keep, out_send = call_mix_out_backward(
        n, me, place_t, hidden, cotangent, vec, mixed, down_bias, got_dsl, w_two, lay_two
    )
    sum_out = line_sum(scatter_all(out_keep, out_send, n)).astype(F32)

    down = add_low(down_keep, swap(down_send, n, 1))
    cut = down.shape[0] // 32 * 16
    sum_down = jnp.concatenate([line_sum(down[:cut]), line_sum(down[cut:])], 0)
    sum_in_bias = sum_down[EXPERTS * ff_shard : EXPERTS * ff_shard + EXPERTS, :ff_shard].astype(F32)
    sum_down = sum_down[: EXPERTS * ff_shard].reshape(EXPERTS, ff_shard, width).astype(F32)
    in_other = swap(in_send, n, 1)
    in_got = scatter_chips([add_low(in_keep[i], in_other[i]) for i in range(n // 2)], n)
    chip_order = index // 2 ^ jnp.arange(n // 2, dtype=jnp.int32)
    lines = [
        line_sum(jnp.stack(in_got[: n // 4])),
        line_sum(jnp.stack(in_got[n // 4 :])),
    ]
    sum_in = jnp.take(jnp.concatenate(lines, 0), chip_order, axis=0)
    sum_in = sum_in.transpose(1, 2, 0, 3).reshape(EXPERTS, shard, n * ff_shard).astype(F32)

    input_grad, keep, send = call_attention_backward(
        n, me, starts, tokens, vec, vec_grads, qkv, lse, n1, g_mixed, g_hidden, w_qkv, lay_qkv, n_vec
    )
    sum_last = line_sum(scatter_all(keep, send, n)).astype(F32)
    sum_vec = sum_last[:, 3 * width : 3 * width + n_vec].T
    return (
        output,
        input_grad,
        sum_vec[0],
        sum_vec[1],
        sum_last[:, :width],
        sum_vec[2],
        sum_last[:, width : 2 * width],
        sum_last[:, 2 * width : 3 * width],
        sum_vec[3],
        sum_out,
        sum_vec[4],
        sum_vec[5],
        sum_vec[6],
        sum_in,
        sum_in_bias,
        sum_down,
        sum_vec[7:],
    )


def plan_of(n, replicas):
    if n == 8 and replicas == 4:
        return lambda *args: per_device_tokens(n, *args)
    return per_device_weights


def solution(mesh):
    in_specs = (
        P(("fsdp", "rep"), None),
        P(("fsdp", "rep"), None),
        P(("fsdp", "rep"), None),
        P("fsdp"),
        P("fsdp"),
        P("fsdp", None),
        P("fsdp"),
        P("fsdp", None),
        P("fsdp", None),
        P("fsdp"),
        P("fsdp", None),
        P("fsdp"),
        P("fsdp"),
        P("fsdp"),
        P(None, "fsdp", None),
        P(None, "fsdp"),
        P(None, "fsdp", None),
        P(None, "fsdp"),
        P(("fsdp", "rep"), None),
    )
    out_specs = (
        P(("fsdp", "rep"), None),
        P(("fsdp", "rep"), None),
        P("fsdp"),
        P("fsdp"),
        P("fsdp", None),
        P("fsdp"),
        P("fsdp", None),
        P("fsdp", None),
        P("fsdp"),
        P("fsdp", None),
        P("fsdp"),
        P("fsdp"),
        P("fsdp"),
        P(None, "fsdp", None),
        P(None, "fsdp"),
        P(None, "fsdp", None),
        P(None, "fsdp"),
    )
    per_device = plan_of(mesh.shape["fsdp"], mesh.shape["rep"])
    return jax.shard_map(
        per_device, mesh=mesh, in_specs=in_specs, out_specs=out_specs, check_vma=False
    )
```

```python
import jax
import jax.numpy as jnp
from jax import lax
from jax.experimental import pallas as pl
from jax.experimental.pallas import tpu as pltpu
from jax.sharding import PartitionSpec as P

FSDP = "fsdp"
REP = "rep"
HEAD = 64
EXPERTS = 3
CAP = 208


EPSILON = 1e-05
MASKED = -1000000000.0


def normalize(inputs, gain, shift):
    mean = jnp.mean(inputs, -1, keepdims=True)
    centred = inputs - mean
    inverse = lax.rsqrt(jnp.mean(centred * centred, -1, keepdims=True) + EPSILON)
    return centred * inverse * gain + shift


def norm_back(inputs, gain, gradient):
    mean = jnp.mean(inputs, -1, keepdims=True)
    centred = inputs - mean
    inverse = lax.rsqrt(jnp.mean(centred * centred, -1, keepdims=True) + EPSILON)
    normed = centred * inverse
    grad_normed = gradient * gain
    grad_inputs = inverse * (
        grad_normed
        - jnp.mean(grad_normed, -1, keepdims=True)
        - normed * jnp.mean(grad_normed * normed, -1, keepdims=True)
    )
    return (grad_inputs, jnp.sum(gradient * normed, 0), jnp.sum(gradient, 0))


def gelu_exact(inputs):
    return 0.5 * inputs * (1.0 + lax.erf(inputs * 0.7071067811865476))


def gelu_slope(inputs):
    return (
        0.5 * (1.0 + lax.erf(inputs * 0.7071067811865476))
        + inputs * jnp.exp(-0.5 * inputs * inputs) * 0.3989422804014327
    )


def per_device_weights(
    tokens,
    starts,
    routes,
    norm1_gain,
    norm1_bias,
    query_weight,
    query_bias,
    key_weight,
    value_weight,
    value_bias,
    out_weight,
    out_bias,
    norm2_gain,
    norm2_bias,
    expert_in,
    expert_in_bias,
    expert_out,
    expert_out_bias,
    cotangent,
):
    seq_rows = starts.shape[0]
    tok_count = tokens.shape[0]
    seq_len = tok_count // seq_rows
    model_width = tokens.shape[1]
    head_count = model_width // HEAD
    head_shape = (seq_rows, seq_len, head_count, HEAD)
    scale_factor = HEAD ** (-0.5)
    gain_one, shift_one, w_query, b_query, w_key, w_value, b_value, w_out, b_out = (
        lax.all_gather(norm1_gain, FSDP, axis=0, tiled=True),
        lax.all_gather(norm1_bias, FSDP, axis=0, tiled=True),
        lax.all_gather(query_weight, FSDP, axis=0, tiled=True),
        lax.all_gather(query_bias, FSDP, axis=0, tiled=True),
        lax.all_gather(key_weight, FSDP, axis=0, tiled=True),
        lax.all_gather(value_weight, FSDP, axis=0, tiled=True),
        lax.all_gather(value_bias, FSDP, axis=0, tiled=True),
        lax.all_gather(out_weight, FSDP, axis=0, tiled=True),
        lax.all_gather(out_bias, FSDP, axis=0, tiled=True),
    )
    resid_in = tokens.astype(jnp.float32)
    normed_one = normalize(
        resid_in, gain_one.astype(jnp.float32), shift_one.astype(jnp.float32)
    ).astype(jnp.bfloat16)
    queries = (
        (
            jnp.dot(normed_one, w_query, preferred_element_type=jnp.float32)
            + b_query.astype(jnp.float32)
        )
        .astype(jnp.bfloat16)
        .reshape(head_shape)
    )
    keys_mat = (
        jnp.dot(normed_one, w_key, preferred_element_type=jnp.float32)
        .astype(jnp.bfloat16)
        .reshape(head_shape)
    )
    values = (
        (
            jnp.dot(normed_one, w_value, preferred_element_type=jnp.float32)
            + b_value.astype(jnp.float32)
        )
        .astype(jnp.bfloat16)
        .reshape(head_shape)
    )
    position = jnp.arange(seq_len, dtype=jnp.int32)
    segment = jnp.sum((position[None, :, None] >= starts[:, None, :]).astype(jnp.int32), -1)
    same_seg = (segment[:, :, None] == segment[:, None, :])[:, None]

    def scores_of(query_part, key_part):
        raw_scores = (
            jnp.einsum("rqhd,rkhd->rhqk", query_part, key_part, preferred_element_type=jnp.float32)
            * scale_factor
        )
        return jnp.where(same_seg, raw_scores, MASKED)

    scores = scores_of(queries, keys_mat)
    row_max = jnp.max(scores, -1, keepdims=True)
    exp_scores = jnp.exp(scores - row_max)
    row_total = jnp.sum(exp_scores, -1, keepdims=True)
    log_total = row_max + jnp.log(row_total)
    probs_low = (exp_scores / row_total).astype(jnp.bfloat16)
    mixed = jnp.einsum("rhqk,rkhd->rqhd", probs_low, values, preferred_element_type=jnp.float32)
    mixed = mixed.reshape(tok_count, model_width).astype(jnp.bfloat16)
    hidden = (
        resid_in
        + jnp.dot(mixed, w_out, preferred_element_type=jnp.float32)
        + b_out.astype(jnp.float32)
    )
    gain_two, shift_two, w_in, b_in, w_down, b_down = (
        lax.all_gather(norm2_gain, FSDP, axis=0, tiled=True),
        lax.all_gather(norm2_bias, FSDP, axis=0, tiled=True),
        lax.all_gather(expert_in, FSDP, axis=1, tiled=True),
        lax.all_gather(expert_in_bias, FSDP, axis=1, tiled=True),
        lax.all_gather(expert_out, FSDP, axis=1, tiled=True),
        lax.all_gather(expert_out_bias, FSDP, axis=1, tiled=True),
    )
    normed_two = normalize(
        hidden, gain_two.astype(jnp.float32), shift_two.astype(jnp.float32)
    ).astype(jnp.bfloat16)
    route_ids = routes[:, 0]
    member = (route_ids[:, None] == jnp.arange(EXPERTS, dtype=jnp.int32)[None, :]).astype(jnp.int32)
    rank = jnp.sum(jnp.cumsum(member, 0) * member, 1) - 1
    slot_ids = route_ids * CAP + rank
    packed = (
        jnp.zeros((EXPERTS * CAP, model_width), jnp.bfloat16)
        .at[slot_ids]
        .set(normed_two)
        .reshape(EXPERTS, CAP, model_width)
    )
    pre_act = (
        jnp.einsum("ecd,edf->ecf", packed, w_in, preferred_element_type=jnp.float32)
        + b_in.astype(jnp.float32)[:, None, :]
    )
    act_low = gelu_exact(pre_act).astype(jnp.bfloat16)
    result = (
        jnp.einsum("ecf,efd->ecd", act_low, w_down, preferred_element_type=jnp.float32)
        + b_down.astype(jnp.float32)[:, None, :]
    )
    routed = result.reshape(EXPERTS * CAP, model_width)[slot_ids]
    output = (hidden + routed).astype(jnp.bfloat16)
    gain_two_back, w_in_back, w_down_back = (
        lax.all_gather(norm2_gain, FSDP, axis=0, tiled=True),
        lax.all_gather(expert_in, FSDP, axis=1, tiled=True),
        lax.all_gather(expert_out, FSDP, axis=1, tiled=True),
    )
    grad_output = cotangent.astype(jnp.float32)
    grad_packed = (
        jnp.zeros((EXPERTS * CAP, model_width), jnp.bfloat16)
        .at[slot_ids]
        .set(cotangent)
        .reshape(EXPERTS, CAP, model_width)
    )
    grad_down_bias = jnp.sum(grad_packed.astype(jnp.float32), 1)
    grad_down = jnp.einsum("ecf,ecd->efd", act_low, grad_packed, preferred_element_type=jnp.float32)
    grad_act = jnp.einsum(
        "ecd,efd->ecf", grad_packed, w_down_back, preferred_element_type=jnp.float32
    )
    grad_pre = (grad_act * gelu_slope(pre_act)).astype(jnp.bfloat16)
    grad_in_bias = jnp.sum(grad_pre.astype(jnp.float32), 1)
    grad_in = jnp.einsum("ecd,ecf->edf", packed, grad_pre, preferred_element_type=jnp.float32)
    grad_slots = jnp.einsum(
        "ecf,edf->ecd", grad_pre, w_in_back, preferred_element_type=jnp.float32
    ).reshape(EXPERTS * CAP, model_width)
    grad_normed_two = grad_slots[slot_ids]
    grad_from_norm, grad_gain_two, grad_shift_two = norm_back(
        hidden, gain_two_back.astype(jnp.float32), grad_normed_two
    )
    grad_hidden = grad_output + grad_from_norm
    column_in, column_down = (
        lax.psum_scatter(
            grad_in.astype(jnp.bfloat16), REP, scatter_dimension=2, tiled=True
        ).astype(jnp.float32),
        lax.psum_scatter(
            grad_down.astype(jnp.bfloat16), REP, scatter_dimension=2, tiled=True
        ).astype(jnp.float32),
    )
    share_in, share_down, part_gain_two, part_shift_two, part_in_bias, part_down_bias = (
        lax.psum_scatter(column_in, FSDP, scatter_dimension=1, tiled=True),
        lax.psum_scatter(column_down, FSDP, scatter_dimension=1, tiled=True),
        lax.psum_scatter(grad_gain_two, FSDP, scatter_dimension=0, tiled=True),
        lax.psum_scatter(grad_shift_two, FSDP, scatter_dimension=0, tiled=True),
        lax.psum_scatter(grad_in_bias, FSDP, scatter_dimension=1, tiled=True),
        lax.psum_scatter(grad_down_bias, FSDP, scatter_dimension=1, tiled=True),
    )
    sum_in, sum_down, stack_gain_two, stack_shift_two, stack_in_bias, stack_down_bias = (
        lax.all_gather(share_in.astype(jnp.bfloat16), REP, axis=2, tiled=True).astype(
            share_in.dtype
        ),
        lax.all_gather(share_down.astype(jnp.bfloat16), REP, axis=2, tiled=True).astype(
            share_down.dtype
        ),
        lax.all_gather(part_gain_two[None].astype(jnp.bfloat16), REP, axis=0, tiled=True).astype(
            jnp.float32
        ),
        lax.all_gather(part_shift_two[None].astype(jnp.bfloat16), REP, axis=0, tiled=True).astype(
            jnp.float32
        ),
        lax.all_gather(part_in_bias[None].astype(jnp.bfloat16), REP, axis=0, tiled=True).astype(
            jnp.float32
        ),
        lax.all_gather(part_down_bias[None].astype(jnp.bfloat16), REP, axis=0, tiled=True).astype(
            jnp.float32
        ),
    )
    sum_gain_two = jnp.sum(stack_gain_two, 0)
    sum_shift_two = jnp.sum(stack_shift_two, 0)
    sum_in_bias = jnp.sum(stack_in_bias, 0)
    sum_down_bias = jnp.sum(stack_down_bias, 0)
    gain_one_back, w_query_back, w_key_back, w_value_back, w_out_back = (
        lax.all_gather(norm1_gain, FSDP, axis=0, tiled=True),
        lax.all_gather(query_weight, FSDP, axis=0, tiled=True),
        lax.all_gather(key_weight, FSDP, axis=0, tiled=True),
        lax.all_gather(value_weight, FSDP, axis=0, tiled=True),
        lax.all_gather(out_weight, FSDP, axis=0, tiled=True),
    )
    grad_branch = grad_hidden.astype(jnp.bfloat16)
    grad_out_bias = jnp.sum(grad_branch.astype(jnp.float32), 0)
    grad_out_weight = jnp.einsum(
        "td,te->de", mixed, grad_branch, preferred_element_type=jnp.float32
    )
    grad_mixed = (
        jnp.einsum("te,de->td", grad_branch, w_out_back, preferred_element_type=jnp.float32)
        .astype(jnp.bfloat16)
        .reshape(head_shape)
    )
    scores_again = scores_of(queries, keys_mat)
    probs = jnp.exp(scores_again - log_total)
    probs_again = probs.astype(jnp.bfloat16)
    grad_values = jnp.einsum(
        "rhqk,rqhd->rkhd", probs_again, grad_mixed, preferred_element_type=jnp.float32
    )
    grad_values = grad_values.astype(jnp.bfloat16).reshape(tok_count, model_width)
    grad_probs = jnp.einsum(
        "rqhd,rkhd->rhqk", grad_mixed, values, preferred_element_type=jnp.float32
    )
    grad_scores = (probs * (grad_probs - jnp.sum(grad_probs * probs, -1, keepdims=True))).astype(
        jnp.bfloat16
    )
    grad_queries = (
        (
            jnp.einsum("rhqk,rkhd->rqhd", grad_scores, keys_mat, preferred_element_type=jnp.float32)
            * scale_factor
        )
        .astype(jnp.bfloat16)
        .reshape(tok_count, model_width)
    )
    grad_keys = (
        (
            jnp.einsum("rhqk,rqhd->rkhd", grad_scores, queries, preferred_element_type=jnp.float32)
            * scale_factor
        )
        .astype(jnp.bfloat16)
        .reshape(tok_count, model_width)
    )
    grad_query_bias = jnp.sum(grad_queries.astype(jnp.float32), 0)
    grad_value_bias = jnp.sum(grad_values.astype(jnp.float32), 0)
    grad_query_weight = jnp.einsum(
        "td,te->de", normed_one, grad_queries, preferred_element_type=jnp.float32
    )
    grad_key_weight = jnp.einsum(
        "td,te->de", normed_one, grad_keys, preferred_element_type=jnp.float32
    )
    grad_value_weight = jnp.einsum(
        "td,te->de", normed_one, grad_values, preferred_element_type=jnp.float32
    )
    grad_normed_one = (
        jnp.einsum("te,de->td", grad_queries, w_query_back, preferred_element_type=jnp.float32)
        + jnp.einsum("te,de->td", grad_keys, w_key_back, preferred_element_type=jnp.float32)
        + jnp.einsum("te,de->td", grad_values, w_value_back, preferred_element_type=jnp.float32)
    )
    grad_from_first, grad_gain_one, grad_shift_one = norm_back(
        resid_in, gain_one_back.astype(jnp.float32), grad_normed_one
    )
    input_grad = grad_hidden + grad_from_first
    column_query, column_key, column_value, column_out = (
        lax.psum_scatter(
            grad_query_weight.astype(jnp.bfloat16), REP, scatter_dimension=1, tiled=True
        ).astype(jnp.float32),
        lax.psum_scatter(
            grad_key_weight.astype(jnp.bfloat16), REP, scatter_dimension=1, tiled=True
        ).astype(jnp.float32),
        lax.psum_scatter(
            grad_value_weight.astype(jnp.bfloat16), REP, scatter_dimension=1, tiled=True
        ).astype(jnp.float32),
        lax.psum_scatter(
            grad_out_weight.astype(jnp.bfloat16), REP, scatter_dimension=1, tiled=True
        ).astype(jnp.float32),
    )
    (
        share_query,
        share_key,
        share_value,
        share_out,
        part_gain_one,
        part_shift_one,
        part_query_bias,
        part_value_bias,
        part_out_bias,
    ) = (
        lax.psum_scatter(column_query, FSDP, scatter_dimension=0, tiled=True),
        lax.psum_scatter(column_key, FSDP, scatter_dimension=0, tiled=True),
        lax.psum_scatter(column_value, FSDP, scatter_dimension=0, tiled=True),
        lax.psum_scatter(column_out, FSDP, scatter_dimension=0, tiled=True),
        lax.psum_scatter(grad_gain_one, FSDP, scatter_dimension=0, tiled=True),
        lax.psum_scatter(grad_shift_one, FSDP, scatter_dimension=0, tiled=True),
        lax.psum_scatter(grad_query_bias, FSDP, scatter_dimension=0, tiled=True),
        lax.psum_scatter(grad_value_bias, FSDP, scatter_dimension=0, tiled=True),
        lax.psum_scatter(grad_out_bias, FSDP, scatter_dimension=0, tiled=True),
    )
    (
        sum_query,
        sum_key,
        sum_value,
        sum_out,
        stack_gain_one,
        stack_shift_one,
        stack_query_bias,
        stack_value_bias,
        stack_out_bias,
    ) = (
        lax.all_gather(share_query.astype(jnp.bfloat16), REP, axis=1, tiled=True).astype(
            share_query.dtype
        ),
        lax.all_gather(share_key.astype(jnp.bfloat16), REP, axis=1, tiled=True).astype(
            share_key.dtype
        ),
        lax.all_gather(share_value.astype(jnp.bfloat16), REP, axis=1, tiled=True).astype(
            share_value.dtype
        ),
        lax.all_gather(share_out.astype(jnp.bfloat16), REP, axis=1, tiled=True).astype(
            share_out.dtype
        ),
        lax.all_gather(part_gain_one[None].astype(jnp.bfloat16), REP, axis=0, tiled=True).astype(
            jnp.float32
        ),
        lax.all_gather(part_shift_one[None].astype(jnp.bfloat16), REP, axis=0, tiled=True).astype(
            jnp.float32
        ),
        lax.all_gather(
            part_query_bias[None].astype(jnp.bfloat16), REP, axis=0, tiled=True
        ).astype(jnp.float32),
        lax.all_gather(
            part_value_bias[None].astype(jnp.bfloat16), REP, axis=0, tiled=True
        ).astype(jnp.float32),
        lax.all_gather(part_out_bias[None].astype(jnp.bfloat16), REP, axis=0, tiled=True).astype(
            jnp.float32
        ),
    )
    sum_gain_one = jnp.sum(stack_gain_one, 0)
    sum_shift_one = jnp.sum(stack_shift_one, 0)
    sum_query_bias = jnp.sum(stack_query_bias, 0)
    sum_value_bias = jnp.sum(stack_value_bias, 0)
    sum_out_bias = jnp.sum(stack_out_bias, 0)
    return (
        output,
        input_grad,
        sum_gain_one,
        sum_shift_one,
        sum_query,
        sum_query_bias,
        sum_key,
        sum_value,
        sum_value_bias,
        sum_out,
        sum_out_bias,
        sum_gain_two,
        sum_shift_two,
        sum_in,
        sum_in_bias,
        sum_down,
        sum_down_bias,
    )


LANES = 128
BF = jnp.bfloat16
F32 = jnp.float32
VMEM_BYTES = 60 * 1024 * 1024
SMEM = pl.BlockSpec(memory_space=pltpu.SMEM)
VMEM = pl.BlockSpec(memory_space=pltpu.VMEM)
ANYWHERE = pl.BlockSpec(memory_space=pl.ANY)


def dot_nn(a, b):
    return lax.dot_general(a, b, (((1,), (0,)), ((), ())), preferred_element_type=F32)


def dot_nt(a, b):
    return lax.dot_general(a, b, (((1,), (1,)), ((), ())), preferred_element_type=F32)


def dot_tn(a, b):
    return lax.dot_general(a, b, (((0,), (0,)), ((), ())), preferred_element_type=F32)


def kernel_call(body, named, out_shape, in_specs, out_specs, scratch, args, alias=None):
    return pl.pallas_call(
        body,
        out_shape=out_shape,
        in_specs=in_specs,
        out_specs=out_specs,
        scratch_shapes=scratch,
        input_output_aliases=alias or {},
        compiler_params=pltpu.CompilerParams(vmem_limit_bytes=VMEM_BYTES),
        name=named.__name__,
    )(*args)


def hold(values, done):
    shapes = tuple(jax.ShapeDtypeStruct(v.shape, v.dtype) for v in values)
    return kernel_call(
        lambda *refs: None,
        hold,
        shapes,
        [ANYWHERE] * (len(values) + len(done)),
        (ANYWHERE,) * len(values),
        [],
        (*values, *done),
        {i: i for i in range(len(values))},
    )


def sds(shape, dtype=BF):
    return jax.ShapeDtypeStruct(shape, dtype)


def center(v):
    mean = jnp.mean(v, -1, keepdims=True)
    centred = v - mean
    inverse = lax.rsqrt(jnp.mean(centred * centred, -1, keepdims=True) + EPSILON)
    return centred * inverse, inverse


def norm_grad(normed, inverse, gain, gradient):
    dn = gradient * gain
    return inverse * (
        dn - jnp.mean(dn, -1, keepdims=True) - normed * jnp.mean(dn * normed, -1, keepdims=True)
    )


def exact_rows(place, v):
    high = v.astype(BF)
    rest = (v - high.astype(F32)).astype(BF)
    return dot_nn(place, high) + dot_nn(place, rest)


def segment_bias(starts, length, segs):
    col = lax.broadcasted_iota(jnp.int32, (length, 1), 0)
    row = lax.broadcasted_iota(jnp.int32, (1, length), 1)
    col_seg = jnp.zeros((length, 1), jnp.int32)
    row_seg = jnp.zeros((1, length), jnp.int32)
    for k in range(segs):
        col_seg = col_seg + jnp.where(col >= starts[0, k], 1, 0)
        row_seg = row_seg + jnp.where(row >= starts[0, k], 1, 0)
    return jnp.where(col_seg == row_seg, 0.0, MASKED)


def cuts(layout, start, count):
    found = []
    for i, part, mask, offset, rows in layout:
        low, high = max(offset, start), min(offset + rows, start + count)
        if low < high:
            found.append((i, part, mask, low - offset, low - start, high - low))
    return found


def rows_of(ref, part, row, rows):
    return ref.at[pl.ds(row, rows)] if part is None else ref.at[part, pl.ds(row, rows)]


def load_weight(me, refs, layout, segment, shard, dst, sems):
    copies = []
    for k, (i, part, mask, row, at, rows) in enumerate(cuts(layout, segment * shard, shard)):
        to = pl.multiple_of((me ^ mask) * shard + at, 16)
        src = rows_of(refs[i], part, row, rows)
        copy = pltpu.make_async_copy(src, dst.at[pl.ds(to, rows)], sems.at[k])
        copy.start()
        copies.append(copy)
    return copies


def attention_forward(n, layout, segs, n_vec, *refs):
    count = 1 + max(i for i, *_ in layout)
    me_ref, starts, tokens = refs[:3]
    pieces = refs[3 : 3 + count]
    qkv, mixed, lse, n1_out, vec, b_in = refs[3 + count : 9 + count]
    weights, smalls, v_t, mixed_t, bias, sems, small_sems = refs[9 + count :]
    tok, width = tokens.shape
    shard = width // n
    me = me_ref[0]
    small_copies = []
    for k, (i, part, mask, row, at, rows) in enumerate(cuts(layout, 4 * shard, 16)):
        copy = pltpu.make_async_copy(
            rows_of(pieces[i], part, row, rows),
            smalls.at[mask, pl.ds(at, rows)],
            small_sems.at[k],
        )
        copy.start()
        small_copies.append(copy)
    copies = []
    for i in range(3):
        cols = weights.at[:, pl.ds(i * width, width)]
        copies.append(load_weight(me, pieces, layout, i, shard, cols, sems.at[i]))
    bias[...] = segment_bias(starts, tok, segs)
    normed, _ = center(tokens[...].astype(F32))
    for copy in small_copies:
        copy.wait()
    lane = lax.broadcasted_iota(jnp.int32, (LANES, width), 0)
    col = lax.broadcasted_iota(jnp.int32, (LANES, width), 1)
    total = jnp.zeros((16, width), F32)
    for m in range(n):
        spread = ((col - (me ^ m) * shard == lane) & (lane < shard)).astype(F32).astype(BF)
        total = total + dot_nn(smalls[m, :, :LANES], spread)
    vec[...] = total
    half_ff = width // 2
    mine, other = smalls[0].astype(F32)[:, :half_ff], smalls[1].astype(F32)[:, :half_ff]
    first = me % 2 == 0
    b_in[:, :half_ff] = jnp.where(first, mine, other)
    b_in[:, half_ff:] = jnp.where(first, other, mine)
    n1_out[...] = (normed * vec[0:1, :] + vec[1:2, :]).astype(BF)
    for i in range(3):
        for copy in copies[i]:
            copy.wait()
        part = dot_nn(n1_out[...], weights[:, i * width : (i + 1) * width])
        if i != 1:
            part = part + (vec[2:3, :] if i == 0 else vec[3:4, :])
        part = part.astype(BF)
        if i == 0:
            part = part * jnp.asarray(HEAD**-0.5, BF)
        qkv[:, i * width : (i + 1) * width] = part
    v_t[...] = qkv[:, 2 * width :].T
    half = lax.broadcasted_iota(jnp.int32, (1, LANES), 1) < HEAD

    def pair(p, carry):
        at = pl.multiple_of(p * LANES, LANES)
        q_pair = qkv[:, pl.ds(at, LANES)]
        k_pair = qkv[:, pl.ds(pl.multiple_of(width + p * LANES, LANES), LANES)]
        for s in range(2):
            q_one = jnp.where(half if s == 0 else ~half, q_pair, jnp.zeros_like(q_pair))
            scores = dot_nt(k_pair, q_one) + bias[...]
            top = jnp.max(scores, 0, keepdims=True)
            e = jnp.exp(scores - top)
            total = jnp.sum(e, 0, keepdims=True)
            probs = (e * (1.0 / total)).astype(BF)
            rows = pl.ds(pl.multiple_of(p * LANES + s * HEAD, HEAD), HEAD)
            mixed_t[rows, :] = dot_nn(v_t[rows, :], probs)
            lse[pl.ds(2 * p + s, 1), :] = top + jnp.log(total)
        return carry

    lax.fori_loop(0, width // LANES, pair, 0)
    mixed[...] = mixed_t[...].T.astype(BF)


def call_attention_forward(n, me, starts, tokens, pieces, layout, n_vec):
    tok, width = tokens.shape
    heads16 = (width // HEAD + 7) // 8 * 8
    f32_row = sds((16, width), F32)
    return kernel_call(
        lambda *refs: attention_forward(n, layout, starts.shape[1], n_vec, *refs),
        attention_forward,
        (sds((tok, 3 * width)), sds((tok, width)), sds((heads16, tok), F32), sds((tok, width)))
        + (f32_row, f32_row),
        [SMEM, SMEM, VMEM] + [ANYWHERE] * len(pieces),
        (VMEM,) * 6,
        [
            pltpu.VMEM((width, 3 * width), BF),
            pltpu.VMEM((n, 16, width), BF),
            pltpu.VMEM((width, tok), BF),
            pltpu.VMEM((width, tok), F32),
            pltpu.VMEM((tok, tok), F32),
            pltpu.SemaphoreType.DMA((3, len(layout))),
            pltpu.SemaphoreType.DMA((len(layout),)),
        ],
        (me, starts, tokens, *pieces),
    )


def head_grads(first, pairs, width, qkv, lse, g_mixed, bias, k_t, gq_t, g_qkv):
    half = lax.broadcasted_iota(jnp.int32, (1, LANES), 1) < HEAD
    span = pairs * LANES

    def pair(p, carry):
        def cols(part):
            return pl.ds(pl.multiple_of(part * width + (first + p) * LANES, LANES), LANES)

        def put(part):
            return pl.ds(pl.multiple_of(part * span + p * LANES, LANES), LANES)

        q_pair, k_pair, v_pair = qkv[:, cols(0)], qkv[:, cols(1)], qkv[:, cols(2)]
        gm_pair = g_mixed[:, cols(0)]
        gv, gk = [], []
        for s in range(2):
            own = half if s == 0 else ~half
            q_one = jnp.where(own, q_pair, jnp.zeros_like(q_pair))
            gm_one = jnp.where(own, gm_pair, jnp.zeros_like(gm_pair))
            scores = dot_nt(k_pair, q_one) + bias[...]
            probs = jnp.exp(scores - lse[pl.ds(2 * (first + p) + s, 1), :])
            g_probs = dot_nt(v_pair, gm_one)
            delta = jnp.sum(probs * g_probs, 0, keepdims=True)
            g_scores = (probs * (g_probs - delta)).astype(BF)
            gv.append(dot_nn(probs.astype(BF), gm_pair))
            gk.append(dot_nn(g_scores, q_pair))
            rows = pl.ds(pl.multiple_of(p * LANES + s * HEAD, HEAD), HEAD)
            gq_t[rows, :] = dot_nn(k_t[rows, :], g_scores)
        g_qkv[:, put(2)] = jnp.where(half, gv[0], gv[1]).astype(BF)
        g_qkv[:, put(1)] = jnp.where(half, gk[0], gk[1]).astype(BF)
        return carry

    at = slice(width + first * LANES, width + first * LANES + span)
    k_t[...] = qkv[:, at].T
    lax.fori_loop(0, pairs, pair, 0)
    g_qkv[:, :span] = (gq_t[...].T * (HEAD**-0.5)).astype(BF)


def share_rows(n, me, shard, whole, keep, send, sems):
    outs = []
    core = me % 2
    for k in range(n // 2):
        for i, dst in enumerate((keep, send)):
            owner = 2 * k + (core if i == 0 else 1 - core)
            src = whole.at[pl.ds(pl.multiple_of(owner * shard, 16), shard)]
            copy = pltpu.make_async_copy(src, dst.at[k], sems.at[2 * k + i])
            copy.start()
            outs.append(copy)
    return outs


def attention_backward_one(n, segs, pairs, deps, *refs):
    me_ref, starts, qkv, lse, n1, g_mixed, g_out = refs[:7]
    g_qkv, keep, send = refs[7 + deps : 10 + deps]
    k_t, gq_t, bias, g_w, out_sems = refs[10 + deps :]
    tok, width = n1.shape
    span = pairs * LANES
    bias[...] = segment_bias(starts, tok, segs)
    head_grads(0, pairs, width, qkv, lse, g_mixed, bias, k_t, gq_t, g_qkv)
    g_w[:, :width] = g_out[...]
    for i in range(3):
        part = dot_tn(n1[...], g_qkv[:, i * span : (i + 1) * span])
        g_w[:, width + i * span : width + (i + 1) * span] = part.astype(BF)
    for copy in share_rows(n, me_ref[0], width // n, g_w, keep, send, out_sems):
        copy.wait()


def call_attention_backward_one(n, me, starts, qkv, lse, n1, g_mixed, g_out, pairs, deps=()):
    tok, width = n1.shape
    shard, span = width // n, pairs * LANES
    cols = width + 3 * span
    return kernel_call(
        lambda *refs: attention_backward_one(n, starts.shape[1], pairs, len(deps), *refs),
        attention_backward_one,
        (sds((tok, 3 * span)),) + (sds((n // 2, shard, cols)),) * 2,
        [SMEM, SMEM] + [VMEM] * 5 + [ANYWHERE] * len(deps),
        (VMEM, ANYWHERE, ANYWHERE),
        [
            pltpu.VMEM((span, tok), BF),
            pltpu.VMEM((span, tok), F32),
            pltpu.VMEM((tok, tok), F32),
            pltpu.VMEM((width, cols), BF),
            pltpu.SemaphoreType.DMA((n,)),
        ],
        (me, starts, qkv, lse, n1, g_mixed, g_out, *deps),
    )


def attention_backward_two(n, layout, segs, n_vec, first, deps, *refs):
    count = 1 + max(i for i, *_ in layout)
    me_ref, starts, tokens, vec, vec_grads, qkv, lse, n1, g_mixed, g_hidden, g_first = refs[:11]
    pieces = refs[11 : 11 + count]
    at = 11 + count + deps
    input_grad, keep, send = refs[at : at + 3]
    weights, k_t, gq_t, bias, g_qkv, g_w, v_rows, sems, out_sems = refs[at + 3 :]
    tok, width = tokens.shape
    shard = width // n
    span_one = first * LANES
    span = width - span_one
    me = me_ref[0]
    copies = []
    for i in range(3):
        cols = weights.at[:, pl.ds(i * width, width)]
        copies += load_weight(me, pieces, layout, i, shard, cols, sems.at[i])
    bias[...] = segment_bias(starts, tok, segs)
    head_grads(first, span // LANES, width, qkv, lse, g_mixed, bias, k_t, gq_t, g_qkv)
    for i in range(3):
        cols = slice(i * span, (i + 1) * span)
        g_w[:, cols] = dot_tn(n1[...], g_qkv[:, cols]).astype(BF)
    for copy in copies:
        copy.wait()
    g_n1 = jnp.zeros((tok, width), F32)
    for i in range(3):
        one = slice(i * width, i * width + span_one)
        two = slice(i * width + span_one, (i + 1) * width)
        g_n1 = g_n1 + dot_nt(g_first[:, i * span_one : (i + 1) * span_one], weights[:, one])
        g_n1 = g_n1 + dot_nt(g_qkv[:, i * span : (i + 1) * span], weights[:, two])
    normed, inverse = center(tokens[...].astype(F32))
    input_grad[...] = g_hidden[...] + norm_grad(normed, inverse, vec[0:1, :], g_n1)
    v_rows[...] = jnp.zeros_like(v_rows)
    v_rows[0:1, :] = jnp.sum(g_n1 * normed, 0, keepdims=True)
    v_rows[1:2, :] = jnp.sum(g_n1, 0, keepdims=True)
    for row, i in ((2, 0), (3, 2)):
        one = g_first[:, i * span_one : (i + 1) * span_one].astype(F32)
        two = g_qkv[:, i * span : (i + 1) * span].astype(F32)
        v_rows[row : row + 1, :span_one] = jnp.sum(one, 0, keepdims=True)
        v_rows[row : row + 1, span_one:] = jnp.sum(two, 0, keepdims=True)
    v_rows[4:n_vec, :] = vec_grads[4:n_vec, :]
    g_w[:, 3 * span :] = v_rows[...].T.astype(BF)
    for copy in share_rows(n, me, shard, g_w, keep, send, out_sems):
        copy.wait()


def call_attention_backward_two(
    n,
    me,
    starts,
    tokens,
    vec,
    vec_grads,
    qkv,
    lse,
    n1,
    g_mixed,
    g_hidden,
    g_first,
    pieces,
    layout,
    n_vec,
    first,
    deps=(),
):
    tok, width = tokens.shape
    shard, span = width // n, width - first * LANES
    cols = 3 * span + LANES
    return kernel_call(
        lambda *refs: attention_backward_two(
            n, layout, starts.shape[1], n_vec, first, len(deps), *refs
        ),
        attention_backward_two,
        (sds((tok, width), F32),) + (sds((n // 2, shard, cols)),) * 2,
        [SMEM, SMEM] + [VMEM] * 9 + [ANYWHERE] * (len(pieces) + len(deps)),
        (VMEM, ANYWHERE, ANYWHERE),
        [
            pltpu.VMEM((width, 3 * width), BF),
            pltpu.VMEM((span, tok), BF),
            pltpu.VMEM((span, tok), F32),
            pltpu.VMEM((tok, tok), F32),
            pltpu.VMEM((tok, 3 * span), BF),
            pltpu.VMEM((width, cols), BF),
            pltpu.VMEM((LANES, width), F32),
            pltpu.SemaphoreType.DMA((3, len(layout))),
            pltpu.SemaphoreType.DMA((n,)),
        ],
        (
            me,
            starts,
            tokens,
            vec,
            vec_grads,
            qkv,
            lse,
            n1,
            g_mixed,
            g_hidden,
            g_first,
            *pieces,
            *deps,
        ),
    )


def place_rows(position, slots):
    row = lax.broadcasted_iota(jnp.int32, (slots, position.shape[1]), 0)
    return (row == position[...]).astype(F32).astype(BF)


def take_rows(position, slots):
    row = lax.broadcasted_iota(jnp.int32, (position.shape[0], slots), 1)
    return (row == position[...]).astype(F32).astype(BF)


def mix_out(n, layout, slots, deps, *refs):
    count = 1 + max(i for i, *_ in layout)
    me_ref, mixed, tokens, vec, position = refs[:5]
    pieces = refs[5 : 5 + count]
    hidden, sorted_two, weights, sems = refs[5 + count + deps :]
    width = tokens.shape[1]
    copies = load_weight(me_ref[0], pieces, layout, 3, width // n, weights, sems)
    place = place_rows(position, slots)
    for copy in copies:
        copy.wait()
    value = tokens[...].astype(F32) + dot_nn(mixed[...], weights[...]) + vec[4:5, :]
    hidden[...] = value
    normed, _ = center(value)
    sorted_two[...] = dot_nn(place, (normed * vec[5:6, :] + vec[6:7, :]).astype(BF)).astype(BF)


def call_mix_out(n, me, mixed, tokens, vec, position, slots, pieces, layout, deps=()):
    tok, width = tokens.shape
    return kernel_call(
        lambda *refs: mix_out(n, layout, slots, len(deps), *refs),
        mix_out,
        (sds((tok, width), F32), sds((slots, width))),
        [SMEM] + [VMEM] * 4 + [ANYWHERE] * (len(pieces) + len(deps)),
        (VMEM, VMEM),
        [pltpu.VMEM((width, width), BF), pltpu.SemaphoreType.DMA((len(layout),))],
        (me, mixed, tokens, vec, position, *pieces, *deps),
    )


def pack(count, *refs):
    weights = refs[:count]
    vectors, down_bias, in_bias, out, small = refs[count:]
    rows = weights[0].shape[0]
    for i, ref in enumerate(weights):
        out[i * rows : (i + 1) * rows, :] = ref[...]
    small[...] = jnp.zeros_like(small)
    n_vec = vectors.shape[0]
    small[:n_vec, :rows] = vectors[...].astype(F32)
    small[n_vec : n_vec + EXPERTS, :rows] = down_bias[...].astype(F32)
    small[n_vec + EXPERTS : n_vec + 2 * EXPERTS, : in_bias.shape[1]] = in_bias[...].astype(F32)
    out[count * rows :, :] = small[...].astype(BF)


def call_pack(weights, vectors, down_bias, in_bias):
    rows, width = weights[0].shape
    return kernel_call(
        lambda *refs: pack(len(weights), *refs),
        pack,
        sds((len(weights) * rows + 16, width)),
        [VMEM] * (len(weights) + 3),
        VMEM,
        [pltpu.VMEM((16, width), F32)],
        (*weights, vectors, down_bias, in_bias),
    )


def load_blocks(refs, layout, dst, sems):
    copies = []
    for i, (ref, (block, offset, rows, row)) in enumerate(zip(refs, layout, strict=True)):
        copy = pltpu.make_async_copy(
            ref.at[pl.ds(row, rows)], dst.at[block, pl.ds(offset, rows)], sems.at[i]
        )
        copy.start()
        copies.append(copy)
    return copies


def start_all(copies):
    for copy in copies:
        copy.start()
    return copies


def wait_all(copies):
    for copy in copies:
        copy.wait()


def window(meta, block, e):
    begin = pl.multiple_of(meta[block, 3 * e], 16)
    row = lax.broadcasted_iota(jnp.int32, (CAP, 1), 0)
    return pl.ds(begin, CAP), (row >= meta[block, 3 * e + 1]) & (row < meta[block, 3 * e + 2])


def experts(chips, bias_row, lay_x, lay_g, deps, *refs):
    nb, cx, cg, cw = len(chips), len(lay_x), len(lay_g), 2
    me_ref, meta, b_in = refs[:3]
    at = 3
    x_refs, at = refs[at : at + cx], at + cx
    g_refs, at = refs[at : at + cg], at + cg
    w_refs, at = refs[at : at + cw], at + cw
    down = refs[at : at + 2]
    at += 2 + deps
    dsl, (res, act_out, dp_out) = refs[at : at + nb], refs[at + nb : at + nb + 3]
    at += nb + 3
    x_all, g_all, w_in, w_down, res_s, dsl_s, xs, gs, act_s, dp_s = refs[at : at + 10]
    sx, sg, sw, sd, so, sa = refs[at + 10 :]
    rows = w_refs[0].shape[2]
    me = me_ref[0]
    half = w_down.shape[1] // 2
    core = me % 2
    loads = load_blocks(x_refs, lay_x, x_all, sx) + load_blocks(g_refs, lay_g, g_all, sg)
    weights = []
    for e in range(EXPERTS):
        copies = []
        for i, ref in enumerate(w_refs):
            for k in range(ref.shape[0]):
                owner = 2 * k + (core if i == 0 else 1 - core)
                to = pl.ds(pl.multiple_of(owner * rows, 16), rows)
                copies.append(pltpu.make_async_copy(ref.at[k, e], w_in.at[e, to], sw.at[e, i, k]))
        for i, ref in enumerate(down):
            to = pl.multiple_of((core if i == 0 else 1 - core) * half, 16)
            copies.append(pltpu.make_async_copy(ref.at[e], w_down.at[e, pl.ds(to, half)], sd.at[e, i]))
        weights.append(start_all(copies))
    res_s[...] = jnp.zeros_like(res_s)
    dsl_s[...] = jnp.zeros_like(dsl_s)
    wait_all(loads)
    outs = []
    for e in range(EXPERTS):
        spans = []
        for b in range(nb):
            span, inside = window(meta, b, e)
            spans.append((span, inside))
            g = g_all[b, span, :]
            xs[b * CAP : (b + 1) * CAP, :] = x_all[b, span, :]
            gs[b * CAP : (b + 1) * CAP, :] = jnp.where(inside, g, jnp.zeros_like(g))
        wait_all(weights[e])
        pre = dot_nn(xs[...], w_in[e]) + b_in[bias_row + e : bias_row + e + 1, :]
        cdf = 0.5 * (1.0 + lax.erf(pre * 0.7071067811865476))
        act = (pre * cdf).astype(BF)
        slope = cdf + pre * jnp.exp(-0.5 * pre * pre) * 0.3989422804014327
        dp = (dot_nt(gs[...], w_down[e]) * slope).astype(BF)
        act_s[e] = act
        dp_s[e] = dp
        outs += start_all(
            [
                pltpu.make_async_copy(act_s.at[e], act_out.at[e], sa.at[0, e]),
                pltpu.make_async_copy(dp_s.at[e], dp_out.at[e], sa.at[1, e]),
            ]
        )
        for dst, value in ((dsl_s, dot_nt(dp, w_in[e])), (res_s, dot_nn(act, w_down[e]))):
            value = value.astype(BF)
            for b, (span, inside) in enumerate(spans):
                dst[b, span, :] = jnp.where(inside, value[b * CAP : (b + 1) * CAP], dst[b, span, :])
    for b in range(nb):
        outs += start_all(
            [
                pltpu.make_async_copy(dsl_s.at[b], dsl[b], so.at[0, b]),
                pltpu.make_async_copy(res_s.at[b], res.at[(me // 2) ^ chips[b]], so.at[1, b]),
            ]
        )
    wait_all(outs)


def call_experts(chips, bias_row, me, meta, b_in, xp, lay_x, gp, lay_g, wp, down, res, blocks):
    nb, rows, width = len(chips), max(o + r for _, o, r, _ in lay_x), xp[0].shape[1]
    ff = 2 * down[0].shape[1]
    dma = pltpu.SemaphoreType.DMA
    deps = () if res is None else (res,)
    alias = {} if res is None else {5 + len(xp) + len(gp) + len(wp): nb}
    out = kernel_call(
        lambda *refs: experts(chips, bias_row, lay_x, lay_g, len(deps), *refs),
        experts,
        (sds((rows, width)),) * nb
        + (sds((blocks, rows, width)),)
        + (sds((EXPERTS, nb * CAP, ff)),) * 2,
        [SMEM, SMEM, VMEM] + [ANYWHERE] * (len(xp) + len(gp) + len(wp) + 2 + len(deps)),
        (ANYWHERE,) * (nb + 3),
        [pltpu.VMEM((nb, rows, width), BF)] * 2
        + [pltpu.VMEM((EXPERTS, width, ff), BF), pltpu.VMEM((EXPERTS, ff, width), BF)]
        + [pltpu.VMEM((nb, rows, width), BF)] * 2
        + [pltpu.VMEM((nb * CAP, width), BF)] * 2
        + [pltpu.VMEM((EXPERTS, nb * CAP, ff), BF)] * 2
        + [dma((len(xp),)), dma((len(gp),)), dma((EXPERTS, 2, blocks)), dma((EXPERTS, 2))]
        + [dma((2, nb)), dma((2, EXPERTS))],
        (me, meta, b_in, *xp, *gp, *wp, *down, *deps),
        alias,
    )
    return list(out[:nb]), out[nb], out[nb + 1], out[nb + 2]


def down_grads(calls, lay_g, deps, *refs):
    cg, cc = len(lay_g), len(calls)
    me_ref, meta = refs[:2]
    g_refs, acts = refs[2 : 2 + cg], refs[2 + cg : 2 + cg + cc]
    at = 2 + cg + cc + deps
    keep, send = refs[at], refs[at + 1 : at + 1 + EXPERTS]
    g_all, act_s, gs, g_down, sg, sa, so = refs[at + 1 + EXPERTS :]
    core = me_ref[0] % 2
    half = g_down.shape[1] // 2
    loads = load_blocks(g_refs, lay_g, g_all, sg)
    hidden = load_hidden(acts, calls, act_s, sa)
    wait_all(loads)
    outs = []
    for e in range(EXPERTS):
        for b in range(sum(calls)):
            span, inside = window(meta, b, e)
            g = g_all[b, span, :]
            gs[b * CAP : (b + 1) * CAP, :] = jnp.where(inside, g, jnp.zeros_like(g))
        wait_all(hidden[e])
        g_down[e] = dot_tn(act_s[e], gs[...]).astype(BF)
        for i, dst in enumerate((keep.at[e], send[e])):
            src = g_down.at[e, pl.ds(pl.multiple_of((core if i == 0 else 1 - core) * half, 16), half)]
            outs.append(pltpu.make_async_copy(src, dst, so.at[e, i]))
            outs[-1].start()
    wait_all(outs)


def load_hidden(parts, calls, dst, sems):
    hidden = []
    for e in range(EXPERTS):
        copies, first = [], 0
        for i, nb in enumerate(calls):
            rows = pl.ds(first * CAP, nb * CAP)
            copies.append(pltpu.make_async_copy(parts[i].at[e], dst.at[e, rows], sems.at[e, i]))
            first += nb
        hidden.append(start_all(copies))
    return hidden


def call_down_grads(me, meta, gp, lay_g, acts, calls, deps=()):
    rows, width = max(o + r for _, o, r, _ in lay_g), gp[0].shape[1]
    ff, blocks = acts[0].shape[2], sum(calls)
    dma = pltpu.SemaphoreType.DMA
    return kernel_call(
        lambda *refs: down_grads(calls, lay_g, len(deps), *refs),
        down_grads,
        (sds((EXPERTS, ff // 2, width)),) + (sds((ff // 2, width)),) * EXPERTS,
        [SMEM, SMEM] + [ANYWHERE] * (len(gp) + len(acts) + len(deps)),
        (ANYWHERE,) * (1 + EXPERTS),
        [
            pltpu.VMEM((blocks, rows, width), BF),
            pltpu.VMEM((EXPERTS, blocks * CAP, ff), BF),
            pltpu.VMEM((blocks * CAP, width), BF),
            pltpu.VMEM((EXPERTS, ff, width), BF),
            dma((len(gp),)),
            dma((EXPERTS, len(calls))),
            dma((EXPERTS, 2)),
        ],
        (me, meta, *gp, *acts, *deps),
    )


def in_grads(n, calls, lay_x, deps, *refs):
    cx, cc = len(lay_x), len(calls)
    me_ref, meta = refs[:2]
    x_refs, dps = refs[2 : 2 + cx], refs[2 + cx : 2 + cx + cc]
    at = 2 + cx + cc + deps
    keep, bias_keep, bias_send = refs[at : at + 3]
    send = refs[at + 3 : at + 3 + EXPERTS]
    x_all, dp_s, xs, g_in, sx, sp, so = refs[at + 3 + EXPERTS :]
    me = me_ref[0]
    _, width, ff = g_in.shape
    shard, half = width // n, ff // 2
    loads = load_blocks(x_refs, lay_x, x_all, sx)
    hidden = load_hidden(dps, calls, dp_s, sp)
    wait_all(loads)
    outs = []
    row = lax.broadcasted_iota(jnp.int32, (16, 1), 0)
    low = jnp.zeros((16, half), F32)
    high = jnp.zeros((16, half), F32)
    for e in range(EXPERTS):
        for b in range(sum(calls)):
            span, _ = window(meta, b, e)
            xs[b * CAP : (b + 1) * CAP, :] = x_all[b, span, :]
        wait_all(hidden[e])
        g_in[e] = dot_tn(xs[...], dp_s[e]).astype(BF)
        outs += share_rows(n, me, shard, g_in.at[e], keep.at[:, e], send[e], so.at[e])
        total = jnp.sum(dp_s[e].astype(F32), 0, keepdims=True)
        low = low + jnp.where(row == e, total[:, :half], 0.0)
        high = high + jnp.where(row == e, total[:, half:], 0.0)
    first_core = me % 2 == 0
    bias_keep[...] = jnp.where(first_core, low, high).astype(BF)
    bias_send[...] = jnp.where(first_core, high, low).astype(BF)
    wait_all(outs)


def call_in_grads(n, me, meta, xp, lay_x, dps, calls, deps=()):
    rows, width = max(o + r for _, o, r, _ in lay_x), xp[0].shape[1]
    ff, blocks = dps[0].shape[2], sum(calls)
    dma = pltpu.SemaphoreType.DMA
    return kernel_call(
        lambda *refs: in_grads(n, calls, lay_x, len(deps), *refs),
        in_grads,
        (sds((n // 2, EXPERTS, width // n, ff)),)
        + (sds((16, ff // 2)),) * 2
        + (sds((n // 2, width // n, ff)),) * EXPERTS,
        [SMEM, SMEM] + [ANYWHERE] * (len(xp) + len(dps) + len(deps)),
        (ANYWHERE, VMEM, VMEM) + (ANYWHERE,) * EXPERTS,
        [
            pltpu.VMEM((blocks, rows, width), BF),
            pltpu.VMEM((EXPERTS, blocks * CAP, ff), BF),
            pltpu.VMEM((blocks * CAP, width), BF),
            pltpu.VMEM((EXPERTS, width, ff), BF),
            dma((len(xp),)),
            dma((EXPERTS, len(calls))),
            dma((EXPERTS, n)),
        ],
        (me, meta, *xp, *dps, *deps),
    )


def mix_out_backward(n, layout, terms, deps, *refs):
    count = 1 + max(i for i, *_ in layout)
    me_ref, position, route, hidden, cot, vec, mixed = refs[:7]
    got = refs[7 : 7 + terms]
    pieces = refs[7 + terms : 7 + terms + count]
    at = 7 + terms + count + deps
    g_hidden, g_mixed, vec_grads, g_w = refs[at : at + 4]
    weights, sems = refs[at + 4 :]
    me = me_ref[0]
    tok, width = hidden.shape
    shard = width // n
    copies = load_weight(me, pieces, layout, 3, shard, weights, sems)
    total = got[0][...].astype(F32)
    for ref in got[1:]:
        total = total + ref[...].astype(F32)
    gradient = exact_rows(take_rows(position, total.shape[0]), total)
    normed, inverse = center(hidden[...])
    value = cot[...].astype(F32) + norm_grad(normed, inverse, vec[5:6, :], gradient)
    g_hidden[...] = value
    branch = value.astype(BF)
    vec_grads[...] = jnp.zeros_like(vec_grads)
    vec_grads[4:5, :] = jnp.sum(branch.astype(F32), 0, keepdims=True)
    vec_grads[5:6, :] = jnp.sum(gradient * normed, 0, keepdims=True)
    vec_grads[6:7, :] = jnp.sum(gradient, 0, keepdims=True)
    lane = lax.broadcasted_iota(jnp.int32, (tok, 16), 1)
    member = (lane == route[...] + 7).astype(F32).astype(BF)
    vec_grads[...] += dot_tn(member, cot[...])
    for copy in copies:
        copy.wait()
    g_mixed[...] = dot_nt(branch, weights[...]).astype(BF)
    g_w[...] = dot_tn(mixed[...], branch).astype(BF)


def call_mix_out_backward(
    n, me, position, route, hidden, cot, vec, mixed, got, pieces, layout, deps=()
):
    tok, width = hidden.shape
    return kernel_call(
        lambda *refs: mix_out_backward(n, layout, len(got), len(deps), *refs),
        mix_out_backward,
        (sds((tok, width), F32), sds((tok, width)), sds((16, width), F32), sds((width, width))),
        [SMEM] + [VMEM] * (6 + len(got)) + [ANYWHERE] * (len(pieces) + len(deps)),
        (VMEM,) * 4,
        [pltpu.VMEM((width, width), BF), pltpu.SemaphoreType.DMA((len(layout),))],
        (me, position, route, hidden, cot, vec, mixed, *got, *pieces, *deps),
    )


def finish_output(deps, *refs):
    position, hidden, route, vec = refs[:4]
    got = refs[4]
    out = refs[5 + deps]
    value = hidden[...] + dot_nn(take_rows(position, got.shape[0]), got[...])
    for e in range(EXPERTS):
        value = value + jnp.where(route[...] == e, vec[7 + e : 8 + e, :], 0.0)
    out[...] = value.astype(BF)


def call_finish_output(position, hidden, route, vec, got, deps=()):
    return kernel_call(
        lambda *refs: finish_output(len(deps), *refs),
        finish_output,
        sds(hidden.shape),
        [VMEM] * 5 + [ANYWHERE] * len(deps),
        VMEM,
        [],
        (position, hidden, route, vec, got, *deps),
    )


def join(body, named, outs, scalars, arrays, deps=()):
    n_s, n_a, n_d, n_o = len(scalars), len(arrays), len(deps), len(outs)

    def kernel(*refs):
        at = n_s + n_a + n_d
        body(refs[:n_s], refs[n_s : n_s + n_a], refs[at : at + n_o])

    return kernel_call(
        kernel,
        named,
        tuple(outs),
        [SMEM] * n_s + [VMEM] * n_a + [ANYWHERE] * n_d,
        (VMEM,) * n_o,
        [],
        (*scalars, *arrays, *deps),
    )


def plus(*values):
    total = values[0].astype(F32)
    for value in values[1:]:
        total = total + value.astype(F32)
    return total


def call_halves(own, along, across, deps=()):
    rows, width = along.shape
    half = rows // 32 * 16

    def body(_, ins, outs):
        outs[0][...] = ins[1][:half]
        outs[1][...] = ins[2][half:]
        for i in range(3):
            outs[2][i] = ins[i][...]

    shapes = (sds((half, width)), sds((rows - half, width)), sds((3, rows, width)))
    return join(body, call_halves, shapes, (), (own, along, across), deps)


def call_two_halves(first, second, deps=()):
    cuts_at = [pair[0].shape[0] // 32 * 16 for pair in (first, second)]
    width = first[0].shape[1]
    split = cuts_at[0]

    def body(_, ins, outs):
        outs[0][:split] = ins[0][:split]
        outs[0][split:] = ins[2][: cuts_at[1]]
        rest = ins[0].shape[0] - split
        outs[1][:rest] = ins[1][split:]
        outs[1][rest:] = ins[3][cuts_at[1] :]

    rows = first[0].shape[0] + second[0].shape[0]
    shapes = (sds((sum(cuts_at), width)), sds((rows - sum(cuts_at), width)))
    return join(body, call_two_halves, shapes, (), (*first, *second), deps)


def call_columns_and_sort(n, whole, position, slots, value, meta, deps):
    experts_, rows, cols = whole.shape
    pair = cols // (n // 2)

    def body(_, ins, outs):
        for k in range(n // 2):
            outs[0][k] = ins[0][:, :, k * pair : (k + 1) * pair]
        outs[1][:slots, :] = dot_nn(place_rows(ins[1], slots), ins[2][...]).astype(BF)
        outs[1][slots:, :] = jnp.zeros((16, value.shape[1]), BF)
        outs[1][slots:, :LANES] = jnp.broadcast_to(ins[3][...], (16, LANES)).astype(BF)

    shapes = (sds((n // 2, experts_, rows, pair)), sds((slots + 16, value.shape[1])))
    return join(body, call_columns_and_sort, shapes, (), (whole, position, value, meta), deps)


def call_pair_down(kept, keep, got, deps=()):
    experts_, rows, width = keep.shape
    half = rows // 2

    def body(scalars, ins, outs):
        mine = pl.multiple_of(scalars[0][0] * half, 16)
        other = pl.multiple_of((1 - scalars[0][0]) * half, 16)
        for out, at in zip(outs, (mine, other), strict=True):
            for e in range(experts_):
                part = plus(ins[0][e, pl.ds(at, half)], ins[1 + e][pl.ds(at, half)])
                out[e] = part.astype(BF)

    shapes = (sds((experts_, half, width)),) * 2
    return join(body, call_pair_down, shapes, (kept,), (keep, *got), deps)


def call_pair_in(keep, got, bias_keep, bias_got, d_keep, d_got, cut, deps=()):
    count = len(got)

    def body(_, ins, outs):
        for e in range(count):
            outs[0][:, e] = plus(ins[0][:, e], ins[5 + e][...]).astype(BF)
        outs[1][...] = plus(ins[1][...], ins[2][...]).astype(BF)
        outs[2][...] = plus(ins[3][:cut], ins[4][:cut]).astype(BF)
        outs[3][...] = plus(ins[3][cut:], ins[4][cut:]).astype(BF)

    shapes = (sds(keep.shape), sds(bias_keep.shape))
    shapes += (sds((cut, *d_keep.shape[1:])), sds((d_keep.shape[0] - cut, *d_keep.shape[1:])))
    arrays = (keep, bias_keep, bias_got, d_keep, d_got, *got)
    return join(body, call_pair_in, shapes, (), arrays, deps)


def call_split_rows(kept, whole, deps=()):
    chips, experts_, rows, ff = whole.shape
    half = rows // 2
    two = chips // 2

    def body(scalars, ins, outs):
        outs[0][...] = ins[0][:, :, pl.ds(pl.multiple_of(scalars[0][0] * half, 16), half)]
        other = pl.ds(pl.multiple_of((1 - scalars[0][0]) * half, 16), half)
        for i in range(2):
            outs[1 + i][...] = ins[0][i * two : (i + 1) * two, :, other]

    shapes = (sds((chips, experts_, half, ff)),) + (sds((two, experts_, half, ff)),) * 2
    return join(body, call_split_rows, shapes, (kept,), (whole,), deps)


def call_pair_shares(one, two, deps=()):
    chips, rows, cols_one = one[0].shape
    cols = cols_one + two[0].shape[2]

    def body(_, ins, outs):
        outs[0][:, :, :cols_one] = plus(ins[0][...], ins[1][...]).astype(BF)
        outs[0][:, :, cols_one:] = plus(ins[2][...], ins[3][...]).astype(BF)

    return join(body, call_pair_shares, (sds((chips, rows, cols)),), (), (*one, *two), deps)[0]


def call_line_sums(parts, across, i_keep, i_got, deps=()):
    cut = parts[0].shape[0]
    rest = parts[1].shape[0]
    two = i_got[0].shape[0]

    def body(_, ins, outs):
        outs[0][:cut] = plus(ins[0][...], ins[2][...]).astype(BF)
        outs[0][cut:] = plus(ins[1][...], ins[3][...]).astype(BF)
        for i in range(2):
            at = slice(i * two, (i + 1) * two)
            outs[1][at] = plus(ins[4][at], ins[5 + i][...]).astype(BF)

    shapes = (sds((cut + rest, *parts[0].shape[1:])), sds(i_keep.shape))
    return join(body, call_line_sums, shapes, (), (*parts, *across, i_keep, *i_got), deps)


def call_sums(jobs, deps=()):
    flat = [v for job in jobs for v in job]

    def body(_, ins, outs):
        at = 0
        for job, out in zip(jobs, outs, strict=True):
            out[...] = plus(*[ref[...] for ref in ins[at : at + len(job)]]).astype(BF)
            at += len(job)

    return join(body, call_sums, [sds(job[0].shape) for job in jobs], (), flat, deps)


def call_attention_shares(kept, got, bias, deps=()):
    chips, rows, cols = got.shape
    half = rows // 2

    def body(scalars, ins, outs):
        mine = pl.multiple_of(scalars[0][0] * half, 16)
        other = pl.multiple_of((1 - scalars[0][0]) * half, 16)
        for out, at in zip(outs, (mine, other), strict=True):
            out[:half, :] = plus(*[ins[0][k, pl.ds(at, half)] for k in range(chips)]).astype(BF)
            out[half:, :] = jnp.zeros((16, cols), BF)
            out[half:, : bias.shape[1]] = ins[1][...]

    shapes = (sds((half + 16, cols)),) * 2
    return join(body, call_attention_shares, shapes, (kept,), (got, bias), deps)


def call_down_result(kept, mine, got, deps=()):
    experts_, half, width = mine.shape

    def body(scalars, ins, outs):
        outs[0][:, pl.ds(pl.multiple_of(scalars[0][0] * half, 16), half)] = ins[0][...].astype(F32)
        at = pl.multiple_of((1 - scalars[0][0]) * half, 16)
        outs[0][:, pl.ds(at, half)] = ins[1][...].astype(F32)

    shape = (sds((experts_, 2 * half, width), F32),)
    return join(body, call_down_result, shape, (kept,), (mine, got), deps)[0]


def call_in_result(kept, mine, got, deps=()):
    chips, experts_, half, ff = mine.shape

    def body(scalars, ins, outs):
        for ref, which in ((ins[0], scalars[0][0]), (ins[1], 1 - scalars[0][0])):
            rows = pl.ds(pl.multiple_of(which * half, 16), half)
            for k in range(chips):
                outs[0][:, rows, k * ff : (k + 1) * ff] = ref[k].astype(F32)

    shape = (sds((experts_, 2 * half, chips * ff), F32),)
    return join(body, call_in_result, shape, (kept,), (mine, got), deps)[0]


def call_attention_result(kept, mine, got, width, span, n_vec, ff_shard, deps=()):
    half = mine.shape[0] - 16
    last = width - span
    cols_one = width + 3 * span

    def body(scalars, ins, outs):
        for ref, which in ((ins[0], scalars[0][0]), (ins[1], 1 - scalars[0][0])):
            rows = pl.ds(pl.multiple_of(which * half, 16), half)
            outs[0][rows, :] = ref[:half, :width].astype(F32)
            for i in range(3):
                one = ref[:half, width + i * span : width + (i + 1) * span]
                two = ref[:half, cols_one + i * last : cols_one + (i + 1) * last]
                outs[1 + i][rows, :span] = one.astype(F32)
                outs[1 + i][rows, span:] = two.astype(F32)
            outs[6][rows, :] = ref[:half, cols_one + 3 * last :].astype(F32)
        outs[4][...] = outs[6][...].T[:16]
        outs[5][...] = ins[0][half:, :ff_shard].astype(F32)

    shapes = (sds((2 * half, width), F32),) * 4 + (sds((16, 2 * half), F32),)
    shapes += (sds((16, ff_shard), F32), sds((2 * half, LANES), F32))
    return join(body, call_attention_result, shapes, (kept,), (mine, got), deps)


def swap(v, n, mask):
    return lax.ppermute(v, FSDP, [(i, i ^ mask) for i in range(n)])


def blocks_of(pieces, here):
    mine = [p for p in pieces if p[1] in here]
    return [p[0] for p in mine], [(here.index(c), at, rows, row) for _, c, at, rows, row in mine]


def scatter_chips(terms, n):
    return [terms[0]] + [swap(terms[i], n, 2 * i) for i in range(1, n // 2)]


def exchange(v, n):
    groups = [list(range(core, n, 2)) for core in range(2)]
    return lax.all_to_all(v, FSDP, 0, 0, axis_index_groups=groups)


def plane_sum(v, n):
    groups = [list(range(core, n, 2)) for core in range(2)]
    return lax.psum_scatter(v, FSDP, scatter_dimension=0, axis_index_groups=groups)


def line(v, step):
    pairs = [(0, 3), (3, 0), (1, 2), (2, 1)] if step == 1 else [(0, 1), (1, 0), (2, 3), (3, 2)]
    return lax.ppermute(v, REP, pairs)


def per_device_tokens(
    n,
    tokens,
    starts,
    routes,
    norm1_gain,
    norm1_bias,
    query_weight,
    query_bias,
    key_weight,
    value_weight,
    value_bias,
    out_weight,
    out_bias,
    norm2_gain,
    norm2_bias,
    expert_in,
    expert_in_bias,
    expert_out,
    expert_out_bias,
    cotangent,
):
    index = lax.axis_index(FSDP)
    me = index.astype(jnp.int32).reshape(1)
    tok_count, width = tokens.shape
    shard = width // n
    ff_shard = expert_out.shape[1]
    ff_pair = 2 * ff_shard

    vectors = [norm1_gain, norm1_bias, query_bias, value_bias, out_bias, norm2_gain, norm2_bias]
    n_vec = len(vectors) + EXPERTS
    payload = call_pack(
        (query_weight, key_weight, value_weight, out_weight),
        jnp.stack(vectors),
        expert_out_bias,
        expert_in_bias,
    )
    along, across = swap(payload, n, 2), swap(payload, n, 4)
    top, bottom, three = call_halves(payload, along, across)
    top_got, bottom_got = swap(top, n, 4), swap(bottom, n, 2)
    rows, half = payload.shape[0], top.shape[0]
    w_attn = [payload, along, across, top_got, bottom_got]
    w_attn += [swap(three, n, 1), swap(top_got, n, 1), swap(bottom_got, n, 1)]
    lay_attn = [(i, None, m, 0, rows) for i, m in enumerate((0, 2, 4))]
    lay_attn += [(5, i, m, 0, rows) for i, m in enumerate((1, 3, 5))]
    lay_attn += [(3, None, 6, 0, half), (4, None, 6, half, rows - half)]
    lay_attn += [(6, None, 7, 0, half), (7, None, 7, half, rows - half)]

    route_ids = routes[:, 0]
    member = (route_ids[:, None] == jnp.arange(EXPERTS, dtype=jnp.int32)[None, :]).astype(jnp.int32)
    rank = jnp.sum(jnp.cumsum(member, 0) * member, 1) - 1
    padded = (jnp.sum(member, 0) + 15) // 16
    base = jnp.cumsum(padded) - padded
    slots = tok_count + 16 * (EXPERTS - 1)
    position = (jnp.sum(member * base[None, :], 1) * 16 + rank).astype(jnp.int32)
    position_row, position_col = position[None, :], position[:, None]
    begin = jnp.minimum(base, (slots - CAP) // 16)
    meta = jnp.stack([begin, base - begin, base - begin + padded], 1).reshape(1, 3 * EXPERTS) * 16
    meta = meta.astype(jnp.int32)
    down_other = swap(expert_out, n, 1)

    meta_row = jnp.pad((meta // 16).astype(F32), ((0, 0), (0, LANES - meta.shape[1])))
    columns, sorted_grad = call_columns_and_sort(
        n, expert_in, position_row, slots, cotangent, meta_row, (top,)
    )
    w_mine = exchange(hold((columns,), (w_attn[6], w_attn[7]))[0], n)
    grad_along, grad_across = swap(sorted_grad, n, 2), swap(sorted_grad, n, 4)

    qkv, mixed, lse, n1, vec, in_bias = call_attention_forward(
        n, me, starts, tokens, w_attn, lay_attn, n_vec
    )
    hidden, sorted_two = call_mix_out(
        n,
        me,
        mixed,
        tokens,
        vec,
        position_row,
        slots,
        w_attn,
        lay_attn,
    )
    tok_along, tok_across = swap(sorted_two, n, 2), swap(sorted_two, n, 4)
    (w_mine,) = hold((w_mine,), (sorted_two,))
    w_pair = (w_mine, swap(w_mine, n, 1))

    calls = ((0,), (1, 2), (3,))
    sizes = tuple(len(call) for call in calls)
    dsl, acts, dps = [], [], []

    def run(call, metas, token_pieces, grad_pieces, res):
        d, res, a, p = call_experts(
            call,
            n_vec,
            me,
            metas,
            in_bias,
            *blocks_of(token_pieces, call),
            *blocks_of(grad_pieces, call),
            w_pair,
            (expert_out, down_other),
            res,
            n // 2,
        )
        dsl.extend(d)
        acts.append(a)
        dps.append(p)
        return res

    def meta_of(rows):
        return rows[:, : 3 * EXPERTS].astype(jnp.int32) * 16

    token_pieces = [(sorted_two, 0, 0, slots, 0)]
    grad_pieces = [(sorted_grad, 0, 0, slots, 0)]
    res = run(calls[0], meta, token_pieces, grad_pieces, None)
    tops, bottoms = call_two_halves((tok_along, tok_across), (grad_along, grad_across), (dps[0],))
    tops, bottoms = swap(tops, n, 4), swap(bottoms, n, 2)
    half, low = slots // 32 * 16, sorted_grad.shape[0] // 32 * 16
    rest = slots - half
    token_pieces += [(tok_along, 1, 0, slots, 0), (tok_across, 2, 0, slots, 0)]
    token_pieces += [(tops, 3, 0, half, 0), (bottoms, 3, half, rest, 0)]
    grad_pieces += [(grad_along, 1, 0, slots, 0), (grad_across, 2, 0, slots, 0)]
    grad_pieces += [(tops, 3, 0, low, half), (bottoms, 3, low, slots - low, rest)]
    meta_xy = meta_of(
        jnp.concatenate([grad_along[slots : slots + 1], grad_across[slots : slots + 1]], 0)
    )
    meta_d = meta_of(bottoms[-16:-15])
    meta_rel = jnp.concatenate([meta, meta_xy, meta_d], 0)
    res = run(calls[1], meta_xy, token_pieces, grad_pieces, res)
    res = run(calls[2], meta_d, token_pieces, grad_pieces, res)
    got_dsl = scatter_chips(dsl, n)

    at = lax.axis_index(REP)
    kept = jnp.where((at == 0) | (at == 3), 1, 0).astype(jnp.int32).reshape(1)
    down_keep, *down_send = call_down_grads(
        me,
        meta_rel,
        *blocks_of(grad_pieces, range(n // 2)),
        acts,
        sizes,
        (got_dsl[1],),
    )
    down_got = [swap(v, n, 1) for v in down_send]

    g_hidden, g_mixed, vec_grads, g_out = call_mix_out_backward(
        n,
        me,
        position_col,
        routes,
        hidden,
        cotangent,
        vec,
        mixed,
        got_dsl,
        w_attn,
        lay_attn,
        (down_keep,),
    )
    (res,) = hold((res,), (g_out,))
    got_res = plane_sum(res, n)
    d_keep, d_send = call_pair_down(kept, down_keep, down_got, (g_out,))
    d_got = line(d_send, 0)
    in_keep, in_bias_keep, in_bias_send, *in_send = call_in_grads(
        n,
        me,
        meta_rel,
        *blocks_of(token_pieces, range(n // 2)),
        dps,
        sizes,
        (d_send,),
    )
    *in_send, in_bias_send = hold((*in_send, in_bias_send), (in_keep,))
    in_other, in_bias_other = [swap(v, n, 1) for v in in_send], swap(in_bias_send, n, 1)

    first = width // LANES // 2
    span = first * LANES
    g_first, keep_one, send_one = call_attention_backward_one(
        n, me, starts, qkv, lse, n1, g_mixed, g_out, first, (in_keep,)
    )
    i_terms, bias_term, *d_parts = call_pair_in(
        in_keep, in_other, in_bias_keep, in_bias_other, d_keep, d_got, 1, (g_first,)
    )
    d_first = line(d_parts[0], 1)
    i_plane = exchange(i_terms, n)
    (send_one,) = hold((send_one,), (i_terms,))
    other_one = swap(send_one, n, 1)
    input_grad, keep_two, send_two = call_attention_backward_two(
        n,
        me,
        starts,
        tokens,
        vec,
        vec_grads,
        qkv,
        lse,
        n1,
        g_mixed,
        g_hidden,
        g_first,
        w_attn,
        lay_attn,
        n_vec,
        first,
        (i_terms,),
    )
    send_two, d_second = hold((send_two, d_parts[1]), (keep_two, d_first))
    other_two = swap(send_two, n, 1)
    d_across = (d_first, line(d_second, 1))
    i_keep, *i_send = call_split_rows(kept, i_plane, (keep_two,))
    i_got = [line(v, 0) for v in i_send]
    p_terms = call_pair_shares((keep_one, other_one), (keep_two, other_two), (keep_two,))
    d_total, i_part = call_line_sums(
        (d_parts[0], d_second), d_across, i_keep, i_got, (p_terms,)
    )
    d_rest, i_across = line(d_total, 2), line(i_part, 1)
    (p_terms,) = hold((p_terms,), (d_total,))
    p_plane = exchange(p_terms, n)
    sum_down = call_down_result(kept, d_total, d_rest)
    p_keep, p_send = call_attention_shares(kept, p_plane, bias_term, (sum_down,))
    p_got = line(p_send, 0)
    (i_total,) = call_sums([(i_part, i_across)], (p_send,))
    i_rest = line(i_total, 2)
    (p_part,) = call_sums([(p_keep, p_got)], (i_total,))
    p_across = line(p_part, 1)
    (p_total,) = call_sums([(p_part, p_across)])
    p_rest = line(p_total, 2)
    output = call_finish_output(position_col, hidden, routes, vec, got_res, (p_total,))
    sum_in = call_in_result(kept, i_total, i_rest, (output,))
    sum_out, sum_query, sum_key, sum_value, sum_vec, bias_rows, _ = call_attention_result(
        kept, p_total, p_rest, width, span, n_vec, ff_shard, (output,)
    )
    sum_in_bias = bias_rows[:EXPERTS]
    return (
        output,
        input_grad,
        sum_vec[0],
        sum_vec[1],
        sum_query,
        sum_vec[2],
        sum_key,
        sum_value,
        sum_vec[3],
        sum_out,
        sum_vec[4],
        sum_vec[5],
        sum_vec[6],
        sum_in,
        sum_in_bias,
        sum_down,
        sum_vec[7:n_vec],
    )


def plan_of(n, replicas):
    if n == 8 and replicas == 4:
        return lambda *args: per_device_tokens(n, *args)
    return per_device_weights


def solution(mesh):
    in_specs = (
        P((FSDP, REP), None),
        P((FSDP, REP), None),
        P((FSDP, REP), None),
        P(FSDP),
        P(FSDP),
        P(FSDP, None),
        P(FSDP),
        P(FSDP, None),
        P(FSDP, None),
        P(FSDP),
        P(FSDP, None),
        P(FSDP),
        P(FSDP),
        P(FSDP),
        P(None, FSDP, None),
        P(None, FSDP),
        P(None, FSDP, None),
        P(None, FSDP),
        P((FSDP, REP), None),
    )
    out_specs = (
        P((FSDP, REP), None),
        P((FSDP, REP), None),
        P(FSDP),
        P(FSDP),
        P(FSDP, None),
        P(FSDP),
        P(FSDP, None),
        P(FSDP, None),
        P(FSDP),
        P(FSDP, None),
        P(FSDP),
        P(FSDP),
        P(FSDP),
        P(None, FSDP, None),
        P(None, FSDP),
        P(None, FSDP, None),
        P(None, FSDP),
    )
    per_device = plan_of(mesh.shape[FSDP], mesh.shape[REP])
    return jax.shard_map(
        per_device, mesh=mesh, in_specs=in_specs, out_specs=out_specs, check_vma=False
    )
```

```python
import jax
import jax.numpy as jnp
from jax import lax
from jax.experimental import pallas as pl
from jax.experimental.pallas import tpu as pltpu
from jax.sharding import PartitionSpec as P

FSDP = "fsdp"
REP = "rep"
HEAD = 64
EXPERTS = 3
CAP = 208


EPSILON = 1e-05
MASKED = -1000000000.0


def normalize(inputs, gain, shift):
    mean = jnp.mean(inputs, -1, keepdims=True)
    centred = inputs - mean
    inverse = lax.rsqrt(jnp.mean(centred * centred, -1, keepdims=True) + EPSILON)
    return centred * inverse * gain + shift


def norm_back(inputs, gain, gradient):
    mean = jnp.mean(inputs, -1, keepdims=True)
    centred = inputs - mean
    inverse = lax.rsqrt(jnp.mean(centred * centred, -1, keepdims=True) + EPSILON)
    normed = centred * inverse
    grad_normed = gradient * gain
    grad_inputs = inverse * (
        grad_normed
        - jnp.mean(grad_normed, -1, keepdims=True)
        - normed * jnp.mean(grad_normed * normed, -1, keepdims=True)
    )
    return (grad_inputs, jnp.sum(gradient * normed, 0), jnp.sum(gradient, 0))


def gelu_exact(inputs):
    return 0.5 * inputs * (1.0 + lax.erf(inputs * 0.7071067811865476))


def gelu_slope(inputs):
    return (
        0.5 * (1.0 + lax.erf(inputs * 0.7071067811865476))
        + inputs * jnp.exp(-0.5 * inputs * inputs) * 0.3989422804014327
    )


def per_device_weights(
    tokens,
    starts,
    routes,
    norm1_gain,
    norm1_bias,
    query_weight,
    query_bias,
    key_weight,
    value_weight,
    value_bias,
    out_weight,
    out_bias,
    norm2_gain,
    norm2_bias,
    expert_in,
    expert_in_bias,
    expert_out,
    expert_out_bias,
    cotangent,
):
    seq_rows = starts.shape[0]
    tok_count = tokens.shape[0]
    seq_len = tok_count // seq_rows
    model_width = tokens.shape[1]
    head_count = model_width // HEAD
    head_shape = (seq_rows, seq_len, head_count, HEAD)
    scale_factor = HEAD ** (-0.5)
    gain_one, shift_one, w_query, b_query, w_key, w_value, b_value, w_out, b_out = (
        lax.all_gather(norm1_gain, FSDP, axis=0, tiled=True),
        lax.all_gather(norm1_bias, FSDP, axis=0, tiled=True),
        lax.all_gather(query_weight, FSDP, axis=0, tiled=True),
        lax.all_gather(query_bias, FSDP, axis=0, tiled=True),
        lax.all_gather(key_weight, FSDP, axis=0, tiled=True),
        lax.all_gather(value_weight, FSDP, axis=0, tiled=True),
        lax.all_gather(value_bias, FSDP, axis=0, tiled=True),
        lax.all_gather(out_weight, FSDP, axis=0, tiled=True),
        lax.all_gather(out_bias, FSDP, axis=0, tiled=True),
    )
    resid_in = tokens.astype(jnp.float32)
    normed_one = normalize(
        resid_in, gain_one.astype(jnp.float32), shift_one.astype(jnp.float32)
    ).astype(jnp.bfloat16)
    queries = (
        (
            jnp.dot(normed_one, w_query, preferred_element_type=jnp.float32)
            + b_query.astype(jnp.float32)
        )
        .astype(jnp.bfloat16)
        .reshape(head_shape)
    )
    keys_mat = (
        jnp.dot(normed_one, w_key, preferred_element_type=jnp.float32)
        .astype(jnp.bfloat16)
        .reshape(head_shape)
    )
    values = (
        (
            jnp.dot(normed_one, w_value, preferred_element_type=jnp.float32)
            + b_value.astype(jnp.float32)
        )
        .astype(jnp.bfloat16)
        .reshape(head_shape)
    )
    position = jnp.arange(seq_len, dtype=jnp.int32)
    segment = jnp.sum((position[None, :, None] >= starts[:, None, :]).astype(jnp.int32), -1)
    same_seg = (segment[:, :, None] == segment[:, None, :])[:, None]

    def scores_of(query_part, key_part):
        raw_scores = (
            jnp.einsum("rqhd,rkhd->rhqk", query_part, key_part, preferred_element_type=jnp.float32)
            * scale_factor
        )
        return jnp.where(same_seg, raw_scores, MASKED)

    scores = scores_of(queries, keys_mat)
    row_max = jnp.max(scores, -1, keepdims=True)
    exp_scores = jnp.exp(scores - row_max)
    row_total = jnp.sum(exp_scores, -1, keepdims=True)
    log_total = row_max + jnp.log(row_total)
    probs_low = (exp_scores / row_total).astype(jnp.bfloat16)
    mixed = jnp.einsum("rhqk,rkhd->rqhd", probs_low, values, preferred_element_type=jnp.float32)
    mixed = mixed.reshape(tok_count, model_width).astype(jnp.bfloat16)
    hidden = (
        resid_in
        + jnp.dot(mixed, w_out, preferred_element_type=jnp.float32)
        + b_out.astype(jnp.float32)
    )
    gain_two, shift_two, w_in, b_in, w_down, b_down = (
        lax.all_gather(norm2_gain, FSDP, axis=0, tiled=True),
        lax.all_gather(norm2_bias, FSDP, axis=0, tiled=True),
        lax.all_gather(expert_in, FSDP, axis=1, tiled=True),
        lax.all_gather(expert_in_bias, FSDP, axis=1, tiled=True),
        lax.all_gather(expert_out, FSDP, axis=1, tiled=True),
        lax.all_gather(expert_out_bias, FSDP, axis=1, tiled=True),
    )
    normed_two = normalize(
        hidden, gain_two.astype(jnp.float32), shift_two.astype(jnp.float32)
    ).astype(jnp.bfloat16)
    route_ids = routes[:, 0]
    member = (route_ids[:, None] == jnp.arange(EXPERTS, dtype=jnp.int32)[None, :]).astype(jnp.int32)
    rank = jnp.sum(jnp.cumsum(member, 0) * member, 1) - 1
    slot_ids = route_ids * CAP + rank
    packed = (
        jnp.zeros((EXPERTS * CAP, model_width), jnp.bfloat16)
        .at[slot_ids]
        .set(normed_two)
        .reshape(EXPERTS, CAP, model_width)
    )
    pre_act = (
        jnp.einsum("ecd,edf->ecf", packed, w_in, preferred_element_type=jnp.float32)
        + b_in.astype(jnp.float32)[:, None, :]
    )
    act_low = gelu_exact(pre_act).astype(jnp.bfloat16)
    result = (
        jnp.einsum("ecf,efd->ecd", act_low, w_down, preferred_element_type=jnp.float32)
        + b_down.astype(jnp.float32)[:, None, :]
    )
    routed = result.reshape(EXPERTS * CAP, model_width)[slot_ids]
    output = (hidden + routed).astype(jnp.bfloat16)
    gain_two_back, w_in_back, w_down_back = (
        lax.all_gather(norm2_gain, FSDP, axis=0, tiled=True),
        lax.all_gather(expert_in, FSDP, axis=1, tiled=True),
        lax.all_gather(expert_out, FSDP, axis=1, tiled=True),
    )
    grad_output = cotangent.astype(jnp.float32)
    grad_packed = (
        jnp.zeros((EXPERTS * CAP, model_width), jnp.bfloat16)
        .at[slot_ids]
        .set(cotangent)
        .reshape(EXPERTS, CAP, model_width)
    )
    grad_down_bias = jnp.sum(grad_packed.astype(jnp.float32), 1)
    grad_down = jnp.einsum("ecf,ecd->efd", act_low, grad_packed, preferred_element_type=jnp.float32)
    grad_act = jnp.einsum(
        "ecd,efd->ecf", grad_packed, w_down_back, preferred_element_type=jnp.float32
    )
    grad_pre = (grad_act * gelu_slope(pre_act)).astype(jnp.bfloat16)
    grad_in_bias = jnp.sum(grad_pre.astype(jnp.float32), 1)
    grad_in = jnp.einsum("ecd,ecf->edf", packed, grad_pre, preferred_element_type=jnp.float32)
    grad_slots = jnp.einsum(
        "ecf,edf->ecd", grad_pre, w_in_back, preferred_element_type=jnp.float32
    ).reshape(EXPERTS * CAP, model_width)
    grad_normed_two = grad_slots[slot_ids]
    grad_from_norm, grad_gain_two, grad_shift_two = norm_back(
        hidden, gain_two_back.astype(jnp.float32), grad_normed_two
    )
    grad_hidden = grad_output + grad_from_norm
    column_in, column_down = (
        lax.psum_scatter(
            grad_in.astype(jnp.bfloat16), REP, scatter_dimension=2, tiled=True
        ).astype(jnp.float32),
        lax.psum_scatter(
            grad_down.astype(jnp.bfloat16), REP, scatter_dimension=2, tiled=True
        ).astype(jnp.float32),
    )
    share_in, share_down, part_gain_two, part_shift_two, part_in_bias, part_down_bias = (
        lax.psum_scatter(column_in, FSDP, scatter_dimension=1, tiled=True),
        lax.psum_scatter(column_down, FSDP, scatter_dimension=1, tiled=True),
        lax.psum_scatter(grad_gain_two, FSDP, scatter_dimension=0, tiled=True),
        lax.psum_scatter(grad_shift_two, FSDP, scatter_dimension=0, tiled=True),
        lax.psum_scatter(grad_in_bias, FSDP, scatter_dimension=1, tiled=True),
        lax.psum_scatter(grad_down_bias, FSDP, scatter_dimension=1, tiled=True),
    )
    sum_in, sum_down, stack_gain_two, stack_shift_two, stack_in_bias, stack_down_bias = (
        lax.all_gather(share_in.astype(jnp.bfloat16), REP, axis=2, tiled=True).astype(
            share_in.dtype
        ),
        lax.all_gather(share_down.astype(jnp.bfloat16), REP, axis=2, tiled=True).astype(
            share_down.dtype
        ),
        lax.all_gather(part_gain_two[None].astype(jnp.bfloat16), REP, axis=0, tiled=True).astype(
            jnp.float32
        ),
        lax.all_gather(part_shift_two[None].astype(jnp.bfloat16), REP, axis=0, tiled=True).astype(
            jnp.float32
        ),
        lax.all_gather(part_in_bias[None].astype(jnp.bfloat16), REP, axis=0, tiled=True).astype(
            jnp.float32
        ),
        lax.all_gather(part_down_bias[None].astype(jnp.bfloat16), REP, axis=0, tiled=True).astype(
            jnp.float32
        ),
    )
    sum_gain_two = jnp.sum(stack_gain_two, 0)
    sum_shift_two = jnp.sum(stack_shift_two, 0)
    sum_in_bias = jnp.sum(stack_in_bias, 0)
    sum_down_bias = jnp.sum(stack_down_bias, 0)
    gain_one_back, w_query_back, w_key_back, w_value_back, w_out_back = (
        lax.all_gather(norm1_gain, FSDP, axis=0, tiled=True),
        lax.all_gather(query_weight, FSDP, axis=0, tiled=True),
        lax.all_gather(key_weight, FSDP, axis=0, tiled=True),
        lax.all_gather(value_weight, FSDP, axis=0, tiled=True),
        lax.all_gather(out_weight, FSDP, axis=0, tiled=True),
    )
    grad_branch = grad_hidden.astype(jnp.bfloat16)
    grad_out_bias = jnp.sum(grad_branch.astype(jnp.float32), 0)
    grad_out_weight = jnp.einsum(
        "td,te->de", mixed, grad_branch, preferred_element_type=jnp.float32
    )
    grad_mixed = (
        jnp.einsum("te,de->td", grad_branch, w_out_back, preferred_element_type=jnp.float32)
        .astype(jnp.bfloat16)
        .reshape(head_shape)
    )
    scores_again = scores_of(queries, keys_mat)
    probs = jnp.exp(scores_again - log_total)
    probs_again = probs.astype(jnp.bfloat16)
    grad_values = jnp.einsum(
        "rhqk,rqhd->rkhd", probs_again, grad_mixed, preferred_element_type=jnp.float32
    )
    grad_values = grad_values.astype(jnp.bfloat16).reshape(tok_count, model_width)
    grad_probs = jnp.einsum(
        "rqhd,rkhd->rhqk", grad_mixed, values, preferred_element_type=jnp.float32
    )
    grad_scores = (probs * (grad_probs - jnp.sum(grad_probs * probs, -1, keepdims=True))).astype(
        jnp.bfloat16
    )
    grad_queries = (
        (
            jnp.einsum("rhqk,rkhd->rqhd", grad_scores, keys_mat, preferred_element_type=jnp.float32)
            * scale_factor
        )
        .astype(jnp.bfloat16)
        .reshape(tok_count, model_width)
    )
    grad_keys = (
        (
            jnp.einsum("rhqk,rqhd->rkhd", grad_scores, queries, preferred_element_type=jnp.float32)
            * scale_factor
        )
        .astype(jnp.bfloat16)
        .reshape(tok_count, model_width)
    )
    grad_query_bias = jnp.sum(grad_queries.astype(jnp.float32), 0)
    grad_value_bias = jnp.sum(grad_values.astype(jnp.float32), 0)
    grad_query_weight = jnp.einsum(
        "td,te->de", normed_one, grad_queries, preferred_element_type=jnp.float32
    )
    grad_key_weight = jnp.einsum(
        "td,te->de", normed_one, grad_keys, preferred_element_type=jnp.float32
    )
    grad_value_weight = jnp.einsum(
        "td,te->de", normed_one, grad_values, preferred_element_type=jnp.float32
    )
    grad_normed_one = (
        jnp.einsum("te,de->td", grad_queries, w_query_back, preferred_element_type=jnp.float32)
        + jnp.einsum("te,de->td", grad_keys, w_key_back, preferred_element_type=jnp.float32)
        + jnp.einsum("te,de->td", grad_values, w_value_back, preferred_element_type=jnp.float32)
    )
    grad_from_first, grad_gain_one, grad_shift_one = norm_back(
        resid_in, gain_one_back.astype(jnp.float32), grad_normed_one
    )
    input_grad = grad_hidden + grad_from_first
    column_query, column_key, column_value, column_out = (
        lax.psum_scatter(
            grad_query_weight.astype(jnp.bfloat16), REP, scatter_dimension=1, tiled=True
        ).astype(jnp.float32),
        lax.psum_scatter(
            grad_key_weight.astype(jnp.bfloat16), REP, scatter_dimension=1, tiled=True
        ).astype(jnp.float32),
        lax.psum_scatter(
            grad_value_weight.astype(jnp.bfloat16), REP, scatter_dimension=1, tiled=True
        ).astype(jnp.float32),
        lax.psum_scatter(
            grad_out_weight.astype(jnp.bfloat16), REP, scatter_dimension=1, tiled=True
        ).astype(jnp.float32),
    )
    (
        share_query,
        share_key,
        share_value,
        share_out,
        part_gain_one,
        part_shift_one,
        part_query_bias,
        part_value_bias,
        part_out_bias,
    ) = (
        lax.psum_scatter(column_query, FSDP, scatter_dimension=0, tiled=True),
        lax.psum_scatter(column_key, FSDP, scatter_dimension=0, tiled=True),
        lax.psum_scatter(column_value, FSDP, scatter_dimension=0, tiled=True),
        lax.psum_scatter(column_out, FSDP, scatter_dimension=0, tiled=True),
        lax.psum_scatter(grad_gain_one, FSDP, scatter_dimension=0, tiled=True),
        lax.psum_scatter(grad_shift_one, FSDP, scatter_dimension=0, tiled=True),
        lax.psum_scatter(grad_query_bias, FSDP, scatter_dimension=0, tiled=True),
        lax.psum_scatter(grad_value_bias, FSDP, scatter_dimension=0, tiled=True),
        lax.psum_scatter(grad_out_bias, FSDP, scatter_dimension=0, tiled=True),
    )
    (
        sum_query,
        sum_key,
        sum_value,
        sum_out,
        stack_gain_one,
        stack_shift_one,
        stack_query_bias,
        stack_value_bias,
        stack_out_bias,
    ) = (
        lax.all_gather(share_query.astype(jnp.bfloat16), REP, axis=1, tiled=True).astype(
            share_query.dtype
        ),
        lax.all_gather(share_key.astype(jnp.bfloat16), REP, axis=1, tiled=True).astype(
            share_key.dtype
        ),
        lax.all_gather(share_value.astype(jnp.bfloat16), REP, axis=1, tiled=True).astype(
            share_value.dtype
        ),
        lax.all_gather(share_out.astype(jnp.bfloat16), REP, axis=1, tiled=True).astype(
            share_out.dtype
        ),
        lax.all_gather(part_gain_one[None].astype(jnp.bfloat16), REP, axis=0, tiled=True).astype(
            jnp.float32
        ),
        lax.all_gather(part_shift_one[None].astype(jnp.bfloat16), REP, axis=0, tiled=True).astype(
            jnp.float32
        ),
        lax.all_gather(
            part_query_bias[None].astype(jnp.bfloat16), REP, axis=0, tiled=True
        ).astype(jnp.float32),
        lax.all_gather(
            part_value_bias[None].astype(jnp.bfloat16), REP, axis=0, tiled=True
        ).astype(jnp.float32),
        lax.all_gather(part_out_bias[None].astype(jnp.bfloat16), REP, axis=0, tiled=True).astype(
            jnp.float32
        ),
    )
    sum_gain_one = jnp.sum(stack_gain_one, 0)
    sum_shift_one = jnp.sum(stack_shift_one, 0)
    sum_query_bias = jnp.sum(stack_query_bias, 0)
    sum_value_bias = jnp.sum(stack_value_bias, 0)
    sum_out_bias = jnp.sum(stack_out_bias, 0)
    return (
        output,
        input_grad,
        sum_gain_one,
        sum_shift_one,
        sum_query,
        sum_query_bias,
        sum_key,
        sum_value,
        sum_value_bias,
        sum_out,
        sum_out_bias,
        sum_gain_two,
        sum_shift_two,
        sum_in,
        sum_in_bias,
        sum_down,
        sum_down_bias,
    )


LANES = 128
BF = jnp.bfloat16
F32 = jnp.float32
VMEM_BYTES = 60 * 1024 * 1024
SMEM = pl.BlockSpec(memory_space=pltpu.SMEM)
VMEM = pl.BlockSpec(memory_space=pltpu.VMEM)
ANYWHERE = pl.BlockSpec(memory_space=pl.ANY)


def dot_nn(a, b):
    return lax.dot_general(a, b, (((1,), (0,)), ((), ())), preferred_element_type=F32)


def dot_nt(a, b):
    return lax.dot_general(a, b, (((1,), (1,)), ((), ())), preferred_element_type=F32)


def dot_tn(a, b):
    return lax.dot_general(a, b, (((0,), (0,)), ((), ())), preferred_element_type=F32)


def kernel_call(body, named, out_shape, in_specs, out_specs, scratch, args, alias=None):
    return pl.pallas_call(
        body,
        out_shape=out_shape,
        in_specs=in_specs,
        out_specs=out_specs,
        scratch_shapes=scratch,
        input_output_aliases=alias or {},
        compiler_params=pltpu.CompilerParams(vmem_limit_bytes=VMEM_BYTES),
        name=named.__name__,
    )(*args)


def hold(values, done):
    shapes = tuple(jax.ShapeDtypeStruct(v.shape, v.dtype) for v in values)
    return kernel_call(
        lambda *refs: None,
        hold,
        shapes,
        [ANYWHERE] * (len(values) + len(done)),
        (ANYWHERE,) * len(values),
        [],
        (*values, *done),
        {i: i for i in range(len(values))},
    )


def sds(shape, dtype=BF):
    return jax.ShapeDtypeStruct(shape, dtype)


def center(v):
    mean = jnp.mean(v, -1, keepdims=True)
    centred = v - mean
    inverse = lax.rsqrt(jnp.mean(centred * centred, -1, keepdims=True) + EPSILON)
    return centred * inverse, inverse


def norm_grad(normed, inverse, gain, gradient):
    dn = gradient * gain
    return inverse * (
        dn - jnp.mean(dn, -1, keepdims=True) - normed * jnp.mean(dn * normed, -1, keepdims=True)
    )


def exact_rows(place, v):
    high = v.astype(BF)
    rest = (v - high.astype(F32)).astype(BF)
    return dot_tn(place, high) + dot_tn(place, rest)


def segment_bias(starts, length, segs):
    col = lax.broadcasted_iota(jnp.int32, (length, 1), 0)
    row = lax.broadcasted_iota(jnp.int32, (1, length), 1)
    col_seg = jnp.zeros((length, 1), jnp.int32)
    row_seg = jnp.zeros((1, length), jnp.int32)
    for k in range(segs):
        col_seg = col_seg + jnp.where(col >= starts[0, k], 1, 0)
        row_seg = row_seg + jnp.where(row >= starts[0, k], 1, 0)
    return jnp.where(col_seg == row_seg, 0.0, MASKED)


def cuts(layout, start, count):
    found = []
    for i, part, mask, offset, rows in layout:
        low, high = max(offset, start), min(offset + rows, start + count)
        if low < high:
            found.append((i, part, mask, low - offset, low - start, high - low))
    return found


def rows_of(ref, part, row, rows):
    return ref.at[pl.ds(row, rows)] if part is None else ref.at[part, pl.ds(row, rows)]


def load_weight(me, refs, layout, segment, shard, dst, sems):
    copies = []
    for k, (i, part, mask, row, at, rows) in enumerate(cuts(layout, segment * shard, shard)):
        to = pl.multiple_of((me ^ mask) * shard + at, 16)
        src = rows_of(refs[i], part, row, rows)
        copy = pltpu.make_async_copy(src, dst.at[pl.ds(to, rows)], sems.at[k])
        copy.start()
        copies.append(copy)
    return copies


def attention_forward(n, layout, segs, n_vec, *refs):
    count = 1 + max(i for i, *_ in layout)
    me_ref, starts, tokens = refs[:3]
    pieces = refs[3 : 3 + count]
    qkv, mixed, lse, n1_out, vec, b_in = refs[3 + count : 9 + count]
    weights, smalls, v_t, mixed_t, bias, sems, small_sems = refs[9 + count :]
    tok, width = tokens.shape
    shard = width // n
    me = me_ref[0]
    small_copies = []
    for k, (i, part, mask, row, at, rows) in enumerate(cuts(layout, 4 * shard, 16)):
        copy = pltpu.make_async_copy(
            rows_of(pieces[i], part, row, rows),
            smalls.at[mask, pl.ds(at, rows)],
            small_sems.at[k],
        )
        copy.start()
        small_copies.append(copy)
    copies = []
    for i in range(3):
        cols = weights.at[:, pl.ds(i * width, width)]
        copies.append(load_weight(me, pieces, layout, i, shard, cols, sems.at[i]))
    bias[...] = segment_bias(starts, tok, segs)
    normed, _ = center(tokens[...].astype(F32))
    for copy in small_copies:
        copy.wait()
    lane = lax.broadcasted_iota(jnp.int32, (LANES, width), 0)
    col = lax.broadcasted_iota(jnp.int32, (LANES, width), 1)
    total = jnp.zeros((16, width), F32)
    for m in range(n):
        spread = ((col - (me ^ m) * shard == lane) & (lane < shard)).astype(F32).astype(BF)
        total = total + dot_nn(smalls[m, :, :LANES], spread)
    vec[...] = total
    half_ff = width // 2
    mine, other = smalls[0].astype(F32)[:, :half_ff], smalls[1].astype(F32)[:, :half_ff]
    first = me % 2 == 0
    b_in[:, :half_ff] = jnp.where(first, mine, other)
    b_in[:, half_ff:] = jnp.where(first, other, mine)
    n1_out[...] = (normed * vec[0:1, :] + vec[1:2, :]).astype(BF)
    for i in range(3):
        for copy in copies[i]:
            copy.wait()
        part = dot_nn(n1_out[...], weights[:, i * width : (i + 1) * width])
        if i != 1:
            part = part + (vec[2:3, :] if i == 0 else vec[3:4, :])
        part = part.astype(BF)
        if i == 0:
            part = part * jnp.asarray(HEAD**-0.5, BF)
        qkv[:, i * width : (i + 1) * width] = part
    v_t[...] = qkv[:, 2 * width :].T
    half = lax.broadcasted_iota(jnp.int32, (1, LANES), 1) < HEAD

    def pair(p, carry):
        at = pl.multiple_of(p * LANES, LANES)
        q_pair = qkv[:, pl.ds(at, LANES)]
        k_pair = qkv[:, pl.ds(pl.multiple_of(width + p * LANES, LANES), LANES)]
        for s in range(2):
            q_one = jnp.where(half if s == 0 else ~half, q_pair, jnp.zeros_like(q_pair))
            scores = dot_nt(k_pair, q_one) + bias[...]
            top = jnp.max(scores, 0, keepdims=True)
            e = jnp.exp(scores - top)
            total = jnp.sum(e, 0, keepdims=True)
            probs = (e * (1.0 / total)).astype(BF)
            rows = pl.ds(pl.multiple_of(p * LANES + s * HEAD, HEAD), HEAD)
            mixed_t[rows, :] = dot_nn(v_t[rows, :], probs)
            lse[pl.ds(2 * p + s, 1), :] = top + jnp.log(total)
        return carry

    lax.fori_loop(0, width // LANES, pair, 0)
    mixed[...] = mixed_t[...].T.astype(BF)


def call_attention_forward(n, me, starts, tokens, pieces, layout, n_vec):
    tok, width = tokens.shape
    heads16 = (width // HEAD + 7) // 8 * 8
    f32_row = sds((16, width), F32)
    return kernel_call(
        lambda *refs: attention_forward(n, layout, starts.shape[1], n_vec, *refs),
        attention_forward,
        (sds((tok, 3 * width)), sds((tok, width)), sds((heads16, tok), F32), sds((tok, width)))
        + (f32_row, f32_row),
        [SMEM, SMEM, VMEM] + [ANYWHERE] * len(pieces),
        (VMEM,) * 6,
        [
            pltpu.VMEM((width, 3 * width), BF),
            pltpu.VMEM((n, 16, width), BF),
            pltpu.VMEM((width, tok), BF),
            pltpu.VMEM((width, tok), F32),
            pltpu.VMEM((tok, tok), F32),
            pltpu.SemaphoreType.DMA((3, len(layout))),
            pltpu.SemaphoreType.DMA((len(layout),)),
        ],
        (me, starts, tokens, *pieces),
    )


def head_grads(first, pairs, width, qkv, lse, g_mixed, bias, k_t, gq_t, g_qkv):
    half = lax.broadcasted_iota(jnp.int32, (1, LANES), 1) < HEAD
    span = pairs * LANES

    def pair(p, carry):
        def cols(part):
            return pl.ds(pl.multiple_of(part * width + (first + p) * LANES, LANES), LANES)

        def put(part):
            return pl.ds(pl.multiple_of(part * span + p * LANES, LANES), LANES)

        q_pair, k_pair, v_pair = qkv[:, cols(0)], qkv[:, cols(1)], qkv[:, cols(2)]
        gm_pair = g_mixed[:, cols(0)]
        gv, gk = [], []
        for s in range(2):
            own = half if s == 0 else ~half
            q_one = jnp.where(own, q_pair, jnp.zeros_like(q_pair))
            gm_one = jnp.where(own, gm_pair, jnp.zeros_like(gm_pair))
            scores = dot_nt(k_pair, q_one) + bias[...]
            probs = jnp.exp(scores - lse[pl.ds(2 * (first + p) + s, 1), :])
            g_probs = dot_nt(v_pair, gm_one)
            delta = jnp.sum(probs * g_probs, 0, keepdims=True)
            g_scores = (probs * (g_probs - delta)).astype(BF)
            gv.append(dot_nn(probs.astype(BF), gm_pair))
            gk.append(dot_nn(g_scores, q_pair))
            rows = pl.ds(pl.multiple_of(p * LANES + s * HEAD, HEAD), HEAD)
            gq_t[rows, :] = dot_nn(k_t[rows, :], g_scores)
        g_qkv[:, put(2)] = jnp.where(half, gv[0], gv[1]).astype(BF)
        g_qkv[:, put(1)] = jnp.where(half, gk[0], gk[1]).astype(BF)
        return carry

    at = slice(width + first * LANES, width + first * LANES + span)
    k_t[...] = qkv[:, at].T
    lax.fori_loop(0, pairs, pair, 0)
    g_qkv[:, :span] = (gq_t[...].T * (HEAD**-0.5)).astype(BF)


def share_rows(n, me, shard, whole, keep, send, sems):
    outs = []
    core = me % 2
    for k in range(n // 2):
        for i, dst in enumerate((keep, send)):
            owner = 2 * k + (core if i == 0 else 1 - core)
            src = whole.at[pl.ds(pl.multiple_of(owner * shard, 16), shard)]
            copy = pltpu.make_async_copy(src, dst.at[k], sems.at[2 * k + i])
            copy.start()
            outs.append(copy)
    return outs


def attention_backward_one(n, segs, pairs, deps, *refs):
    me_ref, starts, qkv, lse, n1, g_mixed, g_out = refs[:7]
    g_qkv, keep, send = refs[7 + deps : 10 + deps]
    k_t, gq_t, bias, g_w, out_sems = refs[10 + deps :]
    tok, width = n1.shape
    span = pairs * LANES
    bias[...] = segment_bias(starts, tok, segs)
    head_grads(0, pairs, width, qkv, lse, g_mixed, bias, k_t, gq_t, g_qkv)
    g_w[:, :width] = g_out[...]
    for i in range(3):
        part = dot_tn(n1[...], g_qkv[:, i * span : (i + 1) * span])
        g_w[:, width + i * span : width + (i + 1) * span] = part.astype(BF)
    for copy in share_rows(n, me_ref[0], width // n, g_w, keep, send, out_sems):
        copy.wait()


def call_attention_backward_one(n, me, starts, qkv, lse, n1, g_mixed, g_out, pairs, deps=()):
    tok, width = n1.shape
    shard, span = width // n, pairs * LANES
    cols = width + 3 * span
    return kernel_call(
        lambda *refs: attention_backward_one(n, starts.shape[1], pairs, len(deps), *refs),
        attention_backward_one,
        (sds((tok, 3 * span)),) + (sds((n // 2, shard, cols)),) * 2,
        [SMEM, SMEM] + [VMEM] * 5 + [ANYWHERE] * len(deps),
        (VMEM, ANYWHERE, ANYWHERE),
        [
            pltpu.VMEM((span, tok), BF),
            pltpu.VMEM((span, tok), F32),
            pltpu.VMEM((tok, tok), F32),
            pltpu.VMEM((width, cols), BF),
            pltpu.SemaphoreType.DMA((n,)),
        ],
        (me, starts, qkv, lse, n1, g_mixed, g_out, *deps),
    )


def attention_backward_two(n, layout, segs, n_vec, first, deps, *refs):
    count = 1 + max(i for i, *_ in layout)
    me_ref, starts, tokens, vec, vec_grads, qkv, lse, n1, g_mixed, g_hidden, g_first = refs[:11]
    pieces = refs[11 : 11 + count]
    at = 11 + count + deps
    input_grad, keep, send = refs[at : at + 3]
    weights, k_t, gq_t, bias, g_qkv, g_w, v_rows, sems, out_sems = refs[at + 3 :]
    tok, width = tokens.shape
    shard = width // n
    span_one = first * LANES
    span = width - span_one
    me = me_ref[0]
    copies = []
    for i in range(3):
        cols = weights.at[:, pl.ds(i * width, width)]
        copies += load_weight(me, pieces, layout, i, shard, cols, sems.at[i])
    bias[...] = segment_bias(starts, tok, segs)
    head_grads(first, span // LANES, width, qkv, lse, g_mixed, bias, k_t, gq_t, g_qkv)
    for i in range(3):
        cols = slice(i * span, (i + 1) * span)
        g_w[:, cols] = dot_tn(n1[...], g_qkv[:, cols]).astype(BF)
    for copy in copies:
        copy.wait()
    g_n1 = jnp.zeros((tok, width), F32)
    for i in range(3):
        one = slice(i * width, i * width + span_one)
        two = slice(i * width + span_one, (i + 1) * width)
        g_n1 = g_n1 + dot_nt(g_first[:, i * span_one : (i + 1) * span_one], weights[:, one])
        g_n1 = g_n1 + dot_nt(g_qkv[:, i * span : (i + 1) * span], weights[:, two])
    normed, inverse = center(tokens[...].astype(F32))
    input_grad[...] = g_hidden[...] + norm_grad(normed, inverse, vec[0:1, :], g_n1)
    v_rows[...] = jnp.zeros_like(v_rows)
    v_rows[0:1, :] = jnp.sum(g_n1 * normed, 0, keepdims=True)
    v_rows[1:2, :] = jnp.sum(g_n1, 0, keepdims=True)
    for row, i in ((2, 0), (3, 2)):
        one = g_first[:, i * span_one : (i + 1) * span_one].astype(F32)
        two = g_qkv[:, i * span : (i + 1) * span].astype(F32)
        v_rows[row : row + 1, :span_one] = jnp.sum(one, 0, keepdims=True)
        v_rows[row : row + 1, span_one:] = jnp.sum(two, 0, keepdims=True)
    v_rows[4:n_vec, :] = vec_grads[4:n_vec, :]
    g_w[:, 3 * span :] = v_rows[...].T.astype(BF)
    for copy in share_rows(n, me, shard, g_w, keep, send, out_sems):
        copy.wait()


def call_attention_backward_two(
    n,
    me,
    starts,
    tokens,
    vec,
    vec_grads,
    qkv,
    lse,
    n1,
    g_mixed,
    g_hidden,
    g_first,
    pieces,
    layout,
    n_vec,
    first,
    deps=(),
):
    tok, width = tokens.shape
    shard, span = width // n, width - first * LANES
    cols = 3 * span + LANES
    return kernel_call(
        lambda *refs: attention_backward_two(
            n, layout, starts.shape[1], n_vec, first, len(deps), *refs
        ),
        attention_backward_two,
        (sds((tok, width), F32),) + (sds((n // 2, shard, cols)),) * 2,
        [SMEM, SMEM] + [VMEM] * 9 + [ANYWHERE] * (len(pieces) + len(deps)),
        (VMEM, ANYWHERE, ANYWHERE),
        [
            pltpu.VMEM((width, 3 * width), BF),
            pltpu.VMEM((span, tok), BF),
            pltpu.VMEM((span, tok), F32),
            pltpu.VMEM((tok, tok), F32),
            pltpu.VMEM((tok, 3 * span), BF),
            pltpu.VMEM((width, cols), BF),
            pltpu.VMEM((LANES, width), F32),
            pltpu.SemaphoreType.DMA((3, len(layout))),
            pltpu.SemaphoreType.DMA((n,)),
        ],
        (
            me,
            starts,
            tokens,
            vec,
            vec_grads,
            qkv,
            lse,
            n1,
            g_mixed,
            g_hidden,
            g_first,
            *pieces,
            *deps,
        ),
    )


def place_rows(position, slots):
    row = lax.broadcasted_iota(jnp.int32, (slots, position.shape[1]), 0)
    return (row == position[...]).astype(F32).astype(BF)


def member_rows(route, first):
    row = lax.broadcasted_iota(jnp.int32, (16, route.shape[1]), 0)
    return (row == route[...] + first).astype(F32).astype(BF)


def mix_out(n, layout, slots, deps, *refs):
    count = 1 + max(i for i, *_ in layout)
    me_ref, mixed, tokens, vec, position = refs[:5]
    pieces = refs[5 : 5 + count]
    hidden, sorted_two, weights, sems = refs[5 + count + deps :]
    width = tokens.shape[1]
    copies = load_weight(me_ref[0], pieces, layout, 3, width // n, weights, sems)
    place = place_rows(position, slots)
    for copy in copies:
        copy.wait()
    value = tokens[...].astype(F32) + dot_nn(mixed[...], weights[...]) + vec[4:5, :]
    hidden[...] = value
    normed, _ = center(value)
    sorted_two[...] = dot_nn(place, (normed * vec[5:6, :] + vec[6:7, :]).astype(BF)).astype(BF)


def call_mix_out(n, me, mixed, tokens, vec, position, slots, pieces, layout, deps=()):
    tok, width = tokens.shape
    return kernel_call(
        lambda *refs: mix_out(n, layout, slots, len(deps), *refs),
        mix_out,
        (sds((tok, width), F32), sds((slots, width))),
        [SMEM] + [VMEM] * 4 + [ANYWHERE] * (len(pieces) + len(deps)),
        (VMEM, VMEM),
        [pltpu.VMEM((width, width), BF), pltpu.SemaphoreType.DMA((len(layout),))],
        (me, mixed, tokens, vec, position, *pieces, *deps),
    )


def pack(count, *refs):
    weights = refs[:count]
    vectors, down_bias, in_bias, out, small = refs[count:]
    rows = weights[0].shape[0]
    for i, ref in enumerate(weights):
        out[i * rows : (i + 1) * rows, :] = ref[...]
    small[...] = jnp.zeros_like(small)
    n_vec = vectors.shape[0]
    small[:n_vec, :rows] = vectors[...].astype(F32)
    small[n_vec : n_vec + EXPERTS, :rows] = down_bias[...].astype(F32)
    small[n_vec + EXPERTS : n_vec + 2 * EXPERTS, : in_bias.shape[1]] = in_bias[...].astype(F32)
    out[count * rows :, :] = small[...].astype(BF)


def call_pack(weights, vectors, down_bias, in_bias):
    rows, width = weights[0].shape
    return kernel_call(
        lambda *refs: pack(len(weights), *refs),
        pack,
        sds((len(weights) * rows + 16, width)),
        [VMEM] * (len(weights) + 3),
        VMEM,
        [pltpu.VMEM((16, width), F32)],
        (*weights, vectors, down_bias, in_bias),
    )


def load_blocks(refs, layout, dst, sems):
    copies = []
    for i, (ref, (block, offset, rows, row)) in enumerate(zip(refs, layout, strict=True)):
        copy = pltpu.make_async_copy(
            ref.at[pl.ds(row, rows)], dst.at[block, pl.ds(offset, rows)], sems.at[i]
        )
        copy.start()
        copies.append(copy)
    return copies


def start_all(copies):
    for copy in copies:
        copy.start()
    return copies


def wait_all(copies):
    for copy in copies:
        copy.wait()


def window(meta, block, e):
    begin = pl.multiple_of(meta[block, 3 * e], 16)
    row = lax.broadcasted_iota(jnp.int32, (CAP, 1), 0)
    return pl.ds(begin, CAP), (row >= meta[block, 3 * e + 1]) & (row < meta[block, 3 * e + 2])


def experts(chips, bias_row, lay_x, lay_g, deps, *refs):
    nb, cx, cg, cw = len(chips), len(lay_x), len(lay_g), 2
    me_ref, meta, b_in = refs[:3]
    at = 3
    x_refs, at = refs[at : at + cx], at + cx
    g_refs, at = refs[at : at + cg], at + cg
    w_refs, at = refs[at : at + cw], at + cw
    down = refs[at : at + 2]
    at += 2 + deps
    dsl, (res, act_out, dp_out) = refs[at : at + nb], refs[at + nb : at + nb + 3]
    at += nb + 3
    x_all, g_all, w_in, w_down, res_s, dsl_s, xs, gs, act_s, dp_s = refs[at : at + 10]
    sx, sg, sw, sd, so, sa = refs[at + 10 :]
    rows = w_refs[0].shape[2]
    me = me_ref[0]
    half = w_down.shape[1] // 2
    core = me % 2
    loads = load_blocks(x_refs, lay_x, x_all, sx) + load_blocks(g_refs, lay_g, g_all, sg)
    weights = []
    for e in range(EXPERTS):
        copies = []
        for i, ref in enumerate(w_refs):
            for k in range(ref.shape[0]):
                owner = 2 * k + (core if i == 0 else 1 - core)
                to = pl.ds(pl.multiple_of(owner * rows, 16), rows)
                copies.append(pltpu.make_async_copy(ref.at[k, e], w_in.at[e, to], sw.at[e, i, k]))
        for i, ref in enumerate(down):
            to = pl.multiple_of((core if i == 0 else 1 - core) * half, 16)
            copies.append(pltpu.make_async_copy(ref.at[e], w_down.at[e, pl.ds(to, half)], sd.at[e, i]))
        weights.append(start_all(copies))
    res_s[...] = jnp.zeros_like(res_s)
    dsl_s[...] = jnp.zeros_like(dsl_s)
    wait_all(loads)
    outs = []
    for e in range(EXPERTS):
        spans = []
        for b in range(nb):
            span, inside = window(meta, b, e)
            spans.append((span, inside))
            g = g_all[b, span, :]
            xs[b * CAP : (b + 1) * CAP, :] = x_all[b, span, :]
            gs[b * CAP : (b + 1) * CAP, :] = jnp.where(inside, g, jnp.zeros_like(g))
        wait_all(weights[e])
        pre = dot_nn(xs[...], w_in[e]) + b_in[bias_row + e : bias_row + e + 1, :]
        cdf = 0.5 * (1.0 + lax.erf(pre * 0.7071067811865476))
        act = (pre * cdf).astype(BF)
        slope = cdf + pre * jnp.exp(-0.5 * pre * pre) * 0.3989422804014327
        dp = (dot_nt(gs[...], w_down[e]) * slope).astype(BF)
        act_s[e] = act
        dp_s[e] = dp
        outs += start_all(
            [
                pltpu.make_async_copy(act_s.at[e], act_out.at[e], sa.at[0, e]),
                pltpu.make_async_copy(dp_s.at[e], dp_out.at[e], sa.at[1, e]),
            ]
        )
        for dst, value in ((dsl_s, dot_nt(dp, w_in[e])), (res_s, dot_nn(act, w_down[e]))):
            value = value.astype(BF)
            for b, (span, inside) in enumerate(spans):
                dst[b, span, :] = jnp.where(inside, value[b * CAP : (b + 1) * CAP], dst[b, span, :])
    for b in range(nb):
        outs += start_all(
            [
                pltpu.make_async_copy(dsl_s.at[b], dsl[b], so.at[0, b]),
                pltpu.make_async_copy(res_s.at[b], res.at[(me // 2) ^ chips[b]], so.at[1, b]),
            ]
        )
    wait_all(outs)


def call_experts(chips, bias_row, me, meta, b_in, xp, lay_x, gp, lay_g, wp, down, res, blocks):
    nb, rows, width = len(chips), max(o + r for _, o, r, _ in lay_x), xp[0].shape[1]
    ff = 2 * down[0].shape[1]
    dma = pltpu.SemaphoreType.DMA
    deps = () if res is None else (res,)
    alias = {} if res is None else {5 + len(xp) + len(gp) + len(wp): nb}
    out = kernel_call(
        lambda *refs: experts(chips, bias_row, lay_x, lay_g, len(deps), *refs),
        experts,
        (sds((rows, width)),) * nb
        + (sds((blocks, rows, width)),)
        + (sds((EXPERTS, nb * CAP, ff)),) * 2,
        [SMEM, SMEM, VMEM] + [ANYWHERE] * (len(xp) + len(gp) + len(wp) + 2 + len(deps)),
        (ANYWHERE,) * (nb + 3),
        [pltpu.VMEM((nb, rows, width), BF)] * 2
        + [pltpu.VMEM((EXPERTS, width, ff), BF), pltpu.VMEM((EXPERTS, ff, width), BF)]
        + [pltpu.VMEM((nb, rows, width), BF)] * 2
        + [pltpu.VMEM((nb * CAP, width), BF)] * 2
        + [pltpu.VMEM((EXPERTS, nb * CAP, ff), BF)] * 2
        + [dma((len(xp),)), dma((len(gp),)), dma((EXPERTS, 2, blocks)), dma((EXPERTS, 2))]
        + [dma((2, nb)), dma((2, EXPERTS))],
        (me, meta, b_in, *xp, *gp, *wp, *down, *deps),
        alias,
    )
    return list(out[:nb]), out[nb], out[nb + 1], out[nb + 2]


def down_grads(calls, lay_g, deps, *refs):
    cg, cc = len(lay_g), len(calls)
    me_ref, meta = refs[:2]
    g_refs, acts = refs[2 : 2 + cg], refs[2 + cg : 2 + cg + cc]
    at = 2 + cg + cc + deps
    keep, send = refs[at], refs[at + 1 : at + 1 + EXPERTS]
    g_all, act_s, gs, g_down, sg, sa, so = refs[at + 1 + EXPERTS :]
    core = me_ref[0] % 2
    half = g_down.shape[1] // 2
    loads = load_blocks(g_refs, lay_g, g_all, sg)
    hidden = load_hidden(acts, calls, act_s, sa)
    wait_all(loads)
    outs = []
    for e in range(EXPERTS):
        for b in range(sum(calls)):
            span, inside = window(meta, b, e)
            g = g_all[b, span, :]
            gs[b * CAP : (b + 1) * CAP, :] = jnp.where(inside, g, jnp.zeros_like(g))
        wait_all(hidden[e])
        g_down[e] = dot_tn(act_s[e], gs[...]).astype(BF)
        for i, dst in enumerate((keep.at[e], send[e])):
            src = g_down.at[e, pl.ds(pl.multiple_of((core if i == 0 else 1 - core) * half, 16), half)]
            outs.append(pltpu.make_async_copy(src, dst, so.at[e, i]))
            outs[-1].start()
    wait_all(outs)


def load_hidden(parts, calls, dst, sems):
    hidden = []
    for e in range(EXPERTS):
        copies, first = [], 0
        for i, nb in enumerate(calls):
            rows = pl.ds(first * CAP, nb * CAP)
            copies.append(pltpu.make_async_copy(parts[i].at[e], dst.at[e, rows], sems.at[e, i]))
            first += nb
        hidden.append(start_all(copies))
    return hidden


def call_down_grads(me, meta, gp, lay_g, acts, calls, deps=()):
    rows, width = max(o + r for _, o, r, _ in lay_g), gp[0].shape[1]
    ff, blocks = acts[0].shape[2], sum(calls)
    dma = pltpu.SemaphoreType.DMA
    return kernel_call(
        lambda *refs: down_grads(calls, lay_g, len(deps), *refs),
        down_grads,
        (sds((EXPERTS, ff // 2, width)),) + (sds((ff // 2, width)),) * EXPERTS,
        [SMEM, SMEM] + [ANYWHERE] * (len(gp) + len(acts) + len(deps)),
        (ANYWHERE,) * (1 + EXPERTS),
        [
            pltpu.VMEM((blocks, rows, width), BF),
            pltpu.VMEM((EXPERTS, blocks * CAP, ff), BF),
            pltpu.VMEM((blocks * CAP, width), BF),
            pltpu.VMEM((EXPERTS, ff, width), BF),
            dma((len(gp),)),
            dma((EXPERTS, len(calls))),
            dma((EXPERTS, 2)),
        ],
        (me, meta, *gp, *acts, *deps),
    )


def in_grads(n, calls, lay_x, deps, *refs):
    cx, cc = len(lay_x), len(calls)
    me_ref, meta = refs[:2]
    x_refs, dps = refs[2 : 2 + cx], refs[2 + cx : 2 + cx + cc]
    at = 2 + cx + cc + deps
    keep, bias_keep, bias_send = refs[at : at + 3]
    send = refs[at + 3 : at + 3 + EXPERTS]
    x_all, dp_s, xs, g_in, sx, sp, so = refs[at + 3 + EXPERTS :]
    me = me_ref[0]
    _, width, ff = g_in.shape
    shard, half = width // n, ff // 2
    loads = load_blocks(x_refs, lay_x, x_all, sx)
    hidden = load_hidden(dps, calls, dp_s, sp)
    wait_all(loads)
    outs = []
    row = lax.broadcasted_iota(jnp.int32, (16, 1), 0)
    low = jnp.zeros((16, half), F32)
    high = jnp.zeros((16, half), F32)
    for e in range(EXPERTS):
        for b in range(sum(calls)):
            span, _ = window(meta, b, e)
            xs[b * CAP : (b + 1) * CAP, :] = x_all[b, span, :]
        wait_all(hidden[e])
        g_in[e] = dot_tn(xs[...], dp_s[e]).astype(BF)
        outs += share_rows(n, me, shard, g_in.at[e], keep.at[:, e], send[e], so.at[e])
        total = jnp.sum(dp_s[e].astype(F32), 0, keepdims=True)
        low = low + jnp.where(row == e, total[:, :half], 0.0)
        high = high + jnp.where(row == e, total[:, half:], 0.0)
    first_core = me % 2 == 0
    bias_keep[...] = jnp.where(first_core, low, high).astype(BF)
    bias_send[...] = jnp.where(first_core, high, low).astype(BF)
    wait_all(outs)


def call_in_grads(n, me, meta, xp, lay_x, dps, calls, deps=()):
    rows, width = max(o + r for _, o, r, _ in lay_x), xp[0].shape[1]
    ff, blocks = dps[0].shape[2], sum(calls)
    dma = pltpu.SemaphoreType.DMA
    return kernel_call(
        lambda *refs: in_grads(n, calls, lay_x, len(deps), *refs),
        in_grads,
        (sds((n // 2, EXPERTS, width // n, ff)),)
        + (sds((16, ff // 2)),) * 2
        + (sds((n // 2, width // n, ff)),) * EXPERTS,
        [SMEM, SMEM] + [ANYWHERE] * (len(xp) + len(dps) + len(deps)),
        (ANYWHERE, VMEM, VMEM) + (ANYWHERE,) * EXPERTS,
        [
            pltpu.VMEM((blocks, rows, width), BF),
            pltpu.VMEM((EXPERTS, blocks * CAP, ff), BF),
            pltpu.VMEM((blocks * CAP, width), BF),
            pltpu.VMEM((EXPERTS, width, ff), BF),
            dma((len(xp),)),
            dma((EXPERTS, len(calls))),
            dma((EXPERTS, n)),
        ],
        (me, meta, *xp, *dps, *deps),
    )


def mix_out_backward(n, layout, terms, deps, *refs):
    count = 1 + max(i for i, *_ in layout)
    me_ref, position, route, hidden, cot, vec, mixed = refs[:7]
    got = refs[7 : 7 + terms]
    pieces = refs[7 + terms : 7 + terms + count]
    at = 7 + terms + count + deps
    g_hidden, g_mixed, vec_grads, g_w = refs[at : at + 4]
    weights, sems = refs[at + 4 :]
    me = me_ref[0]
    tok, width = hidden.shape
    shard = width // n
    copies = load_weight(me, pieces, layout, 3, shard, weights, sems)
    total = got[0][...].astype(F32)
    for ref in got[1:]:
        total = total + ref[...].astype(F32)
    gradient = exact_rows(place_rows(position, total.shape[0]), total)
    normed, inverse = center(hidden[...])
    value = cot[...].astype(F32) + norm_grad(normed, inverse, vec[5:6, :], gradient)
    g_hidden[...] = value
    branch = value.astype(BF)
    vec_grads[...] = jnp.zeros_like(vec_grads)
    vec_grads[4:5, :] = jnp.sum(branch.astype(F32), 0, keepdims=True)
    vec_grads[5:6, :] = jnp.sum(gradient * normed, 0, keepdims=True)
    vec_grads[6:7, :] = jnp.sum(gradient, 0, keepdims=True)
    vec_grads[...] += dot_nn(member_rows(route, 7), cot[...])
    for copy in copies:
        copy.wait()
    g_mixed[...] = dot_nt(branch, weights[...]).astype(BF)
    g_w[...] = dot_tn(mixed[...], branch).astype(BF)


def call_mix_out_backward(
    n, me, position, route, hidden, cot, vec, mixed, got, pieces, layout, deps=()
):
    tok, width = hidden.shape
    return kernel_call(
        lambda *refs: mix_out_backward(n, layout, len(got), len(deps), *refs),
        mix_out_backward,
        (sds((tok, width), F32), sds((tok, width)), sds((16, width), F32), sds((width, width))),
        [SMEM] + [VMEM] * (6 + len(got)) + [ANYWHERE] * (len(pieces) + len(deps)),
        (VMEM,) * 4,
        [pltpu.VMEM((width, width), BF), pltpu.SemaphoreType.DMA((len(layout),))],
        (me, position, route, hidden, cot, vec, mixed, *got, *pieces, *deps),
    )


def finish_output(deps, *refs):
    position, hidden, route, vec = refs[:4]
    got = refs[4]
    out = refs[5 + deps]
    value = hidden[...] + dot_tn(place_rows(position, got.shape[0]), got[...])
    value = value + dot_tn(member_rows(route, 7), vec[...].astype(BF))
    out[...] = value.astype(BF)


def call_finish_output(position, hidden, route, vec, got, deps=()):
    return kernel_call(
        lambda *refs: finish_output(len(deps), *refs),
        finish_output,
        sds(hidden.shape),
        [VMEM] * 5 + [ANYWHERE] * len(deps),
        VMEM,
        [],
        (position, hidden, route, vec, got, *deps),
    )


def join(body, named, outs, scalars, arrays, deps=()):
    n_s, n_a, n_d, n_o = len(scalars), len(arrays), len(deps), len(outs)

    def kernel(*refs):
        at = n_s + n_a + n_d
        body(refs[:n_s], refs[n_s : n_s + n_a], refs[at : at + n_o])

    return kernel_call(
        kernel,
        named,
        tuple(outs),
        [SMEM] * n_s + [VMEM] * n_a + [ANYWHERE] * n_d,
        (VMEM,) * n_o,
        [],
        (*scalars, *arrays, *deps),
    )


def plus(*values):
    total = values[0].astype(F32)
    for value in values[1:]:
        total = total + value.astype(F32)
    return total


def call_halves(own, along, across, deps=()):
    rows, width = along.shape
    half = rows // 32 * 16

    def body(_, ins, outs):
        outs[0][...] = ins[1][:half]
        outs[1][...] = ins[2][half:]
        for i in range(3):
            outs[2][i] = ins[i][...]

    shapes = (sds((half, width)), sds((rows - half, width)), sds((3, rows, width)))
    return join(body, call_halves, shapes, (), (own, along, across), deps)


def call_two_halves(first, second, deps=()):
    cuts_at = [pair[0].shape[0] // 32 * 16 for pair in (first, second)]
    width = first[0].shape[1]
    split = cuts_at[0]

    def body(_, ins, outs):
        outs[0][:split] = ins[0][:split]
        outs[0][split:] = ins[2][: cuts_at[1]]
        rest = ins[0].shape[0] - split
        outs[1][:rest] = ins[1][split:]
        outs[1][rest:] = ins[3][cuts_at[1] :]

    rows = first[0].shape[0] + second[0].shape[0]
    shapes = (sds((sum(cuts_at), width)), sds((rows - sum(cuts_at), width)))
    return join(body, call_two_halves, shapes, (), (*first, *second), deps)


def call_columns_and_sort(n, whole, position, slots, value, meta, deps):
    experts_, rows, cols = whole.shape
    pair = cols // (n // 2)

    def body(_, ins, outs):
        for k in range(n // 2):
            outs[0][k] = ins[0][:, :, k * pair : (k + 1) * pair]
        outs[1][:slots, :] = dot_nn(place_rows(ins[1], slots), ins[2][...]).astype(BF)
        outs[1][slots:, :] = jnp.zeros((16, value.shape[1]), BF)
        outs[1][slots:, :LANES] = jnp.broadcast_to(ins[3][...], (16, LANES)).astype(BF)

    shapes = (sds((n // 2, experts_, rows, pair)), sds((slots + 16, value.shape[1])))
    return join(body, call_columns_and_sort, shapes, (), (whole, position, value, meta), deps)


def call_pair_down(kept, keep, got, deps=()):
    experts_, rows, width = keep.shape
    half = rows // 2

    def body(scalars, ins, outs):
        mine = pl.multiple_of(scalars[0][0] * half, 16)
        other = pl.multiple_of((1 - scalars[0][0]) * half, 16)
        for out, at in zip(outs, (mine, other), strict=True):
            for e in range(experts_):
                part = plus(ins[0][e, pl.ds(at, half)], ins[1 + e][pl.ds(at, half)])
                out[e] = part.astype(BF)

    shapes = (sds((experts_, half, width)),) * 2
    return join(body, call_pair_down, shapes, (kept,), (keep, *got), deps)


def call_pair_in(keep, got, bias_keep, bias_got, d_keep, d_got, cut, deps=()):
    count = len(got)

    def body(_, ins, outs):
        for e in range(count):
            outs[0][:, e] = plus(ins[0][:, e], ins[5 + e][...]).astype(BF)
        outs[1][...] = plus(ins[1][...], ins[2][...]).astype(BF)
        outs[2][...] = plus(ins[3][:cut], ins[4][:cut]).astype(BF)
        outs[3][...] = plus(ins[3][cut:], ins[4][cut:]).astype(BF)

    shapes = (sds(keep.shape), sds(bias_keep.shape))
    shapes += (sds((cut, *d_keep.shape[1:])), sds((d_keep.shape[0] - cut, *d_keep.shape[1:])))
    arrays = (keep, bias_keep, bias_got, d_keep, d_got, *got)
    return join(body, call_pair_in, shapes, (), arrays, deps)


def call_split_rows(kept, whole, deps=()):
    chips, experts_, rows, ff = whole.shape
    half = rows // 2
    two = chips // 2

    def body(scalars, ins, outs):
        outs[0][...] = ins[0][:, :, pl.ds(pl.multiple_of(scalars[0][0] * half, 16), half)]
        other = pl.ds(pl.multiple_of((1 - scalars[0][0]) * half, 16), half)
        for i in range(2):
            outs[1 + i][...] = ins[0][i * two : (i + 1) * two, :, other]

    shapes = (sds((chips, experts_, half, ff)),) + (sds((two, experts_, half, ff)),) * 2
    return join(body, call_split_rows, shapes, (kept,), (whole,), deps)


def call_pair_shares(one, two, deps=()):
    chips, rows, cols_one = one[0].shape
    cols = cols_one + two[0].shape[2]

    def body(_, ins, outs):
        outs[0][:, :, :cols_one] = plus(ins[0][...], ins[1][...]).astype(BF)
        outs[0][:, :, cols_one:] = plus(ins[2][...], ins[3][...]).astype(BF)

    return join(body, call_pair_shares, (sds((chips, rows, cols)),), (), (*one, *two), deps)[0]


def call_line_sums(parts, across, i_keep, i_got, deps=()):
    cut = parts[0].shape[0]
    rest = parts[1].shape[0]
    two = i_got[0].shape[0]

    def body(_, ins, outs):
        outs[0][:cut] = plus(ins[0][...], ins[2][...]).astype(BF)
        outs[0][cut:] = plus(ins[1][...], ins[3][...]).astype(BF)
        for i in range(2):
            at = slice(i * two, (i + 1) * two)
            outs[1][at] = plus(ins[4][at], ins[5 + i][...]).astype(BF)

    shapes = (sds((cut + rest, *parts[0].shape[1:])), sds(i_keep.shape))
    return join(body, call_line_sums, shapes, (), (*parts, *across, i_keep, *i_got), deps)


def call_sums(jobs, deps=()):
    flat = [v for job in jobs for v in job]

    def body(_, ins, outs):
        at = 0
        for job, out in zip(jobs, outs, strict=True):
            out[...] = plus(*[ref[...] for ref in ins[at : at + len(job)]]).astype(BF)
            at += len(job)

    return join(body, call_sums, [sds(job[0].shape) for job in jobs], (), flat, deps)


def call_attention_shares(kept, got, bias, deps=()):
    chips, rows, cols = got.shape
    half = rows // 2

    def body(scalars, ins, outs):
        mine = pl.multiple_of(scalars[0][0] * half, 16)
        other = pl.multiple_of((1 - scalars[0][0]) * half, 16)
        for out, at in zip(outs, (mine, other), strict=True):
            out[:half, :] = plus(*[ins[0][k, pl.ds(at, half)] for k in range(chips)]).astype(BF)
            out[half:, :] = jnp.zeros((16, cols), BF)
            out[half:, : bias.shape[1]] = ins[1][...]

    shapes = (sds((half + 16, cols)),) * 2
    return join(body, call_attention_shares, shapes, (kept,), (got, bias), deps)


def call_down_result(kept, mine, got, deps=()):
    experts_, half, width = mine.shape

    def body(scalars, ins, outs):
        outs[0][:, pl.ds(pl.multiple_of(scalars[0][0] * half, 16), half)] = ins[0][...].astype(F32)
        at = pl.multiple_of((1 - scalars[0][0]) * half, 16)
        outs[0][:, pl.ds(at, half)] = ins[1][...].astype(F32)

    shape = (sds((experts_, 2 * half, width), F32),)
    return join(body, call_down_result, shape, (kept,), (mine, got), deps)[0]


def call_in_result(kept, mine, got, deps=()):
    chips, experts_, half, ff = mine.shape

    def body(scalars, ins, outs):
        for ref, which in ((ins[0], scalars[0][0]), (ins[1], 1 - scalars[0][0])):
            rows = pl.ds(pl.multiple_of(which * half, 16), half)
            for k in range(chips):
                outs[0][:, rows, k * ff : (k + 1) * ff] = ref[k].astype(F32)

    shape = (sds((experts_, 2 * half, chips * ff), F32),)
    return join(body, call_in_result, shape, (kept,), (mine, got), deps)[0]


def call_attention_result(kept, mine, got, width, span, n_vec, ff_shard, deps=()):
    half = mine.shape[0] - 16
    last = width - span
    cols_one = width + 3 * span

    def body(scalars, ins, outs):
        for ref, which in ((ins[0], scalars[0][0]), (ins[1], 1 - scalars[0][0])):
            rows = pl.ds(pl.multiple_of(which * half, 16), half)
            outs[0][rows, :] = ref[:half, :width].astype(F32)
            for i in range(3):
                one = ref[:half, width + i * span : width + (i + 1) * span]
                two = ref[:half, cols_one + i * last : cols_one + (i + 1) * last]
                outs[1 + i][rows, :span] = one.astype(F32)
                outs[1 + i][rows, span:] = two.astype(F32)
            outs[4][rows, :] = ref[:half, cols_one + 3 * last :].astype(F32)
        rows = outs[4][...].T
        outs[5][...] = ins[0][half : half + EXPERTS, :ff_shard].astype(F32)
        outs[6][...] = rows[n_vec - EXPERTS : n_vec]
        for i, out in enumerate(outs[7:]):
            out[...] = rows[i : i + 1]

    shapes = (sds((2 * half, width), F32),) * 4 + (sds((2 * half, LANES), F32),)
    shapes += (sds((EXPERTS, ff_shard), F32), sds((EXPERTS, 2 * half), F32))
    shapes += (sds((1, 2 * half), F32),) * (n_vec - EXPERTS)
    return join(body, call_attention_result, shapes, (kept,), (mine, got), deps)


def swap(v, n, mask):
    return lax.ppermute(v, FSDP, [(i, i ^ mask) for i in range(n)])


def blocks_of(pieces, here):
    mine = [p for p in pieces if p[1] in here]
    return [p[0] for p in mine], [(here.index(c), at, rows, row) for _, c, at, rows, row in mine]


def scatter_chips(terms, n):
    return [terms[0]] + [swap(terms[i], n, 2 * i) for i in range(1, n // 2)]


def exchange(v, n):
    groups = [list(range(core, n, 2)) for core in range(2)]
    return lax.all_to_all(v, FSDP, 0, 0, axis_index_groups=groups)


def plane_sum(v, n):
    groups = [list(range(core, n, 2)) for core in range(2)]
    return lax.psum_scatter(v, FSDP, scatter_dimension=0, axis_index_groups=groups)


def line(v, step):
    pairs = [(0, 3), (3, 0), (1, 2), (2, 1)] if step == 1 else [(0, 1), (1, 0), (2, 3), (3, 2)]
    return lax.ppermute(v, REP, pairs)


def per_device_tokens(
    n,
    tokens,
    starts,
    routes,
    norm1_gain,
    norm1_bias,
    query_weight,
    query_bias,
    key_weight,
    value_weight,
    value_bias,
    out_weight,
    out_bias,
    norm2_gain,
    norm2_bias,
    expert_in,
    expert_in_bias,
    expert_out,
    expert_out_bias,
    cotangent,
):
    index = lax.axis_index(FSDP)
    me = index.astype(jnp.int32).reshape(1)
    tok_count, width = tokens.shape
    shard = width // n
    ff_shard = expert_out.shape[1]
    ff_pair = 2 * ff_shard

    vectors = [norm1_gain, norm1_bias, query_bias, value_bias, out_bias, norm2_gain, norm2_bias]
    n_vec = len(vectors) + EXPERTS
    payload = call_pack(
        (query_weight, key_weight, value_weight, out_weight),
        jnp.stack(vectors),
        expert_out_bias,
        expert_in_bias,
    )
    along, across = swap(payload, n, 2), swap(payload, n, 4)
    top, bottom, three = call_halves(payload, along, across)
    top_got, bottom_got = swap(top, n, 4), swap(bottom, n, 2)
    rows, half = payload.shape[0], top.shape[0]
    w_attn = [payload, along, across, top_got, bottom_got]
    w_attn += [swap(three, n, 1), swap(top_got, n, 1), swap(bottom_got, n, 1)]
    lay_attn = [(i, None, m, 0, rows) for i, m in enumerate((0, 2, 4))]
    lay_attn += [(5, i, m, 0, rows) for i, m in enumerate((1, 3, 5))]
    lay_attn += [(3, None, 6, 0, half), (4, None, 6, half, rows - half)]
    lay_attn += [(6, None, 7, 0, half), (7, None, 7, half, rows - half)]

    route_ids = routes[:, 0]
    member = (route_ids[:, None] == jnp.arange(EXPERTS, dtype=jnp.int32)[None, :]).astype(jnp.int32)
    rank = jnp.sum(jnp.cumsum(member, 0) * member, 1) - 1
    padded = (jnp.sum(member, 0) + 15) // 16
    base = jnp.cumsum(padded) - padded
    slots = tok_count + 16 * (EXPERTS - 1)
    position = (jnp.sum(member * base[None, :], 1) * 16 + rank).astype(jnp.int32)
    position_row, route_row = position[None, :], route_ids[None, :]
    begin = jnp.minimum(base, (slots - CAP) // 16)
    meta = jnp.stack([begin, base - begin, base - begin + padded], 1).reshape(1, 3 * EXPERTS) * 16
    meta = meta.astype(jnp.int32)
    down_other = swap(expert_out, n, 1)

    meta_row = jnp.pad((meta // 16).astype(F32), ((0, 0), (0, LANES - meta.shape[1])))
    columns, sorted_grad = call_columns_and_sort(
        n, expert_in, position_row, slots, cotangent, meta_row, (top,)
    )
    w_mine = exchange(hold((columns,), (w_attn[6], w_attn[7]))[0], n)
    grad_along, grad_across = swap(sorted_grad, n, 2), swap(sorted_grad, n, 4)

    qkv, mixed, lse, n1, vec, in_bias = call_attention_forward(
        n, me, starts, tokens, w_attn, lay_attn, n_vec
    )
    hidden, sorted_two = call_mix_out(
        n,
        me,
        mixed,
        tokens,
        vec,
        position_row,
        slots,
        w_attn,
        lay_attn,
    )
    tok_along, tok_across = swap(sorted_two, n, 2), swap(sorted_two, n, 4)
    (w_mine,) = hold((w_mine,), (sorted_two,))
    w_pair = (w_mine, swap(w_mine, n, 1))

    calls = ((0,), (1, 2), (3,))
    sizes = tuple(len(call) for call in calls)
    dsl, acts, dps = [], [], []

    def run(call, metas, token_pieces, grad_pieces, res):
        d, res, a, p = call_experts(
            call,
            n_vec,
            me,
            metas,
            in_bias,
            *blocks_of(token_pieces, call),
            *blocks_of(grad_pieces, call),
            w_pair,
            (expert_out, down_other),
            res,
            n // 2,
        )
        dsl.extend(d)
        acts.append(a)
        dps.append(p)
        return res

    def meta_of(rows):
        return rows[:, : 3 * EXPERTS].astype(jnp.int32) * 16

    token_pieces = [(sorted_two, 0, 0, slots, 0)]
    grad_pieces = [(sorted_grad, 0, 0, slots, 0)]
    res = run(calls[0], meta, token_pieces, grad_pieces, None)
    tops, bottoms = call_two_halves((tok_along, tok_across), (grad_along, grad_across), (dps[0],))
    tops, bottoms = swap(tops, n, 4), swap(bottoms, n, 2)
    half, low = slots // 32 * 16, sorted_grad.shape[0] // 32 * 16
    rest = slots - half
    token_pieces += [(tok_along, 1, 0, slots, 0), (tok_across, 2, 0, slots, 0)]
    token_pieces += [(tops, 3, 0, half, 0), (bottoms, 3, half, rest, 0)]
    grad_pieces += [(grad_along, 1, 0, slots, 0), (grad_across, 2, 0, slots, 0)]
    grad_pieces += [(tops, 3, 0, low, half), (bottoms, 3, low, slots - low, rest)]
    meta_xy = meta_of(
        jnp.concatenate([grad_along[slots : slots + 1], grad_across[slots : slots + 1]], 0)
    )
    meta_d = meta_of(bottoms[-16:-15])
    meta_rel = jnp.concatenate([meta, meta_xy, meta_d], 0)
    res = run(calls[1], meta_xy, token_pieces, grad_pieces, res)
    res = run(calls[2], meta_d, token_pieces, grad_pieces, res)
    got_dsl = scatter_chips(dsl, n)

    at = lax.axis_index(REP)
    kept = jnp.where((at == 0) | (at == 3), 1, 0).astype(jnp.int32).reshape(1)
    down_keep, *down_send = call_down_grads(
        me,
        meta_rel,
        *blocks_of(grad_pieces, range(n // 2)),
        acts,
        sizes,
        (got_dsl[1],),
    )
    down_got = [swap(v, n, 1) for v in down_send]

    g_hidden, g_mixed, vec_grads, g_out = call_mix_out_backward(
        n,
        me,
        position_row,
        route_row,
        hidden,
        cotangent,
        vec,
        mixed,
        got_dsl,
        w_attn,
        lay_attn,
        (down_keep,),
    )
    (res,) = hold((res,), (g_out,))
    got_res = plane_sum(res, n)
    d_keep, d_send = call_pair_down(kept, down_keep, down_got, (g_out,))
    d_got = line(d_send, 0)
    in_keep, in_bias_keep, in_bias_send, *in_send = call_in_grads(
        n,
        me,
        meta_rel,
        *blocks_of(token_pieces, range(n // 2)),
        dps,
        sizes,
        (d_send,),
    )
    *in_send, in_bias_send = hold((*in_send, in_bias_send), (in_keep,))
    in_other, in_bias_other = [swap(v, n, 1) for v in in_send], swap(in_bias_send, n, 1)

    first = width // LANES // 2
    span = first * LANES
    g_first, keep_one, send_one = call_attention_backward_one(
        n, me, starts, qkv, lse, n1, g_mixed, g_out, first, (in_keep,)
    )
    i_terms, bias_term, *d_parts = call_pair_in(
        in_keep, in_other, in_bias_keep, in_bias_other, d_keep, d_got, 1, (g_first,)
    )
    d_first = line(d_parts[0], 1)
    i_plane = exchange(i_terms, n)
    (send_one,) = hold((send_one,), (i_terms,))
    other_one = swap(send_one, n, 1)
    input_grad, keep_two, send_two = call_attention_backward_two(
        n,
        me,
        starts,
        tokens,
        vec,
        vec_grads,
        qkv,
        lse,
        n1,
        g_mixed,
        g_hidden,
        g_first,
        w_attn,
        lay_attn,
        n_vec,
        first,
        (i_terms,),
    )
    send_two, d_second = hold((send_two, d_parts[1]), (keep_two, d_first))
    other_two = swap(send_two, n, 1)
    d_across = (d_first, line(d_second, 1))
    i_keep, *i_send = call_split_rows(kept, i_plane, (keep_two,))
    i_got = [line(v, 0) for v in i_send]
    p_terms = call_pair_shares((keep_one, other_one), (keep_two, other_two), (keep_two,))
    d_total, i_part = call_line_sums(
        (d_parts[0], d_second), d_across, i_keep, i_got, (p_terms,)
    )
    d_rest, i_across = line(d_total, 2), line(i_part, 1)
    (p_terms,) = hold((p_terms,), (d_total,))
    p_plane = exchange(p_terms, n)
    p_keep, p_send = call_attention_shares(kept, p_plane, bias_term)
    sum_down = call_down_result(kept, d_total, d_rest, (p_send,))
    p_got = line(p_send, 0)
    (i_total,) = call_sums([(i_part, i_across)], (sum_down,))
    i_rest = line(i_total, 2)
    (p_part,) = call_sums([(p_keep, p_got)], (i_total,))
    p_across = line(p_part, 1)
    (p_total,) = call_sums([(p_part, p_across)])
    p_rest = line(p_total, 2)
    output = call_finish_output(position_row, hidden, route_row, vec, got_res, (p_total,))
    sum_in = call_in_result(kept, i_total, i_rest, (output,))
    sum_out, sum_query, sum_key, sum_value, _, sum_in_bias, sum_down_bias, *sum_vec = (
        call_attention_result(
            kept, p_total, p_rest, width, span, n_vec, ff_shard, (output,)
        )
    )
    sum_vec = [v.reshape(shard) for v in sum_vec]
    return (
        output,
        input_grad,
        sum_vec[0],
        sum_vec[1],
        sum_query,
        sum_vec[2],
        sum_key,
        sum_value,
        sum_vec[3],
        sum_out,
        sum_vec[4],
        sum_vec[5],
        sum_vec[6],
        sum_in,
        sum_in_bias,
        sum_down,
        sum_down_bias,
    )


def plan_of(n, replicas):
    if n == 8 and replicas == 4:
        return lambda *args: per_device_tokens(n, *args)
    return per_device_weights


def solution(mesh):
    in_specs = (
        P((FSDP, REP), None),
        P((FSDP, REP), None),
        P((FSDP, REP), None),
        P(FSDP),
        P(FSDP),
        P(FSDP, None),
        P(FSDP),
        P(FSDP, None),
        P(FSDP, None),
        P(FSDP),
        P(FSDP, None),
        P(FSDP),
        P(FSDP),
        P(FSDP),
        P(None, FSDP, None),
        P(None, FSDP),
        P(None, FSDP, None),
        P(None, FSDP),
        P((FSDP, REP), None),
    )
    out_specs = (
        P((FSDP, REP), None),
        P((FSDP, REP), None),
        P(FSDP),
        P(FSDP),
        P(FSDP, None),
        P(FSDP),
        P(FSDP, None),
        P(FSDP, None),
        P(FSDP),
        P(FSDP, None),
        P(FSDP),
        P(FSDP),
        P(FSDP),
        P(None, FSDP, None),
        P(None, FSDP),
        P(None, FSDP, None),
        P(None, FSDP),
    )
    per_device = plan_of(mesh.shape[FSDP], mesh.shape[REP])
    return jax.shard_map(
        per_device, mesh=mesh, in_specs=in_specs, out_specs=out_specs, check_vma=False
    )
```

```python
import jax
import jax.numpy as jnp
from jax import lax
from jax.experimental import pallas as pl
from jax.experimental.pallas import tpu as pltpu
from jax.sharding import PartitionSpec as P

FSDP = "fsdp"
REP = "rep"
HEAD = 64
EXPERTS = 3
CAP = 208


EPSILON = 1e-05
MASKED = -1000000000.0


def normalize(inputs, gain, shift):
    mean = jnp.mean(inputs, -1, keepdims=True)
    centred = inputs - mean
    inverse = lax.rsqrt(jnp.mean(centred * centred, -1, keepdims=True) + EPSILON)
    return centred * inverse * gain + shift


def norm_back(inputs, gain, gradient):
    mean = jnp.mean(inputs, -1, keepdims=True)
    centred = inputs - mean
    inverse = lax.rsqrt(jnp.mean(centred * centred, -1, keepdims=True) + EPSILON)
    normed = centred * inverse
    grad_normed = gradient * gain
    grad_inputs = inverse * (
        grad_normed
        - jnp.mean(grad_normed, -1, keepdims=True)
        - normed * jnp.mean(grad_normed * normed, -1, keepdims=True)
    )
    return (grad_inputs, jnp.sum(gradient * normed, 0), jnp.sum(gradient, 0))


def gelu_exact(inputs):
    return 0.5 * inputs * (1.0 + lax.erf(inputs * 0.7071067811865476))


def gelu_slope(inputs):
    return (
        0.5 * (1.0 + lax.erf(inputs * 0.7071067811865476))
        + inputs * jnp.exp(-0.5 * inputs * inputs) * 0.3989422804014327
    )


def per_device_weights(
    tokens,
    starts,
    routes,
    norm1_gain,
    norm1_bias,
    query_weight,
    query_bias,
    key_weight,
    value_weight,
    value_bias,
    out_weight,
    out_bias,
    norm2_gain,
    norm2_bias,
    expert_in,
    expert_in_bias,
    expert_out,
    expert_out_bias,
    cotangent,
):
    seq_rows = starts.shape[0]
    tok_count = tokens.shape[0]
    seq_len = tok_count // seq_rows
    model_width = tokens.shape[1]
    head_count = model_width // HEAD
    head_shape = (seq_rows, seq_len, head_count, HEAD)
    scale_factor = HEAD ** (-0.5)
    gain_one, shift_one, w_query, b_query, w_key, w_value, b_value, w_out, b_out = (
        lax.all_gather(norm1_gain, FSDP, axis=0, tiled=True),
        lax.all_gather(norm1_bias, FSDP, axis=0, tiled=True),
        lax.all_gather(query_weight, FSDP, axis=0, tiled=True),
        lax.all_gather(query_bias, FSDP, axis=0, tiled=True),
        lax.all_gather(key_weight, FSDP, axis=0, tiled=True),
        lax.all_gather(value_weight, FSDP, axis=0, tiled=True),
        lax.all_gather(value_bias, FSDP, axis=0, tiled=True),
        lax.all_gather(out_weight, FSDP, axis=0, tiled=True),
        lax.all_gather(out_bias, FSDP, axis=0, tiled=True),
    )
    resid_in = tokens.astype(jnp.float32)
    normed_one = normalize(
        resid_in, gain_one.astype(jnp.float32), shift_one.astype(jnp.float32)
    ).astype(jnp.bfloat16)
    queries = (
        (
            jnp.dot(normed_one, w_query, preferred_element_type=jnp.float32)
            + b_query.astype(jnp.float32)
        )
        .astype(jnp.bfloat16)
        .reshape(head_shape)
    )
    keys_mat = (
        jnp.dot(normed_one, w_key, preferred_element_type=jnp.float32)
        .astype(jnp.bfloat16)
        .reshape(head_shape)
    )
    values = (
        (
            jnp.dot(normed_one, w_value, preferred_element_type=jnp.float32)
            + b_value.astype(jnp.float32)
        )
        .astype(jnp.bfloat16)
        .reshape(head_shape)
    )
    position = jnp.arange(seq_len, dtype=jnp.int32)
    segment = jnp.sum((position[None, :, None] >= starts[:, None, :]).astype(jnp.int32), -1)
    same_seg = (segment[:, :, None] == segment[:, None, :])[:, None]

    def scores_of(query_part, key_part):
        raw_scores = (
            jnp.einsum("rqhd,rkhd->rhqk", query_part, key_part, preferred_element_type=jnp.float32)
            * scale_factor
        )
        return jnp.where(same_seg, raw_scores, MASKED)

    scores = scores_of(queries, keys_mat)
    row_max = jnp.max(scores, -1, keepdims=True)
    exp_scores = jnp.exp(scores - row_max)
    row_total = jnp.sum(exp_scores, -1, keepdims=True)
    log_total = row_max + jnp.log(row_total)
    probs_low = (exp_scores / row_total).astype(jnp.bfloat16)
    mixed = jnp.einsum("rhqk,rkhd->rqhd", probs_low, values, preferred_element_type=jnp.float32)
    mixed = mixed.reshape(tok_count, model_width).astype(jnp.bfloat16)
    hidden = (
        resid_in
        + jnp.dot(mixed, w_out, preferred_element_type=jnp.float32)
        + b_out.astype(jnp.float32)
    )
    gain_two, shift_two, w_in, b_in, w_down, b_down = (
        lax.all_gather(norm2_gain, FSDP, axis=0, tiled=True),
        lax.all_gather(norm2_bias, FSDP, axis=0, tiled=True),
        lax.all_gather(expert_in, FSDP, axis=1, tiled=True),
        lax.all_gather(expert_in_bias, FSDP, axis=1, tiled=True),
        lax.all_gather(expert_out, FSDP, axis=1, tiled=True),
        lax.all_gather(expert_out_bias, FSDP, axis=1, tiled=True),
    )
    normed_two = normalize(
        hidden, gain_two.astype(jnp.float32), shift_two.astype(jnp.float32)
    ).astype(jnp.bfloat16)
    route_ids = routes[:, 0]
    member = (route_ids[:, None] == jnp.arange(EXPERTS, dtype=jnp.int32)[None, :]).astype(jnp.int32)
    rank = jnp.sum(jnp.cumsum(member, 0) * member, 1) - 1
    slot_ids = route_ids * CAP + rank
    packed = (
        jnp.zeros((EXPERTS * CAP, model_width), jnp.bfloat16)
        .at[slot_ids]
        .set(normed_two)
        .reshape(EXPERTS, CAP, model_width)
    )
    pre_act = (
        jnp.einsum("ecd,edf->ecf", packed, w_in, preferred_element_type=jnp.float32)
        + b_in.astype(jnp.float32)[:, None, :]
    )
    act_low = gelu_exact(pre_act).astype(jnp.bfloat16)
    result = (
        jnp.einsum("ecf,efd->ecd", act_low, w_down, preferred_element_type=jnp.float32)
        + b_down.astype(jnp.float32)[:, None, :]
    )
    routed = result.reshape(EXPERTS * CAP, model_width)[slot_ids]
    output = (hidden + routed).astype(jnp.bfloat16)
    gain_two_back, w_in_back, w_down_back = (
        lax.all_gather(norm2_gain, FSDP, axis=0, tiled=True),
        lax.all_gather(expert_in, FSDP, axis=1, tiled=True),
        lax.all_gather(expert_out, FSDP, axis=1, tiled=True),
    )
    grad_output = cotangent.astype(jnp.float32)
    grad_packed = (
        jnp.zeros((EXPERTS * CAP, model_width), jnp.bfloat16)
        .at[slot_ids]
        .set(cotangent)
        .reshape(EXPERTS, CAP, model_width)
    )
    grad_down_bias = jnp.sum(grad_packed.astype(jnp.float32), 1)
    grad_down = jnp.einsum("ecf,ecd->efd", act_low, grad_packed, preferred_element_type=jnp.float32)
    grad_act = jnp.einsum(
        "ecd,efd->ecf", grad_packed, w_down_back, preferred_element_type=jnp.float32
    )
    grad_pre = (grad_act * gelu_slope(pre_act)).astype(jnp.bfloat16)
    grad_in_bias = jnp.sum(grad_pre.astype(jnp.float32), 1)
    grad_in = jnp.einsum("ecd,ecf->edf", packed, grad_pre, preferred_element_type=jnp.float32)
    grad_slots = jnp.einsum(
        "ecf,edf->ecd", grad_pre, w_in_back, preferred_element_type=jnp.float32
    ).reshape(EXPERTS * CAP, model_width)
    grad_normed_two = grad_slots[slot_ids]
    grad_from_norm, grad_gain_two, grad_shift_two = norm_back(
        hidden, gain_two_back.astype(jnp.float32), grad_normed_two
    )
    grad_hidden = grad_output + grad_from_norm
    column_in, column_down = (
        lax.psum_scatter(
            grad_in.astype(jnp.bfloat16), REP, scatter_dimension=2, tiled=True
        ).astype(jnp.float32),
        lax.psum_scatter(
            grad_down.astype(jnp.bfloat16), REP, scatter_dimension=2, tiled=True
        ).astype(jnp.float32),
    )
    share_in, share_down, part_gain_two, part_shift_two, part_in_bias, part_down_bias = (
        lax.psum_scatter(column_in, FSDP, scatter_dimension=1, tiled=True),
        lax.psum_scatter(column_down, FSDP, scatter_dimension=1, tiled=True),
        lax.psum_scatter(grad_gain_two, FSDP, scatter_dimension=0, tiled=True),
        lax.psum_scatter(grad_shift_two, FSDP, scatter_dimension=0, tiled=True),
        lax.psum_scatter(grad_in_bias, FSDP, scatter_dimension=1, tiled=True),
        lax.psum_scatter(grad_down_bias, FSDP, scatter_dimension=1, tiled=True),
    )
    sum_in, sum_down, stack_gain_two, stack_shift_two, stack_in_bias, stack_down_bias = (
        lax.all_gather(share_in.astype(jnp.bfloat16), REP, axis=2, tiled=True).astype(
            share_in.dtype
        ),
        lax.all_gather(share_down.astype(jnp.bfloat16), REP, axis=2, tiled=True).astype(
            share_down.dtype
        ),
        lax.all_gather(part_gain_two[None].astype(jnp.bfloat16), REP, axis=0, tiled=True).astype(
            jnp.float32
        ),
        lax.all_gather(part_shift_two[None].astype(jnp.bfloat16), REP, axis=0, tiled=True).astype(
            jnp.float32
        ),
        lax.all_gather(part_in_bias[None].astype(jnp.bfloat16), REP, axis=0, tiled=True).astype(
            jnp.float32
        ),
        lax.all_gather(part_down_bias[None].astype(jnp.bfloat16), REP, axis=0, tiled=True).astype(
            jnp.float32
        ),
    )
    sum_gain_two = jnp.sum(stack_gain_two, 0)
    sum_shift_two = jnp.sum(stack_shift_two, 0)
    sum_in_bias = jnp.sum(stack_in_bias, 0)
    sum_down_bias = jnp.sum(stack_down_bias, 0)
    gain_one_back, w_query_back, w_key_back, w_value_back, w_out_back = (
        lax.all_gather(norm1_gain, FSDP, axis=0, tiled=True),
        lax.all_gather(query_weight, FSDP, axis=0, tiled=True),
        lax.all_gather(key_weight, FSDP, axis=0, tiled=True),
        lax.all_gather(value_weight, FSDP, axis=0, tiled=True),
        lax.all_gather(out_weight, FSDP, axis=0, tiled=True),
    )
    grad_branch = grad_hidden.astype(jnp.bfloat16)
    grad_out_bias = jnp.sum(grad_branch.astype(jnp.float32), 0)
    grad_out_weight = jnp.einsum(
        "td,te->de", mixed, grad_branch, preferred_element_type=jnp.float32
    )
    grad_mixed = (
        jnp.einsum("te,de->td", grad_branch, w_out_back, preferred_element_type=jnp.float32)
        .astype(jnp.bfloat16)
        .reshape(head_shape)
    )
    scores_again = scores_of(queries, keys_mat)
    probs = jnp.exp(scores_again - log_total)
    probs_again = probs.astype(jnp.bfloat16)
    grad_values = jnp.einsum(
        "rhqk,rqhd->rkhd", probs_again, grad_mixed, preferred_element_type=jnp.float32
    )
    grad_values = grad_values.astype(jnp.bfloat16).reshape(tok_count, model_width)
    grad_probs = jnp.einsum(
        "rqhd,rkhd->rhqk", grad_mixed, values, preferred_element_type=jnp.float32
    )
    grad_scores = (probs * (grad_probs - jnp.sum(grad_probs * probs, -1, keepdims=True))).astype(
        jnp.bfloat16
    )
    grad_queries = (
        (
            jnp.einsum("rhqk,rkhd->rqhd", grad_scores, keys_mat, preferred_element_type=jnp.float32)
            * scale_factor
        )
        .astype(jnp.bfloat16)
        .reshape(tok_count, model_width)
    )
    grad_keys = (
        (
            jnp.einsum("rhqk,rqhd->rkhd", grad_scores, queries, preferred_element_type=jnp.float32)
            * scale_factor
        )
        .astype(jnp.bfloat16)
        .reshape(tok_count, model_width)
    )
    grad_query_bias = jnp.sum(grad_queries.astype(jnp.float32), 0)
    grad_value_bias = jnp.sum(grad_values.astype(jnp.float32), 0)
    grad_query_weight = jnp.einsum(
        "td,te->de", normed_one, grad_queries, preferred_element_type=jnp.float32
    )
    grad_key_weight = jnp.einsum(
        "td,te->de", normed_one, grad_keys, preferred_element_type=jnp.float32
    )
    grad_value_weight = jnp.einsum(
        "td,te->de", normed_one, grad_values, preferred_element_type=jnp.float32
    )
    grad_normed_one = (
        jnp.einsum("te,de->td", grad_queries, w_query_back, preferred_element_type=jnp.float32)
        + jnp.einsum("te,de->td", grad_keys, w_key_back, preferred_element_type=jnp.float32)
        + jnp.einsum("te,de->td", grad_values, w_value_back, preferred_element_type=jnp.float32)
    )
    grad_from_first, grad_gain_one, grad_shift_one = norm_back(
        resid_in, gain_one_back.astype(jnp.float32), grad_normed_one
    )
    input_grad = grad_hidden + grad_from_first
    column_query, column_key, column_value, column_out = (
        lax.psum_scatter(
            grad_query_weight.astype(jnp.bfloat16), REP, scatter_dimension=1, tiled=True
        ).astype(jnp.float32),
        lax.psum_scatter(
            grad_key_weight.astype(jnp.bfloat16), REP, scatter_dimension=1, tiled=True
        ).astype(jnp.float32),
        lax.psum_scatter(
            grad_value_weight.astype(jnp.bfloat16), REP, scatter_dimension=1, tiled=True
        ).astype(jnp.float32),
        lax.psum_scatter(
            grad_out_weight.astype(jnp.bfloat16), REP, scatter_dimension=1, tiled=True
        ).astype(jnp.float32),
    )
    (
        share_query,
        share_key,
        share_value,
        share_out,
        part_gain_one,
        part_shift_one,
        part_query_bias,
        part_value_bias,
        part_out_bias,
    ) = (
        lax.psum_scatter(column_query, FSDP, scatter_dimension=0, tiled=True),
        lax.psum_scatter(column_key, FSDP, scatter_dimension=0, tiled=True),
        lax.psum_scatter(column_value, FSDP, scatter_dimension=0, tiled=True),
        lax.psum_scatter(column_out, FSDP, scatter_dimension=0, tiled=True),
        lax.psum_scatter(grad_gain_one, FSDP, scatter_dimension=0, tiled=True),
        lax.psum_scatter(grad_shift_one, FSDP, scatter_dimension=0, tiled=True),
        lax.psum_scatter(grad_query_bias, FSDP, scatter_dimension=0, tiled=True),
        lax.psum_scatter(grad_value_bias, FSDP, scatter_dimension=0, tiled=True),
        lax.psum_scatter(grad_out_bias, FSDP, scatter_dimension=0, tiled=True),
    )
    (
        sum_query,
        sum_key,
        sum_value,
        sum_out,
        stack_gain_one,
        stack_shift_one,
        stack_query_bias,
        stack_value_bias,
        stack_out_bias,
    ) = (
        lax.all_gather(share_query.astype(jnp.bfloat16), REP, axis=1, tiled=True).astype(
            share_query.dtype
        ),
        lax.all_gather(share_key.astype(jnp.bfloat16), REP, axis=1, tiled=True).astype(
            share_key.dtype
        ),
        lax.all_gather(share_value.astype(jnp.bfloat16), REP, axis=1, tiled=True).astype(
            share_value.dtype
        ),
        lax.all_gather(share_out.astype(jnp.bfloat16), REP, axis=1, tiled=True).astype(
            share_out.dtype
        ),
        lax.all_gather(part_gain_one[None].astype(jnp.bfloat16), REP, axis=0, tiled=True).astype(
            jnp.float32
        ),
        lax.all_gather(part_shift_one[None].astype(jnp.bfloat16), REP, axis=0, tiled=True).astype(
            jnp.float32
        ),
        lax.all_gather(
            part_query_bias[None].astype(jnp.bfloat16), REP, axis=0, tiled=True
        ).astype(jnp.float32),
        lax.all_gather(
            part_value_bias[None].astype(jnp.bfloat16), REP, axis=0, tiled=True
        ).astype(jnp.float32),
        lax.all_gather(part_out_bias[None].astype(jnp.bfloat16), REP, axis=0, tiled=True).astype(
            jnp.float32
        ),
    )
    sum_gain_one = jnp.sum(stack_gain_one, 0)
    sum_shift_one = jnp.sum(stack_shift_one, 0)
    sum_query_bias = jnp.sum(stack_query_bias, 0)
    sum_value_bias = jnp.sum(stack_value_bias, 0)
    sum_out_bias = jnp.sum(stack_out_bias, 0)
    return (
        output,
        input_grad,
        sum_gain_one,
        sum_shift_one,
        sum_query,
        sum_query_bias,
        sum_key,
        sum_value,
        sum_value_bias,
        sum_out,
        sum_out_bias,
        sum_gain_two,
        sum_shift_two,
        sum_in,
        sum_in_bias,
        sum_down,
        sum_down_bias,
    )


LANES = 128
BF = jnp.bfloat16
F32 = jnp.float32
VMEM_BYTES = 60 * 1024 * 1024
SMEM = pl.BlockSpec(memory_space=pltpu.SMEM)
VMEM = pl.BlockSpec(memory_space=pltpu.VMEM)
ANYWHERE = pl.BlockSpec(memory_space=pl.ANY)


def dot_nn(a, b):
    return lax.dot_general(a, b, (((1,), (0,)), ((), ())), preferred_element_type=F32)


def dot_nt(a, b):
    return lax.dot_general(a, b, (((1,), (1,)), ((), ())), preferred_element_type=F32)


def dot_tn(a, b):
    return lax.dot_general(a, b, (((0,), (0,)), ((), ())), preferred_element_type=F32)


def kernel_call(body, named, out_shape, in_specs, out_specs, scratch, args, alias=None):
    return pl.pallas_call(
        body,
        out_shape=out_shape,
        in_specs=in_specs,
        out_specs=out_specs,
        scratch_shapes=scratch,
        input_output_aliases=alias or {},
        compiler_params=pltpu.CompilerParams(vmem_limit_bytes=VMEM_BYTES),
        name=named.__name__,
    )(*args)


def hold(values, done):
    shapes = tuple(jax.ShapeDtypeStruct(v.shape, v.dtype) for v in values)
    return kernel_call(
        lambda *refs: None,
        hold,
        shapes,
        [ANYWHERE] * (len(values) + len(done)),
        (ANYWHERE,) * len(values),
        [],
        (*values, *done),
        {i: i for i in range(len(values))},
    )


def sds(shape, dtype=BF):
    return jax.ShapeDtypeStruct(shape, dtype)


def center(v):
    mean = jnp.mean(v, -1, keepdims=True)
    centred = v - mean
    inverse = lax.rsqrt(jnp.mean(centred * centred, -1, keepdims=True) + EPSILON)
    return centred * inverse, inverse


def norm_grad(normed, inverse, gain, gradient):
    dn = gradient * gain
    return inverse * (
        dn - jnp.mean(dn, -1, keepdims=True) - normed * jnp.mean(dn * normed, -1, keepdims=True)
    )


def exact_rows(place, v):
    high = v.astype(BF)
    rest = (v - high.astype(F32)).astype(BF)
    return dot_tn(place, high) + dot_tn(place, rest)


def segment_bias(starts, length, segs):
    col = lax.broadcasted_iota(jnp.int32, (length, 1), 0)
    row = lax.broadcasted_iota(jnp.int32, (1, length), 1)
    col_seg = jnp.zeros((length, 1), jnp.int32)
    row_seg = jnp.zeros((1, length), jnp.int32)
    for k in range(segs):
        col_seg = col_seg + jnp.where(col >= starts[0, k], 1, 0)
        row_seg = row_seg + jnp.where(row >= starts[0, k], 1, 0)
    return jnp.where(col_seg == row_seg, 0.0, MASKED)


def cuts(layout, start, count):
    found = []
    for i, part, mask, offset, rows in layout:
        low, high = max(offset, start), min(offset + rows, start + count)
        if low < high:
            found.append((i, part, mask, low - offset, low - start, high - low))
    return found


def rows_of(ref, part, row, rows):
    return ref.at[pl.ds(row, rows)] if part is None else ref.at[part, pl.ds(row, rows)]


def load_weight(me, refs, layout, segment, shard, dst, sems):
    copies = []
    for k, (i, part, mask, row, at, rows) in enumerate(cuts(layout, segment * shard, shard)):
        to = pl.multiple_of((me ^ mask) * shard + at, 16)
        src = rows_of(refs[i], part, row, rows)
        copy = pltpu.make_async_copy(src, dst.at[pl.ds(to, rows)], sems.at[k])
        copy.start()
        copies.append(copy)
    return copies


def attention_forward(n, layout, segs, n_vec, *refs):
    count = 1 + max(i for i, *_ in layout)
    me_ref, starts, tokens = refs[:3]
    pieces = refs[3 : 3 + count]
    qkv, mixed, lse, n1_out, vec, b_in = refs[3 + count : 9 + count]
    weights, smalls, v_t, mixed_t, bias, sems, small_sems = refs[9 + count :]
    tok, width = tokens.shape
    shard = width // n
    me = me_ref[0]
    small_copies = []
    for k, (i, part, mask, row, at, rows) in enumerate(cuts(layout, 4 * shard, 16)):
        copy = pltpu.make_async_copy(
            rows_of(pieces[i], part, row, rows),
            smalls.at[mask, pl.ds(at, rows)],
            small_sems.at[k],
        )
        copy.start()
        small_copies.append(copy)
    copies = []
    for i in range(3):
        cols = weights.at[:, pl.ds(i * width, width)]
        copies.append(load_weight(me, pieces, layout, i, shard, cols, sems.at[i]))
    bias[...] = segment_bias(starts, tok, segs)
    normed, _ = center(tokens[...].astype(F32))
    for copy in small_copies:
        copy.wait()
    lane = lax.broadcasted_iota(jnp.int32, (LANES, width), 0)
    col = lax.broadcasted_iota(jnp.int32, (LANES, width), 1)
    total = jnp.zeros((16, width), F32)
    for m in range(n):
        spread = ((col - (me ^ m) * shard == lane) & (lane < shard)).astype(F32).astype(BF)
        total = total + dot_nn(smalls[m, :, :LANES], spread)
    vec[...] = total
    half_ff = width // 2
    mine, other = smalls[0].astype(F32)[:, :half_ff], smalls[1].astype(F32)[:, :half_ff]
    first = me % 2 == 0
    b_in[:, :half_ff] = jnp.where(first, mine, other)
    b_in[:, half_ff:] = jnp.where(first, other, mine)
    n1_out[...] = (normed * vec[0:1, :] + vec[1:2, :]).astype(BF)
    for i in range(3):
        for copy in copies[i]:
            copy.wait()
        part = dot_nn(n1_out[...], weights[:, i * width : (i + 1) * width])
        if i != 1:
            part = part + (vec[2:3, :] if i == 0 else vec[3:4, :])
        part = part.astype(BF)
        if i == 0:
            part = part * jnp.asarray(HEAD**-0.5, BF)
        qkv[:, i * width : (i + 1) * width] = part
    v_t[...] = qkv[:, 2 * width :].T
    half = lax.broadcasted_iota(jnp.int32, (1, LANES), 1) < HEAD

    def pair(p, carry):
        at = pl.multiple_of(p * LANES, LANES)
        q_pair = qkv[:, pl.ds(at, LANES)]
        k_pair = qkv[:, pl.ds(pl.multiple_of(width + p * LANES, LANES), LANES)]
        for s in range(2):
            q_one = jnp.where(half if s == 0 else ~half, q_pair, jnp.zeros_like(q_pair))
            scores = dot_nt(k_pair, q_one) + bias[...]
            top = jnp.max(scores, 0, keepdims=True)
            e = jnp.exp(scores - top)
            total = jnp.sum(e, 0, keepdims=True)
            probs = (e * (1.0 / total)).astype(BF)
            rows = pl.ds(pl.multiple_of(p * LANES + s * HEAD, HEAD), HEAD)
            mixed_t[rows, :] = dot_nn(v_t[rows, :], probs)
            lse[pl.ds(2 * p + s, 1), :] = top + jnp.log(total)
        return carry

    lax.fori_loop(0, width // LANES, pair, 0)
    mixed[...] = mixed_t[...].T.astype(BF)


def call_attention_forward(n, me, starts, tokens, pieces, layout, n_vec):
    tok, width = tokens.shape
    heads16 = (width // HEAD + 7) // 8 * 8
    f32_row = sds((16, width), F32)
    return kernel_call(
        lambda *refs: attention_forward(n, layout, starts.shape[1], n_vec, *refs),
        attention_forward,
        (sds((tok, 3 * width)), sds((tok, width)), sds((heads16, tok), F32), sds((tok, width)))
        + (f32_row, f32_row),
        [SMEM, SMEM, VMEM] + [ANYWHERE] * len(pieces),
        (VMEM,) * 6,
        [
            pltpu.VMEM((width, 3 * width), BF),
            pltpu.VMEM((n, 16, width), BF),
            pltpu.VMEM((width, tok), BF),
            pltpu.VMEM((width, tok), F32),
            pltpu.VMEM((tok, tok), F32),
            pltpu.SemaphoreType.DMA((3, len(layout))),
            pltpu.SemaphoreType.DMA((len(layout),)),
        ],
        (me, starts, tokens, *pieces),
    )


def head_grads(first, pairs, width, qkv, lse, g_mixed, bias, k_t, gq_t, g_qkv):
    half = lax.broadcasted_iota(jnp.int32, (1, LANES), 1) < HEAD
    span = pairs * LANES

    def pair(p, carry):
        def cols(part):
            return pl.ds(pl.multiple_of(part * width + (first + p) * LANES, LANES), LANES)

        def put(part):
            return pl.ds(pl.multiple_of(part * span + p * LANES, LANES), LANES)

        q_pair, k_pair, v_pair = qkv[:, cols(0)], qkv[:, cols(1)], qkv[:, cols(2)]
        gm_pair = g_mixed[:, cols(0)]
        gv, gk = [], []
        for s in range(2):
            own = half if s == 0 else ~half
            q_one = jnp.where(own, q_pair, jnp.zeros_like(q_pair))
            gm_one = jnp.where(own, gm_pair, jnp.zeros_like(gm_pair))
            scores = dot_nt(k_pair, q_one) + bias[...]
            probs = jnp.exp(scores - lse[pl.ds(2 * (first + p) + s, 1), :])
            g_probs = dot_nt(v_pair, gm_one)
            delta = jnp.sum(probs * g_probs, 0, keepdims=True)
            g_scores = (probs * (g_probs - delta)).astype(BF)
            gv.append(dot_nn(probs.astype(BF), gm_pair))
            gk.append(dot_nn(g_scores, q_pair))
            rows = pl.ds(pl.multiple_of(p * LANES + s * HEAD, HEAD), HEAD)
            gq_t[rows, :] = dot_nn(k_t[rows, :], g_scores)
        g_qkv[:, put(2)] = jnp.where(half, gv[0], gv[1]).astype(BF)
        g_qkv[:, put(1)] = jnp.where(half, gk[0], gk[1]).astype(BF)
        return carry

    at = slice(width + first * LANES, width + first * LANES + span)
    k_t[...] = qkv[:, at].T
    lax.fori_loop(0, pairs, pair, 0)
    g_qkv[:, :span] = (gq_t[...].T * (HEAD**-0.5)).astype(BF)


def share_rows(n, me, shard, whole, keep, send, sems):
    outs = []
    core = me % 2
    for k in range(n // 2):
        for i, dst in enumerate((keep, send)):
            owner = 2 * k + (core if i == 0 else 1 - core)
            src = whole.at[pl.ds(pl.multiple_of(owner * shard, 16), shard)]
            copy = pltpu.make_async_copy(src, dst.at[k], sems.at[2 * k + i])
            copy.start()
            outs.append(copy)
    return outs


def attention_backward_one(n, segs, pairs, deps, *refs):
    me_ref, starts, qkv, lse, n1, g_mixed, g_out = refs[:7]
    g_qkv, keep, send = refs[7 + deps : 10 + deps]
    k_t, gq_t, bias, g_w, out_sems = refs[10 + deps :]
    tok, width = n1.shape
    span = pairs * LANES
    bias[...] = segment_bias(starts, tok, segs)
    head_grads(0, pairs, width, qkv, lse, g_mixed, bias, k_t, gq_t, g_qkv)
    g_w[:, :width] = g_out[...]
    for i in range(3):
        part = dot_tn(n1[...], g_qkv[:, i * span : (i + 1) * span])
        g_w[:, width + i * span : width + (i + 1) * span] = part.astype(BF)
    for copy in share_rows(n, me_ref[0], width // n, g_w, keep, send, out_sems):
        copy.wait()


def call_attention_backward_one(n, me, starts, qkv, lse, n1, g_mixed, g_out, pairs, deps=()):
    tok, width = n1.shape
    shard, span = width // n, pairs * LANES
    cols = width + 3 * span
    return kernel_call(
        lambda *refs: attention_backward_one(n, starts.shape[1], pairs, len(deps), *refs),
        attention_backward_one,
        (sds((tok, 3 * span)),) + (sds((n // 2, shard, cols)),) * 2,
        [SMEM, SMEM] + [VMEM] * 5 + [ANYWHERE] * len(deps),
        (VMEM, ANYWHERE, ANYWHERE),
        [
            pltpu.VMEM((span, tok), BF),
            pltpu.VMEM((span, tok), F32),
            pltpu.VMEM((tok, tok), F32),
            pltpu.VMEM((width, cols), BF),
            pltpu.SemaphoreType.DMA((n,)),
        ],
        (me, starts, qkv, lse, n1, g_mixed, g_out, *deps),
    )


def attention_backward_two(n, layout, segs, n_vec, first, deps, *refs):
    count = 1 + max(i for i, *_ in layout)
    me_ref, starts, tokens, vec, vec_grads, qkv, lse, n1, g_mixed, g_hidden, g_first = refs[:11]
    pieces = refs[11 : 11 + count]
    at = 11 + count + deps
    input_grad, keep, send = refs[at : at + 3]
    weights, k_t, gq_t, bias, g_qkv, g_w, v_rows, sems, out_sems = refs[at + 3 :]
    tok, width = tokens.shape
    shard = width // n
    span_one = first * LANES
    span = width - span_one
    me = me_ref[0]
    copies = []
    for i in range(3):
        cols = weights.at[:, pl.ds(i * width, width)]
        copies += load_weight(me, pieces, layout, i, shard, cols, sems.at[i])
    bias[...] = segment_bias(starts, tok, segs)
    head_grads(first, span // LANES, width, qkv, lse, g_mixed, bias, k_t, gq_t, g_qkv)
    for i in range(3):
        cols = slice(i * span, (i + 1) * span)
        g_w[:, cols] = dot_tn(n1[...], g_qkv[:, cols]).astype(BF)
    for copy in copies:
        copy.wait()
    g_n1 = jnp.zeros((tok, width), F32)
    for i in range(3):
        one = slice(i * width, i * width + span_one)
        two = slice(i * width + span_one, (i + 1) * width)
        g_n1 = g_n1 + dot_nt(g_first[:, i * span_one : (i + 1) * span_one], weights[:, one])
        g_n1 = g_n1 + dot_nt(g_qkv[:, i * span : (i + 1) * span], weights[:, two])
    normed, inverse = center(tokens[...].astype(F32))
    input_grad[...] = g_hidden[...] + norm_grad(normed, inverse, vec[0:1, :], g_n1)
    v_rows[...] = jnp.zeros_like(v_rows)
    v_rows[0:1, :] = jnp.sum(g_n1 * normed, 0, keepdims=True)
    v_rows[1:2, :] = jnp.sum(g_n1, 0, keepdims=True)
    for row, i in ((2, 0), (3, 2)):
        one = g_first[:, i * span_one : (i + 1) * span_one].astype(F32)
        two = g_qkv[:, i * span : (i + 1) * span].astype(F32)
        v_rows[row : row + 1, :span_one] = jnp.sum(one, 0, keepdims=True)
        v_rows[row : row + 1, span_one:] = jnp.sum(two, 0, keepdims=True)
    v_rows[4:n_vec, :] = vec_grads[4:n_vec, :]
    g_w[:, 3 * span :] = v_rows[...].T.astype(BF)
    for copy in share_rows(n, me, shard, g_w, keep, send, out_sems):
        copy.wait()


def call_attention_backward_two(
    n,
    me,
    starts,
    tokens,
    vec,
    vec_grads,
    qkv,
    lse,
    n1,
    g_mixed,
    g_hidden,
    g_first,
    pieces,
    layout,
    n_vec,
    first,
    deps=(),
):
    tok, width = tokens.shape
    shard, span = width // n, width - first * LANES
    cols = 3 * span + LANES
    return kernel_call(
        lambda *refs: attention_backward_two(
            n, layout, starts.shape[1], n_vec, first, len(deps), *refs
        ),
        attention_backward_two,
        (sds((tok, width), F32),) + (sds((n // 2, shard, cols)),) * 2,
        [SMEM, SMEM] + [VMEM] * 9 + [ANYWHERE] * (len(pieces) + len(deps)),
        (VMEM, ANYWHERE, ANYWHERE),
        [
            pltpu.VMEM((width, 3 * width), BF),
            pltpu.VMEM((span, tok), BF),
            pltpu.VMEM((span, tok), F32),
            pltpu.VMEM((tok, tok), F32),
            pltpu.VMEM((tok, 3 * span), BF),
            pltpu.VMEM((width, cols), BF),
            pltpu.VMEM((LANES, width), F32),
            pltpu.SemaphoreType.DMA((3, len(layout))),
            pltpu.SemaphoreType.DMA((n,)),
        ],
        (
            me,
            starts,
            tokens,
            vec,
            vec_grads,
            qkv,
            lse,
            n1,
            g_mixed,
            g_hidden,
            g_first,
            *pieces,
            *deps,
        ),
    )


def place_rows(position, slots):
    row = lax.broadcasted_iota(jnp.int32, (slots, position.shape[1]), 0)
    return (row == position[...]).astype(F32).astype(BF)


def member_rows(route, first):
    row = lax.broadcasted_iota(jnp.int32, (16, route.shape[1]), 0)
    return (row == route[...] + first).astype(F32).astype(BF)


def mix_out(n, layout, slots, deps, *refs):
    count = 1 + max(i for i, *_ in layout)
    me_ref, mixed, tokens, vec, position = refs[:5]
    pieces = refs[5 : 5 + count]
    hidden, sorted_two, weights, sems = refs[5 + count + deps :]
    width = tokens.shape[1]
    copies = load_weight(me_ref[0], pieces, layout, 3, width // n, weights, sems)
    place = place_rows(position, slots)
    for copy in copies:
        copy.wait()
    value = tokens[...].astype(F32) + dot_nn(mixed[...], weights[...]) + vec[4:5, :]
    hidden[...] = value
    normed, _ = center(value)
    sorted_two[...] = dot_nn(place, (normed * vec[5:6, :] + vec[6:7, :]).astype(BF)).astype(BF)


def call_mix_out(n, me, mixed, tokens, vec, position, slots, pieces, layout, deps=()):
    tok, width = tokens.shape
    return kernel_call(
        lambda *refs: mix_out(n, layout, slots, len(deps), *refs),
        mix_out,
        (sds((tok, width), F32), sds((slots, width))),
        [SMEM] + [VMEM] * 4 + [ANYWHERE] * (len(pieces) + len(deps)),
        (VMEM, VMEM),
        [pltpu.VMEM((width, width), BF), pltpu.SemaphoreType.DMA((len(layout),))],
        (me, mixed, tokens, vec, position, *pieces, *deps),
    )


def pack(count, *refs):
    weights = refs[:count]
    vectors, down_bias, in_bias, out, small = refs[count:]
    rows = weights[0].shape[0]
    for i, ref in enumerate(weights):
        out[i * rows : (i + 1) * rows, :] = ref[...]
    small[...] = jnp.zeros_like(small)
    n_vec = vectors.shape[0]
    small[:n_vec, :rows] = vectors[...].astype(F32)
    small[n_vec : n_vec + EXPERTS, :rows] = down_bias[...].astype(F32)
    small[n_vec + EXPERTS : n_vec + 2 * EXPERTS, : in_bias.shape[1]] = in_bias[...].astype(F32)
    out[count * rows :, :] = small[...].astype(BF)


def call_pack(weights, vectors, down_bias, in_bias):
    rows, width = weights[0].shape
    return kernel_call(
        lambda *refs: pack(len(weights), *refs),
        pack,
        sds((len(weights) * rows + 16, width)),
        [VMEM] * (len(weights) + 3),
        VMEM,
        [pltpu.VMEM((16, width), F32)],
        (*weights, vectors, down_bias, in_bias),
    )


def load_blocks(refs, layout, dst, sems):
    copies = []
    for i, (ref, (block, offset, rows, row)) in enumerate(zip(refs, layout, strict=True)):
        copy = pltpu.make_async_copy(
            ref.at[pl.ds(row, rows)], dst.at[block, pl.ds(offset, rows)], sems.at[i]
        )
        copy.start()
        copies.append(copy)
    return copies


def start_all(copies):
    for copy in copies:
        copy.start()
    return copies


def wait_all(copies):
    for copy in copies:
        copy.wait()


def window(meta, block, e):
    begin = pl.multiple_of(meta[block, 3 * e], 16)
    row = lax.broadcasted_iota(jnp.int32, (CAP, 1), 0)
    return pl.ds(begin, CAP), (row >= meta[block, 3 * e + 1]) & (row < meta[block, 3 * e + 2])


def experts(chips, bias_row, lay_x, lay_g, deps, *refs):
    nb, cx, cg, cw = len(chips), len(lay_x), len(lay_g), 2
    me_ref, meta, b_in = refs[:3]
    at = 3
    x_refs, at = refs[at : at + cx], at + cx
    g_refs, at = refs[at : at + cg], at + cg
    w_refs, at = refs[at : at + cw], at + cw
    down = refs[at : at + 2]
    at += 2 + deps
    dsl, (res, act_out, dp_out) = refs[at : at + nb], refs[at + nb : at + nb + 3]
    at += nb + 3
    x_all, g_all, w_in, w_down, res_s, dsl_s, xs, gs, act_s, dp_s = refs[at : at + 10]
    sx, sg, sw, sd, so, sa = refs[at + 10 :]
    rows = w_refs[0].shape[2]
    me = me_ref[0]
    half = w_down.shape[1] // 2
    core = me % 2
    loads = load_blocks(x_refs, lay_x, x_all, sx) + load_blocks(g_refs, lay_g, g_all, sg)
    weights = []
    for e in range(EXPERTS):
        copies = []
        for i, ref in enumerate(w_refs):
            for k in range(ref.shape[0]):
                owner = 2 * k + (core if i == 0 else 1 - core)
                to = pl.ds(pl.multiple_of(owner * rows, 16), rows)
                copies.append(pltpu.make_async_copy(ref.at[k, e], w_in.at[e, to], sw.at[e, i, k]))
        for i, ref in enumerate(down):
            to = pl.multiple_of((core if i == 0 else 1 - core) * half, 16)
            copies.append(pltpu.make_async_copy(ref.at[e], w_down.at[e, pl.ds(to, half)], sd.at[e, i]))
        weights.append(start_all(copies))
    res_s[...] = jnp.zeros_like(res_s)
    dsl_s[...] = jnp.zeros_like(dsl_s)
    wait_all(loads)
    outs = []
    for e in range(EXPERTS):
        spans = []
        for b in range(nb):
            span, inside = window(meta, b, e)
            spans.append((span, inside))
            g = g_all[b, span, :]
            xs[b * CAP : (b + 1) * CAP, :] = x_all[b, span, :]
            gs[b * CAP : (b + 1) * CAP, :] = jnp.where(inside, g, jnp.zeros_like(g))
        wait_all(weights[e])
        pre = dot_nn(xs[...], w_in[e]) + b_in[bias_row + e : bias_row + e + 1, :]
        cdf = 0.5 * (1.0 + lax.erf(pre * 0.7071067811865476))
        act = (pre * cdf).astype(BF)
        slope = cdf + pre * jnp.exp(-0.5 * pre * pre) * 0.3989422804014327
        dp = (dot_nt(gs[...], w_down[e]) * slope).astype(BF)
        act_s[e] = act
        dp_s[e] = dp
        outs += start_all(
            [
                pltpu.make_async_copy(act_s.at[e], act_out.at[e], sa.at[0, e]),
                pltpu.make_async_copy(dp_s.at[e], dp_out.at[e], sa.at[1, e]),
            ]
        )
        for dst, value in ((dsl_s, dot_nt(dp, w_in[e])), (res_s, dot_nn(act, w_down[e]))):
            value = value.astype(BF)
            for b, (span, inside) in enumerate(spans):
                dst[b, span, :] = jnp.where(inside, value[b * CAP : (b + 1) * CAP], dst[b, span, :])
    for b in range(nb):
        outs += start_all(
            [
                pltpu.make_async_copy(dsl_s.at[b], dsl[b], so.at[0, b]),
                pltpu.make_async_copy(res_s.at[b], res.at[(me // 2) ^ chips[b]], so.at[1, b]),
            ]
        )
    wait_all(outs)


def call_experts(chips, bias_row, me, meta, b_in, xp, lay_x, gp, lay_g, wp, down, res, blocks):
    nb, rows, width = len(chips), max(o + r for _, o, r, _ in lay_x), xp[0].shape[1]
    ff = 2 * down[0].shape[1]
    dma = pltpu.SemaphoreType.DMA
    deps = () if res is None else (res,)
    alias = {} if res is None else {5 + len(xp) + len(gp) + len(wp): nb}
    out = kernel_call(
        lambda *refs: experts(chips, bias_row, lay_x, lay_g, len(deps), *refs),
        experts,
        (sds((rows, width)),) * nb
        + (sds((blocks, rows, width)),)
        + (sds((EXPERTS, nb * CAP, ff)),) * 2,
        [SMEM, SMEM, VMEM] + [ANYWHERE] * (len(xp) + len(gp) + len(wp) + 2 + len(deps)),
        (ANYWHERE,) * (nb + 3),
        [pltpu.VMEM((nb, rows, width), BF)] * 2
        + [pltpu.VMEM((EXPERTS, width, ff), BF), pltpu.VMEM((EXPERTS, ff, width), BF)]
        + [pltpu.VMEM((nb, rows, width), BF)] * 2
        + [pltpu.VMEM((nb * CAP, width), BF)] * 2
        + [pltpu.VMEM((EXPERTS, nb * CAP, ff), BF)] * 2
        + [dma((len(xp),)), dma((len(gp),)), dma((EXPERTS, 2, blocks)), dma((EXPERTS, 2))]
        + [dma((2, nb)), dma((2, EXPERTS))],
        (me, meta, b_in, *xp, *gp, *wp, *down, *deps),
        alias,
    )
    return list(out[:nb]), out[nb], out[nb + 1], out[nb + 2]


def down_grads(calls, lay_g, deps, *refs):
    cg, cc = len(lay_g), len(calls)
    me_ref, meta = refs[:2]
    g_refs, acts = refs[2 : 2 + cg], refs[2 + cg : 2 + cg + cc]
    at = 2 + cg + cc + deps
    keep, send = refs[at], refs[at + 1 : at + 1 + EXPERTS]
    g_all, act_s, gs, g_down, sg, sa, so = refs[at + 1 + EXPERTS :]
    core = me_ref[0] % 2
    half = g_down.shape[1] // 2
    loads = load_blocks(g_refs, lay_g, g_all, sg)
    hidden = load_hidden(acts, calls, act_s, sa)
    wait_all(loads)
    outs = []
    for e in range(EXPERTS):
        for b in range(sum(calls)):
            span, inside = window(meta, b, e)
            g = g_all[b, span, :]
            gs[b * CAP : (b + 1) * CAP, :] = jnp.where(inside, g, jnp.zeros_like(g))
        wait_all(hidden[e])
        g_down[e] = dot_tn(act_s[e], gs[...]).astype(BF)
        for i, dst in enumerate((keep.at[e], send[e])):
            src = g_down.at[e, pl.ds(pl.multiple_of((core if i == 0 else 1 - core) * half, 16), half)]
            outs.append(pltpu.make_async_copy(src, dst, so.at[e, i]))
            outs[-1].start()
    wait_all(outs)


def load_hidden(parts, calls, dst, sems):
    hidden = []
    for e in range(EXPERTS):
        copies, first = [], 0
        for i, nb in enumerate(calls):
            rows = pl.ds(first * CAP, nb * CAP)
            copies.append(pltpu.make_async_copy(parts[i].at[e], dst.at[e, rows], sems.at[e, i]))
            first += nb
        hidden.append(start_all(copies))
    return hidden


def call_down_grads(me, meta, gp, lay_g, acts, calls, deps=()):
    rows, width = max(o + r for _, o, r, _ in lay_g), gp[0].shape[1]
    ff, blocks = acts[0].shape[2], sum(calls)
    dma = pltpu.SemaphoreType.DMA
    return kernel_call(
        lambda *refs: down_grads(calls, lay_g, len(deps), *refs),
        down_grads,
        (sds((EXPERTS, ff // 2, width)),) + (sds((ff // 2, width)),) * EXPERTS,
        [SMEM, SMEM] + [ANYWHERE] * (len(gp) + len(acts) + len(deps)),
        (ANYWHERE,) * (1 + EXPERTS),
        [
            pltpu.VMEM((blocks, rows, width), BF),
            pltpu.VMEM((EXPERTS, blocks * CAP, ff), BF),
            pltpu.VMEM((blocks * CAP, width), BF),
            pltpu.VMEM((EXPERTS, ff, width), BF),
            dma((len(gp),)),
            dma((EXPERTS, len(calls))),
            dma((EXPERTS, 2)),
        ],
        (me, meta, *gp, *acts, *deps),
    )


def in_grads(n, calls, lay_x, deps, *refs):
    cx, cc = len(lay_x), len(calls)
    me_ref, meta = refs[:2]
    x_refs, dps = refs[2 : 2 + cx], refs[2 + cx : 2 + cx + cc]
    at = 2 + cx + cc + deps
    keep, bias_keep, bias_send = refs[at : at + 3]
    send = refs[at + 3 : at + 3 + EXPERTS]
    x_all, dp_s, xs, g_in, sx, sp, so = refs[at + 3 + EXPERTS :]
    me = me_ref[0]
    _, width, ff = g_in.shape
    shard, half = width // n, ff // 2
    loads = load_blocks(x_refs, lay_x, x_all, sx)
    hidden = load_hidden(dps, calls, dp_s, sp)
    wait_all(loads)
    outs = []
    row = lax.broadcasted_iota(jnp.int32, (16, 1), 0)
    low = jnp.zeros((16, half), F32)
    high = jnp.zeros((16, half), F32)
    for e in range(EXPERTS):
        for b in range(sum(calls)):
            span, _ = window(meta, b, e)
            xs[b * CAP : (b + 1) * CAP, :] = x_all[b, span, :]
        wait_all(hidden[e])
        g_in[e] = dot_tn(xs[...], dp_s[e]).astype(BF)
        outs += share_rows(n, me, shard, g_in.at[e], keep.at[:, e], send[e], so.at[e])
        total = jnp.sum(dp_s[e].astype(F32), 0, keepdims=True)
        low = low + jnp.where(row == e, total[:, :half], 0.0)
        high = high + jnp.where(row == e, total[:, half:], 0.0)
    first_core = me % 2 == 0
    bias_keep[...] = jnp.where(first_core, low, high).astype(BF)
    bias_send[...] = jnp.where(first_core, high, low).astype(BF)
    wait_all(outs)


def call_in_grads(n, me, meta, xp, lay_x, dps, calls, deps=()):
    rows, width = max(o + r for _, o, r, _ in lay_x), xp[0].shape[1]
    ff, blocks = dps[0].shape[2], sum(calls)
    dma = pltpu.SemaphoreType.DMA
    return kernel_call(
        lambda *refs: in_grads(n, calls, lay_x, len(deps), *refs),
        in_grads,
        (sds((n // 2, EXPERTS, width // n, ff)),)
        + (sds((16, ff // 2)),) * 2
        + (sds((n // 2, width // n, ff)),) * EXPERTS,
        [SMEM, SMEM] + [ANYWHERE] * (len(xp) + len(dps) + len(deps)),
        (ANYWHERE, VMEM, VMEM) + (ANYWHERE,) * EXPERTS,
        [
            pltpu.VMEM((blocks, rows, width), BF),
            pltpu.VMEM((EXPERTS, blocks * CAP, ff), BF),
            pltpu.VMEM((blocks * CAP, width), BF),
            pltpu.VMEM((EXPERTS, width, ff), BF),
            dma((len(xp),)),
            dma((EXPERTS, len(calls))),
            dma((EXPERTS, n)),
        ],
        (me, meta, *xp, *dps, *deps),
    )


def mix_out_backward(n, layout, terms, deps, *refs):
    count = 1 + max(i for i, *_ in layout)
    me_ref, position, route, hidden, cot, vec, mixed = refs[:7]
    got = refs[7 : 7 + terms]
    pieces = refs[7 + terms : 7 + terms + count]
    at = 7 + terms + count + deps
    g_hidden, g_mixed, vec_grads, g_w = refs[at : at + 4]
    weights, sems = refs[at + 4 :]
    me = me_ref[0]
    tok, width = hidden.shape
    shard = width // n
    copies = load_weight(me, pieces, layout, 3, shard, weights, sems)
    total = got[0][...].astype(F32)
    for ref in got[1:]:
        total = total + ref[...].astype(F32)
    gradient = exact_rows(place_rows(position, total.shape[0]), total)
    normed, inverse = center(hidden[...])
    value = cot[...].astype(F32) + norm_grad(normed, inverse, vec[5:6, :], gradient)
    g_hidden[...] = value
    branch = value.astype(BF)
    vec_grads[...] = jnp.zeros_like(vec_grads)
    vec_grads[4:5, :] = jnp.sum(branch.astype(F32), 0, keepdims=True)
    vec_grads[5:6, :] = jnp.sum(gradient * normed, 0, keepdims=True)
    vec_grads[6:7, :] = jnp.sum(gradient, 0, keepdims=True)
    vec_grads[...] += dot_nn(member_rows(route, 7), cot[...])
    for copy in copies:
        copy.wait()
    g_mixed[...] = dot_nt(branch, weights[...]).astype(BF)
    g_w[...] = dot_tn(mixed[...], branch).astype(BF)


def call_mix_out_backward(
    n, me, position, route, hidden, cot, vec, mixed, got, pieces, layout, deps=()
):
    tok, width = hidden.shape
    return kernel_call(
        lambda *refs: mix_out_backward(n, layout, len(got), len(deps), *refs),
        mix_out_backward,
        (sds((tok, width), F32), sds((tok, width)), sds((16, width), F32), sds((width, width))),
        [SMEM] + [VMEM] * (6 + len(got)) + [ANYWHERE] * (len(pieces) + len(deps)),
        (VMEM,) * 4,
        [pltpu.VMEM((width, width), BF), pltpu.SemaphoreType.DMA((len(layout),))],
        (me, position, route, hidden, cot, vec, mixed, *got, *pieces, *deps),
    )


def finish_output(deps, *refs):
    position, hidden, route, vec = refs[:4]
    got = refs[4]
    out = refs[5 + deps]
    value = hidden[...] + dot_tn(place_rows(position, got.shape[0]), got[...])
    value = value + dot_tn(member_rows(route, 7), vec[...].astype(BF))
    out[...] = value.astype(BF)


def call_finish_output(position, hidden, route, vec, got, deps=()):
    return kernel_call(
        lambda *refs: finish_output(len(deps), *refs),
        finish_output,
        sds(hidden.shape),
        [VMEM] * 5 + [ANYWHERE] * len(deps),
        VMEM,
        [],
        (position, hidden, route, vec, got, *deps),
    )


def join(body, named, outs, scalars, arrays, deps=()):
    n_s, n_a, n_d, n_o = len(scalars), len(arrays), len(deps), len(outs)

    def kernel(*refs):
        at = n_s + n_a + n_d
        body(refs[:n_s], refs[n_s : n_s + n_a], refs[at : at + n_o])

    return kernel_call(
        kernel,
        named,
        tuple(outs),
        [SMEM] * n_s + [VMEM] * n_a + [ANYWHERE] * n_d,
        (VMEM,) * n_o,
        [],
        (*scalars, *arrays, *deps),
    )


def plus(*values):
    total = values[0].astype(F32)
    for value in values[1:]:
        total = total + value.astype(F32)
    return total


def call_halves(own, along, across, deps=()):
    rows, width = along.shape
    half = rows // 32 * 16

    def body(_, ins, outs):
        outs[0][...] = ins[1][:half]
        outs[1][...] = ins[2][half:]
        for i in range(3):
            outs[2][i] = ins[i][...]

    shapes = (sds((half, width)), sds((rows - half, width)), sds((3, rows, width)))
    return join(body, call_halves, shapes, (), (own, along, across), deps)


def call_two_halves(first, second, deps=()):
    cuts_at = [pair[0].shape[0] // 32 * 16 for pair in (first, second)]
    width = first[0].shape[1]
    split = cuts_at[0]

    def body(_, ins, outs):
        outs[0][:split] = ins[0][:split]
        outs[0][split:] = ins[2][: cuts_at[1]]
        rest = ins[0].shape[0] - split
        outs[1][:rest] = ins[1][split:]
        outs[1][rest:] = ins[3][cuts_at[1] :]

    rows = first[0].shape[0] + second[0].shape[0]
    shapes = (sds((sum(cuts_at), width)), sds((rows - sum(cuts_at), width)))
    return join(body, call_two_halves, shapes, (), (*first, *second), deps)


def call_columns_and_sort(n, whole, position, slots, value, meta, deps):
    experts_, rows, cols = whole.shape
    pair = cols // (n // 2)

    def body(_, ins, outs):
        for k in range(n // 2):
            outs[0][k] = ins[0][:, :, k * pair : (k + 1) * pair]
        outs[1][:slots, :] = dot_nn(place_rows(ins[1], slots), ins[2][...]).astype(BF)
        outs[1][slots:, :] = jnp.zeros((16, value.shape[1]), BF)
        outs[1][slots:, :LANES] = jnp.broadcast_to(ins[3][...], (16, LANES)).astype(BF)

    shapes = (sds((n // 2, experts_, rows, pair)), sds((slots + 16, value.shape[1])))
    return join(body, call_columns_and_sort, shapes, (), (whole, position, value, meta), deps)


def call_pair_down(kept, keep, got, deps=()):
    experts_, rows, width = keep.shape
    half = rows // 2

    def body(scalars, ins, outs):
        mine = pl.multiple_of(scalars[0][0] * half, 16)
        other = pl.multiple_of((1 - scalars[0][0]) * half, 16)
        for out, at in zip(outs, (mine, other), strict=True):
            for e in range(experts_):
                part = plus(ins[0][e, pl.ds(at, half)], ins[1 + e][pl.ds(at, half)])
                out[e] = part.astype(BF)

    shapes = (sds((experts_, half, width)),) * 2
    return join(body, call_pair_down, shapes, (kept,), (keep, *got), deps)


def call_pair_in(keep, got, bias_keep, bias_got, d_keep, d_got, cut, deps=()):
    count = len(got)

    def body(_, ins, outs):
        for e in range(count):
            outs[0][:, e] = plus(ins[0][:, e], ins[5 + e][...]).astype(BF)
        outs[1][...] = plus(ins[1][...], ins[2][...]).astype(BF)
        outs[2][...] = plus(ins[3][:cut], ins[4][:cut]).astype(BF)
        outs[3][...] = plus(ins[3][cut:], ins[4][cut:]).astype(BF)

    shapes = (sds(keep.shape), sds(bias_keep.shape))
    shapes += (sds((cut, *d_keep.shape[1:])), sds((d_keep.shape[0] - cut, *d_keep.shape[1:])))
    arrays = (keep, bias_keep, bias_got, d_keep, d_got, *got)
    return join(body, call_pair_in, shapes, (), arrays, deps)


def call_split_rows(kept, whole, deps=()):
    chips, experts_, rows, ff = whole.shape
    half = rows // 2
    two = chips // 2

    def body(scalars, ins, outs):
        outs[0][...] = ins[0][:, :, pl.ds(pl.multiple_of(scalars[0][0] * half, 16), half)]
        other = pl.ds(pl.multiple_of((1 - scalars[0][0]) * half, 16), half)
        for i in range(2):
            outs[1 + i][...] = ins[0][i * two : (i + 1) * two, :, other]

    shapes = (sds((chips, experts_, half, ff)),) + (sds((two, experts_, half, ff)),) * 2
    return join(body, call_split_rows, shapes, (kept,), (whole,), deps)


def call_pair_shares(one, two, deps=()):
    chips, rows, cols_one = one[0].shape
    cols = cols_one + two[0].shape[2]

    def body(_, ins, outs):
        outs[0][:, :, :cols_one] = plus(ins[0][...], ins[1][...]).astype(BF)
        outs[0][:, :, cols_one:] = plus(ins[2][...], ins[3][...]).astype(BF)

    return join(body, call_pair_shares, (sds((chips, rows, cols)),), (), (*one, *two), deps)[0]


def call_line_sums(parts, across, i_keep, i_got, deps=()):
    cut = parts[0].shape[0]
    rest = parts[1].shape[0]
    two = i_got[0].shape[0]

    def body(_, ins, outs):
        outs[0][:cut] = plus(ins[0][...], ins[2][...]).astype(BF)
        outs[0][cut:] = plus(ins[1][...], ins[3][...]).astype(BF)
        for i in range(2):
            at = slice(i * two, (i + 1) * two)
            outs[1][at] = plus(ins[4][at], ins[5 + i][...]).astype(BF)

    shapes = (sds((cut + rest, *parts[0].shape[1:])), sds(i_keep.shape))
    return join(body, call_line_sums, shapes, (), (*parts, *across, i_keep, *i_got), deps)


def call_sums(jobs, deps=()):
    flat = [v for job in jobs for v in job]

    def body(_, ins, outs):
        at = 0
        for job, out in zip(jobs, outs, strict=True):
            out[...] = plus(*[ref[...] for ref in ins[at : at + len(job)]]).astype(BF)
            at += len(job)

    return join(body, call_sums, [sds(job[0].shape) for job in jobs], (), flat, deps)


def call_attention_shares(kept, got, bias, deps=()):
    chips, rows, cols = got.shape
    half = rows // 2

    def body(scalars, ins, outs):
        mine = pl.multiple_of(scalars[0][0] * half, 16)
        other = pl.multiple_of((1 - scalars[0][0]) * half, 16)
        for out, at in zip(outs, (mine, other), strict=True):
            out[:half, :] = plus(*[ins[0][k, pl.ds(at, half)] for k in range(chips)]).astype(BF)
            out[half:, :] = jnp.zeros((16, cols), BF)
            out[half:, : bias.shape[1]] = ins[1][...]

    shapes = (sds((half + 16, cols)),) * 2
    return join(body, call_attention_shares, shapes, (kept,), (got, bias), deps)


def call_down_result(kept, mine, got, deps=()):
    experts_, half, width = mine.shape

    def body(scalars, ins, outs):
        outs[0][:, pl.ds(pl.multiple_of(scalars[0][0] * half, 16), half)] = ins[0][...].astype(F32)
        at = pl.multiple_of((1 - scalars[0][0]) * half, 16)
        outs[0][:, pl.ds(at, half)] = ins[1][...].astype(F32)

    shape = (sds((experts_, 2 * half, width), F32),)
    return join(body, call_down_result, shape, (kept,), (mine, got), deps)[0]


def call_in_result(kept, mine, got, deps=()):
    chips, experts_, half, ff = mine.shape

    def body(scalars, ins, outs):
        for ref, which in ((ins[0], scalars[0][0]), (ins[1], 1 - scalars[0][0])):
            rows = pl.ds(pl.multiple_of(which * half, 16), half)
            for k in range(chips):
                outs[0][:, rows, k * ff : (k + 1) * ff] = ref[k].astype(F32)

    shape = (sds((experts_, 2 * half, chips * ff), F32),)
    return join(body, call_in_result, shape, (kept,), (mine, got), deps)[0]


def call_attention_result(kept, mine, got, width, span, n_vec, ff_shard, deps=()):
    half = mine.shape[0] - 16
    last = width - span
    cols_one = width + 3 * span

    def body(scalars, ins, outs):
        for ref, which in ((ins[0], scalars[0][0]), (ins[1], 1 - scalars[0][0])):
            rows = pl.ds(pl.multiple_of(which * half, 16), half)
            outs[0][rows, :] = ref[:half, :width].astype(F32)
            for i in range(3):
                one = ref[:half, width + i * span : width + (i + 1) * span]
                two = ref[:half, cols_one + i * last : cols_one + (i + 1) * last]
                outs[1 + i][rows, :span] = one.astype(F32)
                outs[1 + i][rows, span:] = two.astype(F32)
            outs[4][rows, :] = ref[:half, cols_one + 3 * last :].astype(F32)
        rows = outs[4][...].T
        outs[5][...] = ins[0][half : half + EXPERTS, :ff_shard].astype(F32)
        outs[6][...] = rows[n_vec - EXPERTS : n_vec]
        for i, out in enumerate(outs[7:]):
            out[...] = rows[i : i + 1]

    shapes = (sds((2 * half, width), F32),) * 4 + (sds((2 * half, LANES), F32),)
    shapes += (sds((EXPERTS, ff_shard), F32), sds((EXPERTS, 2 * half), F32))
    shapes += (sds((1, 2 * half), F32),) * (n_vec - EXPERTS)
    return join(body, call_attention_result, shapes, (kept,), (mine, got), deps)


def swap(v, n, mask):
    return lax.ppermute(v, FSDP, [(i, i ^ mask) for i in range(n)])


def blocks_of(pieces, here):
    mine = [p for p in pieces if p[1] in here]
    return [p[0] for p in mine], [(here.index(c), at, rows, row) for _, c, at, rows, row in mine]


def scatter_chips(terms, n):
    return [terms[0]] + [swap(terms[i], n, 2 * i) for i in range(1, n // 2)]


def exchange(v, n):
    groups = [list(range(core, n, 2)) for core in range(2)]
    return lax.all_to_all(v, FSDP, 0, 0, axis_index_groups=groups)


def plane_sum(v, n):
    groups = [list(range(core, n, 2)) for core in range(2)]
    return lax.psum_scatter(v, FSDP, scatter_dimension=0, axis_index_groups=groups)


def line(v, step):
    pairs = [(0, 3), (3, 0), (1, 2), (2, 1)] if step == 1 else [(0, 1), (1, 0), (2, 3), (3, 2)]
    return lax.ppermute(v, REP, pairs)


def per_device_tokens(
    n,
    tokens,
    starts,
    routes,
    norm1_gain,
    norm1_bias,
    query_weight,
    query_bias,
    key_weight,
    value_weight,
    value_bias,
    out_weight,
    out_bias,
    norm2_gain,
    norm2_bias,
    expert_in,
    expert_in_bias,
    expert_out,
    expert_out_bias,
    cotangent,
):
    index = lax.axis_index(FSDP)
    me = index.astype(jnp.int32).reshape(1)
    tok_count, width = tokens.shape
    shard = width // n
    ff_shard = expert_out.shape[1]
    ff_pair = 2 * ff_shard

    vectors = [norm1_gain, norm1_bias, query_bias, value_bias, out_bias, norm2_gain, norm2_bias]
    n_vec = len(vectors) + EXPERTS
    payload = call_pack(
        (query_weight, key_weight, value_weight, out_weight),
        jnp.stack(vectors),
        expert_out_bias,
        expert_in_bias,
    )
    along, across = swap(payload, n, 2), swap(payload, n, 4)
    top, bottom, three = call_halves(payload, along, across)
    top_got, bottom_got = swap(top, n, 4), swap(bottom, n, 2)
    rows, half = payload.shape[0], top.shape[0]
    w_attn = [payload, along, across, top_got, bottom_got]
    w_attn += [swap(three, n, 1), swap(top_got, n, 1), swap(bottom_got, n, 1)]
    lay_attn = [(i, None, m, 0, rows) for i, m in enumerate((0, 2, 4))]
    lay_attn += [(5, i, m, 0, rows) for i, m in enumerate((1, 3, 5))]
    lay_attn += [(3, None, 6, 0, half), (4, None, 6, half, rows - half)]
    lay_attn += [(6, None, 7, 0, half), (7, None, 7, half, rows - half)]

    route_ids = routes[:, 0]
    member = (route_ids[:, None] == jnp.arange(EXPERTS, dtype=jnp.int32)[None, :]).astype(jnp.int32)
    rank = jnp.sum(jnp.cumsum(member, 0) * member, 1) - 1
    padded = (jnp.sum(member, 0) + 15) // 16
    base = jnp.cumsum(padded) - padded
    slots = tok_count + 16 * (EXPERTS - 1)
    position = (jnp.sum(member * base[None, :], 1) * 16 + rank).astype(jnp.int32)
    position_row, route_row = position[None, :], route_ids[None, :]
    begin = jnp.minimum(base, (slots - CAP) // 16)
    meta = jnp.stack([begin, base - begin, base - begin + padded], 1).reshape(1, 3 * EXPERTS) * 16
    meta = meta.astype(jnp.int32)
    down_other = swap(expert_out, n, 1)

    meta_row = jnp.pad((meta // 16).astype(F32), ((0, 0), (0, LANES - meta.shape[1])))
    columns, sorted_grad = call_columns_and_sort(
        n, expert_in, position_row, slots, cotangent, meta_row, (top,)
    )
    w_mine = exchange(hold((columns,), (w_attn[6], w_attn[7]))[0], n)
    grad_along, grad_across = swap(sorted_grad, n, 2), swap(sorted_grad, n, 4)

    qkv, mixed, lse, n1, vec, in_bias = call_attention_forward(
        n, me, starts, tokens, w_attn, lay_attn, n_vec
    )
    hidden, sorted_two = call_mix_out(
        n,
        me,
        mixed,
        tokens,
        vec,
        position_row,
        slots,
        w_attn,
        lay_attn,
    )
    tok_along, tok_across = swap(sorted_two, n, 2), swap(sorted_two, n, 4)
    (w_mine,) = hold((w_mine,), (sorted_two,))
    w_pair = (w_mine, swap(w_mine, n, 1))

    calls = ((0,), (1, 2), (3,))
    sizes = tuple(len(call) for call in calls)
    dsl, acts, dps = [], [], []

    def run(call, metas, token_pieces, grad_pieces, res):
        d, res, a, p = call_experts(
            call,
            n_vec,
            me,
            metas,
            in_bias,
            *blocks_of(token_pieces, call),
            *blocks_of(grad_pieces, call),
            w_pair,
            (expert_out, down_other),
            res,
            n // 2,
        )
        dsl.extend(d)
        acts.append(a)
        dps.append(p)
        return res

    def meta_of(rows):
        return rows[:, : 3 * EXPERTS].astype(jnp.int32) * 16

    token_pieces = [(sorted_two, 0, 0, slots, 0)]
    grad_pieces = [(sorted_grad, 0, 0, slots, 0)]
    res = run(calls[0], meta, token_pieces, grad_pieces, None)
    tops, bottoms = call_two_halves((tok_along, tok_across), (grad_along, grad_across), (dps[0],))
    tops, bottoms = swap(tops, n, 4), swap(bottoms, n, 2)
    half, low = slots // 32 * 16, sorted_grad.shape[0] // 32 * 16
    rest = slots - half
    token_pieces += [(tok_along, 1, 0, slots, 0), (tok_across, 2, 0, slots, 0)]
    token_pieces += [(tops, 3, 0, half, 0), (bottoms, 3, half, rest, 0)]
    grad_pieces += [(grad_along, 1, 0, slots, 0), (grad_across, 2, 0, slots, 0)]
    grad_pieces += [(tops, 3, 0, low, half), (bottoms, 3, low, slots - low, rest)]
    meta_xy = meta_of(
        jnp.concatenate([grad_along[slots : slots + 1], grad_across[slots : slots + 1]], 0)
    )
    meta_d = meta_of(bottoms[-16:-15])
    meta_rel = jnp.concatenate([meta, meta_xy, meta_d], 0)
    res = run(calls[1], meta_xy, token_pieces, grad_pieces, res)
    res = run(calls[2], meta_d, token_pieces, grad_pieces, res)
    got_dsl = scatter_chips(dsl, n)

    at = lax.axis_index(REP)
    kept = jnp.where((at == 0) | (at == 3), 1, 0).astype(jnp.int32).reshape(1)
    down_keep, *down_send = call_down_grads(
        me,
        meta_rel,
        *blocks_of(grad_pieces, range(n // 2)),
        acts,
        sizes,
        (got_dsl[1],),
    )
    down_got = [swap(v, n, 1) for v in down_send]

    g_hidden, g_mixed, vec_grads, g_out = call_mix_out_backward(
        n,
        me,
        position_row,
        route_row,
        hidden,
        cotangent,
        vec,
        mixed,
        got_dsl,
        w_attn,
        lay_attn,
        (down_keep,),
    )
    (res,) = hold((res,), (g_out,))
    got_res = plane_sum(res, n)
    d_keep, d_send = call_pair_down(kept, down_keep, down_got, (g_out,))
    d_got = line(d_send, 0)
    in_keep, in_bias_keep, in_bias_send, *in_send = call_in_grads(
        n,
        me,
        meta_rel,
        *blocks_of(token_pieces, range(n // 2)),
        dps,
        sizes,
        (d_send,),
    )
    *in_send, in_bias_send = hold((*in_send, in_bias_send), (in_keep,))
    in_other, in_bias_other = [swap(v, n, 1) for v in in_send], swap(in_bias_send, n, 1)

    first = width // LANES // 3
    span = first * LANES
    g_first, keep_one, send_one = call_attention_backward_one(
        n, me, starts, qkv, lse, n1, g_mixed, g_out, first, (in_keep,)
    )
    i_terms, bias_term, *d_parts = call_pair_in(
        in_keep, in_other, in_bias_keep, in_bias_other, d_keep, d_got, 1, (g_first,)
    )
    d_first = line(d_parts[0], 1)
    i_plane = exchange(i_terms, n)
    (send_one,) = hold((send_one,), (i_terms,))
    other_one = swap(send_one, n, 1)
    input_grad, keep_two, send_two = call_attention_backward_two(
        n,
        me,
        starts,
        tokens,
        vec,
        vec_grads,
        qkv,
        lse,
        n1,
        g_mixed,
        g_hidden,
        g_first,
        w_attn,
        lay_attn,
        n_vec,
        first,
        (i_terms,),
    )
    send_two, d_second = hold((send_two, d_parts[1]), (keep_two, d_first))
    other_two = swap(send_two, n, 1)
    d_across = (d_first, line(d_second, 1))
    i_keep, *i_send = call_split_rows(kept, i_plane, (keep_two,))
    i_got = [line(v, 0) for v in i_send]
    p_terms = call_pair_shares((keep_one, other_one), (keep_two, other_two), (keep_two,))
    d_total, i_part = call_line_sums(
        (d_parts[0], d_second), d_across, i_keep, i_got, (p_terms,)
    )
    d_rest, i_across = line(d_total, 2), line(i_part, 1)
    (p_terms,) = hold((p_terms,), (d_total,))
    p_plane = exchange(p_terms, n)
    p_keep, p_send = call_attention_shares(kept, p_plane, bias_term)
    sum_down = call_down_result(kept, d_total, d_rest, (p_send,))
    p_got = line(p_send, 0)
    (i_total,) = call_sums([(i_part, i_across)], (sum_down,))
    i_rest = line(i_total, 2)
    (p_part,) = call_sums([(p_keep, p_got)], (i_total,))
    p_across = line(p_part, 1)
    (p_total,) = call_sums([(p_part, p_across)])
    p_rest = line(p_total, 2)
    output = call_finish_output(position_row, hidden, route_row, vec, got_res, (p_total,))
    sum_in = call_in_result(kept, i_total, i_rest, (output,))
    sum_out, sum_query, sum_key, sum_value, _, sum_in_bias, sum_down_bias, *sum_vec = (
        call_attention_result(
            kept, p_total, p_rest, width, span, n_vec, ff_shard, (output,)
        )
    )
    sum_vec = [v.reshape(shard) for v in sum_vec]
    return (
        output,
        input_grad,
        sum_vec[0],
        sum_vec[1],
        sum_query,
        sum_vec[2],
        sum_key,
        sum_value,
        sum_vec[3],
        sum_out,
        sum_vec[4],
        sum_vec[5],
        sum_vec[6],
        sum_in,
        sum_in_bias,
        sum_down,
        sum_down_bias,
    )


def plan_of(n, replicas):
    if n == 8 and replicas == 4:
        return lambda *args: per_device_tokens(n, *args)
    return per_device_weights


def solution(mesh):
    in_specs = (
        P((FSDP, REP), None),
        P((FSDP, REP), None),
        P((FSDP, REP), None),
        P(FSDP),
        P(FSDP),
        P(FSDP, None),
        P(FSDP),
        P(FSDP, None),
        P(FSDP, None),
        P(FSDP),
        P(FSDP, None),
        P(FSDP),
        P(FSDP),
        P(FSDP),
        P(None, FSDP, None),
        P(None, FSDP),
        P(None, FSDP, None),
        P(None, FSDP),
        P((FSDP, REP), None),
    )
    out_specs = (
        P((FSDP, REP), None),
        P((FSDP, REP), None),
        P(FSDP),
        P(FSDP),
        P(FSDP, None),
        P(FSDP),
        P(FSDP, None),
        P(FSDP, None),
        P(FSDP),
        P(FSDP, None),
        P(FSDP),
        P(FSDP),
        P(FSDP),
        P(None, FSDP, None),
        P(None, FSDP),
        P(None, FSDP, None),
        P(None, FSDP),
    )
    per_device = plan_of(mesh.shape[FSDP], mesh.shape[REP])
    return jax.shard_map(
        per_device, mesh=mesh, in_specs=in_specs, out_specs=out_specs, check_vma=False
    )
```

```python
import jax
import jax.numpy as jnp
from jax import lax
from jax.experimental import pallas as pl
from jax.experimental.pallas import tpu as pltpu
from jax.sharding import PartitionSpec as P

FSDP = "fsdp"
REP = "rep"
HEAD = 64
EXPERTS = 3
CAP = 208


EPSILON = 1e-05
MASKED = -1000000000.0


def normalize(inputs, gain, shift):
    mean = jnp.mean(inputs, -1, keepdims=True)
    centred = inputs - mean
    inverse = lax.rsqrt(jnp.mean(centred * centred, -1, keepdims=True) + EPSILON)
    return centred * inverse * gain + shift


def norm_back(inputs, gain, gradient):
    mean = jnp.mean(inputs, -1, keepdims=True)
    centred = inputs - mean
    inverse = lax.rsqrt(jnp.mean(centred * centred, -1, keepdims=True) + EPSILON)
    normed = centred * inverse
    grad_normed = gradient * gain
    grad_inputs = inverse * (
        grad_normed
        - jnp.mean(grad_normed, -1, keepdims=True)
        - normed * jnp.mean(grad_normed * normed, -1, keepdims=True)
    )
    return (grad_inputs, jnp.sum(gradient * normed, 0), jnp.sum(gradient, 0))


def gelu_exact(inputs):
    return 0.5 * inputs * (1.0 + lax.erf(inputs * 0.7071067811865476))


def gelu_slope(inputs):
    return (
        0.5 * (1.0 + lax.erf(inputs * 0.7071067811865476))
        + inputs * jnp.exp(-0.5 * inputs * inputs) * 0.3989422804014327
    )


def per_device_weights(
    tokens,
    starts,
    routes,
    norm1_gain,
    norm1_bias,
    query_weight,
    query_bias,
    key_weight,
    value_weight,
    value_bias,
    out_weight,
    out_bias,
    norm2_gain,
    norm2_bias,
    expert_in,
    expert_in_bias,
    expert_out,
    expert_out_bias,
    cotangent,
):
    seq_rows = starts.shape[0]
    tok_count = tokens.shape[0]
    seq_len = tok_count // seq_rows
    model_width = tokens.shape[1]
    head_count = model_width // HEAD
    head_shape = (seq_rows, seq_len, head_count, HEAD)
    scale_factor = HEAD ** (-0.5)
    gain_one, shift_one, w_query, b_query, w_key, w_value, b_value, w_out, b_out = (
        lax.all_gather(norm1_gain, FSDP, axis=0, tiled=True),
        lax.all_gather(norm1_bias, FSDP, axis=0, tiled=True),
        lax.all_gather(query_weight, FSDP, axis=0, tiled=True),
        lax.all_gather(query_bias, FSDP, axis=0, tiled=True),
        lax.all_gather(key_weight, FSDP, axis=0, tiled=True),
        lax.all_gather(value_weight, FSDP, axis=0, tiled=True),
        lax.all_gather(value_bias, FSDP, axis=0, tiled=True),
        lax.all_gather(out_weight, FSDP, axis=0, tiled=True),
        lax.all_gather(out_bias, FSDP, axis=0, tiled=True),
    )
    resid_in = tokens.astype(jnp.float32)
    normed_one = normalize(
        resid_in, gain_one.astype(jnp.float32), shift_one.astype(jnp.float32)
    ).astype(jnp.bfloat16)
    queries = (
        (
            jnp.dot(normed_one, w_query, preferred_element_type=jnp.float32)
            + b_query.astype(jnp.float32)
        )
        .astype(jnp.bfloat16)
        .reshape(head_shape)
    )
    keys_mat = (
        jnp.dot(normed_one, w_key, preferred_element_type=jnp.float32)
        .astype(jnp.bfloat16)
        .reshape(head_shape)
    )
    values = (
        (
            jnp.dot(normed_one, w_value, preferred_element_type=jnp.float32)
            + b_value.astype(jnp.float32)
        )
        .astype(jnp.bfloat16)
        .reshape(head_shape)
    )
    position = jnp.arange(seq_len, dtype=jnp.int32)
    segment = jnp.sum((position[None, :, None] >= starts[:, None, :]).astype(jnp.int32), -1)
    same_seg = (segment[:, :, None] == segment[:, None, :])[:, None]

    def scores_of(query_part, key_part):
        raw_scores = (
            jnp.einsum("rqhd,rkhd->rhqk", query_part, key_part, preferred_element_type=jnp.float32)
            * scale_factor
        )
        return jnp.where(same_seg, raw_scores, MASKED)

    scores = scores_of(queries, keys_mat)
    row_max = jnp.max(scores, -1, keepdims=True)
    exp_scores = jnp.exp(scores - row_max)
    row_total = jnp.sum(exp_scores, -1, keepdims=True)
    log_total = row_max + jnp.log(row_total)
    probs_low = (exp_scores / row_total).astype(jnp.bfloat16)
    mixed = jnp.einsum("rhqk,rkhd->rqhd", probs_low, values, preferred_element_type=jnp.float32)
    mixed = mixed.reshape(tok_count, model_width).astype(jnp.bfloat16)
    hidden = (
        resid_in
        + jnp.dot(mixed, w_out, preferred_element_type=jnp.float32)
        + b_out.astype(jnp.float32)
    )
    gain_two, shift_two, w_in, b_in, w_down, b_down = (
        lax.all_gather(norm2_gain, FSDP, axis=0, tiled=True),
        lax.all_gather(norm2_bias, FSDP, axis=0, tiled=True),
        lax.all_gather(expert_in, FSDP, axis=1, tiled=True),
        lax.all_gather(expert_in_bias, FSDP, axis=1, tiled=True),
        lax.all_gather(expert_out, FSDP, axis=1, tiled=True),
        lax.all_gather(expert_out_bias, FSDP, axis=1, tiled=True),
    )
    normed_two = normalize(
        hidden, gain_two.astype(jnp.float32), shift_two.astype(jnp.float32)
    ).astype(jnp.bfloat16)
    route_ids = routes[:, 0]
    member = (route_ids[:, None] == jnp.arange(EXPERTS, dtype=jnp.int32)[None, :]).astype(jnp.int32)
    rank = jnp.sum(jnp.cumsum(member, 0) * member, 1) - 1
    slot_ids = route_ids * CAP + rank
    packed = (
        jnp.zeros((EXPERTS * CAP, model_width), jnp.bfloat16)
        .at[slot_ids]
        .set(normed_two)
        .reshape(EXPERTS, CAP, model_width)
    )
    pre_act = (
        jnp.einsum("ecd,edf->ecf", packed, w_in, preferred_element_type=jnp.float32)
        + b_in.astype(jnp.float32)[:, None, :]
    )
    act_low = gelu_exact(pre_act).astype(jnp.bfloat16)
    result = (
        jnp.einsum("ecf,efd->ecd", act_low, w_down, preferred_element_type=jnp.float32)
        + b_down.astype(jnp.float32)[:, None, :]
    )
    routed = result.reshape(EXPERTS * CAP, model_width)[slot_ids]
    output = (hidden + routed).astype(jnp.bfloat16)
    gain_two_back, w_in_back, w_down_back = (
        lax.all_gather(norm2_gain, FSDP, axis=0, tiled=True),
        lax.all_gather(expert_in, FSDP, axis=1, tiled=True),
        lax.all_gather(expert_out, FSDP, axis=1, tiled=True),
    )
    grad_output = cotangent.astype(jnp.float32)
    grad_packed = (
        jnp.zeros((EXPERTS * CAP, model_width), jnp.bfloat16)
        .at[slot_ids]
        .set(cotangent)
        .reshape(EXPERTS, CAP, model_width)
    )
    grad_down_bias = jnp.sum(grad_packed.astype(jnp.float32), 1)
    grad_down = jnp.einsum("ecf,ecd->efd", act_low, grad_packed, preferred_element_type=jnp.float32)
    grad_act = jnp.einsum(
        "ecd,efd->ecf", grad_packed, w_down_back, preferred_element_type=jnp.float32
    )
    grad_pre = (grad_act * gelu_slope(pre_act)).astype(jnp.bfloat16)
    grad_in_bias = jnp.sum(grad_pre.astype(jnp.float32), 1)
    grad_in = jnp.einsum("ecd,ecf->edf", packed, grad_pre, preferred_element_type=jnp.float32)
    grad_slots = jnp.einsum(
        "ecf,edf->ecd", grad_pre, w_in_back, preferred_element_type=jnp.float32
    ).reshape(EXPERTS * CAP, model_width)
    grad_normed_two = grad_slots[slot_ids]
    grad_from_norm, grad_gain_two, grad_shift_two = norm_back(
        hidden, gain_two_back.astype(jnp.float32), grad_normed_two
    )
    grad_hidden = grad_output + grad_from_norm
    column_in, column_down = (
        lax.psum_scatter(
            grad_in.astype(jnp.bfloat16), REP, scatter_dimension=2, tiled=True
        ).astype(jnp.float32),
        lax.psum_scatter(
            grad_down.astype(jnp.bfloat16), REP, scatter_dimension=2, tiled=True
        ).astype(jnp.float32),
    )
    share_in, share_down, part_gain_two, part_shift_two, part_in_bias, part_down_bias = (
        lax.psum_scatter(column_in, FSDP, scatter_dimension=1, tiled=True),
        lax.psum_scatter(column_down, FSDP, scatter_dimension=1, tiled=True),
        lax.psum_scatter(grad_gain_two, FSDP, scatter_dimension=0, tiled=True),
        lax.psum_scatter(grad_shift_two, FSDP, scatter_dimension=0, tiled=True),
        lax.psum_scatter(grad_in_bias, FSDP, scatter_dimension=1, tiled=True),
        lax.psum_scatter(grad_down_bias, FSDP, scatter_dimension=1, tiled=True),
    )
    sum_in, sum_down, stack_gain_two, stack_shift_two, stack_in_bias, stack_down_bias = (
        lax.all_gather(share_in.astype(jnp.bfloat16), REP, axis=2, tiled=True).astype(
            share_in.dtype
        ),
        lax.all_gather(share_down.astype(jnp.bfloat16), REP, axis=2, tiled=True).astype(
            share_down.dtype
        ),
        lax.all_gather(part_gain_two[None].astype(jnp.bfloat16), REP, axis=0, tiled=True).astype(
            jnp.float32
        ),
        lax.all_gather(part_shift_two[None].astype(jnp.bfloat16), REP, axis=0, tiled=True).astype(
            jnp.float32
        ),
        lax.all_gather(part_in_bias[None].astype(jnp.bfloat16), REP, axis=0, tiled=True).astype(
            jnp.float32
        ),
        lax.all_gather(part_down_bias[None].astype(jnp.bfloat16), REP, axis=0, tiled=True).astype(
            jnp.float32
        ),
    )
    sum_gain_two = jnp.sum(stack_gain_two, 0)
    sum_shift_two = jnp.sum(stack_shift_two, 0)
    sum_in_bias = jnp.sum(stack_in_bias, 0)
    sum_down_bias = jnp.sum(stack_down_bias, 0)
    gain_one_back, w_query_back, w_key_back, w_value_back, w_out_back = (
        lax.all_gather(norm1_gain, FSDP, axis=0, tiled=True),
        lax.all_gather(query_weight, FSDP, axis=0, tiled=True),
        lax.all_gather(key_weight, FSDP, axis=0, tiled=True),
        lax.all_gather(value_weight, FSDP, axis=0, tiled=True),
        lax.all_gather(out_weight, FSDP, axis=0, tiled=True),
    )
    grad_branch = grad_hidden.astype(jnp.bfloat16)
    grad_out_bias = jnp.sum(grad_branch.astype(jnp.float32), 0)
    grad_out_weight = jnp.einsum(
        "td,te->de", mixed, grad_branch, preferred_element_type=jnp.float32
    )
    grad_mixed = (
        jnp.einsum("te,de->td", grad_branch, w_out_back, preferred_element_type=jnp.float32)
        .astype(jnp.bfloat16)
        .reshape(head_shape)
    )
    scores_again = scores_of(queries, keys_mat)
    probs = jnp.exp(scores_again - log_total)
    probs_again = probs.astype(jnp.bfloat16)
    grad_values = jnp.einsum(
        "rhqk,rqhd->rkhd", probs_again, grad_mixed, preferred_element_type=jnp.float32
    )
    grad_values = grad_values.astype(jnp.bfloat16).reshape(tok_count, model_width)
    grad_probs = jnp.einsum(
        "rqhd,rkhd->rhqk", grad_mixed, values, preferred_element_type=jnp.float32
    )
    grad_scores = (probs * (grad_probs - jnp.sum(grad_probs * probs, -1, keepdims=True))).astype(
        jnp.bfloat16
    )
    grad_queries = (
        (
            jnp.einsum("rhqk,rkhd->rqhd", grad_scores, keys_mat, preferred_element_type=jnp.float32)
            * scale_factor
        )
        .astype(jnp.bfloat16)
        .reshape(tok_count, model_width)
    )
    grad_keys = (
        (
            jnp.einsum("rhqk,rqhd->rkhd", grad_scores, queries, preferred_element_type=jnp.float32)
            * scale_factor
        )
        .astype(jnp.bfloat16)
        .reshape(tok_count, model_width)
    )
    grad_query_bias = jnp.sum(grad_queries.astype(jnp.float32), 0)
    grad_value_bias = jnp.sum(grad_values.astype(jnp.float32), 0)
    grad_query_weight = jnp.einsum(
        "td,te->de", normed_one, grad_queries, preferred_element_type=jnp.float32
    )
    grad_key_weight = jnp.einsum(
        "td,te->de", normed_one, grad_keys, preferred_element_type=jnp.float32
    )
    grad_value_weight = jnp.einsum(
        "td,te->de", normed_one, grad_values, preferred_element_type=jnp.float32
    )
    grad_normed_one = (
        jnp.einsum("te,de->td", grad_queries, w_query_back, preferred_element_type=jnp.float32)
        + jnp.einsum("te,de->td", grad_keys, w_key_back, preferred_element_type=jnp.float32)
        + jnp.einsum("te,de->td", grad_values, w_value_back, preferred_element_type=jnp.float32)
    )
    grad_from_first, grad_gain_one, grad_shift_one = norm_back(
        resid_in, gain_one_back.astype(jnp.float32), grad_normed_one
    )
    input_grad = grad_hidden + grad_from_first
    column_query, column_key, column_value, column_out = (
        lax.psum_scatter(
            grad_query_weight.astype(jnp.bfloat16), REP, scatter_dimension=1, tiled=True
        ).astype(jnp.float32),
        lax.psum_scatter(
            grad_key_weight.astype(jnp.bfloat16), REP, scatter_dimension=1, tiled=True
        ).astype(jnp.float32),
        lax.psum_scatter(
            grad_value_weight.astype(jnp.bfloat16), REP, scatter_dimension=1, tiled=True
        ).astype(jnp.float32),
        lax.psum_scatter(
            grad_out_weight.astype(jnp.bfloat16), REP, scatter_dimension=1, tiled=True
        ).astype(jnp.float32),
    )
    (
        share_query,
        share_key,
        share_value,
        share_out,
        part_gain_one,
        part_shift_one,
        part_query_bias,
        part_value_bias,
        part_out_bias,
    ) = (
        lax.psum_scatter(column_query, FSDP, scatter_dimension=0, tiled=True),
        lax.psum_scatter(column_key, FSDP, scatter_dimension=0, tiled=True),
        lax.psum_scatter(column_value, FSDP, scatter_dimension=0, tiled=True),
        lax.psum_scatter(column_out, FSDP, scatter_dimension=0, tiled=True),
        lax.psum_scatter(grad_gain_one, FSDP, scatter_dimension=0, tiled=True),
        lax.psum_scatter(grad_shift_one, FSDP, scatter_dimension=0, tiled=True),
        lax.psum_scatter(grad_query_bias, FSDP, scatter_dimension=0, tiled=True),
        lax.psum_scatter(grad_value_bias, FSDP, scatter_dimension=0, tiled=True),
        lax.psum_scatter(grad_out_bias, FSDP, scatter_dimension=0, tiled=True),
    )
    (
        sum_query,
        sum_key,
        sum_value,
        sum_out,
        stack_gain_one,
        stack_shift_one,
        stack_query_bias,
        stack_value_bias,
        stack_out_bias,
    ) = (
        lax.all_gather(share_query.astype(jnp.bfloat16), REP, axis=1, tiled=True).astype(
            share_query.dtype
        ),
        lax.all_gather(share_key.astype(jnp.bfloat16), REP, axis=1, tiled=True).astype(
            share_key.dtype
        ),
        lax.all_gather(share_value.astype(jnp.bfloat16), REP, axis=1, tiled=True).astype(
            share_value.dtype
        ),
        lax.all_gather(share_out.astype(jnp.bfloat16), REP, axis=1, tiled=True).astype(
            share_out.dtype
        ),
        lax.all_gather(part_gain_one[None].astype(jnp.bfloat16), REP, axis=0, tiled=True).astype(
            jnp.float32
        ),
        lax.all_gather(part_shift_one[None].astype(jnp.bfloat16), REP, axis=0, tiled=True).astype(
            jnp.float32
        ),
        lax.all_gather(
            part_query_bias[None].astype(jnp.bfloat16), REP, axis=0, tiled=True
        ).astype(jnp.float32),
        lax.all_gather(
            part_value_bias[None].astype(jnp.bfloat16), REP, axis=0, tiled=True
        ).astype(jnp.float32),
        lax.all_gather(part_out_bias[None].astype(jnp.bfloat16), REP, axis=0, tiled=True).astype(
            jnp.float32
        ),
    )
    sum_gain_one = jnp.sum(stack_gain_one, 0)
    sum_shift_one = jnp.sum(stack_shift_one, 0)
    sum_query_bias = jnp.sum(stack_query_bias, 0)
    sum_value_bias = jnp.sum(stack_value_bias, 0)
    sum_out_bias = jnp.sum(stack_out_bias, 0)
    return (
        output,
        input_grad,
        sum_gain_one,
        sum_shift_one,
        sum_query,
        sum_query_bias,
        sum_key,
        sum_value,
        sum_value_bias,
        sum_out,
        sum_out_bias,
        sum_gain_two,
        sum_shift_two,
        sum_in,
        sum_in_bias,
        sum_down,
        sum_down_bias,
    )


LANES = 128
BF = jnp.bfloat16
F32 = jnp.float32
VMEM_BYTES = 60 * 1024 * 1024
SMEM = pl.BlockSpec(memory_space=pltpu.SMEM)
VMEM = pl.BlockSpec(memory_space=pltpu.VMEM)
ANYWHERE = pl.BlockSpec(memory_space=pl.ANY)


def dot_nn(a, b):
    return lax.dot_general(a, b, (((1,), (0,)), ((), ())), preferred_element_type=F32)


def dot_nt(a, b):
    return lax.dot_general(a, b, (((1,), (1,)), ((), ())), preferred_element_type=F32)


def dot_tn(a, b):
    return lax.dot_general(a, b, (((0,), (0,)), ((), ())), preferred_element_type=F32)


def kernel_call(body, named, out_shape, in_specs, out_specs, scratch, args, alias=None):
    return pl.pallas_call(
        body,
        out_shape=out_shape,
        in_specs=in_specs,
        out_specs=out_specs,
        scratch_shapes=scratch,
        input_output_aliases=alias or {},
        compiler_params=pltpu.CompilerParams(vmem_limit_bytes=VMEM_BYTES),
        name=named.__name__,
    )(*args)


def hold(values, done):
    shapes = tuple(jax.ShapeDtypeStruct(v.shape, v.dtype) for v in values)
    return kernel_call(
        lambda *refs: None,
        hold,
        shapes,
        [ANYWHERE] * (len(values) + len(done)),
        (ANYWHERE,) * len(values),
        [],
        (*values, *done),
        {i: i for i in range(len(values))},
    )


def sds(shape, dtype=BF):
    return jax.ShapeDtypeStruct(shape, dtype)


def center(v):
    mean = jnp.mean(v, -1, keepdims=True)
    centred = v - mean
    inverse = lax.rsqrt(jnp.mean(centred * centred, -1, keepdims=True) + EPSILON)
    return centred * inverse, inverse


def norm_grad(normed, inverse, gain, gradient):
    dn = gradient * gain
    return inverse * (
        dn - jnp.mean(dn, -1, keepdims=True) - normed * jnp.mean(dn * normed, -1, keepdims=True)
    )


def exact_rows(place, v):
    high = v.astype(BF)
    rest = (v - high.astype(F32)).astype(BF)
    return dot_tn(place, high) + dot_tn(place, rest)


def segment_bias(starts, length, segs):
    col = lax.broadcasted_iota(jnp.int32, (length, 1), 0)
    row = lax.broadcasted_iota(jnp.int32, (1, length), 1)
    col_seg = jnp.zeros((length, 1), jnp.int32)
    row_seg = jnp.zeros((1, length), jnp.int32)
    for k in range(segs):
        col_seg = col_seg + jnp.where(col >= starts[0, k], 1, 0)
        row_seg = row_seg + jnp.where(row >= starts[0, k], 1, 0)
    return jnp.where(col_seg == row_seg, 0.0, MASKED)


def cuts(layout, start, count):
    found = []
    for i, part, mask, offset, rows in layout:
        low, high = max(offset, start), min(offset + rows, start + count)
        if low < high:
            found.append((i, part, mask, low - offset, low - start, high - low))
    return found


def rows_of(ref, part, row, rows):
    return ref.at[pl.ds(row, rows)] if part is None else ref.at[part, pl.ds(row, rows)]


def load_weight(me, refs, layout, segment, shard, dst, sems):
    copies = []
    for k, (i, part, mask, row, at, rows) in enumerate(cuts(layout, segment * shard, shard)):
        to = pl.multiple_of((me ^ mask) * shard + at, 16)
        src = rows_of(refs[i], part, row, rows)
        copy = pltpu.make_async_copy(src, dst.at[pl.ds(to, rows)], sems.at[k])
        copy.start()
        copies.append(copy)
    return copies


def attention_forward(n, layout, segs, n_vec, *refs):
    count = 1 + max(i for i, *_ in layout)
    me_ref, starts, tokens = refs[:3]
    pieces = refs[3 : 3 + count]
    qkv, mixed, lse, n1_out, vec, b_in = refs[3 + count : 9 + count]
    weights, smalls, v_t, mixed_t, bias, sems, small_sems = refs[9 + count :]
    tok, width = tokens.shape
    shard = width // n
    me = me_ref[0]
    small_copies = []
    for k, (i, part, mask, row, at, rows) in enumerate(cuts(layout, 4 * shard, 16)):
        copy = pltpu.make_async_copy(
            rows_of(pieces[i], part, row, rows),
            smalls.at[mask, pl.ds(at, rows)],
            small_sems.at[k],
        )
        copy.start()
        small_copies.append(copy)
    copies = []
    for i in range(3):
        cols = weights.at[:, pl.ds(i * width, width)]
        copies.append(load_weight(me, pieces, layout, i, shard, cols, sems.at[i]))
    bias[...] = segment_bias(starts, tok, segs)
    normed, _ = center(tokens[...].astype(F32))
    for copy in small_copies:
        copy.wait()
    lane = lax.broadcasted_iota(jnp.int32, (LANES, width), 0)
    col = lax.broadcasted_iota(jnp.int32, (LANES, width), 1)
    total = jnp.zeros((16, width), F32)
    for m in range(n):
        spread = ((col - (me ^ m) * shard == lane) & (lane < shard)).astype(F32).astype(BF)
        total = total + dot_nn(smalls[m, :, :LANES], spread)
    vec[...] = total
    half_ff = width // 2
    mine, other = smalls[0].astype(F32)[:, :half_ff], smalls[1].astype(F32)[:, :half_ff]
    first = me % 2 == 0
    b_in[:, :half_ff] = jnp.where(first, mine, other)
    b_in[:, half_ff:] = jnp.where(first, other, mine)
    n1_out[...] = (normed * vec[0:1, :] + vec[1:2, :]).astype(BF)
    for i in range(3):
        for copy in copies[i]:
            copy.wait()
        part = dot_nn(n1_out[...], weights[:, i * width : (i + 1) * width])
        if i != 1:
            part = part + (vec[2:3, :] if i == 0 else vec[3:4, :])
        part = part.astype(BF)
        if i == 0:
            part = part * jnp.asarray(HEAD**-0.5, BF)
        qkv[:, i * width : (i + 1) * width] = part
    v_t[...] = qkv[:, 2 * width :].T
    half = lax.broadcasted_iota(jnp.int32, (1, LANES), 1) < HEAD

    def pair(p, carry):
        at = pl.multiple_of(p * LANES, LANES)
        q_pair = qkv[:, pl.ds(at, LANES)]
        k_pair = qkv[:, pl.ds(pl.multiple_of(width + p * LANES, LANES), LANES)]
        for s in range(2):
            q_one = jnp.where(half if s == 0 else ~half, q_pair, jnp.zeros_like(q_pair))
            scores = dot_nt(k_pair, q_one) + bias[...]
            top = jnp.max(scores, 0, keepdims=True)
            e = jnp.exp(scores - top)
            total = jnp.sum(e, 0, keepdims=True)
            probs = (e * (1.0 / total)).astype(BF)
            rows = pl.ds(pl.multiple_of(p * LANES + s * HEAD, HEAD), HEAD)
            mixed_t[rows, :] = dot_nn(v_t[rows, :], probs)
            lse[pl.ds(2 * p + s, 1), :] = top + jnp.log(total)
        return carry

    lax.fori_loop(0, width // LANES, pair, 0)
    mixed[...] = mixed_t[...].T.astype(BF)


def call_attention_forward(n, me, starts, tokens, pieces, layout, n_vec):
    tok, width = tokens.shape
    heads16 = (width // HEAD + 7) // 8 * 8
    f32_row = sds((16, width), F32)
    return kernel_call(
        lambda *refs: attention_forward(n, layout, starts.shape[1], n_vec, *refs),
        attention_forward,
        (sds((tok, 3 * width)), sds((tok, width)), sds((heads16, tok), F32), sds((tok, width)))
        + (f32_row, f32_row),
        [SMEM, SMEM, VMEM] + [ANYWHERE] * len(pieces),
        (VMEM,) * 6,
        [
            pltpu.VMEM((width, 3 * width), BF),
            pltpu.VMEM((n, 16, width), BF),
            pltpu.VMEM((width, tok), BF),
            pltpu.VMEM((width, tok), F32),
            pltpu.VMEM((tok, tok), F32),
            pltpu.SemaphoreType.DMA((3, len(layout))),
            pltpu.SemaphoreType.DMA((len(layout),)),
        ],
        (me, starts, tokens, *pieces),
    )


def head_grads(first, pairs, width, qkv, lse, g_mixed, bias, k_t, gq_t, g_qkv):
    half = lax.broadcasted_iota(jnp.int32, (1, LANES), 1) < HEAD
    span = pairs * LANES

    def pair(p, carry):
        def cols(part):
            return pl.ds(pl.multiple_of(part * width + (first + p) * LANES, LANES), LANES)

        def put(part):
            return pl.ds(pl.multiple_of(part * span + p * LANES, LANES), LANES)

        q_pair, k_pair, v_pair = qkv[:, cols(0)], qkv[:, cols(1)], qkv[:, cols(2)]
        gm_pair = g_mixed[:, cols(0)]
        gv, gk = [], []
        for s in range(2):
            own = half if s == 0 else ~half
            q_one = jnp.where(own, q_pair, jnp.zeros_like(q_pair))
            gm_one = jnp.where(own, gm_pair, jnp.zeros_like(gm_pair))
            scores = dot_nt(k_pair, q_one) + bias[...]
            probs = jnp.exp(scores - lse[pl.ds(2 * (first + p) + s, 1), :])
            g_probs = dot_nt(v_pair, gm_one)
            delta = jnp.sum(probs * g_probs, 0, keepdims=True)
            g_scores = (probs * (g_probs - delta)).astype(BF)
            gv.append(dot_nn(probs.astype(BF), gm_pair))
            gk.append(dot_nn(g_scores, q_pair))
            rows = pl.ds(pl.multiple_of(p * LANES + s * HEAD, HEAD), HEAD)
            gq_t[rows, :] = dot_nn(k_t[rows, :], g_scores)
        g_qkv[:, put(2)] = jnp.where(half, gv[0], gv[1]).astype(BF)
        g_qkv[:, put(1)] = jnp.where(half, gk[0], gk[1]).astype(BF)
        return carry

    at = slice(width + first * LANES, width + first * LANES + span)
    k_t[...] = qkv[:, at].T
    lax.fori_loop(0, pairs, pair, 0)
    g_qkv[:, :span] = (gq_t[...].T * (HEAD**-0.5)).astype(BF)


def share_rows(n, me, shard, whole, keep, send, sems):
    outs = []
    core = me % 2
    for k in range(n // 2):
        for i, dst in enumerate((keep, send)):
            owner = 2 * k + (core if i == 0 else 1 - core)
            src = whole.at[pl.ds(pl.multiple_of(owner * shard, 16), shard)]
            copy = pltpu.make_async_copy(src, dst.at[k], sems.at[2 * k + i])
            copy.start()
            outs.append(copy)
    return outs


def attention_backward_one(n, segs, pairs, deps, *refs):
    me_ref, starts, qkv, lse, n1, g_mixed, g_out = refs[:7]
    g_qkv, keep, send = refs[7 + deps : 10 + deps]
    k_t, gq_t, bias, g_w, out_sems = refs[10 + deps :]
    tok, width = n1.shape
    span = pairs * LANES
    bias[...] = segment_bias(starts, tok, segs)
    head_grads(0, pairs, width, qkv, lse, g_mixed, bias, k_t, gq_t, g_qkv)
    g_w[:, :width] = g_out[...]
    for i in range(3):
        part = dot_tn(n1[...], g_qkv[:, i * span : (i + 1) * span])
        g_w[:, width + i * span : width + (i + 1) * span] = part.astype(BF)
    for copy in share_rows(n, me_ref[0], width // n, g_w, keep, send, out_sems):
        copy.wait()


def call_attention_backward_one(n, me, starts, qkv, lse, n1, g_mixed, g_out, pairs, deps=()):
    tok, width = n1.shape
    shard, span = width // n, pairs * LANES
    cols = width + 3 * span
    return kernel_call(
        lambda *refs: attention_backward_one(n, starts.shape[1], pairs, len(deps), *refs),
        attention_backward_one,
        (sds((tok, 3 * span)),) + (sds((n // 2, shard, cols)),) * 2,
        [SMEM, SMEM] + [VMEM] * 5 + [ANYWHERE] * len(deps),
        (VMEM, ANYWHERE, ANYWHERE),
        [
            pltpu.VMEM((span, tok), BF),
            pltpu.VMEM((span, tok), F32),
            pltpu.VMEM((tok, tok), F32),
            pltpu.VMEM((width, cols), BF),
            pltpu.SemaphoreType.DMA((n,)),
        ],
        (me, starts, qkv, lse, n1, g_mixed, g_out, *deps),
    )


def attention_backward_two(n, layout, segs, n_vec, first, deps, *refs):
    count = 1 + max(i for i, *_ in layout)
    me_ref, starts, tokens, vec, vec_grads, qkv, lse, n1, g_mixed, g_hidden, g_first = refs[:11]
    pieces = refs[11 : 11 + count]
    at = 11 + count + deps
    input_grad, keep, send = refs[at : at + 3]
    weights, k_t, gq_t, bias, g_qkv, g_w, v_rows, sems, out_sems = refs[at + 3 :]
    tok, width = tokens.shape
    shard = width // n
    span_one = first * LANES
    span = width - span_one
    me = me_ref[0]
    copies = []
    for i in range(3):
        cols = weights.at[:, pl.ds(i * width, width)]
        copies += load_weight(me, pieces, layout, i, shard, cols, sems.at[i])
    bias[...] = segment_bias(starts, tok, segs)
    head_grads(first, span // LANES, width, qkv, lse, g_mixed, bias, k_t, gq_t, g_qkv)
    for i in range(3):
        cols = slice(i * span, (i + 1) * span)
        g_w[:, cols] = dot_tn(n1[...], g_qkv[:, cols]).astype(BF)
    for copy in copies:
        copy.wait()
    g_n1 = jnp.zeros((tok, width), F32)
    for i in range(3):
        one = slice(i * width, i * width + span_one)
        two = slice(i * width + span_one, (i + 1) * width)
        g_n1 = g_n1 + dot_nt(g_first[:, i * span_one : (i + 1) * span_one], weights[:, one])
        g_n1 = g_n1 + dot_nt(g_qkv[:, i * span : (i + 1) * span], weights[:, two])
    normed, inverse = center(tokens[...].astype(F32))
    input_grad[...] = g_hidden[...] + norm_grad(normed, inverse, vec[0:1, :], g_n1)
    v_rows[...] = jnp.zeros_like(v_rows)
    v_rows[0:1, :] = jnp.sum(g_n1 * normed, 0, keepdims=True)
    v_rows[1:2, :] = jnp.sum(g_n1, 0, keepdims=True)
    for row, i in ((2, 0), (3, 2)):
        one = g_first[:, i * span_one : (i + 1) * span_one].astype(F32)
        two = g_qkv[:, i * span : (i + 1) * span].astype(F32)
        v_rows[row : row + 1, :span_one] = jnp.sum(one, 0, keepdims=True)
        v_rows[row : row + 1, span_one:] = jnp.sum(two, 0, keepdims=True)
    v_rows[4:n_vec, :] = vec_grads[4:n_vec, :]
    g_w[:, 3 * span :] = v_rows[...].T.astype(BF)
    for copy in share_rows(n, me, shard, g_w, keep, send, out_sems):
        copy.wait()


def call_attention_backward_two(
    n,
    me,
    starts,
    tokens,
    vec,
    vec_grads,
    qkv,
    lse,
    n1,
    g_mixed,
    g_hidden,
    g_first,
    pieces,
    layout,
    n_vec,
    first,
    deps=(),
):
    tok, width = tokens.shape
    shard, span = width // n, width - first * LANES
    cols = 3 * span + LANES
    return kernel_call(
        lambda *refs: attention_backward_two(
            n, layout, starts.shape[1], n_vec, first, len(deps), *refs
        ),
        attention_backward_two,
        (sds((tok, width), F32),) + (sds((n // 2, shard, cols)),) * 2,
        [SMEM, SMEM] + [VMEM] * 9 + [ANYWHERE] * (len(pieces) + len(deps)),
        (VMEM, ANYWHERE, ANYWHERE),
        [
            pltpu.VMEM((width, 3 * width), BF),
            pltpu.VMEM((span, tok), BF),
            pltpu.VMEM((span, tok), F32),
            pltpu.VMEM((tok, tok), F32),
            pltpu.VMEM((tok, 3 * span), BF),
            pltpu.VMEM((width, cols), BF),
            pltpu.VMEM((LANES, width), F32),
            pltpu.SemaphoreType.DMA((3, len(layout))),
            pltpu.SemaphoreType.DMA((n,)),
        ],
        (
            me,
            starts,
            tokens,
            vec,
            vec_grads,
            qkv,
            lse,
            n1,
            g_mixed,
            g_hidden,
            g_first,
            *pieces,
            *deps,
        ),
    )


def place_rows(position, slots):
    row = lax.broadcasted_iota(jnp.int32, (slots, position.shape[1]), 0)
    return (row == position[...]).astype(F32).astype(BF)


def member_rows(route, first):
    row = lax.broadcasted_iota(jnp.int32, (16, route.shape[1]), 0)
    return (row == route[...] + first).astype(F32).astype(BF)


def mix_out(n, layout, slots, deps, *refs):
    count = 1 + max(i for i, *_ in layout)
    me_ref, mixed, tokens, vec, position = refs[:5]
    pieces = refs[5 : 5 + count]
    hidden, sorted_two, weights, sems = refs[5 + count + deps :]
    width = tokens.shape[1]
    copies = load_weight(me_ref[0], pieces, layout, 3, width // n, weights, sems)
    place = place_rows(position, slots)
    for copy in copies:
        copy.wait()
    value = tokens[...].astype(F32) + dot_nn(mixed[...], weights[...]) + vec[4:5, :]
    hidden[...] = value
    normed, _ = center(value)
    sorted_two[...] = dot_nn(place, (normed * vec[5:6, :] + vec[6:7, :]).astype(BF)).astype(BF)


def call_mix_out(n, me, mixed, tokens, vec, position, slots, pieces, layout, deps=()):
    tok, width = tokens.shape
    return kernel_call(
        lambda *refs: mix_out(n, layout, slots, len(deps), *refs),
        mix_out,
        (sds((tok, width), F32), sds((slots, width))),
        [SMEM] + [VMEM] * 4 + [ANYWHERE] * (len(pieces) + len(deps)),
        (VMEM, VMEM),
        [pltpu.VMEM((width, width), BF), pltpu.SemaphoreType.DMA((len(layout),))],
        (me, mixed, tokens, vec, position, *pieces, *deps),
    )


def pack(count, *refs):
    weights = refs[:count]
    vectors, down_bias, in_bias, out, small = refs[count:]
    rows = weights[0].shape[0]
    for i, ref in enumerate(weights):
        out[i * rows : (i + 1) * rows, :] = ref[...]
    small[...] = jnp.zeros_like(small)
    n_vec = vectors.shape[0]
    small[:n_vec, :rows] = vectors[...].astype(F32)
    small[n_vec : n_vec + EXPERTS, :rows] = down_bias[...].astype(F32)
    small[n_vec + EXPERTS : n_vec + 2 * EXPERTS, : in_bias.shape[1]] = in_bias[...].astype(F32)
    out[count * rows :, :] = small[...].astype(BF)


def call_pack(weights, vectors, down_bias, in_bias):
    rows, width = weights[0].shape
    return kernel_call(
        lambda *refs: pack(len(weights), *refs),
        pack,
        sds((len(weights) * rows + 16, width)),
        [VMEM] * (len(weights) + 3),
        VMEM,
        [pltpu.VMEM((16, width), F32)],
        (*weights, vectors, down_bias, in_bias),
    )


def load_blocks(refs, layout, dst, sems):
    copies = []
    for i, (ref, (block, offset, rows, row)) in enumerate(zip(refs, layout, strict=True)):
        copy = pltpu.make_async_copy(
            ref.at[pl.ds(row, rows)], dst.at[block, pl.ds(offset, rows)], sems.at[i]
        )
        copy.start()
        copies.append(copy)
    return copies


def start_all(copies):
    for copy in copies:
        copy.start()
    return copies


def wait_all(copies):
    for copy in copies:
        copy.wait()


def window(meta, block, e):
    begin = pl.multiple_of(meta[block, 3 * e], 16)
    row = lax.broadcasted_iota(jnp.int32, (CAP, 1), 0)
    return pl.ds(begin, CAP), (row >= meta[block, 3 * e + 1]) & (row < meta[block, 3 * e + 2])


def experts(chips, bias_row, lay_x, lay_g, deps, *refs):
    nb, cx, cg, cw = len(chips), len(lay_x), len(lay_g), 2
    me_ref, meta, b_in = refs[:3]
    at = 3
    x_refs, at = refs[at : at + cx], at + cx
    g_refs, at = refs[at : at + cg], at + cg
    w_refs, at = refs[at : at + cw], at + cw
    down = refs[at : at + 2]
    at += 2 + deps
    dsl, (res, act_out, dp_out) = refs[at : at + nb], refs[at + nb : at + nb + 3]
    at += nb + 3
    x_all, g_all, w_in, w_down, res_s, dsl_s, xs, gs, act_s, dp_s = refs[at : at + 10]
    sx, sg, sw, sd, so, sa = refs[at + 10 :]
    rows = w_refs[0].shape[2]
    me = me_ref[0]
    half = w_down.shape[1] // 2
    core = me % 2
    loads = load_blocks(x_refs, lay_x, x_all, sx) + load_blocks(g_refs, lay_g, g_all, sg)
    weights = []
    for e in range(EXPERTS):
        copies = []
        for i, ref in enumerate(w_refs):
            for k in range(ref.shape[0]):
                owner = 2 * k + (core if i == 0 else 1 - core)
                to = pl.ds(pl.multiple_of(owner * rows, 16), rows)
                copies.append(pltpu.make_async_copy(ref.at[k, e], w_in.at[e, to], sw.at[e, i, k]))
        for i, ref in enumerate(down):
            to = pl.multiple_of((core if i == 0 else 1 - core) * half, 16)
            copies.append(pltpu.make_async_copy(ref.at[e], w_down.at[e, pl.ds(to, half)], sd.at[e, i]))
        weights.append(start_all(copies))
    res_s[...] = jnp.zeros_like(res_s)
    dsl_s[...] = jnp.zeros_like(dsl_s)
    wait_all(loads)
    outs = []
    for e in range(EXPERTS):
        spans = []
        for b in range(nb):
            span, inside = window(meta, b, e)
            spans.append((span, inside))
            g = g_all[b, span, :]
            xs[b * CAP : (b + 1) * CAP, :] = x_all[b, span, :]
            gs[b * CAP : (b + 1) * CAP, :] = jnp.where(inside, g, jnp.zeros_like(g))
        wait_all(weights[e])
        pre = dot_nn(xs[...], w_in[e]) + b_in[bias_row + e : bias_row + e + 1, :]
        cdf = 0.5 * (1.0 + lax.erf(pre * 0.7071067811865476))
        act = (pre * cdf).astype(BF)
        slope = cdf + pre * jnp.exp(-0.5 * pre * pre) * 0.3989422804014327
        dp = (dot_nt(gs[...], w_down[e]) * slope).astype(BF)
        act_s[e] = act
        dp_s[e] = dp
        outs += start_all(
            [
                pltpu.make_async_copy(act_s.at[e], act_out.at[e], sa.at[0, e]),
                pltpu.make_async_copy(dp_s.at[e], dp_out.at[e], sa.at[1, e]),
            ]
        )
        for dst, value in ((dsl_s, dot_nt(dp, w_in[e])), (res_s, dot_nn(act, w_down[e]))):
            value = value.astype(BF)
            for b, (span, inside) in enumerate(spans):
                dst[b, span, :] = jnp.where(inside, value[b * CAP : (b + 1) * CAP], dst[b, span, :])
    for b in range(nb):
        outs += start_all(
            [
                pltpu.make_async_copy(dsl_s.at[b], dsl[b], so.at[0, b]),
                pltpu.make_async_copy(res_s.at[b], res.at[(me // 2) ^ chips[b]], so.at[1, b]),
            ]
        )
    wait_all(outs)


def call_experts(chips, bias_row, me, meta, b_in, xp, lay_x, gp, lay_g, wp, down, res, blocks):
    nb, rows, width = len(chips), max(o + r for _, o, r, _ in lay_x), xp[0].shape[1]
    ff = 2 * down[0].shape[1]
    dma = pltpu.SemaphoreType.DMA
    deps = () if res is None else (res,)
    alias = {} if res is None else {5 + len(xp) + len(gp) + len(wp): nb}
    out = kernel_call(
        lambda *refs: experts(chips, bias_row, lay_x, lay_g, len(deps), *refs),
        experts,
        (sds((rows, width)),) * nb
        + (sds((blocks, rows, width)),)
        + (sds((EXPERTS, nb * CAP, ff)),) * 2,
        [SMEM, SMEM, VMEM] + [ANYWHERE] * (len(xp) + len(gp) + len(wp) + 2 + len(deps)),
        (ANYWHERE,) * (nb + 3),
        [pltpu.VMEM((nb, rows, width), BF)] * 2
        + [pltpu.VMEM((EXPERTS, width, ff), BF), pltpu.VMEM((EXPERTS, ff, width), BF)]
        + [pltpu.VMEM((nb, rows, width), BF)] * 2
        + [pltpu.VMEM((nb * CAP, width), BF)] * 2
        + [pltpu.VMEM((EXPERTS, nb * CAP, ff), BF)] * 2
        + [dma((len(xp),)), dma((len(gp),)), dma((EXPERTS, 2, blocks)), dma((EXPERTS, 2))]
        + [dma((2, nb)), dma((2, EXPERTS))],
        (me, meta, b_in, *xp, *gp, *wp, *down, *deps),
        alias,
    )
    return list(out[:nb]), out[nb], out[nb + 1], out[nb + 2]


def down_grads(calls, lay_g, deps, *refs):
    cg, cc = len(lay_g), len(calls)
    me_ref, meta = refs[:2]
    g_refs, acts = refs[2 : 2 + cg], refs[2 + cg : 2 + cg + cc]
    at = 2 + cg + cc + deps
    keep, send = refs[at], refs[at + 1 : at + 1 + EXPERTS]
    g_all, act_s, gs, g_down, sg, sa, so = refs[at + 1 + EXPERTS :]
    core = me_ref[0] % 2
    half = g_down.shape[1] // 2
    loads = load_blocks(g_refs, lay_g, g_all, sg)
    hidden = load_hidden(acts, calls, act_s, sa)
    wait_all(loads)
    outs = []
    for e in range(EXPERTS):
        for b in range(sum(calls)):
            span, inside = window(meta, b, e)
            g = g_all[b, span, :]
            gs[b * CAP : (b + 1) * CAP, :] = jnp.where(inside, g, jnp.zeros_like(g))
        wait_all(hidden[e])
        g_down[e] = dot_tn(act_s[e], gs[...]).astype(BF)
        for i, dst in enumerate((keep.at[e], send[e])):
            src = g_down.at[e, pl.ds(pl.multiple_of((core if i == 0 else 1 - core) * half, 16), half)]
            outs.append(pltpu.make_async_copy(src, dst, so.at[e, i]))
            outs[-1].start()
    wait_all(outs)


def load_hidden(parts, calls, dst, sems):
    hidden = []
    for e in range(EXPERTS):
        copies, first = [], 0
        for i, nb in enumerate(calls):
            rows = pl.ds(first * CAP, nb * CAP)
            copies.append(pltpu.make_async_copy(parts[i].at[e], dst.at[e, rows], sems.at[e, i]))
            first += nb
        hidden.append(start_all(copies))
    return hidden


def call_down_grads(me, meta, gp, lay_g, acts, calls, deps=()):
    rows, width = max(o + r for _, o, r, _ in lay_g), gp[0].shape[1]
    ff, blocks = acts[0].shape[2], sum(calls)
    dma = pltpu.SemaphoreType.DMA
    return kernel_call(
        lambda *refs: down_grads(calls, lay_g, len(deps), *refs),
        down_grads,
        (sds((EXPERTS, ff // 2, width)),) + (sds((ff // 2, width)),) * EXPERTS,
        [SMEM, SMEM] + [ANYWHERE] * (len(gp) + len(acts) + len(deps)),
        (ANYWHERE,) * (1 + EXPERTS),
        [
            pltpu.VMEM((blocks, rows, width), BF),
            pltpu.VMEM((EXPERTS, blocks * CAP, ff), BF),
            pltpu.VMEM((blocks * CAP, width), BF),
            pltpu.VMEM((EXPERTS, ff, width), BF),
            dma((len(gp),)),
            dma((EXPERTS, len(calls))),
            dma((EXPERTS, 2)),
        ],
        (me, meta, *gp, *acts, *deps),
    )


def in_grads(n, calls, lay_x, deps, *refs):
    cx, cc = len(lay_x), len(calls)
    me_ref, meta = refs[:2]
    x_refs, dps = refs[2 : 2 + cx], refs[2 + cx : 2 + cx + cc]
    at = 2 + cx + cc + deps
    keep, bias_keep, bias_send = refs[at : at + 3]
    send = refs[at + 3 : at + 3 + EXPERTS]
    x_all, dp_s, xs, g_in, sx, sp, so = refs[at + 3 + EXPERTS :]
    me = me_ref[0]
    _, width, ff = g_in.shape
    shard, half = width // n, ff // 2
    loads = load_blocks(x_refs, lay_x, x_all, sx)
    hidden = load_hidden(dps, calls, dp_s, sp)
    wait_all(loads)
    outs = []
    row = lax.broadcasted_iota(jnp.int32, (16, 1), 0)
    low = jnp.zeros((16, half), F32)
    high = jnp.zeros((16, half), F32)
    for e in range(EXPERTS):
        for b in range(sum(calls)):
            span, _ = window(meta, b, e)
            xs[b * CAP : (b + 1) * CAP, :] = x_all[b, span, :]
        wait_all(hidden[e])
        g_in[e] = dot_tn(xs[...], dp_s[e]).astype(BF)
        outs += share_rows(n, me, shard, g_in.at[e], keep.at[:, e], send[e], so.at[e])
        total = jnp.sum(dp_s[e].astype(F32), 0, keepdims=True)
        low = low + jnp.where(row == e, total[:, :half], 0.0)
        high = high + jnp.where(row == e, total[:, half:], 0.0)
    first_core = me % 2 == 0
    bias_keep[...] = jnp.where(first_core, low, high).astype(BF)
    bias_send[...] = jnp.where(first_core, high, low).astype(BF)
    wait_all(outs)


def call_in_grads(n, me, meta, xp, lay_x, dps, calls, deps=()):
    rows, width = max(o + r for _, o, r, _ in lay_x), xp[0].shape[1]
    ff, blocks = dps[0].shape[2], sum(calls)
    dma = pltpu.SemaphoreType.DMA
    return kernel_call(
        lambda *refs: in_grads(n, calls, lay_x, len(deps), *refs),
        in_grads,
        (sds((n // 2, EXPERTS, width // n, ff)),)
        + (sds((16, ff // 2)),) * 2
        + (sds((n // 2, width // n, ff)),) * EXPERTS,
        [SMEM, SMEM] + [ANYWHERE] * (len(xp) + len(dps) + len(deps)),
        (ANYWHERE, VMEM, VMEM) + (ANYWHERE,) * EXPERTS,
        [
            pltpu.VMEM((blocks, rows, width), BF),
            pltpu.VMEM((EXPERTS, blocks * CAP, ff), BF),
            pltpu.VMEM((blocks * CAP, width), BF),
            pltpu.VMEM((EXPERTS, width, ff), BF),
            dma((len(xp),)),
            dma((EXPERTS, len(calls))),
            dma((EXPERTS, n)),
        ],
        (me, meta, *xp, *dps, *deps),
    )


def mix_out_backward(n, layout, terms, deps, *refs):
    count = 1 + max(i for i, *_ in layout)
    me_ref, position, route, hidden, cot, vec, mixed = refs[:7]
    got = refs[7 : 7 + terms]
    pieces = refs[7 + terms : 7 + terms + count]
    at = 7 + terms + count + deps
    g_hidden, g_mixed, vec_grads, g_w = refs[at : at + 4]
    weights, sems = refs[at + 4 :]
    me = me_ref[0]
    tok, width = hidden.shape
    shard = width // n
    copies = load_weight(me, pieces, layout, 3, shard, weights, sems)
    total = got[0][...].astype(F32)
    for ref in got[1:]:
        total = total + ref[...].astype(F32)
    gradient = exact_rows(place_rows(position, total.shape[0]), total)
    normed, inverse = center(hidden[...])
    value = cot[...].astype(F32) + norm_grad(normed, inverse, vec[5:6, :], gradient)
    g_hidden[...] = value
    branch = value.astype(BF)
    vec_grads[...] = jnp.zeros_like(vec_grads)
    vec_grads[4:5, :] = jnp.sum(branch.astype(F32), 0, keepdims=True)
    vec_grads[5:6, :] = jnp.sum(gradient * normed, 0, keepdims=True)
    vec_grads[6:7, :] = jnp.sum(gradient, 0, keepdims=True)
    vec_grads[...] += dot_nn(member_rows(route, 7), cot[...])
    for copy in copies:
        copy.wait()
    g_mixed[...] = dot_nt(branch, weights[...]).astype(BF)
    g_w[...] = dot_tn(mixed[...], branch).astype(BF)


def call_mix_out_backward(
    n, me, position, route, hidden, cot, vec, mixed, got, pieces, layout, deps=()
):
    tok, width = hidden.shape
    return kernel_call(
        lambda *refs: mix_out_backward(n, layout, len(got), len(deps), *refs),
        mix_out_backward,
        (sds((tok, width), F32), sds((tok, width)), sds((16, width), F32), sds((width, width))),
        [SMEM] + [VMEM] * (6 + len(got)) + [ANYWHERE] * (len(pieces) + len(deps)),
        (VMEM,) * 4,
        [pltpu.VMEM((width, width), BF), pltpu.SemaphoreType.DMA((len(layout),))],
        (me, position, route, hidden, cot, vec, mixed, *got, *pieces, *deps),
    )


def finish_output(deps, *refs):
    position, hidden, route, vec = refs[:4]
    got = refs[4]
    out = refs[5 + deps]
    value = hidden[...] + dot_tn(place_rows(position, got.shape[0]), got[...])
    value = value + dot_tn(member_rows(route, 7), vec[...].astype(BF))
    out[...] = value.astype(BF)


def call_finish_output(position, hidden, route, vec, got, deps=()):
    return kernel_call(
        lambda *refs: finish_output(len(deps), *refs),
        finish_output,
        sds(hidden.shape),
        [VMEM] * 5 + [ANYWHERE] * len(deps),
        VMEM,
        [],
        (position, hidden, route, vec, got, *deps),
    )


def join(body, named, outs, scalars, arrays, deps=()):
    n_s, n_a, n_d, n_o = len(scalars), len(arrays), len(deps), len(outs)

    def kernel(*refs):
        at = n_s + n_a + n_d
        body(refs[:n_s], refs[n_s : n_s + n_a], refs[at : at + n_o])

    return kernel_call(
        kernel,
        named,
        tuple(outs),
        [SMEM] * n_s + [VMEM] * n_a + [ANYWHERE] * n_d,
        (VMEM,) * n_o,
        [],
        (*scalars, *arrays, *deps),
    )


def plus(*values):
    total = values[0].astype(F32)
    for value in values[1:]:
        total = total + value.astype(F32)
    return total


def call_halves(along, across, deps=()):
    rows, width = along.shape
    half = rows // 32 * 16

    def body(_, ins, outs):
        outs[0][...] = ins[0][:half]
        outs[1][...] = ins[1][half:]

    shapes = (sds((half, width)), sds((rows - half, width)))
    return join(body, call_halves, shapes, (), (along, across), deps)


def call_stack(parts, deps=()):
    def body(_, ins, outs):
        for i, ref in enumerate(ins):
            outs[0][i] = ref[...]

    shapes = (sds((len(parts), *parts[0].shape)),)
    return join(body, call_stack, shapes, (), parts, deps)[0]


def call_two_halves(first, second, deps=()):
    cuts_at = [pair[0].shape[0] // 32 * 16 for pair in (first, second)]
    width = first[0].shape[1]
    split = cuts_at[0]

    def body(_, ins, outs):
        outs[0][:split] = ins[0][:split]
        outs[0][split:] = ins[2][: cuts_at[1]]
        rest = ins[0].shape[0] - split
        outs[1][:rest] = ins[1][split:]
        outs[1][rest:] = ins[3][cuts_at[1] :]

    rows = first[0].shape[0] + second[0].shape[0]
    shapes = (sds((sum(cuts_at), width)), sds((rows - sum(cuts_at), width)))
    return join(body, call_two_halves, shapes, (), (*first, *second), deps)


def call_columns_and_sort(n, whole, position, slots, value, meta, deps):
    experts_, rows, cols = whole.shape
    pair = cols // (n // 2)

    def body(_, ins, outs):
        for k in range(n // 2):
            outs[0][k] = ins[0][:, :, k * pair : (k + 1) * pair]
        outs[1][:slots, :] = dot_nn(place_rows(ins[1], slots), ins[2][...]).astype(BF)
        outs[1][slots:, :] = jnp.zeros((16, value.shape[1]), BF)
        outs[1][slots:, :LANES] = jnp.broadcast_to(ins[3][...], (16, LANES)).astype(BF)

    shapes = (sds((n // 2, experts_, rows, pair)), sds((slots + 16, value.shape[1])))
    return join(body, call_columns_and_sort, shapes, (), (whole, position, value, meta), deps)


def call_pair_down(kept, keep, got, deps=()):
    experts_, rows, width = keep.shape
    half = rows // 2

    def body(scalars, ins, outs):
        mine = pl.multiple_of(scalars[0][0] * half, 16)
        other = pl.multiple_of((1 - scalars[0][0]) * half, 16)
        for out, at in zip(outs, (mine, other), strict=True):
            for e in range(experts_):
                part = plus(ins[0][e, pl.ds(at, half)], ins[1 + e][pl.ds(at, half)])
                out[e] = part.astype(BF)

    shapes = (sds((experts_, half, width)),) * 2
    return join(body, call_pair_down, shapes, (kept,), (keep, *got), deps)


def call_pair_in(keep, got, bias_keep, bias_got, d_keep, d_got, cut, deps=()):
    count = len(got)

    def body(_, ins, outs):
        for e in range(count):
            outs[0][:, e] = plus(ins[0][:, e], ins[5 + e][...]).astype(BF)
        outs[1][...] = plus(ins[1][...], ins[2][...]).astype(BF)
        outs[2][...] = plus(ins[3][:cut], ins[4][:cut]).astype(BF)
        outs[3][...] = plus(ins[3][cut:], ins[4][cut:]).astype(BF)

    shapes = (sds(keep.shape), sds(bias_keep.shape))
    shapes += (sds((cut, *d_keep.shape[1:])), sds((d_keep.shape[0] - cut, *d_keep.shape[1:])))
    arrays = (keep, bias_keep, bias_got, d_keep, d_got, *got)
    return join(body, call_pair_in, shapes, (), arrays, deps)


def call_split_rows(kept, whole, deps=()):
    chips, experts_, rows, ff = whole.shape
    half = rows // 2
    two = chips // 2

    def body(scalars, ins, outs):
        outs[0][...] = ins[0][:, :, pl.ds(pl.multiple_of(scalars[0][0] * half, 16), half)]
        other = pl.ds(pl.multiple_of((1 - scalars[0][0]) * half, 16), half)
        for i in range(2):
            outs[1 + i][...] = ins[0][i * two : (i + 1) * two, :, other]

    shapes = (sds((chips, experts_, half, ff)),) + (sds((two, experts_, half, ff)),) * 2
    return join(body, call_split_rows, shapes, (kept,), (whole,), deps)


def call_pair_shares(one, two, deps=()):
    chips, rows, cols_one = one[0].shape
    cols = cols_one + two[0].shape[2]

    def body(_, ins, outs):
        outs[0][:, :, :cols_one] = plus(ins[0][...], ins[1][...]).astype(BF)
        outs[0][:, :, cols_one:] = plus(ins[2][...], ins[3][...]).astype(BF)

    return join(body, call_pair_shares, (sds((chips, rows, cols)),), (), (*one, *two), deps)[0]


def call_line_sums(parts, across, i_keep, i_got, deps=()):
    cut = parts[0].shape[0]
    rest = parts[1].shape[0]
    two = i_got[0].shape[0]

    def body(_, ins, outs):
        outs[0][:cut] = plus(ins[0][...], ins[2][...]).astype(BF)
        outs[0][cut:] = plus(ins[1][...], ins[3][...]).astype(BF)
        for i in range(2):
            at = slice(i * two, (i + 1) * two)
            outs[1][at] = plus(ins[4][at], ins[5 + i][...]).astype(BF)

    shapes = (sds((cut + rest, *parts[0].shape[1:])), sds(i_keep.shape))
    return join(body, call_line_sums, shapes, (), (*parts, *across, i_keep, *i_got), deps)


def call_sums(jobs, deps=()):
    flat = [v for job in jobs for v in job]

    def body(_, ins, outs):
        at = 0
        for job, out in zip(jobs, outs, strict=True):
            out[...] = plus(*[ref[...] for ref in ins[at : at + len(job)]]).astype(BF)
            at += len(job)

    return join(body, call_sums, [sds(job[0].shape) for job in jobs], (), flat, deps)


def call_attention_shares(kept, got, bias, deps=()):
    chips, rows, cols = got.shape
    half = rows // 2

    def body(scalars, ins, outs):
        mine = pl.multiple_of(scalars[0][0] * half, 16)
        other = pl.multiple_of((1 - scalars[0][0]) * half, 16)
        for out, at in zip(outs, (mine, other), strict=True):
            out[:half, :] = plus(*[ins[0][k, pl.ds(at, half)] for k in range(chips)]).astype(BF)
            out[half:, :] = jnp.zeros((16, cols), BF)
            out[half:, : bias.shape[1]] = ins[1][...]

    shapes = (sds((half + 16, cols)),) * 2
    return join(body, call_attention_shares, shapes, (kept,), (got, bias), deps)


def call_down_result(kept, mine, got, deps=()):
    experts_, half, width = mine.shape

    def body(scalars, ins, outs):
        outs[0][:, pl.ds(pl.multiple_of(scalars[0][0] * half, 16), half)] = ins[0][...].astype(F32)
        at = pl.multiple_of((1 - scalars[0][0]) * half, 16)
        outs[0][:, pl.ds(at, half)] = ins[1][...].astype(F32)

    shape = (sds((experts_, 2 * half, width), F32),)
    return join(body, call_down_result, shape, (kept,), (mine, got), deps)[0]


def call_in_result(kept, mine, got, deps=()):
    chips, experts_, half, ff = mine.shape

    def body(scalars, ins, outs):
        for ref, which in ((ins[0], scalars[0][0]), (ins[1], 1 - scalars[0][0])):
            rows = pl.ds(pl.multiple_of(which * half, 16), half)
            for k in range(chips):
                outs[0][:, rows, k * ff : (k + 1) * ff] = ref[k].astype(F32)

    shape = (sds((experts_, 2 * half, chips * ff), F32),)
    return join(body, call_in_result, shape, (kept,), (mine, got), deps)[0]


def call_attention_result(kept, mine, got, width, span, n_vec, ff_shard, deps=()):
    half = mine.shape[0] - 16
    last = width - span
    cols_one = width + 3 * span

    def body(scalars, ins, outs):
        for ref, which in ((ins[0], scalars[0][0]), (ins[1], 1 - scalars[0][0])):
            rows = pl.ds(pl.multiple_of(which * half, 16), half)
            outs[0][rows, :] = ref[:half, :width].astype(F32)
            for i in range(3):
                one = ref[:half, width + i * span : width + (i + 1) * span]
                two = ref[:half, cols_one + i * last : cols_one + (i + 1) * last]
                outs[1 + i][rows, :span] = one.astype(F32)
                outs[1 + i][rows, span:] = two.astype(F32)
            outs[4][rows, :] = ref[:half, cols_one + 3 * last :].astype(F32)
        rows = outs[4][...].T
        outs[5][...] = ins[0][half : half + EXPERTS, :ff_shard].astype(F32)
        outs[6][...] = rows[n_vec - EXPERTS : n_vec]
        for i, out in enumerate(outs[7:]):
            out[...] = rows[i : i + 1]

    shapes = (sds((2 * half, width), F32),) * 4 + (sds((2 * half, LANES), F32),)
    shapes += (sds((EXPERTS, ff_shard), F32), sds((EXPERTS, 2 * half), F32))
    shapes += (sds((1, 2 * half), F32),) * (n_vec - EXPERTS)
    return join(body, call_attention_result, shapes, (kept,), (mine, got), deps)


def swap(v, n, mask):
    return lax.ppermute(v, FSDP, [(i, i ^ mask) for i in range(n)])


def blocks_of(pieces, here):
    mine = [p for p in pieces if p[1] in here]
    return [p[0] for p in mine], [(here.index(c), at, rows, row) for _, c, at, rows, row in mine]


def scatter_chips(terms, n):
    return [terms[0]] + [swap(terms[i], n, 2 * i) for i in range(1, n // 2)]


def exchange(v, n):
    groups = [list(range(core, n, 2)) for core in range(2)]
    return lax.all_to_all(v, FSDP, 0, 0, axis_index_groups=groups)


def plane_sum(v, n):
    groups = [list(range(core, n, 2)) for core in range(2)]
    return lax.psum_scatter(v, FSDP, scatter_dimension=0, axis_index_groups=groups)


def line(v, step):
    pairs = [(0, 3), (3, 0), (1, 2), (2, 1)] if step == 1 else [(0, 1), (1, 0), (2, 3), (3, 2)]
    return lax.ppermute(v, REP, pairs)


def per_device_tokens(
    n,
    tokens,
    starts,
    routes,
    norm1_gain,
    norm1_bias,
    query_weight,
    query_bias,
    key_weight,
    value_weight,
    value_bias,
    out_weight,
    out_bias,
    norm2_gain,
    norm2_bias,
    expert_in,
    expert_in_bias,
    expert_out,
    expert_out_bias,
    cotangent,
):
    index = lax.axis_index(FSDP)
    me = index.astype(jnp.int32).reshape(1)
    tok_count, width = tokens.shape
    shard = width // n
    ff_shard = expert_out.shape[1]
    ff_pair = 2 * ff_shard

    vectors = [norm1_gain, norm1_bias, query_bias, value_bias, out_bias, norm2_gain, norm2_bias]
    n_vec = len(vectors) + EXPERTS
    payload = call_pack(
        (query_weight, key_weight, value_weight, out_weight),
        jnp.stack(vectors),
        expert_out_bias,
        expert_in_bias,
    )
    along, across = swap(payload, n, 2), swap(payload, n, 4)
    top, bottom = call_halves(along, across)
    three = call_stack((payload, along, across), (top,))
    top_got, bottom_got = swap(top, n, 4), swap(bottom, n, 2)
    rows, half = payload.shape[0], top.shape[0]
    w_attn = [payload, along, across, top_got, bottom_got]
    w_attn += [swap(three, n, 1), swap(top_got, n, 1), swap(bottom_got, n, 1)]
    lay_attn = [(i, None, m, 0, rows) for i, m in enumerate((0, 2, 4))]
    lay_attn += [(5, i, m, 0, rows) for i, m in enumerate((1, 3, 5))]
    lay_attn += [(3, None, 6, 0, half), (4, None, 6, half, rows - half)]
    lay_attn += [(6, None, 7, 0, half), (7, None, 7, half, rows - half)]

    route_ids = routes[:, 0]
    member = (route_ids[:, None] == jnp.arange(EXPERTS, dtype=jnp.int32)[None, :]).astype(jnp.int32)
    rank = jnp.sum(jnp.cumsum(member, 0) * member, 1) - 1
    padded = (jnp.sum(member, 0) + 15) // 16
    base = jnp.cumsum(padded) - padded
    slots = tok_count + 16 * (EXPERTS - 1)
    position = (jnp.sum(member * base[None, :], 1) * 16 + rank).astype(jnp.int32)
    position_row, route_row = position[None, :], route_ids[None, :]
    begin = jnp.minimum(base, (slots - CAP) // 16)
    meta = jnp.stack([begin, base - begin, base - begin + padded], 1).reshape(1, 3 * EXPERTS) * 16
    meta = meta.astype(jnp.int32)
    down_other = swap(expert_out, n, 1)

    meta_row = jnp.pad((meta // 16).astype(F32), ((0, 0), (0, LANES - meta.shape[1])))
    columns, sorted_grad = call_columns_and_sort(
        n, expert_in, position_row, slots, cotangent, meta_row, (top,)
    )
    w_mine = exchange(hold((columns,), (w_attn[6], w_attn[7]))[0], n)
    grad_along, grad_across = swap(sorted_grad, n, 2), swap(sorted_grad, n, 4)

    qkv, mixed, lse, n1, vec, in_bias = call_attention_forward(
        n, me, starts, tokens, w_attn, lay_attn, n_vec
    )
    hidden, sorted_two = call_mix_out(
        n,
        me,
        mixed,
        tokens,
        vec,
        position_row,
        slots,
        w_attn,
        lay_attn,
    )
    tok_along, tok_across = swap(sorted_two, n, 2), swap(sorted_two, n, 4)
    (w_mine,) = hold((w_mine,), (sorted_two,))
    w_pair = (w_mine, swap(w_mine, n, 1))

    calls = ((0,), (1, 2), (3,))
    sizes = tuple(len(call) for call in calls)
    dsl, acts, dps = [], [], []

    def run(call, metas, token_pieces, grad_pieces, res):
        d, res, a, p = call_experts(
            call,
            n_vec,
            me,
            metas,
            in_bias,
            *blocks_of(token_pieces, call),
            *blocks_of(grad_pieces, call),
            w_pair,
            (expert_out, down_other),
            res,
            n // 2,
        )
        dsl.extend(d)
        acts.append(a)
        dps.append(p)
        return res

    def meta_of(rows):
        return rows[:, : 3 * EXPERTS].astype(jnp.int32) * 16

    token_pieces = [(sorted_two, 0, 0, slots, 0)]
    grad_pieces = [(sorted_grad, 0, 0, slots, 0)]
    res = run(calls[0], meta, token_pieces, grad_pieces, None)
    tops, bottoms = call_two_halves((tok_along, tok_across), (grad_along, grad_across), (dps[0],))
    tops, bottoms = swap(tops, n, 4), swap(bottoms, n, 2)
    half, low = slots // 32 * 16, sorted_grad.shape[0] // 32 * 16
    rest = slots - half
    token_pieces += [(tok_along, 1, 0, slots, 0), (tok_across, 2, 0, slots, 0)]
    token_pieces += [(tops, 3, 0, half, 0), (bottoms, 3, half, rest, 0)]
    grad_pieces += [(grad_along, 1, 0, slots, 0), (grad_across, 2, 0, slots, 0)]
    grad_pieces += [(tops, 3, 0, low, half), (bottoms, 3, low, slots - low, rest)]
    meta_xy = meta_of(
        jnp.concatenate([grad_along[slots : slots + 1], grad_across[slots : slots + 1]], 0)
    )
    meta_d = meta_of(bottoms[-16:-15])
    meta_rel = jnp.concatenate([meta, meta_xy, meta_d], 0)
    res = run(calls[1], meta_xy, token_pieces, grad_pieces, res)
    res = run(calls[2], meta_d, token_pieces, grad_pieces, res)
    got_dsl = scatter_chips(dsl, n)

    at = lax.axis_index(REP)
    kept = jnp.where((at == 0) | (at == 3), 1, 0).astype(jnp.int32).reshape(1)
    down_keep, *down_send = call_down_grads(
        me,
        meta_rel,
        *blocks_of(grad_pieces, range(n // 2)),
        acts,
        sizes,
        (got_dsl[1],),
    )
    down_got = [swap(v, n, 1) for v in down_send]

    g_hidden, g_mixed, vec_grads, g_out = call_mix_out_backward(
        n,
        me,
        position_row,
        route_row,
        hidden,
        cotangent,
        vec,
        mixed,
        got_dsl,
        w_attn,
        lay_attn,
        (down_keep,),
    )
    (res,) = hold((res,), (g_out,))
    got_res = plane_sum(res, n)
    d_keep, d_send = call_pair_down(kept, down_keep, down_got, (g_out,))
    d_got = line(d_send, 0)
    in_keep, in_bias_keep, in_bias_send, *in_send = call_in_grads(
        n,
        me,
        meta_rel,
        *blocks_of(token_pieces, range(n // 2)),
        dps,
        sizes,
        (d_send,),
    )
    *in_send, in_bias_send = hold((*in_send, in_bias_send), (in_keep,))
    in_other, in_bias_other = [swap(v, n, 1) for v in in_send], swap(in_bias_send, n, 1)

    first = width // LANES // 3
    span = first * LANES
    g_first, keep_one, send_one = call_attention_backward_one(
        n, me, starts, qkv, lse, n1, g_mixed, g_out, first, (in_keep,)
    )
    i_terms, bias_term, *d_parts = call_pair_in(
        in_keep, in_other, in_bias_keep, in_bias_other, d_keep, d_got, 1, (g_first,)
    )
    d_first = line(d_parts[0], 1)
    i_plane = exchange(i_terms, n)
    (send_one,) = hold((send_one,), (i_terms,))
    other_one = swap(send_one, n, 1)
    input_grad, keep_two, send_two = call_attention_backward_two(
        n,
        me,
        starts,
        tokens,
        vec,
        vec_grads,
        qkv,
        lse,
        n1,
        g_mixed,
        g_hidden,
        g_first,
        w_attn,
        lay_attn,
        n_vec,
        first,
        (i_terms,),
    )
    send_two, d_second = hold((send_two, d_parts[1]), (keep_two, d_first))
    other_two = swap(send_two, n, 1)
    d_across = (d_first, line(d_second, 1))
    i_keep, *i_send = call_split_rows(kept, i_plane, (keep_two,))
    i_got = [line(v, 0) for v in i_send]
    p_terms = call_pair_shares((keep_one, other_one), (keep_two, other_two), (keep_two,))
    d_total, i_part = call_line_sums(
        (d_parts[0], d_second), d_across, i_keep, i_got, (p_terms,)
    )
    d_rest, i_across = line(d_total, 2), line(i_part, 1)
    (p_terms,) = hold((p_terms,), (d_total,))
    p_plane = exchange(p_terms, n)
    p_keep, p_send = call_attention_shares(kept, p_plane, bias_term)
    sum_down = call_down_result(kept, d_total, d_rest, (p_send,))
    p_got = line(p_send, 0)
    (i_total,) = call_sums([(i_part, i_across)], (sum_down,))
    i_rest = line(i_total, 2)
    (p_part,) = call_sums([(p_keep, p_got)], (i_total,))
    p_across = line(p_part, 1)
    (p_total,) = call_sums([(p_part, p_across)])
    p_rest = line(p_total, 2)
    output = call_finish_output(position_row, hidden, route_row, vec, got_res, (p_total,))
    sum_in = call_in_result(kept, i_total, i_rest, (output,))
    sum_out, sum_query, sum_key, sum_value, _, sum_in_bias, sum_down_bias, *sum_vec = (
        call_attention_result(
            kept, p_total, p_rest, width, span, n_vec, ff_shard, (output,)
        )
    )
    sum_vec = [v.reshape(shard) for v in sum_vec]
    return (
        output,
        input_grad,
        sum_vec[0],
        sum_vec[1],
        sum_query,
        sum_vec[2],
        sum_key,
        sum_value,
        sum_vec[3],
        sum_out,
        sum_vec[4],
        sum_vec[5],
        sum_vec[6],
        sum_in,
        sum_in_bias,
        sum_down,
        sum_down_bias,
    )


def plan_of(n, replicas):
    if n == 8 and replicas == 4:
        return lambda *args: per_device_tokens(n, *args)
    return per_device_weights


def solution(mesh):
    in_specs = (
        P((FSDP, REP), None),
        P((FSDP, REP), None),
        P((FSDP, REP), None),
        P(FSDP),
        P(FSDP),
        P(FSDP, None),
        P(FSDP),
        P(FSDP, None),
        P(FSDP, None),
        P(FSDP),
        P(FSDP, None),
        P(FSDP),
        P(FSDP),
        P(FSDP),
        P(None, FSDP, None),
        P(None, FSDP),
        P(None, FSDP, None),
        P(None, FSDP),
        P((FSDP, REP), None),
    )
    out_specs = (
        P((FSDP, REP), None),
        P((FSDP, REP), None),
        P(FSDP),
        P(FSDP),
        P(FSDP, None),
        P(FSDP),
        P(FSDP, None),
        P(FSDP, None),
        P(FSDP),
        P(FSDP, None),
        P(FSDP),
        P(FSDP),
        P(FSDP),
        P(None, FSDP, None),
        P(None, FSDP),
        P(None, FSDP, None),
        P(None, FSDP),
    )
    per_device = plan_of(mesh.shape[FSDP], mesh.shape[REP])
    return jax.shard_map(
        per_device, mesh=mesh, in_specs=in_specs, out_specs=out_specs, check_vma=False
    )
```
